32 devices in a mesh: replica: 4 (over y, core), shard: 8 (over z, x).
Axes of the slice: x: 2, y: 2, z: 4, core: 2. Of those that a mesh axis runs over, the one named last changes fastest.
Arguments:
- images: bfloat16 [256, 197, 768], P(('replica', 'shard')), may hold values from -6 to 6
- image_adapter_index: int32 [256], P(('replica', 'shard')), may hold values from 0 to 7
- device_image_count: int32 [32], P(('replica', 'shard')), may hold values from 1 to 8, as said below
- cotangent: bfloat16 [256, 197, 768], P(('replica', 'shard')), may hold values from -6 to 6
- query_key_value_weight: bfloat16 [768, 2304], P('shard'), may hold values from -0.21875 to 0.21875
- frozen_output_weight: bfloat16 [768, 768], P('shard'), may hold values from -0.875 to 0.875
- frozen_dispatch_weight: bfloat16 [768, 16], P('shard'), may hold values from -0.109375 to 0.109375
- query_key_value_first: bfloat16 [768, 128], P('shard'), may hold values from -0.21875 to 0.21875
- query_key_value_second: bfloat16 [128, 2304], P(None, 'shard'), may hold values from -0.75 to 0.75
- output_adapter_first: bfloat16 [768, 128], P('shard'), may hold values from -0.875 to 0.875
- output_adapter_second: bfloat16 [128, 768], P(None, 'shard'), may hold values from -0.75 to 0.75
- dispatch_adapter_first: bfloat16 [768, 128], P('shard'), may hold values from -0.21875 to 0.21875
- dispatch_adapter_second: bfloat16 [128, 16], P(None, 'shard'), may hold values from -0.375 to 0.375
- frozen_up_weight: bfloat16 [16, 768, 3072], P('shard'), may hold values from -2.5 to 2.5
- frozen_down_weight: bfloat16 [16, 3072, 768], P('shard'), may hold values from -0.875 to 0.875
- up_adapter_first: bfloat16 [16, 768, 128], P('shard'), may hold values from -2.5 to 2.5
- up_adapter_second: bfloat16 [16, 128, 3072], P('shard'), may hold values from -0.75 to 0.75
- down_adapter_first: bfloat16 [16, 3072, 128], P('shard'), may hold values from -0.109375 to 0.109375
- down_adapter_second: bfloat16 [16, 128, 768], P('shard'), may hold values from -4 to 4
Outputs:
- block_out: bfloat16 [256, 197, 768], P(('replica', 'shard'))
- input_grad: float32 [256, 197, 768], P(('replica', 'shard'))
- grad_qkv_a: float32 [768, 128], P('shard')
- grad_qkv_b: float32 [128, 2304], P(None, 'shard')
- grad_out_a: float32 [768, 128], P('shard')
- grad_out_b: float32 [128, 768], P(None, 'shard')
- grad_route_a: float32 [768, 128], P('shard')
- grad_route_b: float32 [128, 16], P(None, 'shard')
- grad_up_a: float32 [16, 768, 128], P('shard')
- grad_up_b: float32 [16, 128, 3072], P('shard')
- grad_down_a: float32 [16, 3072, 128], P('shard')
- grad_down_b: float32 [16, 128, 768], P('shard')
The draws below stay inside these ranges and needn't reach their ends.
Inputs may be any that keep to these rules, and one draw needn't show every extreme that they name: `device_image_count`: each device's live images are its first slots; some device holds 8 live images.
All inputs are finite; a program needn't handle non-finite values.
Results may differ from the reference program's by a relative error of at most 0.025.
Values may be sent and summed in bfloat16 or wider, within the bound.
No kernel may reach another device: no remote copies, remote signals or barrier semaphores. Data moves between devices by JAX's collectives and lax.ppermute only.
A program may use at most 256 MiB of HBM per device.

```python
import jax
import jax.numpy as jnp
from jax import lax

MODEL_WIDTH = 768
HEADS = 12
HEAD_DIM = 64
EXPERT_HIDDEN = 3072
TOK = 197
ADAPTERS = 8
RANK = 16
IMG_DEV = 8
EXPERT_SLOTS = 16
RANK_LANES = 128
IMAGES = 256
DEVICES = 32


def draw_device_image_count(key, part):
    key = jax.random.fold_in(key, 11)
    first, second = jax.random.split(key)
    counts = jax.random.randint(first, (DEVICES,), 1, IMG_DEV + 1)
    chosen = jax.random.randint(second, (), 0, DEVICES)
    return counts.at[chosen].set(IMG_DEV).astype(jnp.int32)


def with_ends(drawn, key, smallest, top_value):
    place = [jax.random.randint(jax.random.fold_in(key, axis), (), 0, length) for axis, length in enumerate(drawn.shape)]
    main_axis = drawn.shape.index(max(drawn.shape))
    neighbour = place[:main_axis] + [(place[main_axis] + 1) % drawn.shape[main_axis]] + place[main_axis + 1:]
    return drawn.at[tuple(place)].set(smallest).at[tuple(neighbour)].set(top_value)


def block_scale(key, extent, cuts, least, top_value):
    loudness, own = 1.0, jax.random.fold_in(key, 6)
    for dim, shards_of in cuts:
        steps = jnp.exp(jax.random.uniform(jax.random.fold_in(own, dim), (shards_of,), jnp.float32, least / len(cuts), top_value / len(cuts)))
        loudness = loudness * jnp.repeat(steps, extent[dim] // shards_of).reshape([-1 if axis == dim else 1 for axis in range(len(extent))])
    return loudness


def gaussian(stream_key, dims, scale, limit, cuts=(), held_as=jnp.bfloat16):
    factor_of = block_scale(stream_key, dims, cuts, -0.22, 0.18) if cuts else 1.0
    array = jax.random.normal(stream_key, dims, jnp.float32) * scale * factor_of
    return jnp.minimum(jnp.maximum(array, -limit), limit).astype(held_as)


def setup_inputs(seed: int = 0) -> dict:
    streams_of = jax.random.split(jax.random.key(seed), 20)
    return {
        "images": gaussian(streams_of[0], (IMAGES, TOK, MODEL_WIDTH), 1.0, 6.0, ((0, 32),)),
        "image_adapter_index": with_ends(jax.random.randint(streams_of[1], (IMAGES,), 0, ADAPTERS), jax.random.fold_in(streams_of[1], 1), 0, ADAPTERS - 1).astype(jnp.int32),
        "device_image_count": draw_device_image_count(jax.random.fold_in(streams_of[19], 71), 0),
        "cotangent": gaussian(streams_of[3], (IMAGES, TOK, MODEL_WIDTH), 1.0, 6.0, ((0, 32),)),
        "query_key_value_weight": gaussian(streams_of[4], (MODEL_WIDTH, 3 * MODEL_WIDTH), MODEL_WIDTH ** -0.5, 0.21875, ((0, 8),)),
        "frozen_output_weight": gaussian(streams_of[5], (MODEL_WIDTH, MODEL_WIDTH), (MODEL_WIDTH // 16) ** -0.5, 0.875, ((0, 8),)),
        "frozen_dispatch_weight": gaussian(streams_of[6], (MODEL_WIDTH, EXPERT_SLOTS), (4 * MODEL_WIDTH) ** -0.5, 0.109375, ((0, 8),)),
        "query_key_value_first": gaussian(streams_of[7], (MODEL_WIDTH, RANK_LANES), MODEL_WIDTH ** -0.5, 0.21875, ((0, 8),)),
        "query_key_value_second": gaussian(streams_of[8], (RANK_LANES, 3 * MODEL_WIDTH), 64 ** -0.5, 0.75, ((1, 8),)),
        "output_adapter_first": gaussian(streams_of[9], (MODEL_WIDTH, RANK_LANES), (MODEL_WIDTH // 16) ** -0.5, 0.875, ((0, 8),)),
        "output_adapter_second": gaussian(streams_of[10], (RANK_LANES, MODEL_WIDTH), 64 ** -0.5, 0.75, ((1, 8),)),
        "dispatch_adapter_first": gaussian(streams_of[11], (MODEL_WIDTH, RANK_LANES), MODEL_WIDTH ** -0.5, 0.21875, ((0, 8),)),
        "dispatch_adapter_second": gaussian(streams_of[12], (RANK_LANES, EXPERT_SLOTS), 256 ** -0.5, 0.375, ((1, 8),)),
        "frozen_up_weight": gaussian(streams_of[13], (EXPERT_SLOTS, MODEL_WIDTH, EXPERT_HIDDEN), (max(MODEL_WIDTH // 128, 1)) ** -0.5, 2.5, ((0, 8),)),
        "frozen_down_weight": gaussian(streams_of[14], (EXPERT_SLOTS, EXPERT_HIDDEN, MODEL_WIDTH), (EXPERT_HIDDEN // 64) ** -0.5, 0.875, ((0, 8),)),
        "up_adapter_first": gaussian(streams_of[15], (EXPERT_SLOTS, MODEL_WIDTH, RANK_LANES), (max(MODEL_WIDTH // 128, 1)) ** -0.5, 2.5, ((0, 8),)),
        "up_adapter_second": gaussian(streams_of[16], (EXPERT_SLOTS, RANK_LANES, EXPERT_HIDDEN), 64 ** -0.5, 0.75, ((0, 8),)),
        "down_adapter_first": gaussian(streams_of[17], (EXPERT_SLOTS, EXPERT_HIDDEN, RANK_LANES), EXPERT_HIDDEN ** -0.5, 0.109375, ((0, 8),)),
        "down_adapter_second": gaussian(streams_of[18], (EXPERT_SLOTS, RANK_LANES, MODEL_WIDTH), 2 ** -0.5, 4.0, ((0, 8),)),
    }


@jax.custom_vjp
def low(v):
    return lax.optimization_barrier(v.astype(jnp.bfloat16)).astype(jnp.float32)

@jax.custom_vjp
def low_back(v):
    return v

def low_keep(v):
    return (low(v), None)

def low_pass(kept, grad):
    return (grad,)

def back_keep(v):
    return (v, None)

def back_low(kept, grad):
    return (low(grad),)
low.defvjp(low_keep, low_pass)
low_back.defvjp(back_keep, back_low)
HIGHEST = lax.Precision.HIGHEST

def einsum_high(form, left, right):
    return jnp.einsum(form, left, right, precision=HIGHEST)

def layer_norm(inputs):
    centre = inputs - lax.optimization_barrier(jnp.mean(inputs, axis=-1, keepdims=True))
    spread = lax.optimization_barrier(jnp.mean(centre * centre, axis=-1, keepdims=True))
    return centre * lax.rsqrt(spread + 1e-06)

def softmax_along(inputs, axis):
    shifted = inputs - lax.optimization_barrier(jnp.max(inputs, axis=axis, keepdims=True))
    powers = jnp.exp(shifted)
    return powers / lax.optimization_barrier(jnp.sum(powers, axis=axis, keepdims=True))

def image_block(adapter_banks, frozen, tokens, selector, living):
    qkv_a, qkv_b, out_a, out_b, route_a, route_b, up_a, up_b, down_a, down_b = adapter_banks
    query_key_value_weight, frozen_output_weight, frozen_dispatch_weight, frozen_up_weight, frozen_down_weight = frozen
    normed = low(layer_norm(tokens))
    low_qkv = low(low_back(einsum_high('td,dk->tk', normed, qkv_a))) * selector
    joined = low(low_back(einsum_high('td,dc->tc', normed, query_key_value_weight) + einsum_high('tk,kc->tc', low_qkv, qkv_b)))
    query_h = joined[:, :MODEL_WIDTH].reshape(TOK, HEADS, HEAD_DIM)
    key_h = joined[:, MODEL_WIDTH:2 * MODEL_WIDTH].reshape(TOK, HEADS, HEAD_DIM)
    value_h = joined[:, 2 * MODEL_WIDTH:].reshape(TOK, HEADS, HEAD_DIM)
    scores = low_back(einsum_high('thd,shd->hts', query_h, key_h) * 0.125)
    weights = low(softmax_along(scores, 2))
    attended = low(low_back(einsum_high('hts,shd->thd', weights, value_h).reshape(TOK, MODEL_WIDTH)))
    low_out = low(low_back(einsum_high('td,dk->tk', attended, out_a))) * selector
    branch = low_back(einsum_high('td,de->te', attended, frozen_output_weight) + einsum_high('tk,ke->te', low_out, out_b))
    middle = tokens + branch
    normed_two = low(layer_norm(middle))
    low_route = low(low_back(einsum_high('td,dk->tk', normed_two, route_a))) * selector
    logits = low_back(einsum_high('td,de->te', normed_two, frozen_dispatch_weight) + einsum_high('tk,ke->te', low_route, route_b))
    dispatch = low(softmax_along(logits, 0))
    combine = low(softmax_along(logits, 1))
    slot_in = low(low_back(einsum_high('te,td->ed', dispatch, normed_two)))
    rank_up_output = low(low_back(einsum_high('ed,edk->ek', slot_in, up_a))) * selector
    preact = low_back(einsum_high('ed,edf->ef', slot_in, frozen_up_weight) + einsum_high('ek,ekf->ef', rank_up_output, up_b))
    hidden_units = low(jax.nn.gelu(preact))
    rank_down_output = low(low_back(einsum_high('ef,efk->ek', hidden_units, down_a))) * selector
    expert_out = low(low_back(einsum_high('ef,efd->ed', hidden_units, frozen_down_weight) + einsum_high('ek,ekd->ed', rank_down_output, down_b)))
    mixed = einsum_high('te,ed->td', combine, expert_out)
    return living * (middle + mixed)

def reference(images, image_adapter_index, device_image_count, cotangent, query_key_value_weight, frozen_output_weight, frozen_dispatch_weight, query_key_value_first, query_key_value_second, output_adapter_first, output_adapter_second, dispatch_adapter_first, dispatch_adapter_second, frozen_up_weight, frozen_down_weight, up_adapter_first, up_adapter_second, down_adapter_first, down_adapter_second):
    frozen = (query_key_value_weight.astype(jnp.float32), frozen_output_weight.astype(jnp.float32), frozen_dispatch_weight.astype(jnp.float32), frozen_up_weight.astype(jnp.float32), frozen_down_weight.astype(jnp.float32))
    adapter_banks = (query_key_value_first.astype(jnp.float32), query_key_value_second.astype(jnp.float32), output_adapter_first.astype(jnp.float32), output_adapter_second.astype(jnp.float32), dispatch_adapter_first.astype(jnp.float32), dispatch_adapter_second.astype(jnp.float32), up_adapter_first.astype(jnp.float32), up_adapter_second.astype(jnp.float32), down_adapter_first.astype(jnp.float32), down_adapter_second.astype(jnp.float32))
    slot_index = jnp.arange(IMAGES, dtype=jnp.int32)
    owner = (slot_index // IMG_DEV).astype(jnp.int32)
    living = (slot_index % IMG_DEV < device_image_count[owner]).astype(jnp.float32)
    lane_group = (jnp.arange(ADAPTERS * RANK, dtype=jnp.int32) // RANK).astype(jnp.int32)
    selectors = (image_adapter_index[:, None] == lane_group[None, :]).astype(jnp.float32)

    def forward(tokens, bank_set):

        def single(item):
            return image_block(bank_set, frozen, item[0], item[1], item[2])
        return lax.map(jax.checkpoint(single), (tokens, selectors, living))
    result, pull = jax.vjp(forward, images.astype(jnp.float32), adapter_banks)
    input_grad, grads = pull(cotangent.astype(jnp.float32))
    return (result.astype(jnp.bfloat16), input_grad, grads[0], grads[1], grads[2], grads[3], grads[4], grads[5], grads[6], grads[7], grads[8], grads[9])
```

```python
import functools

import jax
import jax.numpy as jnp
from jax import lax
from jax.experimental import pallas as pl
from jax.experimental.pallas import tpu as pltpu
from jax.sharding import PartitionSpec as P

HEADS = 12
RANK = 16
LANES = 128
HEAD_DIM = 64
GROUP = 256
F32 = jnp.float32
BF16 = jnp.bfloat16
NN = (((1,), (0,)), ((), ()))
NT = (((1,), (1,)), ((), ()))
TN = (((0,), (0,)), ((), ()))
NEG = -1e30
VMEM_LIMIT = 56 * 1024 * 1024
GELU_C = 0.7978845608028654
GELU_A = 0.044715


def dot(left, right, dims=NN):
    return lax.dot_general(left, right, dims, preferred_element_type=F32)


def params(*axes):
    return pltpu.CompilerParams(
        dimension_semantics=axes or None, vmem_limit_bytes=VMEM_LIMIT
    )


def cost(flops, moved, exps=0):
    return pl.CostEstimate(flops=int(flops), bytes_accessed=int(moved), transcendentals=int(exps))


def normalise(rows):
    centre = rows - jnp.mean(rows, axis=-1, keepdims=True)
    spread = jnp.mean(centre * centre, axis=-1, keepdims=True)
    scale = lax.rsqrt(spread + 1e-06)
    return centre * scale, scale


def normalise_back(unit, scale, upstream):
    inner = jnp.mean(upstream * unit, axis=-1, keepdims=True)
    return scale * (upstream - jnp.mean(upstream, axis=-1, keepdims=True) - unit * inner)


def rank_row(index):
    lane = lax.broadcasted_iota(jnp.int32, (1, LANES), 1) // RANK
    return (lane == index).astype(F32)


def zero_tail(rows, n_tok):
    total = rows.shape[0]
    cut = n_tok // 16 * 16
    if n_tok == total:
        return rows
    row = lax.broadcasted_iota(jnp.int32, (total - cut, rows.shape[1]), 0) + cut
    tail = jnp.where(row < n_tok, rows[cut:].astype(F32), 0.0).astype(rows.dtype)
    return jnp.concatenate([rows[:cut], tail], axis=0)


def mask_tail(scores, n_tok):
    total = scores.shape[0]
    cut = n_tok // 16 * 16
    if n_tok == total:
        return scores
    row = lax.broadcasted_iota(jnp.int32, (total - cut, scores.shape[1]), 0) + cut
    tail = jnp.where(row < n_tok, scores[cut:], NEG)
    return jnp.concatenate([scores[:cut], tail], axis=0)


def pad_rows(scratch, rows, n_tok):
    total = scratch.shape[0]
    scratch[n_tok // 8 * 8 :, :] = jnp.zeros((total - n_tok // 8 * 8, scratch.shape[1]), F32)
    scratch[0:n_tok, :] = rows.astype(F32)
    return scratch[...]


def assemble(place, chunks, wall, sems):
    part = wall.shape[1] // 4
    copies = []
    for step in range(4):
        column = pl.multiple_of((place ^ step) * part, LANES)
        copies.append(
            pltpu.make_async_copy(chunks[step], wall.at[:, pl.ds(column, part)], sems.at[step])
        )
    for copy in copies:
        copy.start()
    for copy in copies:
        copy.wait()


def norm_kernel(n_tok, image_ref, out_ref, pad_ref):
    unit, _ = normalise(pad_rows(pad_ref, image_ref[0], n_tok))
    out_ref[0] = unit.astype(BF16)


def head_mask(value):
    lane = lax.broadcasted_iota(jnp.int32, (1, LANES), 1)
    low = jnp.where(lane < HEAD_DIM, value, 0.0).astype(BF16)
    high = jnp.where(lane < HEAD_DIM, 0.0, value).astype(BF16)
    return low, high


def attention_forward(qkv, n_tok):
    masks = head_mask(0.125)
    value_t = qkv[:, 2 * GROUP :].T
    outs = []
    for pair in range(GROUP // LANES):
        q_pair = qkv[:, pair * LANES : (pair + 1) * LANES]
        k_pair = qkv[:, GROUP + pair * LANES : GROUP + (pair + 1) * LANES]
        for side in range(2):
            scores = mask_tail(dot(k_pair * masks[side], q_pair, NT), n_tok)
            top = jnp.max(scores, axis=0, keepdims=True)
            powers = jnp.exp(scores - top)
            total = jnp.sum(powers, axis=0, keepdims=True)
            head = 2 * pair + side
            mixed = dot(value_t[head * HEAD_DIM : (head + 1) * HEAD_DIM], powers.astype(BF16))
            outs.append((mixed * (1.0 / total)).astype(BF16))
    return zero_tail(jnp.concatenate(outs, axis=0).T, n_tok)


def first_attention_kernel(
    n_tok, shards, place_ref, index_ref, h1_ref, c0, c1, c2, c3,
    qkv_ref, att_ref, uq_ref, a_ref, bt_ref, ao_ref, ra_ref, wall, sems,
):
    image = pl.program_id(0)
    width = wall.shape[0]

    @pl.when(image == 0)
    def _():
        assemble(place_ref[0], (c0, c1, c2, c3), wall, sems)
        a_ref[...] = wall[:, width : width + LANES]
        ao_ref[...] = wall[:, width + 4 * LANES : width + 5 * LANES]
        ra_ref[...] = wall[:, width + 5 * LANES : width + 6 * LANES]
        rows = width // shards
        for shard in range(shards):
            for part in range(3):
                bt_ref[(shard * 3 + part) * rows : (shard * 3 + part + 1) * rows, :] = wall[
                    shard * rows : (shard + 1) * rows,
                    width + (1 + part) * LANES : width + (2 + part) * LANES,
                ]

    h1 = h1_ref[0]
    selector = rank_row(index_ref[image])
    uq = (dot(h1, a_ref[...]).astype(BF16).astype(F32) * selector).astype(BF16)
    uq_ref[0] = uq
    qkv = project_group(0, h1, uq, wall, bt_ref)
    qkv_ref[0] = qkv
    att_ref[0] = attention_forward(qkv, n_tok)


def group_rows(group, width, bt_ref):
    return jnp.concatenate(
        [bt_ref[part * width + group * GROUP : part * width + (group + 1) * GROUP, :] for part in range(3)],
        axis=0,
    )


def project_group(group, h1, uq, wall, bt_ref):
    width = wall.shape[0]
    second = group_rows(group, width, bt_ref)
    return (dot(h1, wall[:, : 3 * GROUP]) + dot(uq, second, NT)).astype(BF16)


def next_attention_kernel(
    n_tok, group, extra, place_ref, h1_ref, uq_ref, bt_ref, c0, c1, c2, c3, *rest
):
    qkv_ref, att_ref = rest[:2]
    wall, sems = rest[-2:]
    image = pl.program_id(0)

    @pl.when(image == 0)
    def _():
        assemble(place_ref[0], (c0, c1, c2, c3), wall, sems)
        for position in range(extra):
            column = 3 * GROUP + position * LANES
            rest[2 + position][...] = wall[:, column : column + LANES]

    qkv = project_group(group, h1_ref[0], uq_ref[0], wall, bt_ref)
    qkv_ref[0] = qkv
    att_ref[0] = attention_forward(qkv, n_tok)


def route_kernel(
    n_tok, n_exp, place_ref, index_ref, count_ref, image_ref, cot_ref, att0, att1, att2,
    ao_ref, bo_ref, ra_ref, wr_ref, rb_ref, c0, c1, c2, c3,
    x2_ref, uo_ref, ur_ref, disp_ref, comb_ref, sg_ref, wrt_ref, wall, pad_a, pad_b, sems,
):
    image = pl.program_id(0)
    width = wall.shape[0]

    @pl.when(image == 0)
    def _():
        assemble(place_ref[0], (c0, c1, c2, c3), wall, sems)
        wrt_ref[...] = wr_ref[...].astype(F32).T[:n_exp].astype(BF16)

    selector = rank_row(index_ref[image])
    living = (image < count_ref[0]).astype(F32)
    att = jnp.concatenate([att0[0], att1[0], att2[0]], axis=1)
    uo = (dot(att, ao_ref[...]).astype(BF16).astype(F32) * selector).astype(BF16)
    uo_ref[0] = uo
    x2 = pad_rows(pad_a, image_ref[0], n_tok) + dot(att, wall[:, :width]) + dot(uo, bo_ref[...], NT)
    x2_ref[0] = x2
    h2 = normalise(x2)[0].astype(BF16)
    ur = (dot(h2, ra_ref[...]).astype(BF16).astype(F32) * selector).astype(BF16)
    ur_ref[0] = ur
    logits = dot(wrt_ref[...], h2, NT) + dot(rb_ref[...], ur, NT)
    token = lax.broadcasted_iota(jnp.int32, logits.shape, 1)
    alive = token < n_tok
    over_tokens = jnp.where(alive, logits, NEG)
    powers = jnp.exp(over_tokens - jnp.max(over_tokens, axis=1, keepdims=True))
    disp = powers / jnp.sum(powers, axis=1, keepdims=True)
    powers = jnp.exp(logits - jnp.max(logits, axis=0, keepdims=True))
    comb = jnp.where(alive, powers / jnp.sum(powers, axis=0, keepdims=True), 0.0)
    disp_ref[0] = disp
    comb_ref[0] = comb
    upstream = (pad_rows(pad_b, cot_ref[0], n_tok) * living).astype(BF16)
    sg_ref[0, :, :width] = dot(disp.astype(BF16), h2).astype(BF16)
    sg_ref[0, :, width : 2 * width] = dot(comb.astype(BF16), upstream).astype(BF16)
    sg_ref[0, :, 2 * width :] = jnp.broadcast_to(selector, (n_exp, LANES)).astype(BF16)


def gelu_both(pre):
    square = pre * pre
    half = jnp.tanh(GELU_C * pre * (1.0 + GELU_A * square))
    both = 0.5 * (1.0 + half)
    slope = both + 0.5 * pre * (1.0 - half * half) * (GELU_C * (1.0 + 3.0 * GELU_A * square))
    return pre * both, slope


def expert_kernel(
    sg_ref, wu_ref, wd_ref, ua_ref, ub_ref, da_ref, db_ref, out_ref,
    u1_ref, gu2_ref, acc_y, acc_s, acc_u2, acc_gu1,
):
    step = pl.program_id(1)
    width = wu_ref.shape[1]
    selector = sg_ref[0, :, 2 * width :].astype(F32)

    @pl.when(step == 0)
    def _():
        u1_ref[...] = (
            dot(sg_ref[0, :, :width], ua_ref[0]).astype(BF16).astype(F32) * selector
        ).astype(BF16)
        gu2_ref[...] = (dot(sg_ref[0, :, width : 2 * width], db_ref[0], NT) * selector).astype(BF16)
        acc_y[...] = jnp.zeros_like(acc_y)
        acc_s[...] = jnp.zeros_like(acc_s)
        acc_u2[...] = jnp.zeros_like(acc_u2)
        acc_gu1[...] = jnp.zeros_like(acc_gu1)

    pre = dot(sg_ref[0, :, :width], wu_ref[0]) + dot(u1_ref[...], ub_ref[0])
    ghid = dot(sg_ref[0, :, width : 2 * width], wd_ref[0], NT) + dot(gu2_ref[...], da_ref[0], NT)
    hidden, slope = gelu_both(pre)
    hidden = hidden.astype(BF16)
    gpre = (slope * ghid).astype(BF16)
    acc_y[...] += dot(hidden, wd_ref[0])
    acc_u2[...] += dot(hidden, da_ref[0])
    acc_s[...] += dot(gpre, wu_ref[0], NT)
    acc_gu1[...] += dot(gpre, ub_ref[0], NT)

    @pl.when(step == pl.num_programs(1) - 1)
    def _():
        u2 = (acc_u2[...].astype(BF16).astype(F32) * selector).astype(BF16)
        gu1 = (acc_gu1[...] * selector).astype(BF16)
        out_ref[0, :, :width] = (acc_y[...] + dot(u2, db_ref[0])).astype(BF16)
        out_ref[0, :, width:] = (acc_s[...] + dot(gu1, ua_ref[0], NT)).astype(BF16)


def expert_grad_kernel(
    sg_ref, wu_ref, wd_ref, ua_ref, ub_ref, da_ref, db_ref,
    gua_ref, gub_ref, gda_ref, gdb_ref, u1_ref, gu2_ref, acc_u2, acc_gu1,
):
    step = pl.program_id(1)
    width = wu_ref.shape[1]
    selector = sg_ref[0, :, 2 * width :].astype(F32)

    @pl.when(step == 0)
    def _():
        u1_ref[...] = (
            dot(sg_ref[0, :, :width], ua_ref[0]).astype(BF16).astype(F32) * selector
        ).astype(BF16)
        gu2_ref[...] = (dot(sg_ref[0, :, width : 2 * width], db_ref[0], NT) * selector).astype(BF16)
        acc_u2[...] = jnp.zeros_like(acc_u2)
        acc_gu1[...] = jnp.zeros_like(acc_gu1)

    pre = dot(sg_ref[0, :, :width], wu_ref[0]) + dot(u1_ref[...], ub_ref[0])
    ghid = dot(sg_ref[0, :, width : 2 * width], wd_ref[0], NT) + dot(gu2_ref[...], da_ref[0], NT)
    hidden, slope = gelu_both(pre)
    hidden = hidden.astype(BF16)
    gpre = (slope * ghid).astype(BF16)
    gub_ref[0] = dot(u1_ref[...], gpre, TN)
    gda_ref[0] = dot(hidden, gu2_ref[...], TN)
    acc_u2[...] += dot(hidden, da_ref[0])
    acc_gu1[...] += dot(gpre, ub_ref[0], NT)

    @pl.when(step == pl.num_programs(1) - 1)
    def _():
        u2 = (acc_u2[...].astype(BF16).astype(F32) * selector).astype(BF16)
        gu1 = (acc_gu1[...] * selector).astype(BF16)
        gdb_ref[0] = dot(u2, sg_ref[0, :, width : 2 * width], TN)
        gua_ref[0] = dot(sg_ref[0, :, :width], gu1, TN)


def route_back_kernel(
    n_tok, n_exp, place_ref, index_ref, count_ref, cot_ref, x2_ref, uo_ref, ur_ref, disp_ref,
    comb_ref, att0, att1, att2, ret_ref, ao_ref, bo_ref, ra_ref, wrt_ref, rb_ref, c0, c1, c2, c3,
    block_ref, gx2_ref, gatt_ref, goa_ref, gob_ref, gra_ref, grb_ref,
    wall, pad_b, acc_oa, acc_ob, acc_ra, acc_rb, sems,
):
    image = pl.program_id(0)
    width = wall.shape[0]

    @pl.when(image == 0)
    def _():
        assemble(place_ref[0], (c0, c1, c2, c3), wall, sems)
        acc_oa[...] = jnp.zeros_like(acc_oa)
        acc_ob[...] = jnp.zeros_like(acc_ob)
        acc_ra[...] = jnp.zeros_like(acc_ra)
        acc_rb[...] = jnp.zeros_like(acc_rb)

    selector = rank_row(index_ref[image])
    living = (image < count_ref[0]).astype(F32)
    upstream = pad_rows(pad_b, cot_ref[0], n_tok) * living
    upstream_low = upstream.astype(BF16)
    x2 = x2_ref[0]
    disp, comb = disp_ref[0], comb_ref[0]
    yexp, gslot = ret_ref[0, :, :width], ret_ref[0, :, width:]
    mixed = dot(comb.T.astype(BF16), yexp)
    block_ref[0] = (living * (x2 + mixed)).astype(BF16)[:n_tok]
    unit, scale = normalise(x2)
    h2 = unit.astype(BF16)
    gcomb = dot(yexp, upstream_low, NT)
    gdisp = dot(gslot, h2, NT)
    glog = (
        disp * (gdisp - jnp.sum(gdisp * disp, axis=1, keepdims=True))
        + comb * (gcomb - jnp.sum(gcomb * comb, axis=0, keepdims=True))
    ).astype(BF16)
    acc_rb[...] += dot(glog, ur_ref[0])
    pair = jnp.concatenate([disp, glog.astype(F32)], axis=0).T.astype(BF16)
    gur = (dot(pair[:, n_exp:], rb_ref[...]) * selector).astype(BF16)
    acc_ra[...] += dot(gur, h2, TN)
    below = jnp.concatenate([gslot, wrt_ref[...]], axis=0)
    gh2 = dot(pair, below) + dot(gur, ra_ref[...], NT)
    gx2 = upstream + normalise_back(unit, scale, gh2)
    gx2_ref[0] = gx2
    gbr = gx2.astype(BF16)
    acc_ob[...] += dot(uo_ref[0], gbr, TN)
    guo = (dot(gbr, bo_ref[...]) * selector).astype(BF16)
    att = jnp.concatenate([att0[0], att1[0], att2[0]], axis=1)
    acc_oa[...] += dot(guo, att, TN)
    gatt_ref[0] = (dot(gbr, wall[:, :width], NT) + dot(guo, ao_ref[...], NT)).astype(BF16)

    @pl.when(image == pl.num_programs(0) - 1)
    def _():
        goa_ref[...] = acc_oa[...].T.astype(BF16)
        gob_ref[...] = acc_ob[...].T.astype(BF16)
        gra_ref[...] = acc_ra[...].T.astype(BF16)
        grb_ref[...] = acc_rb[...].astype(BF16)


def attention_backward(qkv, gatt, n_tok):
    masks = head_mask(0.125)
    keep = head_mask(1.0)
    key_t = qkv[:, GROUP : 2 * GROUP].T
    lane = lax.broadcasted_iota(jnp.int32, (1, LANES), 1)
    gq_parts, gk_parts, gv_parts = [], [], []
    for pair in range(GROUP // LANES):
        span = slice(pair * LANES, (pair + 1) * LANES)
        q_pair, ga_pair = qkv[:, span], gatt[:, span]
        k_pair = qkv[:, GROUP + pair * LANES : GROUP + (pair + 1) * LANES]
        v_pair = qkv[:, 2 * GROUP + pair * LANES : 2 * GROUP + (pair + 1) * LANES]
        gks, gvs = [], []
        for side in range(2):
            scores = mask_tail(dot(k_pair * masks[side], q_pair, NT), n_tok)
            top = jnp.max(scores, axis=0, keepdims=True)
            powers = jnp.exp(scores - top)
            probs = powers * (1.0 / jnp.sum(powers, axis=0, keepdims=True))
            gvs.append(dot(probs.astype(BF16), ga_pair))
            gprobs = dot(v_pair * keep[side], ga_pair, NT)
            inner = jnp.sum(gprobs * probs, axis=0, keepdims=True)
            gscores = (probs * (gprobs - inner)).astype(BF16)
            gks.append(dot(gscores, q_pair))
            head = 2 * pair + side
            gq_parts.append(
                (dot(key_t[head * HEAD_DIM : (head + 1) * HEAD_DIM], gscores) * 0.125).astype(BF16)
            )
        gk_parts.append((jnp.where(lane < HEAD_DIM, gks[0], gks[1]) * 0.125).astype(BF16))
        gv_parts.append(jnp.where(lane < HEAD_DIM, gvs[0], gvs[1]).astype(BF16))
    gq = jnp.concatenate(gq_parts, axis=0).T
    return jnp.concatenate([gq] + gk_parts + gv_parts, axis=1)


def attention_back_kernel(n_tok, group, last, *refs):
    refs = list(refs)
    index_ref = refs.pop(0) if last else None
    qkv_ref, gatt_ref, uq_ref, bt_ref = refs[:4]
    refs = refs[4:]
    before_ref = refs.pop(0) if group else None
    h1_ref = refs.pop(0) if last else None
    gqkv_ref, guq_ref, gb_ref = refs[:3]
    refs = refs[3:]
    ga_ref = refs.pop(0) if last else None
    acc_b = refs.pop(0)
    acc_a = refs.pop(0) if last else None
    image = pl.program_id(0)
    width = bt_ref.shape[0] // 3

    @pl.when(image == 0)
    def _():
        acc_b[...] = jnp.zeros_like(acc_b)
        if last:
            acc_a[...] = jnp.zeros_like(acc_a)

    gqkv = attention_backward(qkv_ref[0], gatt_ref[0], n_tok)
    gqkv_ref[0] = gqkv
    acc_b[...] += dot(uq_ref[0], gqkv, TN)
    guq = dot(gqkv, group_rows(group, width, bt_ref))
    if group:
        guq = guq + before_ref[0]
    if last:
        guq = (guq * rank_row(index_ref[image])).astype(BF16)
        acc_a[...] += dot(guq, h1_ref[0], TN)
    guq_ref[0] = guq

    @pl.when(image == pl.num_programs(0) - 1)
    def _():
        gb_ref[...] = acc_b[...].T.astype(BF16)
        if last:
            ga_ref[...] = acc_a[...].T.astype(BF16)


def input_grad_kernel(
    n_tok, groups, place_ref, image_ref, gx2_ref, guq_ref, a_ref, *refs
):
    gqkv = refs[:groups]
    chunks = refs[groups : groups + 4 * groups]
    out_ref = refs[5 * groups]
    walls = refs[5 * groups + 1 : 6 * groups + 1]
    pad_a, sems = refs[6 * groups + 1 :]
    image = pl.program_id(0)

    @pl.when(image == 0)
    def _():
        for group in range(groups):
            assemble(
                place_ref[0], chunks[4 * group : 4 * group + 4], walls[group], sems.at[group]
            )

    gh1 = dot(guq_ref[0], a_ref[...], NT)
    for group in range(groups):
        gh1 = gh1 + dot(gqkv[group][0], walls[group][:, : 3 * GROUP], NT)
    unit, scale = normalise(pad_rows(pad_a, image_ref[0], n_tok))
    out_ref[0] = (gx2_ref[0] + normalise_back(unit, scale, gh1))[:n_tok]


ANY = pl.BlockSpec(memory_space=pl.ANY)


def whole(shape):
    return pl.BlockSpec(shape, lambda *_: (0,) * len(shape))


def per_image(*shape):
    return pl.BlockSpec((1,) + shape, lambda i, *_: (i,) + (0,) * len(shape))


def call(kernel, scalars, grid, inputs, outputs, scratch, flops, exps=0):
    arrays = [array for array, _ in inputs]
    shapes = [jax.ShapeDtypeStruct(shape, dtype) for shape, dtype, _ in outputs]
    moved = sum(array.size * array.dtype.itemsize for array in arrays) + sum(
        shape.size * shape.dtype.itemsize for shape in shapes
    )
    return pl.pallas_call(
        kernel,
        out_shape=shapes,
        grid_spec=pltpu.PrefetchScalarGridSpec(
            num_scalar_prefetch=len(scalars),
            grid=grid,
            in_specs=[spec for _, spec in inputs],
            out_specs=[spec for _, _, spec in outputs],
            scratch_shapes=scratch,
        ),
        compiler_params=params(*(("arbitrary",) * len(grid))),
        cost_estimate=cost(flops, moved, exps),
    )(*scalars, *arrays)


def norm_call(images, total):
    n_img, n_tok, width = images.shape
    return call(
        functools.partial(norm_kernel, n_tok), (), (n_img,),
        [(images, per_image(n_tok, width))],
        [((n_img, total, width), BF16, per_image(total, width))],
        [pltpu.VMEM((total, width), F32)],
        8 * images.size,
    )[0]


def attention_flops(n_img, total, width, parts):
    return n_img * total * (2 * width * 3 * GROUP + parts * 8 * total * HEAD_DIM)


def first_attention_call(place, index, h1, chunks, n_tok, shards):
    n_img, total, width = h1.shape
    columns = 4 * chunks[0].shape[1]
    return call(
        functools.partial(first_attention_kernel, n_tok, shards), (place, index), (n_img,),
        [(h1, per_image(total, width))] + [(chunk, ANY) for chunk in chunks],
        [
            ((n_img, total, 3 * GROUP), BF16, per_image(total, 3 * GROUP)),
            ((n_img, total, GROUP), BF16, per_image(total, GROUP)),
            ((n_img, total, LANES), BF16, per_image(total, LANES)),
            ((width, LANES), BF16, whole((width, LANES))),
            ((3 * width, LANES), BF16, whole((3 * width, LANES))),
            ((width, LANES), BF16, whole((width, LANES))),
            ((width, LANES), BF16, whole((width, LANES))),
        ],
        [pltpu.VMEM((width, columns), BF16), pltpu.SemaphoreType.DMA((4,))],
        attention_flops(n_img, total, width, 2), n_img * total * total * 4,
    )


def next_attention_call(place, h1, uq, bt, chunks, n_tok, group, extra):
    n_img, total, width = h1.shape
    columns = 4 * chunks[0].shape[1]
    return call(
        functools.partial(next_attention_kernel, n_tok, group, extra), (place,), (n_img,),
        [
            (h1, per_image(total, width)),
            (uq, per_image(total, LANES)),
            (bt, whole(bt.shape)),
        ]
        + [(chunk, ANY) for chunk in chunks],
        [
            ((n_img, total, 3 * GROUP), BF16, per_image(total, 3 * GROUP)),
            ((n_img, total, GROUP), BF16, per_image(total, GROUP)),
        ]
        + [((width, LANES), BF16, whole((width, LANES)))] * extra,
        [pltpu.VMEM((width, columns), BF16), pltpu.SemaphoreType.DMA((4,))],
        attention_flops(n_img, total, width, 2), n_img * total * total * 4,
    )


def route_call(place, index, count, images, cotangent, atts, banks, chunks, n_exp, total):
    n_img, n_tok, width = images.shape
    return call(
        functools.partial(route_kernel, n_tok, n_exp), (place, index, count), (n_img,),
        [(images, per_image(n_tok, width)), (cotangent, per_image(n_tok, width))]
        + [(att, per_image(total, GROUP)) for att in atts]
        + [(bank, whole(bank.shape)) for bank in banks]
        + [(chunk, ANY) for chunk in chunks],
        [
            ((n_img, total, width), F32, per_image(total, width)),
            ((n_img, total, LANES), BF16, per_image(total, LANES)),
            ((n_img, total, LANES), BF16, per_image(total, LANES)),
            ((n_img, n_exp, total), F32, per_image(n_exp, total)),
            ((n_img, n_exp, total), F32, per_image(n_exp, total)),
            ((n_img, n_exp, 2 * width + LANES), BF16, per_image(n_exp, 2 * width + LANES)),
            ((n_exp, width), BF16, whole((n_exp, width))),
        ],
        [
            pltpu.VMEM((width, 4 * chunks[0].shape[1]), BF16),
            pltpu.VMEM((total, width), F32),
            pltpu.VMEM((total, width), F32),
            pltpu.SemaphoreType.DMA((4,)),
        ],
        n_img * total * 2 * width * (width + 3 * LANES), n_img * total * 2 * n_exp,
    )


def hidden_tile(hidden, limit):
    tile = hidden
    while tile > limit:
        tile //= 2
    return tile


def expert_specs(rows, width, tile):
    return (
        pl.BlockSpec((1, rows, 2 * width + LANES), lambda e, f: (e, 0, 0)),
        pl.BlockSpec((1, width, tile), lambda e, f: (e, 0, f)),
        pl.BlockSpec((1, tile, width), lambda e, f: (e, f, 0)),
        pl.BlockSpec((1, width, LANES), lambda e, f: (e, 0, 0)),
        pl.BlockSpec((1, LANES, tile), lambda e, f: (e, 0, f)),
        pl.BlockSpec((1, tile, LANES), lambda e, f: (e, f, 0)),
        pl.BlockSpec((1, LANES, width), lambda e, f: (e, 0, 0)),
    )


def expert_call(sg, weights):
    n_loc, rows, _ = sg.shape
    width, hidden = weights[0].shape[1:]
    tile = hidden_tile(hidden, 768)
    return call(
        expert_kernel, (), (n_loc, hidden // tile),
        list(zip((sg,) + weights, expert_specs(rows, width, tile))),
        [((n_loc, rows, 2 * width), BF16, pl.BlockSpec((1, rows, 2 * width), lambda e, f: (e, 0, 0)))],
        [
            pltpu.VMEM((rows, LANES), BF16),
            pltpu.VMEM((rows, LANES), BF16),
            pltpu.VMEM((rows, width), F32),
            pltpu.VMEM((rows, width), F32),
            pltpu.VMEM((rows, LANES), F32),
            pltpu.VMEM((rows, LANES), F32),
        ],
        n_loc * rows * 8 * width * hidden, n_loc * rows * hidden,
    )[0]


def expert_grad_call(sg, weights):
    n_loc, rows, _ = sg.shape
    width, hidden = weights[0].shape[1:]
    tile = hidden_tile(hidden, 768 if rows <= 512 else 384)
    return call(
        expert_grad_kernel, (), (n_loc, hidden // tile),
        list(zip((sg,) + weights, expert_specs(rows, width, tile))),
        [
            ((n_loc, width, LANES), F32, pl.BlockSpec((1, width, LANES), lambda e, f: (e, 0, 0))),
            ((n_loc, LANES, hidden), F32, pl.BlockSpec((1, LANES, tile), lambda e, f: (e, 0, f))),
            ((n_loc, hidden, LANES), F32, pl.BlockSpec((1, tile, LANES), lambda e, f: (e, f, 0))),
            ((n_loc, LANES, width), F32, pl.BlockSpec((1, LANES, width), lambda e, f: (e, 0, 0))),
        ],
        [
            pltpu.VMEM((rows, LANES), BF16),
            pltpu.VMEM((rows, LANES), BF16),
            pltpu.VMEM((rows, LANES), F32),
            pltpu.VMEM((rows, LANES), F32),
        ],
        n_loc * rows * 4 * width * hidden, n_loc * rows * hidden,
    )


def route_back_call(
    place, index, count, cotangent, x2, uo, ur, disp, comb, atts, ret, banks, chunks
):
    n_img, n_tok, width = cotangent.shape
    total, n_exp = x2.shape[1], disp.shape[1]
    return call(
        functools.partial(route_back_kernel, n_tok, n_exp), (place, index, count), (n_img,),
        [
            (cotangent, per_image(n_tok, width)),
            (x2, per_image(total, width)),
            (uo, per_image(total, LANES)),
            (ur, per_image(total, LANES)),
            (disp, per_image(n_exp, total)),
            (comb, per_image(n_exp, total)),
        ]
        + [(att, per_image(total, GROUP)) for att in atts]
        + [(ret, per_image(n_exp, 2 * width))]
        + [(bank, whole(bank.shape)) for bank in banks]
        + [(chunk, ANY) for chunk in chunks],
        [
            ((n_img, n_tok, width), BF16, per_image(n_tok, width)),
            ((n_img, total, width), F32, per_image(total, width)),
            ((n_img, total, width), BF16, per_image(total, width)),
            ((width, LANES), BF16, whole((width, LANES))),
            ((width, LANES), BF16, whole((width, LANES))),
            ((width, LANES), BF16, whole((width, LANES))),
            ((n_exp, LANES), BF16, whole((n_exp, LANES))),
        ],
        [
            pltpu.VMEM((width, 4 * chunks[0].shape[1]), BF16),
            pltpu.VMEM((total, width), F32),
            pltpu.VMEM((LANES, width), F32),
            pltpu.VMEM((LANES, width), F32),
            pltpu.VMEM((LANES, width), F32),
            pltpu.VMEM((n_exp, LANES), F32),
            pltpu.SemaphoreType.DMA((4,)),
        ],
        n_img * total * 2 * width * (width + 6 * LANES),
    )


def attention_back_call(index, qkv, gatt, uq, bt, before, h1, n_tok, group):
    n_img, total, _ = qkv.shape
    width = bt.shape[0] // 3
    last = h1 is not None
    inputs = [
        (qkv, per_image(total, 3 * GROUP)),
        (gatt, pl.BlockSpec((1, total, GROUP), lambda i, *_: (i, 0, group))),
        (uq, per_image(total, LANES)),
        (bt, whole(bt.shape)),
    ]
    outputs = [
        ((n_img, total, 3 * GROUP), BF16, per_image(total, 3 * GROUP)),
        ((n_img, total, LANES), BF16 if last else F32, per_image(total, LANES)),
        ((3 * GROUP, LANES), BF16, whole((3 * GROUP, LANES))),
    ]
    scratch = [pltpu.VMEM((LANES, 3 * GROUP), F32)]
    if group:
        inputs.append((before, per_image(total, LANES)))
    if last:
        inputs.append((h1, per_image(total, width)))
        outputs.append(((width, LANES), BF16, whole((width, LANES))))
        scratch.append(pltpu.VMEM((LANES, width), F32))
    return call(
        functools.partial(attention_back_kernel, n_tok, group, last),
        (index,) if last else (), (n_img,), inputs, outputs, scratch,
        attention_flops(n_img, total, LANES, 5), n_img * total * total * 4,
    )


def input_grad_call(place, images, gx2, guq, bank_a, gqkvs, packs):
    n_img, n_tok, width = images.shape
    total = gx2.shape[1]
    groups = len(gqkvs)
    return call(
        functools.partial(input_grad_kernel, n_tok, groups), (place,), (n_img,),
        [
            (images, per_image(n_tok, width)),
            (gx2, per_image(total, width)),
            (guq, per_image(total, LANES)),
            (bank_a, whole(bank_a.shape)),
        ]
        + [(gqkv, per_image(total, 3 * GROUP)) for gqkv in gqkvs]
        + [(chunk, ANY) for pack in packs for chunk in pack],
        [((n_img, n_tok, width), F32, per_image(n_tok, width))],
        [pltpu.VMEM((width, 4 * pack[0].shape[1]), BF16) for pack in packs]
        + [pltpu.VMEM((total, width), F32), pltpu.SemaphoreType.DMA((groups, 4))],
        n_img * total * 2 * width * (3 * width + LANES),
    )[0]


def swap(array, axis, size, bit):
    return lax.ppermute(array, axis, [(i, i ^ bit) for i in range(size)])


def gather_pack(pack, shards, replicas, quarter):
    rows, columns = pack.shape
    part = columns // 4
    mine = lax.dynamic_slice(pack, (0, quarter * part), (rows, part))
    spread = jnp.broadcast_to(mine[None], (shards, rows, part))
    own = lax.all_to_all(spread, "shard", split_axis=0, concat_axis=0, tiled=True)
    own = own.reshape(shards * rows, part)
    over_y = swap(own, "replica", replicas, 2)
    return own, swap(own, "replica", replicas, 1), over_y, swap(over_y, "replica", replicas, 1)


def reduce_pack(pack, replicas):
    where = lax.axis_index("replica")
    bits = []
    bit = 1
    while bit < replicas:
        half = pack.shape[1] // 2
        side = (where // bit) % 2
        keep = lax.dynamic_slice_in_dim(pack, side * half, half, axis=1)
        give = lax.dynamic_slice_in_dim(pack, (1 - side) * half, half, axis=1)
        got = swap(give, "replica", replicas, bit)
        pack = (keep.astype(F32) + got.astype(F32)).astype(BF16)
        bits.append(bit)
        bit *= 2
    landed = lax.all_to_all(pack, "shard", split_axis=0, concat_axis=0, tiled=True)
    total = jnp.sum(landed.astype(F32), axis=0).astype(BF16)
    for bit in reversed(bits):
        got = swap(total, "replica", replicas, bit)
        side = (where // bit) % 2
        total = jnp.where(
            side == 0,
            jnp.concatenate([total, got], axis=0),
            jnp.concatenate([got, total], axis=0),
        )
    return total


def per_device(
    replicas,
    shards,
    images,
    image_adapter_index,
    device_image_count,
    cotangent,
    query_key_value_weight,
    frozen_output_weight,
    frozen_dispatch_weight,
    query_key_value_first,
    query_key_value_second,
    output_adapter_first,
    output_adapter_second,
    dispatch_adapter_first,
    dispatch_adapter_second,
    frozen_up_weight,
    frozen_down_weight,
    up_adapter_first,
    up_adapter_second,
    down_adapter_first,
    down_adapter_second,
):
    n_img, n_tok, width = images.shape
    total = -(-n_tok // 16) * 16
    rows = width // shards
    n_loc = frozen_up_weight.shape[0]
    n_exp = n_loc * shards
    groups = width // GROUP
    quarter = lax.axis_index("replica") % 4
    place = quarter.astype(jnp.int32).reshape(1)

    def qkv_columns(group):
        return [
            query_key_value_weight[:, part * width + group * GROUP : part * width + (group + 1) * GROUP]
            for part in range(3)
        ]

    second_t = query_key_value_second.T.reshape(3, rows, LANES)
    route_block = jnp.concatenate(
        [
            frozen_dispatch_weight,
            jnp.zeros((rows, 64 - n_exp), BF16),
            jnp.pad(dispatch_adapter_second.T.reshape(16, n_loc * 8), ((0, rows - 16), (0, 0))),
            jnp.zeros((rows, 64 - n_loc * 8), BF16),
        ],
        axis=1,
    )
    empty = jnp.zeros((rows, LANES), BF16)
    packs = [
        qkv_columns(0)
        + [query_key_value_first, second_t[0], second_t[1], second_t[2], output_adapter_first, dispatch_adapter_first],
        qkv_columns(1) + [output_adapter_second.T, route_block],
        qkv_columns(2) + [empty, empty],
        [frozen_output_weight, empty, empty],
    ]
    packs = [jnp.concatenate(pack, axis=1) for pack in packs]
    packs = [gather_pack(pack, shards, replicas, quarter) for pack in packs]

    h1 = norm_call(images, total)
    qkv0, att0, uq, bank_a, bank_bt, bank_ao, bank_ra = first_attention_call(
        place, image_adapter_index, h1, packs[0], n_tok, shards
    )
    qkv1, att1, bank_bo, bank_wr = next_attention_call(place, h1, uq, bank_bt, packs[1], n_tok, 1, 2)
    qkv2, att2 = next_attention_call(place, h1, uq, bank_bt, packs[2], n_tok, 2, 0)
    atts = (att0, att1, att2)
    bank_rb = bank_wr.reshape(shards, rows, LANES)[:, :16, 64 : 64 + n_loc * 8].reshape(n_exp, LANES)
    x2, uo, ur, disp, comb, sg, bank_wrt = route_call(
        place, image_adapter_index, device_image_count, images, cotangent, atts,
        (bank_ao, bank_bo, bank_ra, bank_wr, bank_rb), packs[3], n_exp, total,
    )

    sent = sg.reshape(n_img, shards, n_loc, -1).transpose(1, 2, 0, 3)
    landed = lax.all_to_all(sent, "shard", split_axis=0, concat_axis=0, tiled=True)
    landed = landed.transpose(1, 0, 2, 3).reshape(n_loc, shards * n_img, -1)
    weights = (
        frozen_up_weight, frozen_down_weight, up_adapter_first, up_adapter_second,
        down_adapter_first, down_adapter_second,
    )
    ret = expert_call(landed, weights)
    every = landed
    bit = replicas // 2
    while bit:
        every = jnp.concatenate([every, swap(every, "replica", replicas, bit)], axis=1)
        bit //= 2
    back = ret.reshape(n_loc, shards, n_img, 2 * width).transpose(1, 0, 2, 3)
    back = lax.all_to_all(back, "shard", split_axis=0, concat_axis=0, tiled=True)
    back = back.transpose(2, 0, 1, 3).reshape(n_img, n_exp, 2 * width)
    grad_up_a, grad_up_b, grad_down_a, grad_down_b = expert_grad_call(every, weights)

    block_out, gx2, gatt, goa, gob, gra, grb = route_back_call(
        place, image_adapter_index, device_image_count, cotangent, x2, uo, ur, disp, comb, atts, back,
        (bank_ao, bank_bo, bank_ra, bank_wrt, bank_rb), packs[3],
    )
    fill = -(3 * rows + n_loc) % (8 * replicas)
    out_pack = jnp.concatenate(
        [
            goa.reshape(shards, rows, LANES),
            gob.reshape(shards, rows, LANES),
            gra.reshape(shards, rows, LANES),
            grb.reshape(shards, n_loc, LANES),
            jnp.zeros((shards, fill, LANES), BF16),
        ],
        axis=1,
    )
    out_sum = reduce_pack(out_pack, replicas).astype(F32)

    gqkv0, guq, gb0 = attention_back_call(None, qkv0, gatt, uq, bank_bt, None, None, n_tok, 0)
    gqkv1, guq, gb1 = attention_back_call(None, qkv1, gatt, uq, bank_bt, guq, None, n_tok, 1)
    gqkv2, guq, gb2, gqa = attention_back_call(
        image_adapter_index, qkv2, gatt, uq, bank_bt, guq, h1, n_tok, 2
    )
    gbt = jnp.concatenate(
        [gb[part * GROUP : (part + 1) * GROUP] for part in range(3) for gb in (gb0, gb1, gb2)], axis=0
    )
    qkv_pack = jnp.concatenate(
        [gbt.reshape(shards, 3 * rows, LANES), gqa.reshape(shards, rows, LANES)], axis=1
    )
    qkv_sum = reduce_pack(qkv_pack, replicas).astype(F32)
    input_grad = input_grad_call(
        place, images, gx2, guq, bank_a, (gqkv0, gqkv1, gqkv2), packs[:3]
    )
    return (
        block_out,
        input_grad,
        qkv_sum[3 * rows :],
        qkv_sum[: 3 * rows].T,
        out_sum[:rows],
        out_sum[rows : 2 * rows].T,
        out_sum[2 * rows : 3 * rows],
        out_sum[3 * rows : 3 * rows + n_loc].T,
        grad_up_a,
        grad_up_b,
        grad_down_a,
        grad_down_b,
    )


def solution(mesh):
    images = P(("replica", "shard"), None, None)
    each = P(("replica", "shard"))
    by_row, by_column, by_expert = P("shard", None), P(None, "shard"), P("shard", None, None)
    in_specs = (
        (images, each, each, images)
        + (by_row, by_row, by_row)
        + (by_row, by_column) * 3
        + (by_expert,) * 6
    )
    out_specs = (images, images) + (by_row, by_column) * 3 + (by_expert,) * 4
    return jax.shard_map(
        functools.partial(per_device, mesh.shape["replica"], mesh.shape["shard"]),
        mesh=mesh,
        in_specs=in_specs,
        out_specs=out_specs,
        check_vma=False,
    )
```

```python
import functools

import jax
import jax.numpy as jnp
from jax import lax
from jax.experimental import pallas as pl
from jax.experimental.pallas import tpu as pltpu
from jax.sharding import PartitionSpec as P

HEADS = 12
RANK = 16
LANES = 128
HEAD_DIM = 64
GROUP = 256
F32 = jnp.float32
BF16 = jnp.bfloat16
NN = (((1,), (0,)), ((), ()))
NT = (((1,), (1,)), ((), ()))
TN = (((0,), (0,)), ((), ()))
NEG = -1e30
VMEM_LIMIT = 56 * 1024 * 1024
GELU_C = 0.7978845608028654
GELU_A = 0.044715
IMAGES_FORWARD = 2
IMAGES_BACK = 2
IMAGES_ROUTE = 2
IMAGES_LAST = 2


def dot(left, right, dims=NN):
    return lax.dot_general(left, right, dims, preferred_element_type=F32)


def params(*axes):
    return pltpu.CompilerParams(
        dimension_semantics=axes or None, vmem_limit_bytes=VMEM_LIMIT
    )


def cost(flops, moved, exps=0):
    return pl.CostEstimate(flops=int(flops), bytes_accessed=int(moved), transcendentals=int(exps))


def normalise(rows):
    centre = rows - jnp.mean(rows, axis=-1, keepdims=True)
    spread = jnp.mean(centre * centre, axis=-1, keepdims=True)
    scale = lax.rsqrt(spread + 1e-06)
    return centre * scale, scale


def normalise_back(unit, scale, upstream):
    inner = jnp.mean(upstream * unit, axis=-1, keepdims=True)
    return scale * (upstream - jnp.mean(upstream, axis=-1, keepdims=True) - unit * inner)


def rank_row(index):
    lane = lax.broadcasted_iota(jnp.int32, (1, LANES), 1) // RANK
    return (lane == index).astype(F32)


def zero_tail(rows, n_tok):
    total = rows.shape[0]
    cut = n_tok // 16 * 16
    if n_tok == total:
        return rows
    row = lax.broadcasted_iota(jnp.int32, (total - cut, rows.shape[1]), 0) + cut
    tail = jnp.where(row < n_tok, rows[cut:].astype(F32), 0.0).astype(rows.dtype)
    return jnp.concatenate([rows[:cut], tail], axis=0)


def mask_tail(scores, n_tok):
    total = scores.shape[0]
    cut = n_tok // 16 * 16
    if n_tok == total:
        return scores
    row = lax.broadcasted_iota(jnp.int32, (total - cut, scores.shape[1]), 0) + cut
    tail = jnp.where(row < n_tok, scores[cut:], NEG)
    return jnp.concatenate([scores[:cut], tail], axis=0)


def pad_rows(scratch, ref):
    n_img, n_tok, width = ref.shape
    total = scratch.shape[0] // n_img
    cut = n_tok // 8 * 8
    for slot in range(n_img):
        base = slot * total
        scratch[base + cut : base + total, :] = jnp.zeros((total - cut, width), F32)
        scratch[base : base + n_tok, :] = ref[slot].astype(F32)
    return scratch[...]


def select_rows(rows, index_ref, first, n_img):
    total = rows.shape[0] // n_img
    return jnp.concatenate(
        [
            (rows[i * total : (i + 1) * total] * rank_row(index_ref[first + i])).astype(BF16)
            for i in range(n_img)
        ],
        axis=0,
    )


def flat(ref):
    return ref[...].reshape(ref.shape[0] * ref.shape[1], ref.shape[2])


def assemble(place, chunks, starts, wall, sems):
    pieces = len(chunks)
    part = wall.shape[1] // pieces
    copies = []
    for step in range(pieces):
        column = pl.multiple_of(((place % pieces) ^ step) * part, LANES)
        copies.append(
            pltpu.make_async_copy(
                chunks[step].at[:, pl.ds(starts[step], part)], wall.at[:, pl.ds(column, part)], sems.at[step]
            )
        )
    for copy in copies:
        copy.start()
    for copy in copies:
        copy.wait()


def norm_kernel(image_ref, _, out_ref, pad_ref):
    unit, _ = normalise(pad_rows(pad_ref, image_ref))
    out_ref[...] = unit.astype(BF16).reshape(out_ref.shape)


def pack_kernel(place_ref, qkv_ref, a_ref, b_ref, ao_ref, ra_ref, out_ref, pack):
    shards, rows, part = out_ref.shape
    width = qkv_ref.shape[1] // 3
    for piece in range(3):
        pack[:, piece * GROUP : (piece + 1) * GROUP] = qkv_ref[:, piece * width : piece * width + GROUP]
        column = width + (1 + piece) * LANES
        pack[:, column : column + LANES] = b_ref[piece * rows : (piece + 1) * rows, :]
    pack[:, width : width + LANES] = a_ref[...]
    pack[:, width + 4 * LANES : width + 5 * LANES] = ao_ref[...]
    pack[:, width + 5 * LANES : width + 6 * LANES] = ra_ref[...]
    mine = pack[:, pl.ds(pl.multiple_of(place_ref[0] * part, LANES), part)]
    for shard in range(shards):
        out_ref[shard] = mine


def head_mask(value):
    lane = lax.broadcasted_iota(jnp.int32, (1, LANES), 1)
    low = jnp.where(lane < HEAD_DIM, value, 0.0).astype(BF16)
    high = jnp.where(lane < HEAD_DIM, 0.0, value).astype(BF16)
    return low, high


def attention_forward(qkv, n_tok, prob_ref, slot):
    masks = head_mask(0.125)
    value_t = qkv[:, 2 * GROUP :].T
    outs = []
    for pair in range(GROUP // LANES):
        q_pair = qkv[:, pair * LANES : (pair + 1) * LANES]
        k_pair = qkv[:, GROUP + pair * LANES : GROUP + (pair + 1) * LANES]
        both = dot(jnp.concatenate([k_pair * masks[0], k_pair * masks[1]], axis=0), q_pair, NT)
        for side in range(2):
            total = k_pair.shape[0]
            scores = mask_tail(both[side * total : (side + 1) * total], n_tok)
            powers = jnp.exp(scores - jnp.max(scores, axis=0, keepdims=True))
            probs = (powers * (1.0 / jnp.sum(powers, axis=0, keepdims=True))).astype(BF16)
            head = 2 * pair + side
            prob_ref[slot, head] = probs
            outs.append(dot(value_t[head * HEAD_DIM : (head + 1) * HEAD_DIM], probs).astype(BF16))
    return zero_tail(jnp.concatenate(outs, axis=0).T, n_tok)


def first_attention_kernel(
    n_tok, shards, starts, place_ref, index_ref, h1_ref, *rest,
):
    chunks, rest = rest[: len(starts)], rest[len(starts) :]
    qkv_ref, att_ref, prob_ref, uq_ref, a_ref, bt_ref, ao_ref, ra_ref, wall, sems = rest
    step = pl.program_id(0)
    n_img, total, width = h1_ref.shape

    @pl.when(step == 0)
    def _():
        assemble(place_ref[0], chunks, starts, wall, sems)
        a_ref[...] = wall[:, width : width + LANES]
        ao_ref[...] = wall[:, width + 4 * LANES : width + 5 * LANES]
        ra_ref[...] = wall[:, width + 5 * LANES : width + 6 * LANES]
        rows = width // shards
        for shard in range(shards):
            for part in range(3):
                bt_ref[(shard * 3 + part) * rows : (shard * 3 + part + 1) * rows, :] = wall[
                    shard * rows : (shard + 1) * rows,
                    width + (1 + part) * LANES : width + (2 + part) * LANES,
                ]

    h1 = flat(h1_ref)
    low = dot(h1, a_ref[...]).astype(BF16).astype(F32)
    uq = select_rows(low, index_ref, step * n_img, n_img)
    uq_ref[...] = uq.reshape(uq_ref.shape)
    attend_group(0, n_tok, h1, uq, wall, bt_ref, qkv_ref, att_ref, prob_ref)


def group_rows(group, width, bt_ref):
    return jnp.concatenate(
        [bt_ref[part * width + group * GROUP : part * width + (group + 1) * GROUP, :] for part in range(3)],
        axis=0,
    )


def attend_group(group, n_tok, h1, uq, wall, bt_ref, qkv_ref, att_ref, prob_ref):
    n_img, total, _ = att_ref.shape
    second = group_rows(group, wall.shape[0], bt_ref)
    qkv = (dot(h1, wall[:, : 3 * GROUP]) + dot(uq, second, NT)).astype(BF16)
    qkv_ref[...] = qkv.reshape(qkv_ref.shape)
    for slot in range(n_img):
        att_ref[slot] = attention_forward(
            qkv[slot * total : (slot + 1) * total], n_tok, prob_ref, slot
        )


def next_attention_kernel(
    n_tok, group, extra, starts, place_ref, h1_ref, uq_ref, bt_ref, *rest
):
    chunks, rest = rest[: len(starts)], rest[len(starts) :]
    qkv_ref, att_ref, prob_ref = rest[:3]
    wall, sems = rest[-2:]

    @pl.when(pl.program_id(0) == 0)
    def _():
        assemble(place_ref[0], chunks, starts, wall, sems)
        for position in range(extra):
            column = 3 * GROUP + position * LANES
            rest[3 + position][...] = wall[:, column : column + LANES]

    attend_group(
        group, n_tok, flat(h1_ref), flat(uq_ref), wall, bt_ref, qkv_ref, att_ref, prob_ref,
    )


def route_kernel(
    n_exp, starts, place_ref, index_ref, count_ref, image_ref, cot_ref, att0, att1, att2,
    ao_ref, bo_ref, ra_ref, wr_ref, rb_ref, *rest,
):
    chunks, rest = rest[: len(starts)], rest[len(starts) :]
    x2_ref, uo_ref, ur_ref, disp_ref, comb_ref, sg_ref, wrt_ref, wall, pad_a, pad_b, sems = rest
    n_img, n_tok, width = image_ref.shape
    first = pl.program_id(0) * n_img
    total = x2_ref.shape[1]

    @pl.when(first == 0)
    def _():
        assemble(place_ref[0], chunks, starts, wall, sems)
        wrt_ref[...] = wr_ref[...].astype(F32).T[:n_exp].astype(BF16)

    att = jnp.concatenate([flat(att0), flat(att1), flat(att2)], axis=1)
    uo = select_rows(dot(att, ao_ref[...]).astype(BF16).astype(F32), index_ref, first, n_img)
    uo_ref[...] = uo.reshape(uo_ref.shape)
    x2 = pad_rows(pad_a, image_ref) + dot(att, wall[:, :width]) + dot(uo, bo_ref[...], NT)
    x2_ref[...] = x2.reshape(x2_ref.shape)
    h2 = normalise(x2)[0].astype(BF16)
    ur = select_rows(dot(h2, ra_ref[...]).astype(BF16).astype(F32), index_ref, first, n_img)
    ur_ref[...] = ur.reshape(ur_ref.shape)
    cot = pad_rows(pad_b, cot_ref)
    for slot in range(n_img):
        rows = slice(slot * total, (slot + 1) * total)
        living = (first + slot < count_ref[0]).astype(F32)
        logits = dot(wrt_ref[...], h2[rows], NT) + dot(rb_ref[...], ur[rows], NT)
        alive = lax.broadcasted_iota(jnp.int32, logits.shape, 1) < n_tok
        over_tokens = jnp.where(alive, logits, NEG)
        powers = jnp.exp(over_tokens - jnp.max(over_tokens, axis=1, keepdims=True))
        disp = powers / jnp.sum(powers, axis=1, keepdims=True)
        powers = jnp.exp(logits - jnp.max(logits, axis=0, keepdims=True))
        comb = jnp.where(alive, powers / jnp.sum(powers, axis=0, keepdims=True), 0.0)
        disp_ref[slot] = disp
        comb_ref[slot] = comb
        upstream = (cot[rows] * living).astype(BF16)
        sg_ref[slot, :, :width] = dot(disp.astype(BF16), h2[rows]).astype(BF16)
        sg_ref[slot, :, width : 2 * width] = dot(comb.astype(BF16), upstream).astype(BF16)
        selector = rank_row(index_ref[first + slot])
        sg_ref[slot, :, 2 * width :] = jnp.broadcast_to(selector, (n_exp, LANES)).astype(BF16)


def gelu_both(pre):
    square = pre * pre
    half = jnp.tanh(GELU_C * pre * (1.0 + GELU_A * square))
    both = 0.5 * (1.0 + half)
    slope = both + 0.5 * pre * (1.0 - half * half) * (GELU_C * (1.0 + 3.0 * GELU_A * square))
    return pre * both, slope


def expert_tile(slots, gy, u1, gu2, wu_ref, wd_ref, ub_ref, da_ref):
    pre = dot(slots, wu_ref[0]) + dot(u1, ub_ref[0])
    ghid = (dot(wd_ref[0], gy, NT) + dot(da_ref[0], gu2, NT)).T
    hidden, slope = gelu_both(pre)
    return hidden.astype(BF16), (slope * ghid).astype(BF16)


def expert_kernel(
    sg_ref, wu_ref, wd_ref, ua_ref, ub_ref, da_ref, db_ref, out_ref,
    u1_ref, gu2_ref, acc_y, acc_s, acc_u2, acc_gu1,
):
    step = pl.program_id(1)
    width = wu_ref.shape[1]
    selector = sg_ref[0, :, 2 * width :].astype(F32)

    @pl.when(step == 0)
    def _():
        u1_ref[...] = (
            dot(sg_ref[0, :, :width], ua_ref[0]).astype(BF16).astype(F32) * selector
        ).astype(BF16)
        gu2_ref[...] = (dot(sg_ref[0, :, width : 2 * width], db_ref[0], NT) * selector).astype(BF16)
        acc_y[...] = jnp.zeros_like(acc_y)
        acc_s[...] = jnp.zeros_like(acc_s)
        acc_u2[...] = jnp.zeros_like(acc_u2)
        acc_gu1[...] = jnp.zeros_like(acc_gu1)

    hidden, gpre = expert_tile(
        sg_ref[0, :, :width], sg_ref[0, :, width : 2 * width], u1_ref[...], gu2_ref[...],
        wu_ref, wd_ref, ub_ref, da_ref,
    )
    acc_y[...] += dot(hidden, wd_ref[0])
    acc_u2[...] += dot(hidden, da_ref[0])
    acc_s[...] += dot(wu_ref[0], gpre, NT)
    acc_gu1[...] += dot(ub_ref[0], gpre, NT)

    @pl.when(step == pl.num_programs(1) - 1)
    def _():
        u2 = (acc_u2[...].astype(BF16).astype(F32) * selector).astype(BF16)
        gu1 = (acc_gu1[...].T * selector).astype(BF16)
        out_ref[0, :, :width] = (acc_y[...] + dot(u2, db_ref[0])).astype(BF16)
        out_ref[0, :, width:] = (acc_s[...].T + dot(gu1, ua_ref[0], NT)).astype(BF16)


def expert_grad_kernel(
    sg_ref, wu_ref, wd_ref, ua_ref, ub_ref, da_ref, db_ref,
    gua_ref, gub_ref, gda_ref, gdb_ref, u1_ref, gu2_ref, u1t_ref, gu2t_ref, acc_u2, acc_gu1,
):
    step = pl.program_id(1)
    width = wu_ref.shape[1]
    selector = sg_ref[0, :, 2 * width :].astype(F32)

    @pl.when(step == 0)
    def _():
        u1 = dot(sg_ref[0, :, :width], ua_ref[0]).astype(BF16).astype(F32) * selector
        gu2 = dot(sg_ref[0, :, width : 2 * width], db_ref[0], NT) * selector
        u1_ref[...] = u1.astype(BF16)
        gu2_ref[...] = gu2.astype(BF16)
        u1t_ref[...] = u1.T.astype(BF16)
        gu2t_ref[...] = gu2.T.astype(BF16)
        acc_u2[...] = jnp.zeros_like(acc_u2)
        acc_gu1[...] = jnp.zeros_like(acc_gu1)

    hidden, gpre = expert_tile(
        sg_ref[0, :, :width], sg_ref[0, :, width : 2 * width], u1_ref[...], gu2_ref[...],
        wu_ref, wd_ref, ub_ref, da_ref,
    )
    gub_ref[0] = dot(u1t_ref[...], gpre)
    gda_ref[0] = dot(gu2t_ref[...], hidden).T
    acc_u2[...] += dot(hidden, da_ref[0])
    acc_gu1[...] += dot(ub_ref[0], gpre, NT)

    @pl.when(step == pl.num_programs(1) - 1)
    def _():
        u2 = acc_u2[...].astype(BF16).astype(F32) * selector
        gu1 = (acc_gu1[...] * selector.T).astype(BF16)
        gdb_ref[0] = dot(u2.T.astype(BF16), sg_ref[0, :, width : 2 * width])
        gua_ref[0] = dot(gu1, sg_ref[0, :, :width]).T


def route_back_kernel(
    n_exp, starts, place_ref, index_ref, count_ref, cot_ref, x2_ref, uo_ref, ur_ref, disp_ref,
    comb_ref, att0, att1, att2, ret_ref, ao_ref, bo_ref, ra_ref, wrt_ref, rb_ref, *rest,
):
    chunks, rest = rest[: len(starts)], rest[len(starts) :]
    block_ref, gx2_ref, gatt_ref, pack_ref, *rest = rest
    wall, pad_b, acc_oa, acc_ob, acc_ra, acc_rb, sems = rest
    n_img, n_tok, width = cot_ref.shape
    first = pl.program_id(0) * n_img
    total = x2_ref.shape[1]

    @pl.when(first == 0)
    def _():
        assemble(place_ref[0], chunks, starts, wall, sems)
        acc_oa[...] = jnp.zeros_like(acc_oa)
        acc_ob[...] = jnp.zeros_like(acc_ob)
        acc_ra[...] = jnp.zeros_like(acc_ra)
        acc_rb[...] = jnp.zeros_like(acc_rb)

    cot = pad_rows(pad_b, cot_ref)
    x2 = flat(x2_ref)
    unit, scale = normalise(x2)
    h2 = unit.astype(BF16)
    pairs, belows, upstreams = [], [], []
    for slot in range(n_img):
        rows = slice(slot * total, (slot + 1) * total)
        living = (first + slot < count_ref[0]).astype(F32)
        upstream = cot[rows] * living
        upstreams.append(upstream)
        disp, comb = disp_ref[slot], comb_ref[slot]
        yexp, gslot = ret_ref[slot, :, :width], ret_ref[slot, :, width:]
        gcomb = dot(yexp, upstream.astype(BF16), NT)
        gdisp = dot(gslot, h2[rows], NT)
        glog = (
            disp * (gdisp - jnp.sum(gdisp * disp, axis=1, keepdims=True))
            + comb * (gcomb - jnp.sum(gcomb * comb, axis=0, keepdims=True))
        )
        acc_rb[...] += dot(glog.astype(BF16), ur_ref[slot])
        three = jnp.concatenate([disp, glog, comb], axis=0).T.astype(BF16)
        mixed = dot(three[:, 2 * n_exp :], yexp)
        block_ref[slot] = (living * (x2[rows] + mixed)).astype(BF16)[:n_tok]
        pairs.append(three[:, : 2 * n_exp])
        belows.append(jnp.concatenate([gslot, wrt_ref[...]], axis=0))
    glog_rows = jnp.concatenate([pair[:, n_exp:] for pair in pairs], axis=0)
    gur = select_rows(dot(glog_rows, rb_ref[...]), index_ref, first, n_img)
    acc_ra[...] += dot(gur, h2, TN)
    gh2 = dot(gur, ra_ref[...], NT) + jnp.concatenate(
        [dot(pair, below) for pair, below in zip(pairs, belows)], axis=0
    )
    gx2 = jnp.concatenate(upstreams, axis=0) + normalise_back(unit, scale, gh2)
    gx2_ref[...] = gx2.reshape(gx2_ref.shape)
    gbr = gx2.astype(BF16)
    acc_ob[...] += dot(flat(uo_ref), gbr, TN)
    guo = select_rows(dot(gbr, bo_ref[...]), index_ref, first, n_img)
    att = jnp.concatenate([flat(att0), flat(att1), flat(att2)], axis=1)
    acc_oa[...] += dot(guo, att, TN)
    gatt = (dot(gbr, wall[:, :width], NT) + dot(guo, ao_ref[...], NT)).astype(BF16)
    gatt_ref[...] = gatt.reshape(gatt_ref.shape)

    @pl.when(pl.program_id(0) == pl.num_programs(0) - 1)
    def _():
        shards = pack_ref.shape[0]
        rows = width // shards
        n_loc = n_exp // shards
        for position, acc in enumerate((acc_oa, acc_ob, acc_ra)):
            summed = acc[...].T.astype(BF16)
            for shard in range(shards):
                pack_ref[shard, position * rows : (position + 1) * rows, :] = summed[
                    shard * rows : (shard + 1) * rows
                ]
        tail = pack_ref.shape[1] - 3 * rows
        for shard in range(shards):
            last = jnp.concatenate(
                [acc_rb[shard * n_loc : (shard + 1) * n_loc, :], jnp.zeros((tail - n_loc, LANES), F32)],
                axis=0,
            )
            pack_ref[shard, 3 * rows :, :] = last.astype(BF16)


def attention_backward(qkv, gatt, prob_ref, slot):
    keep = head_mask(1.0)
    key_t = qkv[:, GROUP : 2 * GROUP].T
    total = qkv.shape[0]
    lane = lax.broadcasted_iota(jnp.int32, (1, LANES), 1)
    gq_parts, gk_parts, gv_parts = [], [], []
    for pair in range(GROUP // LANES):
        span = slice(pair * LANES, (pair + 1) * LANES)
        q_pair, ga_pair = qkv[:, span], gatt[:, span]
        v_pair = qkv[:, 2 * GROUP + pair * LANES : 2 * GROUP + (pair + 1) * LANES]
        lows = [prob_ref[slot, 2 * pair], prob_ref[slot, 2 * pair + 1]]
        gv = dot(jnp.concatenate(lows, axis=0), ga_pair)
        gprobs = dot(jnp.concatenate([v_pair * keep[0], v_pair * keep[1]], axis=0), ga_pair, NT)
        gscores = []
        for side in range(2):
            probs = lows[side].astype(F32)
            gprob = gprobs[side * total : (side + 1) * total]
            inner = jnp.sum(gprob * probs, axis=0, keepdims=True)
            gscores.append((probs * (gprob - inner)).astype(BF16))
            head = 2 * pair + side
            gq_parts.append(
                (dot(key_t[head * HEAD_DIM : (head + 1) * HEAD_DIM], gscores[side]) * 0.125).astype(BF16)
            )
        gk = dot(jnp.concatenate(gscores, axis=0), q_pair)
        gk_parts.append((jnp.where(lane < HEAD_DIM, gk[:total], gk[total:]) * 0.125).astype(BF16))
        gv_parts.append(jnp.where(lane < HEAD_DIM, gv[:total], gv[total:]).astype(BF16))
    gq = jnp.concatenate(gq_parts, axis=0).T
    return jnp.concatenate([gq] + gk_parts + gv_parts, axis=1)


def attention_back_kernel(group, last, *refs):
    refs = list(refs)
    index_ref = refs.pop(0) if last else None
    qkv_ref, gatt_ref, prob_ref, uq_ref, bt_ref = refs[:5]
    refs = refs[5:]
    before_ref = refs.pop(0) if group else None
    h1_ref = refs.pop(0) if last else None
    befores = [refs.pop(0) for _ in range(group)] if last else ()
    gqkv_ref, guq_ref, gb_ref = refs[:3]
    refs = refs[3:]
    acc_b = refs.pop(0)
    acc_a = refs.pop(0) if last else None
    step = pl.program_id(0)
    width = bt_ref.shape[0] // 3
    n_img, total, _ = qkv_ref.shape

    @pl.when(step == 0)
    def _():
        acc_b[...] = jnp.zeros_like(acc_b)
        if last:
            acc_a[...] = jnp.zeros_like(acc_a)

    parts = [attention_backward(qkv_ref[i], gatt_ref[i], prob_ref, i) for i in range(n_img)]
    for i in range(n_img):
        gqkv_ref[i] = parts[i]
    gqkv = jnp.concatenate(parts, axis=0)
    acc_b[...] += dot(flat(uq_ref), gqkv, TN)
    guq = dot(gqkv, group_rows(group, width, bt_ref))
    if group:
        guq = guq + flat(before_ref)
    if last:
        guq = select_rows(guq, index_ref, step * n_img, n_img)
        acc_a[...] += dot(guq, flat(h1_ref), TN)
    guq_ref[...] = guq.reshape(guq_ref.shape)

    @pl.when(step == pl.num_programs(0) - 1)
    def _():
        summed = acc_b[...].T.astype(BF16)
        if not last:
            gb_ref[...] = summed
            return
        shards = gb_ref.shape[0]
        rows = width // shards
        own = acc_a[...].T.astype(BF16)
        for shard in range(shards):
            gb_ref[shard, 3 * rows :, :] = own[shard * rows : (shard + 1) * rows]
        sources = [before[...] for before in befores] + [summed]
        for part in range(3):
            for source in range(group + 1):
                start = part * width + source * GROUP
                place = start
                while place < start + GROUP:
                    shard, offset = divmod(place, 3 * rows)
                    length = min(start + GROUP - place, 3 * rows - offset)
                    take = part * GROUP + place - start
                    gb_ref[shard, offset : offset + length, :] = sources[source][take : take + length]
                    place += length


def input_grad_kernel(starts, place_ref, image_ref, gx2_ref, guq_ref, a_ref, *refs):
    refs = list(refs)
    groups = len(starts)
    gqkv = [refs.pop(0) for _ in starts]
    chunks = [[refs.pop(0) for _ in start] for start in starts]
    out_ref = refs.pop(0)
    walls = [refs.pop(0) for _ in starts]
    pad_a, sems = refs
    n_img, n_tok, width = image_ref.shape
    step = pl.program_id(0)
    parts = width // LANES
    every = out_ref.shape[0] // (n_tok * parts)

    @pl.when(step == 0)
    def _():
        for group in range(groups):
            assemble(place_ref[0], chunks[group], starts[group], walls[group], sems.at[group])

    gh1 = dot(flat(guq_ref), a_ref[...], NT)
    for group in range(groups):
        gh1 = gh1 + dot(flat(gqkv[group]), walls[group][:, : 3 * GROUP], NT)
    unit, scale = normalise(pad_rows(pad_a, image_ref))
    total = gx2_ref.shape[1]
    result = flat(gx2_ref) + normalise_back(unit, scale, gh1)
    for slot in range(n_img):
        for part in range(parts):
            out_ref[pl.ds(part * every + step * n_img + slot, n_tok, stride=parts * every), :] = result[
                slot * total : slot * total + n_tok, part * LANES : (part + 1) * LANES
            ]


ANY = pl.BlockSpec(memory_space=pl.ANY)


def whole(shape):
    return pl.BlockSpec(shape, lambda *_: (0,) * len(shape))


def per_image(*shape, images=1):
    return pl.BlockSpec((images,) + shape, lambda i, *_: (i,) + (0,) * len(shape))


def several(images, limit):
    return max(n for n in range(1, limit + 1) if images % n == 0)


def call(kernel, scalars, grid, inputs, outputs, scratch, flops, exps=0, aliases=None):
    arrays = [array for array, _ in inputs]
    shapes = [jax.ShapeDtypeStruct(shape, dtype) for shape, dtype, _ in outputs]
    moved = sum(array.size * array.dtype.itemsize for array in arrays) + sum(
        shape.size * shape.dtype.itemsize for shape in shapes
    )
    return pl.pallas_call(
        kernel,
        out_shape=shapes,
        grid_spec=pltpu.PrefetchScalarGridSpec(
            num_scalar_prefetch=len(scalars),
            grid=grid,
            in_specs=[spec for _, spec in inputs],
            out_specs=[spec for _, _, spec in outputs],
            scratch_shapes=scratch,
        ),
        input_output_aliases=aliases or {},
        compiler_params=params(*(("arbitrary",) * len(grid))),
        cost_estimate=cost(flops, moved, exps),
    )(*scalars, *arrays)


def norm_call(images, cotangent, total):
    n_img, n_tok, width = images.shape
    each = several(n_img, 4)
    return call(
        norm_kernel, (), (n_img // each,),
        [(images, per_image(n_tok, width, images=each)), (cotangent, ANY)],
        [((n_img, total, width), BF16, per_image(total, width, images=each))],
        [pltpu.VMEM((each * total, width), F32)],
        8 * images.size,
    )[0]


def pack_call(place, weights, shards):
    rows, columns = weights[0].shape
    part = (columns // 3 + 6 * LANES) // 4
    return call(
        pack_kernel, (place,), (1,), [(weight, whole(weight.shape)) for weight in weights],
        [((shards, rows, part), BF16, whole((shards, rows, part)))],
        [pltpu.VMEM((rows, 4 * part), BF16)],
        rows * columns,
    )[0]


def attention_flops(n_img, total, width, parts):
    return n_img * total * (2 * width * 3 * GROUP + parts * 8 * total * HEAD_DIM)


def attention_outputs(n_img, total, each):
    return [
        ((n_img, total, 3 * GROUP), BF16, per_image(total, 3 * GROUP, images=each)),
        ((n_img, total, GROUP), BF16, per_image(total, GROUP, images=each)),
        (
            (n_img, GROUP // HEAD_DIM, total, total), BF16,
            per_image(GROUP // HEAD_DIM, total, total, images=each),
        ),
    ]


def first_attention_call(place, index, h1, pack, n_tok, shards):
    n_img, total, width = h1.shape
    chunks, starts, columns = pack
    each = several(n_img, IMAGES_FORWARD)
    return call(
        functools.partial(first_attention_kernel, n_tok, shards, starts), (place, index), (n_img // each,),
        [(h1, per_image(total, width, images=each))] + [(chunk, ANY) for chunk in chunks],
        attention_outputs(n_img, total, each)
        + [
            ((n_img, total, LANES), BF16, per_image(total, LANES, images=each)),
            ((width, LANES), BF16, whole((width, LANES))),
            ((3 * width, LANES), BF16, whole((3 * width, LANES))),
            ((width, LANES), BF16, whole((width, LANES))),
            ((width, LANES), BF16, whole((width, LANES))),
        ],
        [pltpu.VMEM((width, columns), BF16), pltpu.SemaphoreType.DMA((4,))],
        attention_flops(n_img, total, width, 2), n_img * total * total * 4,
    )


def next_attention_call(place, h1, uq, bt, pack, n_tok, group, extra):
    n_img, total, width = h1.shape
    chunks, starts, columns = pack
    each = several(n_img, IMAGES_FORWARD)
    return call(
        functools.partial(next_attention_kernel, n_tok, group, extra, starts), (place,), (n_img // each,),
        [
            (h1, per_image(total, width, images=each)),
            (uq, per_image(total, LANES, images=each)),
            (bt, whole(bt.shape)),
        ]
        + [(chunk, ANY) for chunk in chunks],
        attention_outputs(n_img, total, each)
        + [((width, LANES), BF16, whole((width, LANES)))] * extra,
        [pltpu.VMEM((width, columns), BF16), pltpu.SemaphoreType.DMA((4,))],
        attention_flops(n_img, total, width, 2), n_img * total * total * 4,
    )


def route_call(place, index, count, images, cotangent, atts, banks, pack, n_exp, total):
    n_img, n_tok, width = images.shape
    chunks, starts, columns = pack
    each = several(n_img, IMAGES_ROUTE)
    here = functools.partial(per_image, images=each)
    return call(
        functools.partial(route_kernel, n_exp, starts), (place, index, count), (n_img // each,),
        [(images, here(n_tok, width)), (cotangent, here(n_tok, width))]
        + [(att, here(total, GROUP)) for att in atts]
        + [(bank, whole(bank.shape)) for bank in banks]
        + [(chunk, ANY) for chunk in chunks],
        [
            ((n_img, total, width), F32, here(total, width)),
            ((n_img, total, LANES), BF16, here(total, LANES)),
            ((n_img, total, LANES), BF16, here(total, LANES)),
            ((n_img, n_exp, total), F32, here(n_exp, total)),
            ((n_img, n_exp, total), F32, here(n_exp, total)),
            ((n_img, n_exp, 2 * width + LANES), BF16, here(n_exp, 2 * width + LANES)),
            ((n_exp, width), BF16, whole((n_exp, width))),
        ],
        [
            pltpu.VMEM((width, columns), BF16),
            pltpu.VMEM((each * total, width), F32),
            pltpu.VMEM((each * total, width), F32),
            pltpu.SemaphoreType.DMA((4,)),
        ],
        n_img * total * 2 * width * (width + 3 * LANES), n_img * total * 2 * n_exp,
    )


def hidden_tile(hidden, limit):
    tile = hidden
    while tile > limit:
        tile //= 2
    return tile


def expert_specs(rows, width, tile, first=0):
    return (
        pl.BlockSpec((1, rows, 2 * width + LANES), lambda e, f: (e + first, 0, 0)),
        pl.BlockSpec((1, width, tile), lambda e, f: (e + first, 0, f)),
        pl.BlockSpec((1, tile, width), lambda e, f: (e + first, f, 0)),
        pl.BlockSpec((1, width, LANES), lambda e, f: (e + first, 0, 0)),
        pl.BlockSpec((1, LANES, tile), lambda e, f: (e + first, 0, f)),
        pl.BlockSpec((1, tile, LANES), lambda e, f: (e + first, f, 0)),
        pl.BlockSpec((1, LANES, width), lambda e, f: (e + first, 0, 0)),
    )


def expert_call(sg, weights):
    n_loc, rows, _ = sg.shape
    width, hidden = weights[0].shape[1:]
    tile = hidden_tile(hidden, 768)
    return call(
        expert_kernel, (), (n_loc, hidden // tile),
        list(zip((sg,) + weights, expert_specs(rows, width, tile))),
        [((n_loc, rows, 2 * width), BF16, pl.BlockSpec((1, rows, 2 * width), lambda e, f: (e, 0, 0)))],
        [
            pltpu.VMEM((rows, LANES), BF16),
            pltpu.VMEM((rows, LANES), BF16),
            pltpu.VMEM((rows, width), F32),
            pltpu.VMEM((width, rows), F32),
            pltpu.VMEM((rows, LANES), F32),
            pltpu.VMEM((LANES, rows), F32),
        ],
        n_loc * rows * 8 * width * hidden, n_loc * rows * hidden,
    )[0]


def expert_grad_call(sg, weights, first, before):
    n_loc, rows, _ = sg.shape
    width, hidden = weights[0].shape[1:]
    tile = hidden_tile(hidden, 768 if rows <= 512 else 384)
    kernel = expert_grad_kernel
    if before:
        kernel = lambda *refs: expert_grad_kernel(*refs[:7], *refs[11:])
    return call(
        kernel, (), (1, hidden // tile),
        list(zip((sg,) + weights, expert_specs(rows, width, tile, first)))
        + [(array, ANY) for array in before],
        [
            ((n_loc, width, LANES), F32, pl.BlockSpec((1, width, LANES), lambda e, f: (e + first, 0, 0))),
            ((n_loc, LANES, hidden), F32, pl.BlockSpec((1, LANES, tile), lambda e, f: (e + first, 0, f))),
            ((n_loc, hidden, LANES), F32, pl.BlockSpec((1, tile, LANES), lambda e, f: (e + first, f, 0))),
            ((n_loc, LANES, width), F32, pl.BlockSpec((1, LANES, width), lambda e, f: (e + first, 0, 0))),
        ],
        [
            pltpu.VMEM((rows, LANES), BF16),
            pltpu.VMEM((rows, LANES), BF16),
            pltpu.VMEM((LANES, rows), BF16),
            pltpu.VMEM((LANES, rows), BF16),
            pltpu.VMEM((rows, LANES), F32),
            pltpu.VMEM((LANES, rows), F32),
        ],
        rows * 4 * width * hidden, rows * hidden,
        {7 + i: i for i in range(4)} if before else {},
    )


def route_back_call(
    place, index, count, cotangent, x2, uo, ur, disp, comb, atts, ret, banks, pack, shards, replicas
):
    n_img, n_tok, width = cotangent.shape
    chunks, starts, columns = pack
    total, n_exp = x2.shape[1], disp.shape[1]
    rows = width // shards
    unit = 16 * replicas
    pack_rows = -(-(3 * rows + n_exp // shards) // unit) * unit
    each = several(n_img, IMAGES_ROUTE)
    here = functools.partial(per_image, images=each)
    return call(
        functools.partial(route_back_kernel, n_exp, starts), (place, index, count), (n_img // each,),
        [
            (cotangent, here(n_tok, width)),
            (x2, here(total, width)),
            (uo, here(total, LANES)),
            (ur, here(total, LANES)),
            (disp, here(n_exp, total)),
            (comb, here(n_exp, total)),
        ]
        + [(att, here(total, GROUP)) for att in atts]
        + [(ret, here(n_exp, 2 * width))]
        + [(bank, whole(bank.shape)) for bank in banks]
        + [(chunk, ANY) for chunk in chunks],
        [
            ((n_img, n_tok, width), BF16, here(n_tok, width)),
            ((n_img, total, width), F32, here(total, width)),
            ((n_img, total, width), BF16, here(total, width)),
            ((shards, pack_rows, LANES), BF16, whole((shards, pack_rows, LANES))),
        ],
        [
            pltpu.VMEM((width, columns), BF16),
            pltpu.VMEM((each * total, width), F32),
            pltpu.VMEM((LANES, width), F32),
            pltpu.VMEM((LANES, width), F32),
            pltpu.VMEM((LANES, width), F32),
            pltpu.VMEM((n_exp, LANES), F32),
            pltpu.SemaphoreType.DMA((4,)),
        ],
        n_img * total * 2 * width * (width + 6 * LANES),
    )


def attention_back_call(index, qkv, gatt, prob, uq, bt, before, h1, group, gbs=(), shards=1):
    n_img, total, _ = qkv.shape
    width = bt.shape[0] // 3
    last = h1 is not None
    each = several(n_img, IMAGES_BACK)
    inputs = [
        (qkv, per_image(total, 3 * GROUP, images=each)),
        (gatt, pl.BlockSpec((each, total, GROUP), lambda i, *_: (i, 0, group))),
        (prob, per_image(GROUP // HEAD_DIM, total, total, images=each)),
        (uq, per_image(total, LANES, images=each)),
        (bt, whole(bt.shape)),
    ]
    outputs = [
        ((n_img, total, 3 * GROUP), BF16, per_image(total, 3 * GROUP, images=each)),
        ((n_img, total, LANES), BF16 if last else F32, per_image(total, LANES, images=each)),
        ((3 * GROUP, LANES), BF16, whole((3 * GROUP, LANES))),
    ]
    scratch = [pltpu.VMEM((LANES, 3 * GROUP), F32)]
    if group:
        inputs.append((before, per_image(total, LANES, images=each)))
    if last:
        inputs.append((h1, per_image(total, width, images=each)))
        inputs.extend((gb, whole(gb.shape)) for gb in gbs)
        shape = (shards, 4 * width // shards, LANES)
        outputs[-1] = (shape, BF16, whole(shape))
        scratch.append(pltpu.VMEM((LANES, width), F32))
    return call(
        functools.partial(attention_back_kernel, group, last),
        (index,) if last else (), (n_img // each,), inputs, outputs, scratch,
        attention_flops(n_img, total, LANES, 5), n_img * total * total * 4,
    )


def input_grad_call(place, images, gx2, guq, bank_a, gqkvs, packs):
    n_img, n_tok, width = images.shape
    total = gx2.shape[1]
    groups = len(gqkvs)
    each = several(n_img, IMAGES_LAST)
    here = functools.partial(per_image, images=each)
    out = call(
        functools.partial(input_grad_kernel, tuple(pack[1] for pack in packs)), (place,), (n_img // each,),
        [
            (images, here(n_tok, width)),
            (gx2, here(total, width)),
            (guq, here(total, LANES)),
            (bank_a, whole(bank_a.shape)),
        ]
        + [(gqkv, here(total, 3 * GROUP)) for gqkv in gqkvs]
        + [(chunk, ANY) for pack in packs for chunk in pack[0]],
        [((images.size // LANES, LANES), F32, whole((images.size // LANES, LANES)))],
        [pltpu.VMEM((width, pack[2]), BF16) for pack in packs]
        + [pltpu.VMEM((each * total, width), F32), pltpu.SemaphoreType.DMA((groups, 4))],
        n_img * total * 2 * width * (3 * width + LANES),
    )[0]
    out = out.reshape(n_tok, width // LANES, n_img, LANES).transpose(2, 0, 1, 3)
    return out.reshape(n_img, n_tok, width)


def swap(array, axis, size, bit):
    return lax.ppermute(array, axis, [(i, i ^ bit) for i in range(size)])


def tie(*arrays):
    return lax.optimization_barrier(arrays)


def own_columns(pack, quarter, pieces):
    part = pack.shape[1] // pieces
    return lax.dynamic_slice(pack, (0, quarter % pieces * part), (pack.shape[0], part))


def spread(rows, shards):
    return jnp.broadcast_to(rows[None], (shards,) + rows.shape)


def over_shard(spread):
    own = lax.all_to_all(spread, "shard", split_axis=0, concat_axis=0, tiled=True)
    return own.reshape(-1, spread.shape[2])


def reduce_pack(pack, replicas):
    where = lax.axis_index("replica")
    bits = []
    bit = 1
    while bit < replicas:
        half = pack.shape[1] // 2
        side = (where // bit) % 2
        keep = lax.dynamic_slice_in_dim(pack, side * half, half, axis=1)
        give = lax.dynamic_slice_in_dim(pack, (1 - side) * half, half, axis=1)
        got = swap(give, "replica", replicas, bit)
        pack = (keep.astype(F32) + got.astype(F32)).astype(BF16)
        bits.append(bit)
        bit *= 2
    landed = lax.all_to_all(pack, "shard", split_axis=0, concat_axis=0, tiled=True)
    total = jnp.sum(landed.astype(F32), axis=0).astype(BF16)
    for bit in reversed(bits):
        got = swap(total, "replica", replicas, bit)
        side = (where // bit) % 2
        total = jnp.where(
            side == 0,
            jnp.concatenate([total, got], axis=0),
            jnp.concatenate([got, total], axis=0),
        )
    return total


def per_device(
    replicas,
    shards,
    images,
    image_adapter_index,
    device_image_count,
    cotangent,
    query_key_value_weight,
    frozen_output_weight,
    frozen_dispatch_weight,
    query_key_value_first,
    query_key_value_second,
    output_adapter_first,
    output_adapter_second,
    dispatch_adapter_first,
    dispatch_adapter_second,
    frozen_up_weight,
    frozen_down_weight,
    up_adapter_first,
    up_adapter_second,
    down_adapter_first,
    down_adapter_second,
):
    n_img, n_tok, width = images.shape
    total = -(-n_tok // 16) * 16
    rows = width // shards
    n_loc = frozen_up_weight.shape[0]
    n_exp = n_loc * shards
    groups = width // GROUP
    quarter = lax.axis_index("replica") % 4
    place = quarter.astype(jnp.int32).reshape(1)

    def qkv_columns(group):
        return [
            query_key_value_weight[:, part * width + group * GROUP : part * width + (group + 1) * GROUP]
            for part in range(3)
        ]

    route_block = jnp.concatenate(
        [
            frozen_dispatch_weight,
            jnp.zeros((rows, 64 - n_exp), BF16),
            jnp.pad(dispatch_adapter_second.T.reshape(16, n_loc * 8), ((0, rows - 16), (0, 0))),
            jnp.zeros((rows, 64 - n_loc * 8), BF16),
        ],
        axis=1,
    )
    empty = jnp.zeros((rows, LANES), BF16)
    packs = [
        (qkv_columns(1) + [output_adapter_second.T, route_block], 2),
        (qkv_columns(2) + [empty, empty], 4),
        ([frozen_output_weight, empty, empty], 4),
    ]
    spread0 = pack_call(
        place,
        (
            query_key_value_weight, query_key_value_first, query_key_value_second.T,
            output_adapter_first, dispatch_adapter_first,
        ),
        shards,
    )
    mine = [own_columns(jnp.concatenate(pack, axis=1), quarter, pieces) for pack, pieces in packs]
    near = functools.partial(swap, axis="replica", size=replicas, bit=1)
    far = functools.partial(swap, axis="replica", size=replicas, bit=2)

    own0 = over_shard(spread0)
    h1 = norm_call(images, cotangent, total)
    own0, h1, mine1, mine2 = tie(own0, h1, *mine[:2])
    own12 = over_shard(spread(jnp.concatenate([mine1, mine2], axis=1), shards))
    y0 = far(own0)
    chunks0 = (own0, near(own0), y0, near(y0))
    *chunks0, h1 = tie(*chunks0, h1)
    pack0 = (chunks0, (0,) * 4, 3 * GROUP + 6 * LANES)
    qkv0, att0, prob0, uq, bank_a, bank_bt, bank_ao, bank_ra = first_attention_call(
        place, image_adapter_index, h1, pack0, n_tok, shards
    )
    uq, own12, mine3 = tie(uq, own12, mine[2])
    first = mine1.shape[1]
    own1, own2 = own12[:, :first], own12[:, first:]
    pack1 = ((own12, near(own1)), (0, 0), 3 * GROUP + 2 * LANES)
    y2 = far(own2)
    own3 = over_shard(spread(mine3, shards))
    qkv1, att1, prob1, bank_bo, bank_wr = next_attention_call(
        place, h1, uq, bank_bt, pack1, n_tok, 1, 2
    )
    att1, uq, own2, y2, own3 = tie(att1, uq, own2, y2, own3)
    pack2 = ((own12, near(own2), y2, near(y2)), (first, 0, 0, 0), 3 * GROUP + 2 * LANES)
    y3 = far(own3)
    qkv2, att2, prob2 = next_attention_call(place, h1, uq, bank_bt, pack2, n_tok, 2, 0)
    att2, own3, y3 = tie(att2, own3, y3)
    pack3 = ((own3, near(own3), y3, near(y3)), (0,) * 4, width + 2 * LANES)
    packs = (pack0, pack1, pack2, pack3)
    atts = (att0, att1, att2)
    bank_rb = bank_wr.reshape(shards, rows, LANES)[:, :16, 64 : 64 + n_loc * 8].reshape(n_exp, LANES)
    x2, uo, ur, disp, comb, sg, bank_wrt = route_call(
        place, image_adapter_index, device_image_count, images, cotangent, atts,
        (bank_ao, bank_bo, bank_ra, bank_wr, bank_rb), packs[3], n_exp, total,
    )

    sent = sg.reshape(n_img, shards, n_loc, -1).transpose(1, 2, 0, 3)
    landed = lax.all_to_all(sent, "shard", split_axis=0, concat_axis=0, tiled=True)
    landed = landed.transpose(1, 0, 2, 3).reshape(n_loc, shards * n_img, -1)
    weights = (
        frozen_up_weight, frozen_down_weight, up_adapter_first, up_adapter_second,
        down_adapter_first, down_adapter_second,
    )
    ret = expert_call(landed, weights)
    over_y = [swap(landed, "replica", replicas, bit) for bit in range(2, replicas, 2)]
    ret, *over_y = tie(ret, *over_y)
    back = ret.reshape(n_loc, shards, n_img, 2 * width).transpose(1, 0, 2, 3)
    back = lax.all_to_all(back, "shard", split_axis=0, concat_axis=0, tiled=True)
    every = jnp.concatenate([landed] + over_y, axis=1)
    every = jnp.concatenate([every, swap(every, "replica", replicas, 1)], axis=1)
    grads = expert_grad_call(every, weights, 0, ())
    back, *grads = tie(back, *grads)
    back = back.transpose(2, 0, 1, 3).reshape(n_img, n_exp, 2 * width)

    block_out, gx2, gatt, out_pack = route_back_call(
        place, image_adapter_index, device_image_count, cotangent, x2, uo, ur, disp, comb, atts, back,
        (bank_ao, bank_bo, bank_ra, bank_wrt, bank_rb), packs[3], shards, replicas,
    )
    out_sum = reduce_pack(out_pack, replicas).astype(F32)

    gqkv0, guq, gb0 = attention_back_call(None, qkv0, gatt, prob0, uq, bank_bt, None, None, 0)
    gqkv1, guq, gb1 = attention_back_call(None, qkv1, gatt, prob1, uq, bank_bt, guq, None, 1)
    gqkv2, guq, qkv_pack = attention_back_call(
        image_adapter_index, qkv2, gatt, prob2, uq, bank_bt, guq, h1, 2, (gb0, gb1), shards
    )
    qkv_sum = reduce_pack(qkv_pack, replicas).astype(F32)
    input_grad = input_grad_call(
        place, images, gx2, guq, bank_a, (gqkv0, gqkv1, gqkv2), packs[:3]
    )
    for expert in range(1, n_loc):
        grads = expert_grad_call(every, weights, expert, tuple(grads))
    return (
        block_out,
        input_grad,
        qkv_sum[3 * rows :],
        qkv_sum[: 3 * rows].T,
        out_sum[:rows],
        out_sum[rows : 2 * rows].T,
        out_sum[2 * rows : 3 * rows],
        out_sum[3 * rows : 3 * rows + n_loc].T,
        *grads,
    )


def solution(mesh):
    images = P(("replica", "shard"), None, None)
    each = P(("replica", "shard"))
    by_row, by_column, by_expert = P("shard", None), P(None, "shard"), P("shard", None, None)
    in_specs = (
        (images, each, each, images)
        + (by_row, by_row, by_row)
        + (by_row, by_column) * 3
        + (by_expert,) * 6
    )
    out_specs = (images, images) + (by_row, by_column) * 3 + (by_expert,) * 4
    return jax.shard_map(
        functools.partial(per_device, mesh.shape["replica"], mesh.shape["shard"]),
        mesh=mesh,
        in_specs=in_specs,
        out_specs=out_specs,
        check_vma=False,
    )
```

```python
import functools

import jax
import jax.numpy as jnp
from jax import lax
from jax.experimental import pallas as pl
from jax.experimental.pallas import tpu as pltpu
from jax.sharding import PartitionSpec as P

HEADS = 12
RANK = 16
LANES = 128
HEAD_DIM = 64
GROUP = 256
F32 = jnp.float32
BF16 = jnp.bfloat16
NN = (((1,), (0,)), ((), ()))
NT = (((1,), (1,)), ((), ()))
TN = (((0,), (0,)), ((), ()))
NEG = -1e30
VMEM_LIMIT = 56 * 1024 * 1024
GELU_C = 0.7978845608028654
GELU_A = 0.044715
IMAGES_FORWARD = 2
IMAGES_BACK = 1
IMAGES_ROUTE = 2
IMAGES_LAST = 2
STRIPS = 4


def dot(left, right, dims=NN):
    return lax.dot_general(left, right, dims, preferred_element_type=F32)


def params(*axes):
    return pltpu.CompilerParams(
        dimension_semantics=axes or None, vmem_limit_bytes=VMEM_LIMIT
    )


def cost(flops, moved, exps=0):
    return pl.CostEstimate(flops=int(flops), bytes_accessed=int(moved), transcendentals=int(exps))


def normalise(rows):
    centre = rows - jnp.mean(rows, axis=-1, keepdims=True)
    spread = jnp.mean(centre * centre, axis=-1, keepdims=True)
    scale = lax.rsqrt(spread + 1e-06)
    return centre * scale, scale


def normalise_back(unit, scale, upstream):
    inner = jnp.mean(upstream * unit, axis=-1, keepdims=True)
    return scale * (upstream - jnp.mean(upstream, axis=-1, keepdims=True) - unit * inner)


def rank_row(index):
    lane = lax.broadcasted_iota(jnp.int32, (1, LANES), 1) // RANK
    return (lane == index).astype(F32)


def zero_tail(rows, n_tok):
    total = rows.shape[0]
    cut = n_tok // 16 * 16
    if n_tok == total:
        return rows
    row = lax.broadcasted_iota(jnp.int32, (total - cut, rows.shape[1]), 0) + cut
    tail = jnp.where(row < n_tok, rows[cut:].astype(F32), 0.0).astype(rows.dtype)
    return jnp.concatenate([rows[:cut], tail], axis=0)


def mask_tail(scores, n_tok):
    total = scores.shape[0]
    cut = n_tok // 16 * 16
    if n_tok == total:
        return scores
    row = lax.broadcasted_iota(jnp.int32, (total - cut, scores.shape[1]), 0) + cut
    tail = jnp.where(row < n_tok, scores[cut:], NEG)
    return jnp.concatenate([scores[:cut], tail], axis=0)


def pad_rows(scratch, ref):
    n_img, n_tok, width = ref.shape
    total = scratch.shape[0] // n_img
    cut = n_tok // 8 * 8
    for slot in range(n_img):
        base = slot * total
        scratch[base + cut : base + total, :] = jnp.zeros((total - cut, width), F32)
        scratch[base : base + n_tok, :] = ref[slot].astype(F32)
    return scratch[...]


def select_rows(rows, index_ref, first, n_img):
    total = rows.shape[0] // n_img
    return jnp.concatenate(
        [
            (rows[i * total : (i + 1) * total] * rank_row(index_ref[first + i])).astype(BF16)
            for i in range(n_img)
        ],
        axis=0,
    )


def flat(ref):
    return ref[...].reshape(ref.shape[0] * ref.shape[1], ref.shape[2])


def assemble(place_ref, chunks, layout, wall):
    pieces, entries = layout
    part = wall.shape[1] // pieces
    for chunk, (replica, neighbour, start) in zip(chunks, entries):
        column = pl.multiple_of(((place_ref[0] % pieces) ^ replica) * part, LANES)
        if neighbour is None:
            wall[:, pl.ds(column, part)] = chunk[:, start : start + part]
            continue
        strips = STRIPS
        rows = chunk.shape[0] // strips
        for strip in range(strips):
            row = pl.multiple_of((2 * strip + (place_ref[1] ^ neighbour)) * rows, 16)
            wall[pl.ds(row, rows), pl.ds(column, part)] = chunk[
                strip * rows : (strip + 1) * rows, start : start + part
            ]


def norm_kernel(image_ref, _, out_ref, pad_ref):
    unit, _ = normalise(pad_rows(pad_ref, image_ref))
    out_ref[...] = unit.astype(BF16).reshape(out_ref.shape)


def pack_kernel(place_ref, qkv_ref, a_ref, b_ref, ao_ref, ra_ref, out_ref, pack):
    copies, rows, part = out_ref.shape
    width = qkv_ref.shape[1] // 3
    for piece in range(3):
        pack[:, piece * GROUP : (piece + 1) * GROUP] = qkv_ref[:, piece * width : piece * width + GROUP]
        column = width + (1 + piece) * LANES
        pack[:, column : column + LANES] = b_ref[piece * rows : (piece + 1) * rows, :]
    pack[:, width : width + LANES] = a_ref[...]
    pack[:, width + 4 * LANES : width + 5 * LANES] = ao_ref[...]
    pack[:, width + 5 * LANES : width + 6 * LANES] = ra_ref[...]
    mine = pack[:, pl.ds(pl.multiple_of(place_ref[0] * part, LANES), part)]
    for copy in range(copies):
        out_ref[copy] = mine


def head_mask(value):
    lane = lax.broadcasted_iota(jnp.int32, (1, LANES), 1)
    low = jnp.where(lane < HEAD_DIM, value, 0.0).astype(BF16)
    high = jnp.where(lane < HEAD_DIM, 0.0, value).astype(BF16)
    return low, high


def each_head(columns, value):
    head = lax.broadcasted_iota(jnp.int32, (1, GROUP), 1) // HEAD_DIM
    return jnp.concatenate(
        [
            columns * jnp.where(head == number, value, 0.0).astype(BF16)
            for number in range(GROUP // HEAD_DIM)
        ],
        axis=0,
    )


def merge_pair(low, high):
    lane = lax.broadcasted_iota(jnp.int32, (1, LANES), 1)
    return jnp.where(lane < HEAD_DIM, low, high)


def attention_forward(qkv, n_tok, prob_ref, slot):
    total = qkv.shape[0]
    every = dot(each_head(qkv[:, GROUP : 2 * GROUP], 0.125), qkv[:, :GROUP], NT)
    outs = []
    for head in range(GROUP // HEAD_DIM):
        scores = mask_tail(every[head * total : (head + 1) * total], n_tok)
        powers = jnp.exp(scores - jnp.max(scores, axis=0, keepdims=True))
        probs = (powers * (1.0 / jnp.sum(powers, axis=0, keepdims=True))).astype(BF16)
        prob_ref[slot, head] = probs
        column = 2 * GROUP + head // 2 * LANES
        outs.append(dot(probs, qkv[:, column : column + LANES], TN))
    pairs = [merge_pair(outs[head], outs[head + 1]) for head in range(0, len(outs), 2)]
    return zero_tail(jnp.concatenate(pairs, axis=1).astype(BF16), n_tok)


def first_attention_kernel(
    n_tok, shards, layout, place_ref, index_ref, h1_ref, *rest,
):
    chunks, rest = rest[: len(layout[1])], rest[len(layout[1]) :]
    qkv_ref, att_ref, prob_ref, uq_ref, a_ref, bt_ref, ao_ref, ra_ref, wall = rest
    step = pl.program_id(0)
    n_img, total, width = h1_ref.shape

    @pl.when(step == 0)
    def _():
        assemble(place_ref, chunks, layout, wall)
        a_ref[...] = wall[:, width : width + LANES]
        ao_ref[...] = wall[:, width + 4 * LANES : width + 5 * LANES]
        ra_ref[...] = wall[:, width + 5 * LANES : width + 6 * LANES]
        rows = width // shards
        for shard in range(shards):
            for part in range(3):
                bt_ref[(shard * 3 + part) * rows : (shard * 3 + part + 1) * rows, :] = wall[
                    shard * rows : (shard + 1) * rows,
                    width + (1 + part) * LANES : width + (2 + part) * LANES,
                ]

    h1 = flat(h1_ref)
    low = dot(h1, a_ref[...]).astype(BF16).astype(F32)
    uq = select_rows(low, index_ref, step * n_img, n_img)
    uq_ref[...] = uq.reshape(uq_ref.shape)
    attend_group(0, n_tok, h1, uq, wall, bt_ref, qkv_ref, att_ref, prob_ref)


def group_rows(group, width, bt_ref):
    return jnp.concatenate(
        [bt_ref[part * width + group * GROUP : part * width + (group + 1) * GROUP, :] for part in range(3)],
        axis=0,
    )


def attend_group(group, n_tok, h1, uq, wall, bt_ref, qkv_ref, att_ref, prob_ref):
    n_img, total, _ = att_ref.shape
    second = group_rows(group, wall.shape[0], bt_ref)
    qkv = (dot(h1, wall[:, : 3 * GROUP]) + dot(uq, second, NT)).astype(BF16)
    qkv_ref[...] = qkv.reshape(qkv_ref.shape)
    for slot in range(n_img):
        att_ref[slot] = attention_forward(
            qkv[slot * total : (slot + 1) * total], n_tok, prob_ref, slot
        )


def next_attention_kernel(
    n_tok, group, extra, layout, place_ref, h1_ref, uq_ref, bt_ref, *rest
):
    chunks, rest = rest[: len(layout[1])], rest[len(layout[1]) :]
    qkv_ref, att_ref, prob_ref = rest[:3]
    wall = rest[-1]

    @pl.when(pl.program_id(0) == 0)
    def _():
        assemble(place_ref, chunks, layout, wall)
        for position in range(extra):
            column = 3 * GROUP + position * LANES
            rest[3 + position][...] = wall[:, column : column + LANES]

    attend_group(
        group, n_tok, flat(h1_ref), flat(uq_ref), wall, bt_ref, qkv_ref, att_ref, prob_ref,
    )


def route_kernel(
    n_exp, layout, place_ref, index_ref, count_ref, image_ref, cot_ref, att0, att1, att2,
    ao_ref, bo_ref, ra_ref, wr_ref, rb_ref, *rest,
):
    chunks, rest = rest[: len(layout[1])], rest[len(layout[1]) :]
    x2_ref, uo_ref, ur_ref, disp_ref, comb_ref, sg_ref, wrt_ref, wall, pad_a, pad_b = rest
    n_img, n_tok, width = image_ref.shape
    first = pl.program_id(0) * n_img
    total = x2_ref.shape[1]

    @pl.when(first == 0)
    def _():
        assemble(place_ref, chunks, layout, wall)
        wrt_ref[...] = wr_ref[...].astype(F32).T[:n_exp].astype(BF16)

    att = jnp.concatenate([flat(att0), flat(att1), flat(att2)], axis=1)
    uo = select_rows(dot(att, ao_ref[...]).astype(BF16).astype(F32), index_ref, first, n_img)
    uo_ref[...] = uo.reshape(uo_ref.shape)
    x2 = pad_rows(pad_a, image_ref) + dot(att, wall[:, :width]) + dot(uo, bo_ref[...], NT)
    x2_ref[...] = x2.reshape(x2_ref.shape)
    h2 = normalise(x2)[0].astype(BF16)
    ur = select_rows(dot(h2, ra_ref[...]).astype(BF16).astype(F32), index_ref, first, n_img)
    ur_ref[...] = ur.reshape(ur_ref.shape)
    cot = pad_rows(pad_b, cot_ref)
    for slot in range(n_img):
        rows = slice(slot * total, (slot + 1) * total)
        living = (first + slot < count_ref[0]).astype(F32)
        logits = dot(wrt_ref[...], h2[rows], NT) + dot(rb_ref[...], ur[rows], NT)
        alive = lax.broadcasted_iota(jnp.int32, logits.shape, 1) < n_tok
        over_tokens = jnp.where(alive, logits, NEG)
        powers = jnp.exp(over_tokens - jnp.max(over_tokens, axis=1, keepdims=True))
        disp = powers / jnp.sum(powers, axis=1, keepdims=True)
        powers = jnp.exp(logits - jnp.max(logits, axis=0, keepdims=True))
        comb = jnp.where(alive, powers / jnp.sum(powers, axis=0, keepdims=True), 0.0)
        disp_ref[slot] = disp
        comb_ref[slot] = comb
        upstream = (cot[rows] * living).astype(BF16)
        sg_ref[slot, :, :width] = dot(disp.astype(BF16), h2[rows]).astype(BF16)
        sg_ref[slot, :, width : 2 * width] = dot(comb.astype(BF16), upstream).astype(BF16)
        selector = rank_row(index_ref[first + slot])
        sg_ref[slot, :, 2 * width :] = jnp.broadcast_to(selector, (n_exp, LANES)).astype(BF16)


def gelu_both(pre):
    square = pre * pre
    half = jnp.tanh(GELU_C * pre * (1.0 + GELU_A * square))
    both = 0.5 * (1.0 + half)
    slope = both + 0.5 * pre * (1.0 - half * half) * (GELU_C * (1.0 + 3.0 * GELU_A * square))
    return pre * both, slope


def expert_tile(slots, gy, u1, gu2, wu_ref, wd_ref, ub_ref, da_ref):
    pre = dot(slots, wu_ref[0]) + dot(u1, ub_ref[0])
    ghid = (dot(wd_ref[0], gy, NT) + dot(da_ref[0], gu2, NT)).T
    hidden, slope = gelu_both(pre)
    return hidden.astype(BF16), (slope * ghid).astype(BF16)


def gather_rows(part_refs, out_ref):
    rows = part_refs[0].shape[0] * part_refs[0].shape[2]
    for number, part_ref in enumerate(part_refs):
        part = part_ref[:, 0].astype(F32).reshape(rows, part_ref.shape[3])
        out_ref[number * rows : (number + 1) * rows, :] = part.astype(BF16)


def expert_kernel(
    wu_ref, wd_ref, ua_ref, ub_ref, da_ref, db_ref, part_ref, out_ref,
    sg_ref, u1_ref, gu2_ref, acc_y, acc_s, acc_u2, acc_gu1,
):
    step = pl.program_id(1)
    width = wu_ref.shape[1]

    @pl.when(step == 0)
    def _():
        gather_rows((part_ref,), sg_ref)
        selector = sg_ref[:, 2 * width :].astype(F32)
        u1_ref[...] = (
            dot(sg_ref[:, :width], ua_ref[0]).astype(BF16).astype(F32) * selector
        ).astype(BF16)
        gu2_ref[...] = (dot(sg_ref[:, width : 2 * width], db_ref[0], NT) * selector).astype(BF16)
        acc_y[...] = jnp.zeros_like(acc_y)
        acc_s[...] = jnp.zeros_like(acc_s)
        acc_u2[...] = jnp.zeros_like(acc_u2)
        acc_gu1[...] = jnp.zeros_like(acc_gu1)

    hidden, gpre = expert_tile(
        sg_ref[:, :width], sg_ref[:, width : 2 * width], u1_ref[...], gu2_ref[...],
        wu_ref, wd_ref, ub_ref, da_ref,
    )
    acc_y[...] += dot(hidden, wd_ref[0])
    acc_u2[...] += dot(hidden, da_ref[0])
    acc_s[...] += dot(wu_ref[0], gpre, NT)
    acc_gu1[...] += dot(ub_ref[0], gpre, NT)

    @pl.when(step == pl.num_programs(1) - 1)
    def _():
        selector = sg_ref[:, 2 * width :].astype(F32)
        u2 = (acc_u2[...].astype(BF16).astype(F32) * selector).astype(BF16)
        gu1 = (acc_gu1[...].T * selector).astype(BF16)
        shards, _, n_img, _ = out_ref.shape
        result = acc_y[...] + dot(u2, db_ref[0])
        out_ref[:, 0, :, :width] = result.reshape(shards, n_img, width).astype(BF16)
        result = acc_s[...].T + dot(gu1, ua_ref[0], NT)
        out_ref[:, 0, :, width:] = result.reshape(shards, n_img, width).astype(BF16)


def expert_grad_kernel(
    copies, wu_ref, wd_ref, ua_ref, ub_ref, da_ref, db_ref, *rest
):
    part_refs = rest[:copies]
    gua_ref, gub_ref, gda_ref, gdb_ref = rest[-11:-7]
    sg_ref, u1_ref, gu2_ref, u1t_ref, gu2t_ref, acc_u2, acc_gu1 = rest[-7:]
    step = pl.program_id(1)
    width = wu_ref.shape[1]

    @pl.when(step == 0)
    def _():
        gather_rows(part_refs, sg_ref)
        selector = sg_ref[:, 2 * width :].astype(F32)
        u1 = dot(sg_ref[:, :width], ua_ref[0]).astype(BF16).astype(F32) * selector
        gu2 = dot(sg_ref[:, width : 2 * width], db_ref[0], NT) * selector
        u1_ref[...] = u1.astype(BF16)
        gu2_ref[...] = gu2.astype(BF16)
        u1t_ref[...] = u1.T.astype(BF16)
        gu2t_ref[...] = gu2.T.astype(BF16)
        acc_u2[...] = jnp.zeros_like(acc_u2)
        acc_gu1[...] = jnp.zeros_like(acc_gu1)

    hidden, gpre = expert_tile(
        sg_ref[:, :width], sg_ref[:, width : 2 * width], u1_ref[...], gu2_ref[...],
        wu_ref, wd_ref, ub_ref, da_ref,
    )
    gub_ref[0] = dot(u1t_ref[...], gpre)
    gda_ref[0] = dot(gu2t_ref[...], hidden).T
    acc_u2[...] += dot(hidden, da_ref[0])
    acc_gu1[...] += dot(ub_ref[0], gpre, NT)

    @pl.when(step == pl.num_programs(1) - 1)
    def _():
        selector = sg_ref[:, 2 * width :].astype(F32)
        u2 = acc_u2[...].astype(BF16).astype(F32) * selector
        gu1 = (acc_gu1[...] * selector.T).astype(BF16)
        gdb_ref[0] = dot(u2.T.astype(BF16), sg_ref[:, width : 2 * width])
        gua_ref[0] = dot(gu1, sg_ref[:, :width]).T


def route_back_kernel(
    n_exp, layout, place_ref, index_ref, count_ref, cot_ref, x2_ref, uo_ref, ur_ref, disp_ref,
    comb_ref, att0, att1, att2, ret_ref, ao_ref, bo_ref, ra_ref, wrt_ref, rb_ref, *rest,
):
    chunks, rest = rest[: len(layout[1])], rest[len(layout[1]) :]
    block_ref, gx2_ref, gatt_ref, pack_ref, *rest = rest
    wall, pad_b, acc_oa, acc_ob, acc_ra, acc_rb = rest
    n_img, n_tok, width = cot_ref.shape
    first = pl.program_id(0) * n_img
    total = x2_ref.shape[1]

    @pl.when(first == 0)
    def _():
        assemble(place_ref, chunks, layout, wall)
        acc_oa[...] = jnp.zeros_like(acc_oa)
        acc_ob[...] = jnp.zeros_like(acc_ob)
        acc_ra[...] = jnp.zeros_like(acc_ra)
        acc_rb[...] = jnp.zeros_like(acc_rb)

    cot = pad_rows(pad_b, cot_ref)
    x2 = flat(x2_ref)
    unit, scale = normalise(x2)
    h2 = unit.astype(BF16)
    pairs, belows, upstreams = [], [], []
    for slot in range(n_img):
        rows = slice(slot * total, (slot + 1) * total)
        living = (first + slot < count_ref[0]).astype(F32)
        upstream = cot[rows] * living
        upstreams.append(upstream)
        disp, comb = disp_ref[slot], comb_ref[slot]
        yexp, gslot = ret_ref[slot, :, :width], ret_ref[slot, :, width:]
        gcomb = dot(yexp, upstream.astype(BF16), NT)
        gdisp = dot(gslot, h2[rows], NT)
        glog = (
            disp * (gdisp - jnp.sum(gdisp * disp, axis=1, keepdims=True))
            + comb * (gcomb - jnp.sum(gcomb * comb, axis=0, keepdims=True))
        )
        acc_rb[...] += dot(glog.astype(BF16), ur_ref[slot])
        three = jnp.concatenate([disp, glog, comb], axis=0).T.astype(BF16)
        mixed = dot(three[:, 2 * n_exp :], yexp)
        block_ref[slot] = (living * (x2[rows] + mixed)).astype(BF16)[:n_tok]
        pairs.append(three[:, : 2 * n_exp])
        belows.append(jnp.concatenate([gslot, wrt_ref[...]], axis=0))
    glog_rows = jnp.concatenate([pair[:, n_exp:] for pair in pairs], axis=0)
    gur = select_rows(dot(glog_rows, rb_ref[...]), index_ref, first, n_img)
    acc_ra[...] += dot(gur, h2, TN)
    gh2 = dot(gur, ra_ref[...], NT) + jnp.concatenate(
        [dot(pair, below) for pair, below in zip(pairs, belows)], axis=0
    )
    gx2 = jnp.concatenate(upstreams, axis=0) + normalise_back(unit, scale, gh2)
    gx2_ref[...] = gx2.reshape(gx2_ref.shape)
    gbr = gx2.astype(BF16)
    acc_ob[...] += dot(flat(uo_ref), gbr, TN)
    guo = select_rows(dot(gbr, bo_ref[...]), index_ref, first, n_img)
    att = jnp.concatenate([flat(att0), flat(att1), flat(att2)], axis=1)
    acc_oa[...] += dot(guo, att, TN)
    gatt = (dot(gbr, wall[:, :width], NT) + dot(guo, ao_ref[...], NT)).astype(BF16)
    gatt_ref[...] = gatt.reshape(gatt_ref.shape)

    @pl.when(pl.program_id(0) == pl.num_programs(0) - 1)
    def _():
        shards = pack_ref.shape[0]
        rows = width // shards
        n_loc = n_exp // shards
        for position, acc in enumerate((acc_oa, acc_ob, acc_ra)):
            summed = acc[...].T.astype(BF16)
            for shard in range(shards):
                pack_ref[shard, position * rows : (position + 1) * rows, :] = summed[
                    shard * rows : (shard + 1) * rows
                ]
        tail = pack_ref.shape[1] - 3 * rows
        for shard in range(shards):
            last = jnp.concatenate(
                [acc_rb[shard * n_loc : (shard + 1) * n_loc, :], jnp.zeros((tail - n_loc, LANES), F32)],
                axis=0,
            )
            pack_ref[shard, 3 * rows :, :] = last.astype(BF16)


def attention_backward(qkv, gatt, prob_ref, slot):
    keep = head_mask(1.0)
    key_t = qkv[:, GROUP : 2 * GROUP].T
    total = qkv.shape[0]
    gq_parts, gk_parts, gv_parts = [], [], []
    for pair in range(GROUP // LANES):
        span = slice(pair * LANES, (pair + 1) * LANES)
        q_pair, ga_pair = qkv[:, span], gatt[:, span]
        v_pair = qkv[:, 2 * GROUP + pair * LANES : 2 * GROUP + (pair + 1) * LANES]
        lows = [prob_ref[slot, 2 * pair], prob_ref[slot, 2 * pair + 1]]
        gv = dot(jnp.concatenate(lows, axis=0), ga_pair)
        gprobs = dot(jnp.concatenate([v_pair * keep[0], v_pair * keep[1]], axis=0), ga_pair, NT)
        gscores = []
        for side in range(2):
            probs = lows[side].astype(F32)
            gprob = gprobs[side * total : (side + 1) * total]
            inner = jnp.sum(gprob * probs, axis=0, keepdims=True)
            gscores.append((probs * (gprob - inner)).astype(BF16))
            head = 2 * pair + side
            gq_parts.append(
                (dot(key_t[head * HEAD_DIM : (head + 1) * HEAD_DIM], gscores[side]) * 0.125).astype(BF16)
            )
        gk = dot(jnp.concatenate(gscores, axis=0), q_pair)
        gk_parts.append((merge_pair(gk[:total], gk[total:]) * 0.125).astype(BF16))
        gv_parts.append(merge_pair(gv[:total], gv[total:]).astype(BF16))
    gq = jnp.concatenate(gq_parts, axis=0).T
    return jnp.concatenate([gq] + gk_parts + gv_parts, axis=1)


def attention_back_kernel(groups, index_ref, *refs):
    refs = list(refs)
    qkv_refs = [refs.pop(0) for _ in range(groups)]
    prob_refs = [refs.pop(0) for _ in range(groups)]
    gatt_ref, uq_ref, h1_ref, bt_ref, others_ref = refs[:5]
    refs = refs[5:]
    gqkv_refs = [refs.pop(0) for _ in range(groups)]
    guq_ref, pack_ref, acc_b, acc_a = refs
    step = pl.program_id(0)
    n_img, total, width = h1_ref.shape

    @pl.when(step == 0)
    def _():
        acc_b[...] = jnp.zeros_like(acc_b)
        acc_a[...] = jnp.zeros_like(acc_a)

    uq_t = flat(uq_ref).T
    guq = None
    for group in range(groups):
        parts = []
        for i in range(n_img):
            part = attention_backward(
                qkv_refs[group][i], gatt_ref[i, :, group * GROUP : (group + 1) * GROUP],
                prob_refs[group], i,
            )
            gqkv_refs[group][i] = part
            parts.append(part)
        gqkv = jnp.concatenate(parts, axis=0)
        acc_b[:, group * 3 * GROUP : (group + 1) * 3 * GROUP] += dot(uq_t, gqkv)
        part = dot(gqkv, group_rows(group, width, bt_ref))
        guq = part if guq is None else guq + part
    guq = select_rows(guq, index_ref, step * n_img, n_img)
    acc_a[...] += dot(guq, flat(h1_ref), TN)
    guq_ref[...] = guq.reshape(guq_ref.shape)

    @pl.when(step == pl.num_programs(0) - 1)
    def _():
        shards = pack_ref.shape[0]
        rows = width // shards
        pack_ref[:, 4 * rows :, :] = others_ref[...]
        own = acc_a[...].T.astype(BF16)
        for shard in range(shards):
            pack_ref[shard, 3 * rows : 4 * rows, :] = own[shard * rows : (shard + 1) * rows]
        for group in range(groups):
            summed = acc_b[:, group * 3 * GROUP : (group + 1) * 3 * GROUP].T.astype(BF16)
            for part in range(3):
                start = part * width + group * GROUP
                place = start
                while place < start + GROUP:
                    shard, offset = divmod(place, 3 * rows)
                    length = min(start + GROUP - place, 3 * rows - offset)
                    take = part * GROUP + place - start
                    pack_ref[shard, offset : offset + length, :] = summed[take : take + length]
                    place += length


def input_grad_kernel(layouts, place_ref, image_ref, gx2_ref, guq_ref, a_ref, *refs):
    refs = list(refs)
    groups = len(layouts)
    gqkv = [refs.pop(0) for _ in layouts]
    chunks = [[refs.pop(0) for _ in layout[1]] for layout in layouts]
    out_ref = refs.pop(0)
    walls = [refs.pop(0) for _ in layouts]
    pad_a = refs.pop(0)
    n_img, n_tok, width = image_ref.shape
    step = pl.program_id(0)
    parts = width // LANES
    every = out_ref.shape[0] // (n_tok * parts)

    @pl.when(step == 0)
    def _():
        for group in range(groups):
            assemble(place_ref, chunks[group], layouts[group], walls[group])

    gh1 = dot(flat(guq_ref), a_ref[...], NT)
    for group in range(groups):
        gh1 = gh1 + dot(flat(gqkv[group]), walls[group][:, : 3 * GROUP], NT)
    unit, scale = normalise(pad_rows(pad_a, image_ref))
    total = gx2_ref.shape[1]
    result = flat(gx2_ref) + normalise_back(unit, scale, gh1)
    for slot in range(n_img):
        for part in range(parts):
            out_ref[pl.ds(part * every + step * n_img + slot, n_tok, stride=parts * every), :] = result[
                slot * total : slot * total + n_tok, part * LANES : (part + 1) * LANES
            ]


ANY = pl.BlockSpec(memory_space=pl.ANY)


def whole(shape):
    return pl.BlockSpec(shape, lambda *_: (0,) * len(shape))


def once(shape):
    return pl.BlockSpec(shape, lambda *_: (0,) * len(shape), pipeline_mode=pl.Buffered(1))


def per_image(*shape, images=1):
    return pl.BlockSpec((images,) + shape, lambda i, *_: (i,) + (0,) * len(shape))


def several(images, limit):
    return max(n for n in range(1, limit + 1) if images % n == 0)


def call(kernel, scalars, grid, inputs, outputs, scratch, flops, exps=0, aliases=None):
    arrays = [array for array, _ in inputs]
    shapes = [jax.ShapeDtypeStruct(shape, dtype) for shape, dtype, _ in outputs]
    moved = sum(array.size * array.dtype.itemsize for array in arrays) + sum(
        shape.size * shape.dtype.itemsize for shape in shapes
    )
    return pl.pallas_call(
        kernel,
        out_shape=shapes,
        grid_spec=pltpu.PrefetchScalarGridSpec(
            num_scalar_prefetch=len(scalars),
            grid=grid,
            in_specs=[spec for _, spec in inputs],
            out_specs=[spec for _, _, spec in outputs],
            scratch_shapes=scratch,
        ),
        input_output_aliases=aliases or {},
        compiler_params=params(*(("arbitrary",) * len(grid))),
        cost_estimate=cost(flops, moved, exps),
    )(*scalars, *arrays)


def norm_call(images, cotangent, total):
    n_img, n_tok, width = images.shape
    each = several(n_img, 4)
    return call(
        norm_kernel, (), (n_img // each,),
        [(images, per_image(n_tok, width, images=each)), (cotangent, ANY)],
        [((n_img, total, width), BF16, per_image(total, width, images=each))],
        [pltpu.VMEM((each * total, width), F32)],
        8 * images.size,
    )[0]


def pack_call(place, weights, copies):
    rows, columns = weights[0].shape
    part = (columns // 3 + 6 * LANES) // 4
    return call(
        pack_kernel, (place,), (1,), [(weight, whole(weight.shape)) for weight in weights],
        [((copies, rows, part), BF16, whole((copies, rows, part)))],
        [pltpu.VMEM((rows, 4 * part), BF16)],
        rows * columns,
    )[0]


def attention_flops(n_img, total, width, parts):
    return n_img * total * (2 * width * 3 * GROUP + parts * 8 * total * HEAD_DIM)


def attention_outputs(n_img, total, each):
    return [
        ((n_img, total, 3 * GROUP), BF16, per_image(total, 3 * GROUP, images=each)),
        ((n_img, total, GROUP), BF16, per_image(total, GROUP, images=each)),
        (
            (n_img, GROUP // HEAD_DIM, total, total), BF16,
            per_image(GROUP // HEAD_DIM, total, total, images=each),
        ),
    ]


def first_attention_call(place, index, h1, pack, n_tok, shards):
    n_img, total, width = h1.shape
    chunks, layout, columns = pack
    each = several(n_img, IMAGES_FORWARD)
    return call(
        functools.partial(first_attention_kernel, n_tok, shards, layout), (place, index), (n_img // each,),
        [(h1, per_image(total, width, images=each))] + [(chunk, once(chunk.shape)) for chunk in chunks],
        attention_outputs(n_img, total, each)
        + [
            ((n_img, total, LANES), BF16, per_image(total, LANES, images=each)),
            ((width, LANES), BF16, whole((width, LANES))),
            ((3 * width, LANES), BF16, whole((3 * width, LANES))),
            ((width, LANES), BF16, whole((width, LANES))),
            ((width, LANES), BF16, whole((width, LANES))),
        ],
        [pltpu.VMEM((width, columns), BF16)],
        attention_flops(n_img, total, width, 2), n_img * total * total * 4,
    )


def next_attention_call(place, h1, uq, bt, pack, n_tok, group, extra):
    n_img, total, width = h1.shape
    chunks, layout, columns = pack
    each = several(n_img, IMAGES_FORWARD)
    return call(
        functools.partial(next_attention_kernel, n_tok, group, extra, layout), (place,), (n_img // each,),
        [
            (h1, per_image(total, width, images=each)),
            (uq, per_image(total, LANES, images=each)),
            (bt, whole(bt.shape)),
        ]
        + [(chunk, once(chunk.shape)) for chunk in chunks],
        attention_outputs(n_img, total, each)
        + [((width, LANES), BF16, whole((width, LANES)))] * extra,
        [pltpu.VMEM((width, columns), BF16)],
        attention_flops(n_img, total, width, 2), n_img * total * total * 4,
    )


def route_call(place, index, count, images, cotangent, atts, banks, pack, n_exp, total):
    n_img, n_tok, width = images.shape
    chunks, layout, columns = pack
    each = several(n_img, IMAGES_ROUTE)
    here = functools.partial(per_image, images=each)
    return call(
        functools.partial(route_kernel, n_exp, layout), (place, index, count), (n_img // each,),
        [(images, here(n_tok, width)), (cotangent, here(n_tok, width))]
        + [(att, here(total, GROUP)) for att in atts]
        + [(bank, whole(bank.shape)) for bank in banks]
        + [(chunk, once(chunk.shape)) for chunk in chunks],
        [
            ((n_img, total, width), F32, here(total, width)),
            ((n_img, total, LANES), BF16, here(total, LANES)),
            ((n_img, total, LANES), BF16, here(total, LANES)),
            ((n_img, n_exp, total), F32, here(n_exp, total)),
            ((n_img, n_exp, total), F32, here(n_exp, total)),
            ((n_img, n_exp, 2 * width + LANES), BF16, here(n_exp, 2 * width + LANES)),
            ((n_exp, width), BF16, whole((n_exp, width))),
        ],
        [
            pltpu.VMEM((width, columns), BF16),
            pltpu.VMEM((each * total, width), F32),
            pltpu.VMEM((each * total, width), F32),
        ],
        n_img * total * 2 * width * (width + 3 * LANES), n_img * total * 2 * n_exp,
    )


def hidden_tile(hidden, limit):
    tile = hidden
    while tile > limit:
        tile //= 2
    return tile


def expert_specs(width, tile, first=0):
    return (
        pl.BlockSpec((1, width, tile), lambda e, f: (e + first, 0, f)),
        pl.BlockSpec((1, tile, width), lambda e, f: (e + first, f, 0)),
        pl.BlockSpec((1, width, LANES), lambda e, f: (e + first, 0, 0)),
        pl.BlockSpec((1, LANES, tile), lambda e, f: (e + first, 0, f)),
        pl.BlockSpec((1, tile, LANES), lambda e, f: (e + first, f, 0)),
        pl.BlockSpec((1, LANES, width), lambda e, f: (e + first, 0, 0)),
    )


def expert_rows(shape, first=0):
    shards, _, n_img, columns = shape
    return pl.BlockSpec((shards, 1, n_img, columns), lambda e, f: (0, e + first, 0, 0))


def expert_call(landed, weights):
    shards, n_loc, n_img, columns = landed.shape
    rows = shards * n_img
    width, hidden = weights[0].shape[1:]
    tile = hidden_tile(hidden, 1536)
    out = (shards, n_loc, n_img, 2 * width)
    return call(
        expert_kernel, (), (n_loc, hidden // tile),
        list(zip(weights, expert_specs(width, tile))) + [(landed, expert_rows(landed.shape))],
        [(out, BF16, expert_rows(out))],
        [
            pltpu.VMEM((rows, columns), BF16),
            pltpu.VMEM((rows, LANES), BF16),
            pltpu.VMEM((rows, LANES), BF16),
            pltpu.VMEM((rows, width), F32),
            pltpu.VMEM((width, rows), F32),
            pltpu.VMEM((rows, LANES), F32),
            pltpu.VMEM((LANES, rows), F32),
        ],
        n_loc * rows * 8 * width * hidden, n_loc * rows * hidden,
    )[0]


def expert_grad_call(every, weights, first, before):
    shards, n_loc, n_img, columns = every[0].shape
    rows = shards * n_img * len(every)
    width, hidden = weights[0].shape[1:]
    tile = hidden_tile(hidden, 768 if rows <= 512 else 384)
    aliases = {len(weights) + len(every) + i: i for i in range(4)} if before else {}
    return call(
        functools.partial(expert_grad_kernel, len(every)), (), (1, hidden // tile),
        list(zip(weights, expert_specs(width, tile, first)))
        + [(part, expert_rows(part.shape, first)) for part in every]
        + [(array, ANY) for array in before],
        [
            ((n_loc, width, LANES), F32, pl.BlockSpec((1, width, LANES), lambda e, f: (e + first, 0, 0))),
            ((n_loc, LANES, hidden), F32, pl.BlockSpec((1, LANES, tile), lambda e, f: (e + first, 0, f))),
            ((n_loc, hidden, LANES), F32, pl.BlockSpec((1, tile, LANES), lambda e, f: (e + first, f, 0))),
            ((n_loc, LANES, width), F32, pl.BlockSpec((1, LANES, width), lambda e, f: (e + first, 0, 0))),
        ],
        [
            pltpu.VMEM((rows, columns), BF16),
            pltpu.VMEM((rows, LANES), BF16),
            pltpu.VMEM((rows, LANES), BF16),
            pltpu.VMEM((LANES, rows), BF16),
            pltpu.VMEM((LANES, rows), BF16),
            pltpu.VMEM((rows, LANES), F32),
            pltpu.VMEM((LANES, rows), F32),
        ],
        rows * 4 * width * hidden, rows * hidden, aliases,
    )


def route_back_call(
    place, index, count, cotangent, x2, uo, ur, disp, comb, atts, ret, banks, pack, shards, replicas
):
    n_img, n_tok, width = cotangent.shape
    chunks, layout, columns = pack
    total, n_exp = x2.shape[1], disp.shape[1]
    rows = width // shards
    unit = 16 * replicas
    pack_rows = -(-(7 * rows + n_exp // shards) // unit) * unit - 4 * rows
    each = several(n_img, IMAGES_ROUTE)
    here = functools.partial(per_image, images=each)
    return call(
        functools.partial(route_back_kernel, n_exp, layout), (place, index, count), (n_img // each,),
        [
            (cotangent, here(n_tok, width)),
            (x2, here(total, width)),
            (uo, here(total, LANES)),
            (ur, here(total, LANES)),
            (disp, here(n_exp, total)),
            (comb, here(n_exp, total)),
        ]
        + [(att, here(total, GROUP)) for att in atts]
        + [(ret, here(n_exp, 2 * width))]
        + [(bank, whole(bank.shape)) for bank in banks]
        + [(chunk, once(chunk.shape)) for chunk in chunks],
        [
            ((n_img, n_tok, width), BF16, here(n_tok, width)),
            ((n_img, total, width), F32, here(total, width)),
            ((n_img, total, width), BF16, here(total, width)),
            ((shards, pack_rows, LANES), BF16, whole((shards, pack_rows, LANES))),
        ],
        [
            pltpu.VMEM((width, columns), BF16),
            pltpu.VMEM((each * total, width), F32),
            pltpu.VMEM((LANES, width), F32),
            pltpu.VMEM((LANES, width), F32),
            pltpu.VMEM((LANES, width), F32),
            pltpu.VMEM((n_exp, LANES), F32),
        ],
        n_img * total * 2 * width * (width + 6 * LANES),
    )


def attention_back_call(index, qkvs, probs, gatt, uq, h1, bt, others):
    n_img, total, width = h1.shape
    groups = len(qkvs)
    shards = others.shape[0]
    each = several(n_img, IMAGES_BACK)
    here = functools.partial(per_image, images=each)
    pack = (shards, 4 * width // shards + others.shape[1], LANES)
    return call(
        functools.partial(attention_back_kernel, groups), (index,), (n_img // each,),
        [(qkv, here(total, 3 * GROUP)) for qkv in qkvs]
        + [(prob, here(GROUP // HEAD_DIM, total, total)) for prob in probs]
        + [
            (gatt, here(total, width)),
            (uq, here(total, LANES)),
            (h1, here(total, width)),
            (bt, whole(bt.shape)),
            (others, whole(others.shape)),
        ],
        [((n_img, total, 3 * GROUP), BF16, here(total, 3 * GROUP))] * groups
        + [((n_img, total, LANES), BF16, here(total, LANES)), (pack, BF16, whole(pack))],
        [pltpu.VMEM((LANES, 3 * width), F32), pltpu.VMEM((LANES, width), F32)],
        groups * attention_flops(n_img, total, LANES, 5), groups * n_img * total * total * 4,
    )


def input_grad_call(place, images, gx2, guq, bank_a, gqkvs, packs):
    n_img, n_tok, width = images.shape
    total = gx2.shape[1]
    groups = len(gqkvs)
    each = several(n_img, IMAGES_LAST)
    here = functools.partial(per_image, images=each)
    out = call(
        functools.partial(input_grad_kernel, tuple(pack[1] for pack in packs)), (place,), (n_img // each,),
        [
            (images, here(n_tok, width)),
            (gx2, here(total, width)),
            (guq, here(total, LANES)),
            (bank_a, whole(bank_a.shape)),
        ]
        + [(gqkv, here(total, 3 * GROUP)) for gqkv in gqkvs]
        + [(chunk, once(chunk.shape)) for pack in packs for chunk in pack[0]],
        [((images.size // LANES, LANES), F32, whole((images.size // LANES, LANES)))],
        [pltpu.VMEM((width, pack[2]), BF16) for pack in packs]
        + [pltpu.VMEM((each * total, width), F32)],
        n_img * total * 2 * width * (3 * width + LANES),
    )[0]
    out = out.reshape(n_tok, width // LANES, n_img, LANES).transpose(2, 0, 1, 3)
    return out.reshape(n_img, n_tok, width)


def swap(array, axis, size, bit):
    return lax.ppermute(array, axis, [(i, i ^ bit) for i in range(size)])


def tie(*arrays):
    return lax.optimization_barrier(arrays)


def own_columns(pack, quarter, pieces):
    part = pack.shape[1] // pieces
    return lax.dynamic_slice(pack, (0, quarter % pieces * part), (pack.shape[0], part))


def spread(rows, shards):
    return jnp.broadcast_to(rows[None], (shards,) + rows.shape)


def over_shard(spread, lines=None):
    own = lax.all_to_all(
        spread, "shard", split_axis=0, concat_axis=0, tiled=True, axis_index_groups=lines
    )
    return own.reshape(-1, spread.shape[2])


def reduce_pack(pack, replicas, beside_swap, beside_spread):
    where = lax.axis_index("replica")
    bits = []
    bit = 1
    while bit < replicas:
        half = pack.shape[1] // 2
        side = (where // bit) % 2
        keep = lax.dynamic_slice_in_dim(pack, side * half, half, axis=1)
        give = lax.dynamic_slice_in_dim(pack, (1 - side) * half, half, axis=1)
        got = swap(give, "replica", replicas, bit)
        if 2 * bit == replicas:
            got, *swap_work = tie(got, *beside_swap())
        pack = (keep.astype(F32) + got.astype(F32)).astype(BF16)
        bits.append(bit)
        bit *= 2
    landed = lax.all_to_all(pack, "shard", split_axis=0, concat_axis=0, tiled=True)
    landed, *spread_work = tie(landed, *beside_spread())
    total = jnp.sum(landed.astype(F32), axis=0).astype(BF16)
    for bit in reversed(bits):
        got = swap(total, "replica", replicas, bit)
        side = (where // bit) % 2
        total = jnp.where(
            side == 0,
            jnp.concatenate([total, got], axis=0),
            jnp.concatenate([got, total], axis=0),
        )
    return total, swap_work, spread_work


def per_device(
    replicas,
    shards,
    images,
    image_adapter_index,
    device_image_count,
    cotangent,
    query_key_value_weight,
    frozen_output_weight,
    frozen_dispatch_weight,
    query_key_value_first,
    query_key_value_second,
    output_adapter_first,
    output_adapter_second,
    dispatch_adapter_first,
    dispatch_adapter_second,
    frozen_up_weight,
    frozen_down_weight,
    up_adapter_first,
    up_adapter_second,
    down_adapter_first,
    down_adapter_second,
):
    n_img, n_tok, width = images.shape
    total = -(-n_tok // 16) * 16
    rows = width // shards
    n_loc = frozen_up_weight.shape[0]
    n_exp = n_loc * shards
    groups = width // GROUP
    quarter = lax.axis_index("replica") % 4
    place = jnp.stack([quarter, lax.axis_index("shard") % 2]).astype(jnp.int32)
    by_axis = shards == 2 * STRIPS and replicas == 4

    def qkv_columns(group):
        return [
            query_key_value_weight[:, part * width + group * GROUP : part * width + (group + 1) * GROUP]
            for part in range(3)
        ]

    route_block = jnp.concatenate(
        [
            frozen_dispatch_weight,
            jnp.zeros((rows, 64 - n_exp), BF16),
            jnp.pad(dispatch_adapter_second.T.reshape(16, n_loc * 8), ((0, rows - 16), (0, 0))),
            jnp.zeros((rows, 64 - n_loc * 8), BF16),
        ],
        axis=1,
    )
    empty = jnp.zeros((rows, LANES), BF16)
    empty = jnp.zeros((rows, 2 * LANES), BF16)
    packs = [
        (qkv_columns(1) + [output_adapter_second.T, route_block], 4),
        (qkv_columns(2), 2),
        ([frozen_output_weight, empty], 4),
    ]
    spread0 = pack_call(
        place,
        (
            query_key_value_weight, query_key_value_first, query_key_value_second.T,
            output_adapter_first, dispatch_adapter_first,
        ),
        STRIPS if by_axis else shards,
    )
    mine = [own_columns(jnp.concatenate(pack, axis=1), quarter, pieces) for pack, pieces in packs]
    near = functools.partial(swap, axis="replica", size=replicas, bit=1)
    far = functools.partial(swap, axis="replica", size=replicas, bit=2)
    beside = functools.partial(swap, axis="shard", size=shards, bit=1)

    h1 = norm_call(images, cotangent, total)
    if by_axis:
        lines = [[2 * strip + side for strip in range(STRIPS)] for side in range(2)]
        own0 = over_shard(spread0, lines)
        beside0, far0, h1, mine1 = tie(beside(own0), far(own0), h1, mine[0])
        held = [(own0, 0, 0), (beside0, 0, 1), (far0, 2, 0)]
        own1 = over_shard(spread(mine1, shards))
        held.append((far(held[1][0]), 2, 1))
    else:
        own0 = over_shard(spread0)
        own0, h1, mine1 = tie(own0, h1, mine[0])
        held = [(own0, 0, None), (far(own0), 2, None)]
        own1 = over_shard(spread(mine1, shards))
    chunks0 = [chunk for chunk, _, _ in held] + [near(chunk) for chunk, _, _ in held]
    layout0 = [(replica, side, 0) for _, replica, side in held]
    layout0 += [(replica ^ 1, side, 0) for _, replica, side in held]
    *chunks0, own1, mine2, mine3 = tie(*chunks0, own1, *mine[1:])
    pack0 = (tuple(chunks0), (4, tuple(layout0)), 3 * GROUP + 6 * LANES)
    far1 = far(own1)
    own23 = over_shard(spread(jnp.concatenate([mine2, mine3], axis=1), shards))
    qkv0, att0, prob0, uq, bank_a, bank_bt, bank_ao, bank_ra = first_attention_call(
        place, image_adapter_index, h1, pack0, n_tok, shards
    )
    uq, own1, far1 = tie(uq, own1, far1)
    four = (4, ((0, None, 0), (1, None, 0), (2, None, 0), (3, None, 0)))
    pack1 = ((own1, near(own1), far1, near(far1)), four, 3 * GROUP + 2 * LANES)
    qkv1, att1, prob1, bank_bo, bank_wr = next_attention_call(
        place, h1, uq, bank_bt, pack1, n_tok, 1, 2
    )
    att1, uq, own23 = tie(att1, uq, own23)
    own2, own3 = own23[:, : mine2.shape[1]], own23[:, mine2.shape[1] :]
    far3 = far(own3)
    pack2 = ((own2, near(own2)), (2, ((0, None, 0), (1, None, 0))), 3 * GROUP)
    qkv2, att2, prob2 = next_attention_call(place, h1, uq, bank_bt, pack2, n_tok, 2, 0)
    att2, own3, far3 = tie(att2, own3, far3)
    pack3 = ((own3, near(own3), far3, near(far3)), four, width + 2 * LANES)
    packs = (pack0, pack1, pack2, pack3)
    atts = (att0, att1, att2)
    bank_rb = bank_wr.reshape(shards, rows, LANES)[:, :16, 64 : 64 + n_loc * 8].reshape(n_exp, LANES)
    x2, uo, ur, disp, comb, sg, bank_wrt = route_call(
        place, image_adapter_index, device_image_count, images, cotangent, atts,
        (bank_ao, bank_bo, bank_ra, bank_wr, bank_rb), packs[3], n_exp, total,
    )

    sent = sg.reshape(n_img, shards, n_loc, -1).transpose(1, 2, 0, 3)
    landed = lax.all_to_all(sent, "shard", split_axis=0, concat_axis=0, tiled=True)
    weights = (
        frozen_up_weight, frozen_down_weight, up_adapter_first, up_adapter_second,
        down_adapter_first, down_adapter_second,
    )
    ret = expert_call(landed, weights)
    every = [landed]
    for bit in range(2, replicas, 2):
        every.append(swap(landed, "replica", replicas, bit))
    ret, *every = tie(ret, *every)
    back = lax.all_to_all(ret, "shard", split_axis=0, concat_axis=0, tiled=True)
    every = every + [swap(part, "replica", replicas, 1) for part in every]
    grads = expert_grad_call(every, weights, 0, ())
    back, *grads = tie(back, *grads)
    back = back.transpose(2, 0, 1, 3).reshape(n_img, n_exp, 2 * width)

    block_out, gx2, gatt, out_pack = route_back_call(
        place, image_adapter_index, device_image_count, cotangent, x2, uo, ur, disp, comb, atts, back,
        (bank_ao, bank_bo, bank_ra, bank_wrt, bank_rb), packs[3], shards, replicas,
    )
    *gqkvs, guq, pack = attention_back_call(
        image_adapter_index, (qkv0, qkv1, qkv2), (prob0, prob1, prob2), gatt, uq, h1, bank_bt, out_pack
    )

    def rest_of_experts():
        done = tuple(grads)
        for expert in range(1, n_loc):
            done = expert_grad_call(every, weights, expert, tuple(done))
        return done

    summed, (input_grad,), grads = reduce_pack(
        pack, replicas,
        lambda: (input_grad_call(place, images, gx2, guq, bank_a, gqkvs, packs[:3]),),
        rest_of_experts,
    )
    summed = summed.astype(F32)
    return (
        block_out,
        input_grad,
        summed[3 * rows : 4 * rows],
        summed[: 3 * rows].T,
        summed[4 * rows : 5 * rows],
        summed[5 * rows : 6 * rows].T,
        summed[6 * rows : 7 * rows],
        summed[7 * rows : 7 * rows + n_loc].T,
        *grads,
    )


def solution(mesh):
    images = P(("replica", "shard"), None, None)
    each = P(("replica", "shard"))
    by_row, by_column, by_expert = P("shard", None), P(None, "shard"), P("shard", None, None)
    in_specs = (
        (images, each, each, images)
        + (by_row, by_row, by_row)
        + (by_row, by_column) * 3
        + (by_expert,) * 6
    )
    out_specs = (images, images) + (by_row, by_column) * 3 + (by_expert,) * 4
    return jax.shard_map(
        functools.partial(per_device, mesh.shape["replica"], mesh.shape["shard"]),
        mesh=mesh,
        in_specs=in_specs,
        out_specs=out_specs,
        check_vma=False,
    )
```

```python
import functools

import jax
import jax.numpy as jnp
from jax import lax
from jax.experimental import pallas as pl
from jax.experimental.pallas import tpu as pltpu
from jax.sharding import PartitionSpec as P

HEADS = 12
RANK = 16
LANES = 128
HEAD_DIM = 64
GROUP = 256
F32 = jnp.float32
BF16 = jnp.bfloat16
NN = (((1,), (0,)), ((), ()))
NT = (((1,), (1,)), ((), ()))
TN = (((0,), (0,)), ((), ()))
NEG = -1e30
VMEM_LIMIT = 56 * 1024 * 1024
GELU_C = 0.7978845608028654
GELU_A = 0.044715
IMAGES_FORWARD = 2
IMAGES_BACK = 2
IMAGES_ROUTE = 2
IMAGES_LAST = 2
STRIPS = 4


def dot(left, right, dims=NN):
    return lax.dot_general(left, right, dims, preferred_element_type=F32)


def params(*axes):
    return pltpu.CompilerParams(
        dimension_semantics=axes or None, vmem_limit_bytes=VMEM_LIMIT
    )


def cost(flops, moved, exps=0):
    return pl.CostEstimate(flops=int(flops), bytes_accessed=int(moved), transcendentals=int(exps))


def normalise(rows):
    centre = rows - jnp.mean(rows, axis=-1, keepdims=True)
    spread = jnp.mean(centre * centre, axis=-1, keepdims=True)
    scale = lax.rsqrt(spread + 1e-06)
    return centre * scale, scale


def normalise_back(unit, scale, upstream):
    inner = jnp.mean(upstream * unit, axis=-1, keepdims=True)
    return scale * (upstream - jnp.mean(upstream, axis=-1, keepdims=True) - unit * inner)


def rank_row(index):
    lane = lax.broadcasted_iota(jnp.int32, (1, LANES), 1) // RANK
    return (lane == index).astype(F32)


def zero_tail(rows, n_tok):
    total = rows.shape[0]
    cut = n_tok // 16 * 16
    if n_tok == total:
        return rows
    row = lax.broadcasted_iota(jnp.int32, (total - cut, rows.shape[1]), 0) + cut
    tail = jnp.where(row < n_tok, rows[cut:].astype(F32), 0.0).astype(rows.dtype)
    return jnp.concatenate([rows[:cut], tail], axis=0)


def mask_tail(scores, n_tok):
    total = scores.shape[0]
    cut = n_tok // 16 * 16
    if n_tok == total:
        return scores
    row = lax.broadcasted_iota(jnp.int32, (total - cut, scores.shape[1]), 0) + cut
    tail = jnp.where(row < n_tok, scores[cut:], NEG)
    return jnp.concatenate([scores[:cut], tail], axis=0)


def pad_rows(scratch, ref):
    n_img, n_tok, width = ref.shape
    total = scratch.shape[0] // n_img
    cut = n_tok // 8 * 8
    for slot in range(n_img):
        base = slot * total
        scratch[base + cut : base + total, :] = jnp.zeros((total - cut, width), F32)
        scratch[base : base + n_tok, :] = ref[slot].astype(F32)
    return scratch[...]


def select_rows(rows, index_ref, first, n_img):
    total = rows.shape[0] // n_img
    return jnp.concatenate(
        [
            (rows[i * total : (i + 1) * total] * rank_row(index_ref[first + i])).astype(BF16)
            for i in range(n_img)
        ],
        axis=0,
    )


def flat(ref):
    return ref[...].reshape(ref.shape[0] * ref.shape[1], ref.shape[2])


def assemble(place_ref, chunks, layout, wall):
    pieces, entries = layout
    part = wall.shape[1] // pieces
    for chunk, (replica, neighbour, start) in zip(chunks, entries):
        column = pl.multiple_of(((place_ref[0] % pieces) ^ replica) * part, LANES)
        if neighbour is None:
            wall[:, pl.ds(column, part)] = chunk[:, start : start + part]
            continue
        strips = STRIPS
        rows = chunk.shape[0] // strips
        for strip in range(strips):
            row = pl.multiple_of((2 * strip + (place_ref[1] ^ neighbour)) * rows, 16)
            wall[pl.ds(row, rows), pl.ds(column, part)] = chunk[
                strip * rows : (strip + 1) * rows, start : start + part
            ]


def norm_kernel(image_ref, _, out_ref, pad_ref):
    unit, _ = normalise(pad_rows(pad_ref, image_ref))
    out_ref[...] = unit.astype(BF16).reshape(out_ref.shape)


def pack_kernel(place_ref, qkv_ref, a_ref, b_ref, ao_ref, ra_ref, out_ref, pack):
    copies, rows, part = out_ref.shape
    width = qkv_ref.shape[1] // 3
    for piece in range(3):
        pack[:, piece * GROUP : (piece + 1) * GROUP] = qkv_ref[:, piece * width : piece * width + GROUP]
        column = width + (1 + piece) * LANES
        pack[:, column : column + LANES] = b_ref[piece * rows : (piece + 1) * rows, :]
    pack[:, width : width + LANES] = a_ref[...]
    pack[:, width + 4 * LANES : width + 5 * LANES] = ao_ref[...]
    pack[:, width + 5 * LANES : width + 6 * LANES] = ra_ref[...]
    mine = pack[:, pl.ds(pl.multiple_of(place_ref[0] * part, LANES), part)]
    for copy in range(copies):
        out_ref[copy] = mine


def later_pack_kernel(
    place_ref, qkv_ref, bo_ref, wr_ref, wo_ref, rb_ref, first_ref, second_ref, pack1, pack2, pack3
):
    shards, rows, part = first_ref.shape
    width = wo_ref.shape[1]
    for piece in range(3):
        for group, pack in ((1, pack1), (2, pack2)):
            start = piece * width + group * GROUP
            pack[:, piece * GROUP : (piece + 1) * GROUP] = qkv_ref[:, start : start + GROUP]
    pack1[:, width : width + LANES] = bo_ref[...]
    n_exp, n_loc = wr_ref.shape[0], rb_ref.shape[0]
    route = jnp.concatenate([wr_ref[...].astype(F32), jnp.zeros((LANES - n_exp, rows), F32)], axis=0)
    pack1[:, width + LANES :] = route.T.astype(BF16)
    pack3[:, :width] = wo_ref[...]
    second = jnp.concatenate([rb_ref[...].astype(F32), jnp.zeros((rows - n_loc, LANES), F32)], axis=0)
    pack3[:, width : width + LANES] = second.astype(BF16)
    pack3[:, width + LANES :] = jnp.zeros((rows, LANES), BF16)
    half = pack2.shape[1] // 2

    def own(pack, pieces, size):
        return pack[:, pl.ds(pl.multiple_of(place_ref[0] % pieces * size, LANES), size)]

    one, two, three = own(pack1, 4, part), own(pack2, 2, half), own(pack3, 4, part)
    for shard in range(shards):
        first_ref[shard] = one
        second_ref[shard, :, :half] = two
        second_ref[shard, :, half:] = three


def head_mask(value):
    lane = lax.broadcasted_iota(jnp.int32, (1, LANES), 1)
    low = jnp.where(lane < HEAD_DIM, value, 0.0).astype(BF16)
    high = jnp.where(lane < HEAD_DIM, 0.0, value).astype(BF16)
    return low, high


def each_head(columns, value):
    head = lax.broadcasted_iota(jnp.int32, (1, GROUP), 1) // HEAD_DIM
    return jnp.concatenate(
        [
            columns * jnp.where(head == number, value, 0.0).astype(BF16)
            for number in range(GROUP // HEAD_DIM)
        ],
        axis=0,
    )


def merge_pair(low, high):
    lane = lax.broadcasted_iota(jnp.int32, (1, LANES), 1)
    return jnp.where(lane < HEAD_DIM, low, high)


def attention_forward(qkv, n_tok, prob_ref, slot):
    total = qkv.shape[0]
    every = dot(each_head(qkv[:, GROUP : 2 * GROUP], 0.125), qkv[:, :GROUP], NT)
    outs = []
    for head in range(GROUP // HEAD_DIM):
        scores = mask_tail(every[head * total : (head + 1) * total], n_tok)
        powers = jnp.exp(scores - jnp.max(scores, axis=0, keepdims=True))
        probs = (powers * (1.0 / jnp.sum(powers, axis=0, keepdims=True))).astype(BF16)
        prob_ref[slot, head] = probs
        column = 2 * GROUP + head // 2 * LANES
        outs.append(dot(probs, qkv[:, column : column + LANES], TN))
    pairs = [merge_pair(outs[head], outs[head + 1]) for head in range(0, len(outs), 2)]
    return zero_tail(jnp.concatenate(pairs, axis=1).astype(BF16), n_tok)


def first_attention_kernel(
    n_tok, shards, layout, place_ref, index_ref, h1_ref, *rest,
):
    chunks, rest = rest[: len(layout[1])], rest[len(layout[1]) :]
    qkv_ref, att_ref, prob_ref, uq_ref, a_ref, bt_ref, ao_ref, ra_ref, wall = rest
    step = pl.program_id(0)
    n_img, total, width = h1_ref.shape

    @pl.when(step == 0)
    def _():
        assemble(place_ref, chunks, layout, wall)
        a_ref[...] = wall[:, width : width + LANES]
        ao_ref[...] = wall[:, width + 4 * LANES : width + 5 * LANES]
        ra_ref[...] = wall[:, width + 5 * LANES : width + 6 * LANES]
        rows = width // shards
        for shard in range(shards):
            for part in range(3):
                bt_ref[(shard * 3 + part) * rows : (shard * 3 + part + 1) * rows, :] = wall[
                    shard * rows : (shard + 1) * rows,
                    width + (1 + part) * LANES : width + (2 + part) * LANES,
                ]

    h1 = flat(h1_ref)
    low = dot(h1, a_ref[...]).astype(BF16).astype(F32)
    uq = select_rows(low, index_ref, step * n_img, n_img)
    uq_ref[...] = uq.reshape(uq_ref.shape)
    attend_group(0, n_tok, h1, uq, wall, bt_ref, qkv_ref, att_ref, prob_ref)


def group_rows(group, width, bt_ref):
    return jnp.concatenate(
        [bt_ref[part * width + group * GROUP : part * width + (group + 1) * GROUP, :] for part in range(3)],
        axis=0,
    )


def attend_group(group, n_tok, h1, uq, wall, bt_ref, qkv_ref, att_ref, prob_ref):
    n_img, total, _ = att_ref.shape
    second = group_rows(group, wall.shape[0], bt_ref)
    qkv = (dot(h1, wall[:, : 3 * GROUP]) + dot(uq, second, NT)).astype(BF16)
    qkv_ref[...] = qkv.reshape(qkv_ref.shape)
    for slot in range(n_img):
        att_ref[slot] = attention_forward(
            qkv[slot * total : (slot + 1) * total], n_tok, prob_ref, slot
        )


def next_attention_kernel(
    n_tok, group, extra, layout, place_ref, h1_ref, uq_ref, bt_ref, *rest
):
    chunks, rest = rest[: len(layout[1])], rest[len(layout[1]) :]
    qkv_ref, att_ref, prob_ref = rest[:3]
    wall = rest[-1]

    @pl.when(pl.program_id(0) == 0)
    def _():
        assemble(place_ref, chunks, layout, wall)
        for position in range(extra):
            column = 3 * GROUP + position * LANES
            rest[3 + position][...] = wall[:, column : column + LANES]

    attend_group(
        group, n_tok, flat(h1_ref), flat(uq_ref), wall, bt_ref, qkv_ref, att_ref, prob_ref,
    )


def route_kernel(
    n_exp, shards, layout, place_ref, index_ref, count_ref, image_ref, cot_ref, att0, att1, att2,
    ao_ref, bo_ref, ra_ref, wr_ref, *rest,
):
    chunks, rest = rest[: len(layout[1])], rest[len(layout[1]) :]
    x2_ref, uo_ref, ur_ref, disp_ref, comb_ref, sg_ref, wrt_ref, rb_ref, *rest = rest
    wall, rb_f, pad_a, pad_b, sent_ref = rest
    every = sg_ref.shape[2]
    n_img, n_tok, width = image_ref.shape
    first = pl.program_id(0) * n_img
    total = x2_ref.shape[1]

    @pl.when(first == 0)
    def _():
        assemble(place_ref, chunks, layout, wall)
        wrt_ref[...] = wr_ref[...].astype(F32).T[:n_exp].astype(BF16)
        n_loc, rows = n_exp // shards, width // shards
        for shard in range(shards):
            rb_f[shard * n_loc : (shard + 1) * n_loc, :] = wall[
                shard * rows : shard * rows + 8, width : width + LANES
            ].astype(F32)[:n_loc]
        rb_ref[...] = rb_f[...].astype(BF16)

    att = jnp.concatenate([flat(att0), flat(att1), flat(att2)], axis=1)
    uo = select_rows(dot(att, ao_ref[...]).astype(BF16).astype(F32), index_ref, first, n_img)
    uo_ref[...] = uo.reshape(uo_ref.shape)
    x2 = pad_rows(pad_a, image_ref) + dot(att, wall[:, :width]) + dot(uo, bo_ref[...], NT)
    x2_ref[...] = x2.reshape(x2_ref.shape)
    h2 = normalise(x2)[0].astype(BF16)
    ur = select_rows(dot(h2, ra_ref[...]).astype(BF16).astype(F32), index_ref, first, n_img)
    ur_ref[...] = ur.reshape(ur_ref.shape)
    cot = pad_rows(pad_b, cot_ref)
    for slot in range(n_img):
        rows = slice(slot * total, (slot + 1) * total)
        living = (first + slot < count_ref[0]).astype(F32)
        logits = dot(wrt_ref[...], h2[rows], NT) + dot(rb_ref[...], ur[rows], NT)
        alive = lax.broadcasted_iota(jnp.int32, logits.shape, 1) < n_tok
        over_tokens = jnp.where(alive, logits, NEG)
        powers = jnp.exp(over_tokens - jnp.max(over_tokens, axis=1, keepdims=True))
        disp = powers / jnp.sum(powers, axis=1, keepdims=True)
        powers = jnp.exp(logits - jnp.max(logits, axis=0, keepdims=True))
        comb = jnp.where(alive, powers / jnp.sum(powers, axis=0, keepdims=True), 0.0)
        disp_ref[slot] = disp
        comb_ref[slot] = comb
        upstream = (cot[rows] * living).astype(BF16)
        sent = jnp.concatenate(
            [
                dot(disp.astype(BF16), h2[rows]),
                dot(comb.astype(BF16), upstream),
                jnp.broadcast_to(rank_row(index_ref[first + slot]), (n_exp, LANES)),
            ],
            axis=1,
        )
        for block in range(sent.shape[1] // LANES):
            start = block * n_exp * every + first + slot
            sent_ref[pl.ds(start, n_exp, stride=every), :] = sent[:, block * LANES : (block + 1) * LANES]

    @pl.when(pl.program_id(0) == pl.num_programs(0) - 1)
    def _():
        for block in range(sg_ref.shape[3] // LANES):
            span = slice(block * LANES, (block + 1) * LANES)
            piece = sent_ref[block * n_exp * every : (block + 1) * n_exp * every, :]
            sg_ref[:, :, :, span] = piece.reshape(sg_ref.shape[:3] + (LANES,)).astype(BF16)


def gelu_both(pre):
    square = pre * pre
    half = jnp.tanh(GELU_C * pre * (1.0 + GELU_A * square))
    both = 0.5 * (1.0 + half)
    slope = both + 0.5 * pre * (1.0 - half * half) * (GELU_C * (1.0 + 3.0 * GELU_A * square))
    return pre * both, slope


def expert_tile(slots, gy, u1, gu2, wu_ref, wd_ref, ub_ref, da_ref):
    pre = dot(slots, wu_ref[0]) + dot(u1, ub_ref[0])
    ghid = (dot(wd_ref[0], gy, NT) + dot(da_ref[0], gu2, NT)).T
    hidden, slope = gelu_both(pre)
    return hidden.astype(BF16), (slope * ghid).astype(BF16)


def gather_rows(part_refs, out_ref):
    rows = part_refs[0].shape[0] * part_refs[0].shape[2]
    for number, part_ref in enumerate(part_refs):
        part = part_ref[:, 0].astype(F32).reshape(rows, part_ref.shape[3])
        out_ref[number * rows : (number + 1) * rows, :] = part.astype(BF16)


def expert_kernel(
    wu_ref, wd_ref, ua_ref, ub_ref, da_ref, db_ref, part_ref, out_ref, hidden_ref, gpre_ref, low_ref,
    sg_ref, u1_ref, gu2_ref, acc_y, acc_s, acc_u2, acc_gu1,
):
    step = pl.program_id(1)
    width = wu_ref.shape[1]

    @pl.when(step == 0)
    def _():
        gather_rows((part_ref,), sg_ref)
        selector = sg_ref[:, 2 * width :].astype(F32)
        u1_ref[...] = (
            dot(sg_ref[:, :width], ua_ref[0]).astype(BF16).astype(F32) * selector
        ).astype(BF16)
        gu2_ref[...] = (dot(sg_ref[:, width : 2 * width], db_ref[0], NT) * selector).astype(BF16)
        acc_y[...] = jnp.zeros_like(acc_y)
        acc_s[...] = jnp.zeros_like(acc_s)
        acc_u2[...] = jnp.zeros_like(acc_u2)
        acc_gu1[...] = jnp.zeros_like(acc_gu1)

    hidden, gpre = expert_tile(
        sg_ref[:, :width], sg_ref[:, width : 2 * width], u1_ref[...], gu2_ref[...],
        wu_ref, wd_ref, ub_ref, da_ref,
    )
    hidden_ref[0] = hidden
    gpre_ref[0] = gpre
    acc_y[...] += dot(hidden, wd_ref[0])
    acc_u2[...] += dot(hidden, da_ref[0])
    acc_s[...] += dot(wu_ref[0], gpre, NT)
    acc_gu1[...] += dot(ub_ref[0], gpre, NT)

    @pl.when(step == pl.num_programs(1) - 1)
    def _():
        selector = sg_ref[:, 2 * width :].astype(F32)
        u2 = (acc_u2[...].astype(BF16).astype(F32) * selector).astype(BF16)
        gu1 = (acc_gu1[...].T * selector).astype(BF16)
        shards, _, n_img, _ = out_ref.shape
        result = acc_y[...] + dot(u2, db_ref[0])
        out_ref[:, 0, :, :width] = result.reshape(shards, n_img, width).astype(BF16)
        result = acc_s[...].T + dot(gu1, ua_ref[0], NT)
        out_ref[:, 0, :, width:] = result.reshape(shards, n_img, width).astype(BF16)
        for place, low in enumerate((u1_ref[...], u2, gu1, gu2_ref[...])):
            low_ref[0, :, place * LANES : (place + 1) * LANES] = low


def expert_grad_kernel(copies, *refs):
    refs = list(refs)
    part_refs, hidden_refs, gpre_refs, low_refs = (
        [refs.pop(0) for _ in range(copies)] for _ in range(4)
    )
    gua_ref, gub_ref, gda_ref, gdb_ref, sg_ref, low_t, rows_ref = refs
    rows = hidden_refs[0].shape[1]
    width = gua_ref.shape[1]

    @pl.when(pl.program_id(1) == 0)
    def _():
        gather_rows(part_refs, sg_ref)
        low = jnp.concatenate([ref[0] for ref in low_refs], axis=0)
        low_t[...] = low.astype(F32).T.astype(BF16)
        u2_t, gu1_t = low_t[LANES : 2 * LANES, :], low_t[2 * LANES : 3 * LANES, :]
        gdb_ref[0] = dot(u2_t, sg_ref[:, width : 2 * width])
        gua_ref[0] = dot(gu1_t, sg_ref[:, :width]).T

    for number in range(copies):
        rows_ref[number * rows : (number + 1) * rows, :] = gpre_refs[number][0]
    gub_ref[0] = dot(low_t[:LANES, :], rows_ref[...])
    for number in range(copies):
        rows_ref[number * rows : (number + 1) * rows, :] = hidden_refs[number][0]
    gda_ref[0] = dot(low_t[3 * LANES :, :], rows_ref[...]).T


def turn_kernel(layouts, place_ref, ao_ref, ra_ref, *refs):
    refs = list(refs)
    chunks = [[refs.pop(0) for _ in layout[1]] for layout in layouts]
    qkv_ref, out_ref, route_ref = refs[:3]
    walls = refs[3:]
    for chunk, layout, wall in zip(chunks, layouts, walls):
        assemble(place_ref, chunk, layout, wall)
    width = walls[0].shape[0]
    for group, wall in enumerate(walls[:-1]):
        qkv_ref[group * 3 * GROUP : (group + 1) * 3 * GROUP, :] = wall[:, : 3 * GROUP].T
    qkv_ref[3 * width :, :] = walls[0][:, 3 * GROUP : 3 * GROUP + LANES].T
    out_ref[:width, :] = walls[-1][:, :width].T
    out_ref[width:, :] = ao_ref[...].T
    route_ref[...] = ra_ref[...].T


def route_back_kernel(
    n_exp, index_ref, count_ref, cot_ref, x2_ref, uo_ref, ur_ref, disp_ref, comb_ref,
    att0, att1, att2, ret_ref, bo_ref, wrt_ref, rb_ref, out_ref, route_ref,
    block_ref, gx2_ref, gatt_ref, pack_ref, pad_b, back_ref, acc_oa, acc_ob, acc_ra, acc_rb,
):
    n_img, n_tok, width = cot_ref.shape
    first = pl.program_id(0) * n_img
    total = x2_ref.shape[1]

    every = ret_ref.shape[2]

    @pl.when(first == 0)
    def _():
        for block in range(2 * width // LANES):
            piece = ret_ref[:, :, :, block * LANES : (block + 1) * LANES].astype(F32)
            back_ref[block * n_exp * every : (block + 1) * n_exp * every, :] = piece.reshape(
                n_exp * every, LANES
            )
        acc_oa[...] = jnp.zeros_like(acc_oa)
        acc_ob[...] = jnp.zeros_like(acc_ob)
        acc_ra[...] = jnp.zeros_like(acc_ra)
        acc_rb[...] = jnp.zeros_like(acc_rb)

    cot = pad_rows(pad_b, cot_ref)
    x2 = flat(x2_ref)
    unit, scale = normalise(x2)
    h2 = unit.astype(BF16)
    pairs, belows, upstreams = [], [], []
    for slot in range(n_img):
        rows = slice(slot * total, (slot + 1) * total)
        living = (first + slot < count_ref[0]).astype(F32)
        upstream = cot[rows] * living
        upstreams.append(upstream)
        disp, comb = disp_ref[slot], comb_ref[slot]
        blocks = [
            back_ref[pl.ds(block * n_exp * every + first + slot, n_exp, stride=every), :]
            for block in range(2 * width // LANES)
        ]
        back = jnp.concatenate(blocks, axis=1).astype(BF16)
        yexp, gslot = back[:, :width], back[:, width:]
        gcomb = dot(yexp, upstream.astype(BF16), NT)
        gdisp = dot(gslot, h2[rows], NT)
        glog = (
            disp * (gdisp - jnp.sum(gdisp * disp, axis=1, keepdims=True))
            + comb * (gcomb - jnp.sum(gcomb * comb, axis=0, keepdims=True))
        )
        acc_rb[...] += dot(glog.astype(BF16), ur_ref[slot])
        three = jnp.concatenate([disp, glog, comb], axis=0).T.astype(BF16)
        mixed = dot(three[:, 2 * n_exp :], yexp)
        block_ref[slot] = (living * (x2[rows] + mixed)).astype(BF16)[:n_tok]
        pairs.append(three[:, : 2 * n_exp])
        belows.append(jnp.concatenate([gslot, wrt_ref[...]], axis=0))
    glog_rows = jnp.concatenate([pair[:, n_exp:] for pair in pairs], axis=0)
    gur = select_rows(dot(glog_rows, rb_ref[...]), index_ref, first, n_img)
    acc_ra[...] += dot(gur, h2, TN)
    gh2 = dot(gur, route_ref[...]) + jnp.concatenate(
        [dot(pair, below) for pair, below in zip(pairs, belows)], axis=0
    )
    gx2 = jnp.concatenate(upstreams, axis=0) + normalise_back(unit, scale, gh2)
    gbr = gx2.astype(BF16)
    gx2_ref[...] = gbr.reshape(gx2_ref.shape)
    acc_ob[...] += dot(flat(uo_ref), gbr, TN)
    guo = select_rows(dot(gbr, bo_ref[...]), index_ref, first, n_img)
    att = jnp.concatenate([flat(att0), flat(att1), flat(att2)], axis=1)
    acc_oa[...] += dot(guo, att, TN)
    gatt = dot(jnp.concatenate([gbr, guo], axis=1), out_ref[...]).astype(BF16)
    gatt_ref[...] = gatt.reshape(gatt_ref.shape)

    @pl.when(pl.program_id(0) == pl.num_programs(0) - 1)
    def _():
        shards = pack_ref.shape[0]
        rows = width // shards
        n_loc = n_exp // shards
        for position, acc in enumerate((acc_oa, acc_ob, acc_ra)):
            summed = acc[...].T.astype(BF16)
            for shard in range(shards):
                pack_ref[shard, position * rows : (position + 1) * rows, :] = summed[
                    shard * rows : (shard + 1) * rows
                ]
        tail = pack_ref.shape[1] - 3 * rows
        for shard in range(shards):
            last = jnp.concatenate(
                [acc_rb[shard * n_loc : (shard + 1) * n_loc, :], jnp.zeros((tail - n_loc, LANES), F32)],
                axis=0,
            )
            pack_ref[shard, 3 * rows :, :] = last.astype(BF16)


def attention_backward(qkv, gatt, prob_ref, slot):
    keep = head_mask(1.0)
    key_t = qkv[:, GROUP : 2 * GROUP].T
    total = qkv.shape[0]
    gq_parts, gk_parts, gv_parts = [], [], []
    for pair in range(GROUP // LANES):
        span = slice(pair * LANES, (pair + 1) * LANES)
        q_pair, ga_pair = qkv[:, span], gatt[:, span]
        v_pair = qkv[:, 2 * GROUP + pair * LANES : 2 * GROUP + (pair + 1) * LANES]
        lows = [prob_ref[slot, 2 * pair], prob_ref[slot, 2 * pair + 1]]
        gv = dot(jnp.concatenate(lows, axis=0), ga_pair)
        gprobs = dot(jnp.concatenate([v_pair * keep[0], v_pair * keep[1]], axis=0), ga_pair, NT)
        gscores = []
        for side in range(2):
            probs = lows[side].astype(F32)
            gprob = gprobs[side * total : (side + 1) * total]
            inner = jnp.sum(gprob * probs, axis=0, keepdims=True)
            gscores.append((probs * (gprob - inner)).astype(BF16))
            head = 2 * pair + side
            gq_parts.append(
                (dot(key_t[head * HEAD_DIM : (head + 1) * HEAD_DIM], gscores[side]) * 0.125).astype(BF16)
            )
        gk = dot(jnp.concatenate(gscores, axis=0), q_pair)
        gk_parts.append((merge_pair(gk[:total], gk[total:]) * 0.125).astype(BF16))
        gv_parts.append(merge_pair(gv[:total], gv[total:]).astype(BF16))
    gq = jnp.concatenate(gq_parts, axis=0).T
    return jnp.concatenate([gq] + gk_parts + gv_parts, axis=1)


def attention_back_kernel(groups, place_ref, index_ref, *refs):
    refs = list(refs)
    qkv_refs = [refs.pop(0) for _ in range(groups)]
    prob_refs = [refs.pop(0) for _ in range(groups)]
    gatt_ref, uq_ref, h1_ref, bt_ref, others_ref = refs[:5]
    refs = refs[5:]
    gqkv_refs = [refs.pop(0) for _ in range(groups)]
    guq_ref, keep_ref, give_ref, pack_ref, acc_b, acc_a = refs
    step = pl.program_id(0)
    n_img, total, width = h1_ref.shape

    @pl.when(step == 0)
    def _():
        acc_b[...] = jnp.zeros_like(acc_b)
        acc_a[...] = jnp.zeros_like(acc_a)

    uq_t = flat(uq_ref).T
    guq = None
    for group in range(groups):
        parts = []
        for i in range(n_img):
            part = attention_backward(
                qkv_refs[group][i], gatt_ref[i, :, group * GROUP : (group + 1) * GROUP],
                prob_refs[group], i,
            )
            gqkv_refs[group][i] = part
            parts.append(part)
        gqkv = jnp.concatenate(parts, axis=0)
        acc_b[:, group * 3 * GROUP : (group + 1) * 3 * GROUP] += dot(uq_t, gqkv)
        part = dot(gqkv, group_rows(group, width, bt_ref))
        guq = part if guq is None else guq + part
    guq = select_rows(guq, index_ref, step * n_img, n_img)
    acc_a[...] += dot(guq, flat(h1_ref), TN)
    guq_ref[...] = guq.reshape(guq_ref.shape)

    @pl.when(step == pl.num_programs(0) - 1)
    def _():
        shards = pack_ref.shape[0]
        rows = width // shards
        pack_ref[:, 4 * rows :, :] = others_ref[...]
        own = acc_a[...].T.astype(BF16)
        for shard in range(shards):
            pack_ref[shard, 3 * rows : 4 * rows, :] = own[shard * rows : (shard + 1) * rows]
        for group in range(groups):
            summed = acc_b[:, group * 3 * GROUP : (group + 1) * 3 * GROUP].T.astype(BF16)
            for part in range(3):
                start = part * width + group * GROUP
                place = start
                while place < start + GROUP:
                    shard, offset = divmod(place, 3 * rows)
                    length = min(start + GROUP - place, 3 * rows - offset)
                    take = part * GROUP + place - start
                    pack_ref[shard, offset : offset + length, :] = summed[take : take + length]
                    place += length
        half = keep_ref.shape[1]
        side = place_ref[2] % 2
        keep_ref[...] = pack_ref[:, pl.ds(pl.multiple_of(side * half, 16), half), :]
        give_ref[...] = pack_ref[:, pl.ds(pl.multiple_of((1 - side) * half, 16), half), :]


def input_grad_kernel(image_ref, gx2_ref, guq_ref, turned_ref, *refs):
    *gqkv, out_ref, pad_a = refs
    n_img, n_tok, width = image_ref.shape
    step = pl.program_id(0)
    parts = width // LANES
    every = out_ref.shape[0] // (n_tok * parts)
    total = gx2_ref.shape[1]
    gh1 = dot(jnp.concatenate([flat(ref) for ref in gqkv] + [flat(guq_ref)], axis=1), turned_ref[...])
    unit, scale = normalise(pad_rows(pad_a, image_ref))
    result = flat(gx2_ref).astype(F32) + normalise_back(unit, scale, gh1)
    for slot in range(n_img):
        for part in range(parts):
            out_ref[pl.ds(part * every + step * n_img + slot, n_tok, stride=parts * every), :] = result[
                slot * total : slot * total + n_tok, part * LANES : (part + 1) * LANES
            ]


ANY = pl.BlockSpec(memory_space=pl.ANY)


def whole(shape):
    return pl.BlockSpec(shape, lambda *_: (0,) * len(shape))


def once(shape):
    return pl.BlockSpec(shape, lambda *_: (0,) * len(shape), pipeline_mode=pl.Buffered(1))


def per_image(*shape, images=1):
    return pl.BlockSpec((images,) + shape, lambda i, *_: (i,) + (0,) * len(shape))


def several(images, limit):
    return max(n for n in range(1, limit + 1) if images % n == 0)


def call(kernel, scalars, grid, inputs, outputs, scratch, flops, exps=0, aliases=None):
    arrays = [array for array, _ in inputs]
    shapes = [jax.ShapeDtypeStruct(shape, dtype) for shape, dtype, _ in outputs]
    moved = sum(array.size * array.dtype.itemsize for array in arrays) + sum(
        shape.size * shape.dtype.itemsize for shape in shapes
    )
    return pl.pallas_call(
        kernel,
        out_shape=shapes,
        grid_spec=pltpu.PrefetchScalarGridSpec(
            num_scalar_prefetch=len(scalars),
            grid=grid,
            in_specs=[spec for _, spec in inputs],
            out_specs=[spec for _, _, spec in outputs],
            scratch_shapes=scratch,
        ),
        input_output_aliases=aliases or {},
        compiler_params=params(*(("arbitrary",) * len(grid))),
        cost_estimate=cost(flops, moved, exps),
    )(*scalars, *arrays)


def norm_call(images, cotangent, total):
    n_img, n_tok, width = images.shape
    each = several(n_img, 4)
    return call(
        norm_kernel, (), (n_img // each,),
        [(images, per_image(n_tok, width, images=each)), (cotangent, ANY)],
        [((n_img, total, width), BF16, per_image(total, width, images=each))],
        [pltpu.VMEM((each * total, width), F32)],
        8 * images.size,
    )[0]


def pack_call(place, weights, copies):
    rows, columns = weights[0].shape
    part = (columns // 3 + 6 * LANES) // 4
    return call(
        pack_kernel, (place,), (1,), [(weight, whole(weight.shape)) for weight in weights],
        [((copies, rows, part), BF16, whole((copies, rows, part)))],
        [pltpu.VMEM((rows, 4 * part), BF16)],
        rows * columns,
    )[0]


def later_pack_call(place, weights, shards):
    rows, width = weights[3].shape
    part, half = (width + 2 * LANES) // 4, width // 2
    return call(
        later_pack_kernel, (place,), (1,), [(weight, whole(weight.shape)) for weight in weights],
        [
            ((shards, rows, part), BF16, whole((shards, rows, part))),
            ((shards, rows, half + part), BF16, whole((shards, rows, half + part))),
        ],
        [pltpu.VMEM((rows, columns), BF16) for columns in (4 * part, 2 * half, 4 * part)],
        rows * width,
    )


def attention_flops(n_img, total, width, parts):
    return n_img * total * (2 * width * 3 * GROUP + parts * 8 * total * HEAD_DIM)


def attention_outputs(n_img, total, each):
    return [
        ((n_img, total, 3 * GROUP), BF16, per_image(total, 3 * GROUP, images=each)),
        ((n_img, total, GROUP), BF16, per_image(total, GROUP, images=each)),
        (
            (n_img, GROUP // HEAD_DIM, total, total), BF16,
            per_image(GROUP // HEAD_DIM, total, total, images=each),
        ),
    ]


def first_attention_call(place, index, h1, pack, n_tok, shards):
    n_img, total, width = h1.shape
    chunks, layout, columns = pack
    each = several(n_img, IMAGES_FORWARD)
    return call(
        functools.partial(first_attention_kernel, n_tok, shards, layout), (place, index), (n_img // each,),
        [(h1, per_image(total, width, images=each))] + [(chunk, once(chunk.shape)) for chunk in chunks],
        attention_outputs(n_img, total, each)
        + [
            ((n_img, total, LANES), BF16, per_image(total, LANES, images=each)),
            ((width, LANES), BF16, whole((width, LANES))),
            ((3 * width, LANES), BF16, whole((3 * width, LANES))),
            ((width, LANES), BF16, whole((width, LANES))),
            ((width, LANES), BF16, whole((width, LANES))),
        ],
        [pltpu.VMEM((width, columns), BF16)],
        attention_flops(n_img, total, width, 2), n_img * total * total * 4,
    )


def next_attention_call(place, h1, uq, bt, pack, n_tok, group, extra):
    n_img, total, width = h1.shape
    chunks, layout, columns = pack
    each = several(n_img, IMAGES_FORWARD)
    return call(
        functools.partial(next_attention_kernel, n_tok, group, extra, layout), (place,), (n_img // each,),
        [
            (h1, per_image(total, width, images=each)),
            (uq, per_image(total, LANES, images=each)),
            (bt, whole(bt.shape)),
        ]
        + [(chunk, once(chunk.shape)) for chunk in chunks],
        attention_outputs(n_img, total, each)
        + [((width, LANES), BF16, whole((width, LANES)))] * extra,
        [pltpu.VMEM((width, columns), BF16)],
        attention_flops(n_img, total, width, 2), n_img * total * total * 4,
    )


def route_call(place, index, count, images, cotangent, atts, banks, pack, n_exp, total, shards):
    n_img, n_tok, width = images.shape
    chunks, layout, columns = pack
    each = several(n_img, IMAGES_ROUTE)
    here = functools.partial(per_image, images=each)
    sent = (shards, n_exp // shards, n_img, 2 * width + LANES)
    return call(
        functools.partial(route_kernel, n_exp, shards, layout), (place, index, count), (n_img // each,),
        [(images, here(n_tok, width)), (cotangent, here(n_tok, width))]
        + [(att, here(total, GROUP)) for att in atts]
        + [(bank, whole(bank.shape)) for bank in banks]
        + [(chunk, once(chunk.shape)) for chunk in chunks],
        [
            ((n_img, total, width), F32, here(total, width)),
            ((n_img, total, LANES), BF16, here(total, LANES)),
            ((n_img, total, LANES), BF16, here(total, LANES)),
            ((n_img, n_exp, total), F32, here(n_exp, total)),
            ((n_img, n_exp, total), F32, here(n_exp, total)),
            (sent, BF16, whole(sent)),
            ((n_exp, width), BF16, whole((n_exp, width))),
            ((n_exp, LANES), BF16, whole((n_exp, LANES))),
        ],
        [
            pltpu.VMEM((width, columns), BF16),
            pltpu.VMEM((n_exp, LANES), F32),
            pltpu.VMEM((each * total, width), F32),
            pltpu.VMEM((each * total, width), F32),
            pltpu.VMEM(((2 * width // LANES + 1) * n_exp * n_img, LANES), F32),
        ],
        n_img * total * 2 * width * (width + 3 * LANES), n_img * total * 2 * n_exp,
    )


def hidden_tile(hidden, limit):
    tile = hidden
    while tile > limit:
        tile //= 2
    return tile


def expert_specs(width, tile, first=0):
    return (
        pl.BlockSpec((1, width, tile), lambda e, f: (e + first, 0, f)),
        pl.BlockSpec((1, tile, width), lambda e, f: (e + first, f, 0)),
        pl.BlockSpec((1, width, LANES), lambda e, f: (e + first, 0, 0)),
        pl.BlockSpec((1, LANES, tile), lambda e, f: (e + first, 0, f)),
        pl.BlockSpec((1, tile, LANES), lambda e, f: (e + first, f, 0)),
        pl.BlockSpec((1, LANES, width), lambda e, f: (e + first, 0, 0)),
    )


def expert_rows(shape, first=0):
    shards, _, n_img, columns = shape
    return pl.BlockSpec((shards, 1, n_img, columns), lambda e, f: (0, e + first, 0, 0))


def expert_call(landed, weights):
    shards, n_loc, n_img, columns = landed.shape
    rows = shards * n_img
    width, hidden = weights[0].shape[1:]
    tile = hidden_tile(hidden, 1536)
    out = (shards, n_loc, n_img, 2 * width)
    tiled = pl.BlockSpec((1, rows, tile), lambda e, f: (e, 0, f))
    return call(
        expert_kernel, (), (n_loc, hidden // tile),
        list(zip(weights, expert_specs(width, tile))) + [(landed, expert_rows(landed.shape))],
        [
            (out, BF16, expert_rows(out)),
            ((n_loc, rows, hidden), BF16, tiled),
            ((n_loc, rows, hidden), BF16, tiled),
            (
                (n_loc, rows, 4 * LANES), BF16,
                pl.BlockSpec((1, rows, 4 * LANES), lambda e, f: (e, 0, 0)),
            ),
        ],
        [
            pltpu.VMEM((rows, columns), BF16),
            pltpu.VMEM((rows, LANES), BF16),
            pltpu.VMEM((rows, LANES), BF16),
            pltpu.VMEM((rows, width), F32),
            pltpu.VMEM((width, rows), F32),
            pltpu.VMEM((rows, LANES), F32),
            pltpu.VMEM((LANES, rows), F32),
        ],
        n_loc * rows * 8 * width * hidden, n_loc * rows * hidden,
    )


def expert_grad_call(every, width):
    parts, hiddens, gpres, lows = zip(*every)
    shards, n_loc, n_img, columns = parts[0].shape
    rows, hidden = hiddens[0].shape[1:]
    total = rows * len(every)
    tile = hidden_tile(hidden, 1536 if total <= 512 else 384)
    tiled = pl.BlockSpec((1, rows, tile), lambda e, f: (e, 0, f))
    low = pl.BlockSpec((1, rows, 4 * LANES), lambda e, f: (e, 0, 0))
    return call(
        functools.partial(expert_grad_kernel, len(every)), (), (n_loc, hidden // tile),
        [(part, expert_rows(part.shape)) for part in parts]
        + [(array, tiled) for array in hiddens + gpres]
        + [(array, low) for array in lows],
        [
            ((n_loc, width, LANES), F32, pl.BlockSpec((1, width, LANES), lambda e, f: (e, 0, 0))),
            ((n_loc, LANES, hidden), F32, pl.BlockSpec((1, LANES, tile), lambda e, f: (e, 0, f))),
            ((n_loc, hidden, LANES), F32, pl.BlockSpec((1, tile, LANES), lambda e, f: (e, f, 0))),
            ((n_loc, LANES, width), F32, pl.BlockSpec((1, LANES, width), lambda e, f: (e, 0, 0))),
        ],
        [
            pltpu.VMEM((total, columns), BF16),
            pltpu.VMEM((4 * LANES, total), BF16),
            pltpu.VMEM((total, tile), BF16),
        ],
        4 * n_loc * total * LANES * hidden,
    )


def route_back_call(
    index, count, cotangent, x2, uo, ur, disp, comb, atts, ret, banks, shards, replicas
):
    n_img, n_tok, width = cotangent.shape
    total, n_exp = x2.shape[1], disp.shape[1]
    rows = width // shards
    unit = 16 * replicas
    pack_rows = -(-(7 * rows + n_exp // shards) // unit) * unit - 4 * rows
    each = several(n_img, IMAGES_ROUTE)
    here = functools.partial(per_image, images=each)
    return call(
        functools.partial(route_back_kernel, n_exp), (index, count), (n_img // each,),
        [
            (cotangent, here(n_tok, width)),
            (x2, here(total, width)),
            (uo, here(total, LANES)),
            (ur, here(total, LANES)),
            (disp, here(n_exp, total)),
            (comb, here(n_exp, total)),
        ]
        + [(att, here(total, GROUP)) for att in atts]
        + [(ret, once(ret.shape))]
        + [(bank, once(bank.shape)) for bank in banks],
        [
            ((n_img, n_tok, width), BF16, here(n_tok, width)),
            ((n_img, total, width), BF16, here(total, width)),
            ((n_img, total, width), BF16, here(total, width)),
            ((shards, pack_rows, LANES), BF16, whole((shards, pack_rows, LANES))),
        ],
        [
            pltpu.VMEM((each * total, width), F32),
            pltpu.VMEM((2 * width // LANES * n_exp * n_img, LANES), F32),
            pltpu.VMEM((LANES, width), F32),
            pltpu.VMEM((LANES, width), F32),
            pltpu.VMEM((LANES, width), F32),
            pltpu.VMEM((n_exp, LANES), F32),
        ],
        n_img * total * 2 * width * (width + 6 * LANES),
    )


def attention_back_call(place, index, qkvs, probs, gatt, uq, h1, bt, others):
    n_img, total, width = h1.shape
    groups = len(qkvs)
    shards = others.shape[0]
    each = several(n_img, IMAGES_BACK)
    here = functools.partial(per_image, images=each)
    pack = (shards, 4 * width // shards + others.shape[1], LANES)
    half = (shards, pack[1] // 2, LANES)
    return call(
        functools.partial(attention_back_kernel, groups), (place, index), (n_img // each,),
        [(qkv, here(total, 3 * GROUP)) for qkv in qkvs]
        + [(prob, here(GROUP // HEAD_DIM, total, total)) for prob in probs]
        + [
            (gatt, here(total, width)),
            (uq, here(total, LANES)),
            (h1, here(total, width)),
            (bt, whole(bt.shape)),
            (others, whole(others.shape)),
        ],
        [((n_img, total, 3 * GROUP), BF16, here(total, 3 * GROUP))] * groups
        + [((n_img, total, LANES), BF16, here(total, LANES))]
        + [(half, BF16, whole(half))] * 2,
        [
            pltpu.VMEM(pack, BF16),
            pltpu.VMEM((LANES, 3 * width), F32),
            pltpu.VMEM((LANES, width), F32),
        ],
        groups * attention_flops(n_img, total, LANES, 5), groups * n_img * total * total * 4,
    )


def input_grad_call(images, gx2, guq, gqkvs, turned):
    n_img, n_tok, width = images.shape
    total = gx2.shape[1]
    each = several(n_img, IMAGES_LAST)
    here = functools.partial(per_image, images=each)
    out = call(
        input_grad_kernel, (), (n_img // each,),
        [
            (images, here(n_tok, width)),
            (gx2, here(total, width)),
            (guq, here(total, LANES)),
            (turned, once(turned.shape)),
        ]
        + [(gqkv, here(total, 3 * GROUP)) for gqkv in gqkvs],
        [((images.size // LANES, LANES), F32, whole((images.size // LANES, LANES)))],
        [pltpu.VMEM((each * total, width), F32)],
        n_img * total * 2 * width * (3 * width + LANES),
    )[0]
    out = out.reshape(n_tok, width // LANES, n_img, LANES).transpose(2, 0, 1, 3)
    return out.reshape(n_img, n_tok, width)


def turn_call(place, bank_ao, bank_ra, packs):
    width = bank_ao.shape[0]
    shapes = [(3 * width + LANES, width), (width + LANES, width), (LANES, width)]
    return call(
        functools.partial(turn_kernel, tuple(pack[1] for pack in packs)), (place,), (1,),
        [(bank, once(bank.shape)) for bank in (bank_ao, bank_ra)]
        + [(chunk, once(chunk.shape)) for pack in packs for chunk in pack[0]],
        [(shape, BF16, once(shape)) for shape in shapes],
        [pltpu.VMEM((width, pack[2]), BF16) for pack in packs],
        8 * width * width,
    )


def swap(array, axis, size, bit):
    return lax.ppermute(array, axis, [(i, i ^ bit) for i in range(size)])


def tie(*arrays):
    return lax.optimization_barrier(arrays)


def over_shard(spread, lines=None):
    own = lax.all_to_all(
        spread, "shard", split_axis=0, concat_axis=0, tiled=True, axis_index_groups=lines
    )
    return own.reshape(-1, spread.shape[2])


def reduce_pack(keep, give, replicas, beside_first, beside_swap, beside_spread):
    where = lax.axis_index("replica")
    bits = []
    bit = 1
    first_work = swap_work = ()
    while bit < replicas:
        got = swap(give, "replica", replicas, bit)
        if bit == 1:
            got, *first_work = tie(got, *beside_first())
        if 2 * bit == replicas:
            got, *swap_work = tie(got, *beside_swap())
        pack = (keep.astype(F32) + got.astype(F32)).astype(BF16)
        bits.append(bit)
        bit *= 2
        if bit < replicas:
            half = pack.shape[1] // 2
            side = (where // bit) % 2
            keep = lax.dynamic_slice_in_dim(pack, side * half, half, axis=1)
            give = lax.dynamic_slice_in_dim(pack, (1 - side) * half, half, axis=1)
    landed = lax.all_to_all(pack, "shard", split_axis=0, concat_axis=0, tiled=True)
    landed, *spread_work = tie(landed, *beside_spread(*first_work))
    total = jnp.sum(landed.astype(F32), axis=0).astype(BF16)
    for bit in reversed(bits):
        got = swap(total, "replica", replicas, bit)
        side = (where // bit) % 2
        total = jnp.where(
            side == 0,
            jnp.concatenate([total, got], axis=0),
            jnp.concatenate([got, total], axis=0),
        )
    return total, first_work, swap_work, spread_work


def per_device(
    replicas,
    shards,
    images,
    image_adapter_index,
    device_image_count,
    cotangent,
    query_key_value_weight,
    frozen_output_weight,
    frozen_dispatch_weight,
    query_key_value_first,
    query_key_value_second,
    output_adapter_first,
    output_adapter_second,
    dispatch_adapter_first,
    dispatch_adapter_second,
    frozen_up_weight,
    frozen_down_weight,
    up_adapter_first,
    up_adapter_second,
    down_adapter_first,
    down_adapter_second,
):
    n_img, n_tok, width = images.shape
    total = -(-n_tok // 16) * 16
    rows = width // shards
    n_loc = frozen_up_weight.shape[0]
    n_exp = n_loc * shards
    groups = width // GROUP
    quarter = lax.axis_index("replica") % 4
    place = jnp.stack(
        [quarter, lax.axis_index("shard") % 2, lax.axis_index("replica")]
    ).astype(jnp.int32)
    by_axis = shards == 2 * STRIPS and replicas == 4

    spread0 = pack_call(
        place,
        (
            query_key_value_weight, query_key_value_first, query_key_value_second.T,
            output_adapter_first, dispatch_adapter_first,
        ),
        STRIPS if by_axis else shards,
    )
    spread1, spread23 = later_pack_call(
        place,
        (
            query_key_value_weight, output_adapter_second.T, frozen_dispatch_weight.T,
            frozen_output_weight, dispatch_adapter_second.T,
        ),
        shards,
    )
    near = functools.partial(swap, axis="replica", size=replicas, bit=1)
    far = functools.partial(swap, axis="replica", size=replicas, bit=2)
    beside = functools.partial(swap, axis="shard", size=shards, bit=1)

    h1 = norm_call(images, cotangent, total)
    if by_axis:
        lines = [[2 * strip + side for strip in range(STRIPS)] for side in range(2)]
        own0, spread1, spread23 = tie(over_shard(spread0, lines), spread1, spread23)
        beside0, far0, h1, spread1 = tie(beside(own0), far(own0), h1, spread1)
        held = [(own0, 0, 0), (beside0, 0, 1), (far0, 2, 0)]
        own1 = over_shard(spread1)
        held.append((far(held[1][0]), 2, 1))
    else:
        own0 = over_shard(spread0)
        own0, h1, spread1 = tie(own0, h1, spread1)
        held = [(own0, 0, None), (far(own0), 2, None)]
        own1 = over_shard(spread1)
    chunks0 = [chunk for chunk, _, _ in held] + [near(chunk) for chunk, _, _ in held]
    layout0 = [(replica, side, 0) for _, replica, side in held]
    layout0 += [(replica ^ 1, side, 0) for _, replica, side in held]
    *chunks0, own1, spread23 = tie(*chunks0, own1, spread23)
    pack0 = (tuple(chunks0), (4, tuple(layout0)), 3 * GROUP + 6 * LANES)
    far1 = far(own1)
    own23 = over_shard(spread23)
    qkv0, att0, prob0, uq, bank_a, bank_bt, bank_ao, bank_ra = first_attention_call(
        place, image_adapter_index, h1, pack0, n_tok, shards
    )
    uq, own1, far1 = tie(uq, own1, far1)
    four = (4, ((0, None, 0), (1, None, 0), (2, None, 0), (3, None, 0)))
    pack1 = ((own1, near(own1), far1, near(far1)), four, 3 * GROUP + 2 * LANES)
    qkv1, att1, prob1, bank_bo, bank_wr = next_attention_call(
        place, h1, uq, bank_bt, pack1, n_tok, 1, 2
    )
    att1, uq, own23 = tie(att1, uq, own23)
    own2, own3 = own23[:, : width // 2], own23[:, width // 2 :]
    far3 = far(own3)
    pack2 = ((own2, near(own2)), (2, ((0, None, 0), (1, None, 0))), 3 * GROUP)
    qkv2, att2, prob2 = next_attention_call(place, h1, uq, bank_bt, pack2, n_tok, 2, 0)
    att2, own3, far3 = tie(att2, own3, far3)
    pack3 = ((own3, near(own3), far3, near(far3)), four, width + 2 * LANES)
    packs = (pack0, pack1, pack2, pack3)
    atts = (att0, att1, att2)
    x2, uo, ur, disp, comb, sg, bank_wrt, bank_rb = route_call(
        place, image_adapter_index, device_image_count, images, cotangent, atts,
        (bank_ao, bank_bo, bank_ra, bank_wr), packs[3], n_exp, total, shards,
    )

    landed = lax.all_to_all(sg, "shard", split_axis=0, concat_axis=0, tiled=True)
    landed, *turned = tie(landed, *turn_call(place, bank_ao, bank_ra, packs))
    turned_qkv, turned_out, turned_route = turned
    weights = (
        frozen_up_weight, frozen_down_weight, up_adapter_first, up_adapter_second,
        down_adapter_first, down_adapter_second,
    )
    far_landed = [swap(landed, "replica", replicas, bit) for bit in range(2, replicas, 2)]
    ret, *kept = expert_call(landed, weights)
    ret, *far_landed = tie(ret, *far_landed)
    back = lax.all_to_all(ret, "shard", split_axis=0, concat_axis=0, tiled=True)
    every = [(landed, *kept)]
    for number, bit in enumerate(range(2, replicas, 2)):
        far_kept = [swap(array, "replica", replicas, bit) for array in kept]
        every.append((far_landed[number], *far_kept))

    block_out, gx2, gatt, out_pack = route_back_call(
        image_adapter_index, device_image_count, cotangent, x2, uo, ur, disp, comb, atts, back,
        (bank_bo, bank_wrt, bank_rb, turned_out, turned_route), shards, replicas,
    )
    gatt, *lows = tie(gatt, *[row[3] for row in every])
    held = [array for row, low in zip(every, lows) for array in (*row[:3], low)]
    *gqkvs, guq, keep, give = attention_back_call(
        place, image_adapter_index, (qkv0, qkv1, qkv2), (prob0, prob1, prob2), gatt, uq, h1, bank_bt, out_pack
    )

    def expert_grads(block, *arrays):
        arrays = list(arrays) + [swap(array, "replica", replicas, 1) for array in arrays]
        rows_of = [tuple(arrays[place : place + 4]) for place in range(0, len(arrays), 4)]
        return expert_grad_call(rows_of, width)

    summed, (block_out, *_), (input_grad,), grads = reduce_pack(
        keep, give, replicas,
        lambda: (block_out.transpose(1, 0, 2), *held),
        lambda: (input_grad_call(images, gx2, guq, gqkvs, turned_qkv),),
        expert_grads,
    )
    block_out = block_out.transpose(1, 0, 2)
    summed = summed.astype(F32)
    return (
        block_out,
        input_grad,
        summed[3 * rows : 4 * rows],
        summed[: 3 * rows].T,
        summed[4 * rows : 5 * rows],
        summed[5 * rows : 6 * rows].T,
        summed[6 * rows : 7 * rows],
        summed[7 * rows : 7 * rows + n_loc].T,
        *grads,
    )


def solution(mesh):
    images = P(("replica", "shard"), None, None)
    each = P(("replica", "shard"))
    by_row, by_column, by_expert = P("shard", None), P(None, "shard"), P("shard", None, None)
    in_specs = (
        (images, each, each, images)
        + (by_row, by_row, by_row)
        + (by_row, by_column) * 3
        + (by_expert,) * 6
    )
    out_specs = (images, images) + (by_row, by_column) * 3 + (by_expert,) * 4
    return jax.shard_map(
        functools.partial(per_device, mesh.shape["replica"], mesh.shape["shard"]),
        mesh=mesh,
        in_specs=in_specs,
        out_specs=out_specs,
        check_vma=False,
    )
```

```python
import functools

import jax
import jax.numpy as jnp
from jax import lax
from jax.experimental import pallas as pl
from jax.experimental.pallas import tpu as pltpu
from jax.sharding import PartitionSpec as P

HEADS = 12
RANK = 16
LANES = 128
HEAD_DIM = 64
GROUP = 256
F32 = jnp.float32
BF16 = jnp.bfloat16
NN = (((1,), (0,)), ((), ()))
NT = (((1,), (1,)), ((), ()))
TN = (((0,), (0,)), ((), ()))
NEG = -1e30
VMEM_LIMIT = 56 * 1024 * 1024
GELU_C = 0.7978845608028654
GELU_A = 0.044715
IMAGES_FORWARD = 2
IMAGES_BACK = 2
IMAGES_ROUTE = 2
IMAGES_LAST = 2
STRIPS = 4


def dot(left, right, dims=NN):
    return lax.dot_general(left, right, dims, preferred_element_type=F32)


def params(*axes):
    return pltpu.CompilerParams(
        dimension_semantics=axes or None, vmem_limit_bytes=VMEM_LIMIT
    )


def cost(flops, moved, exps=0):
    return pl.CostEstimate(flops=int(flops), bytes_accessed=int(moved), transcendentals=int(exps))


def normalise(rows):
    centre = rows - jnp.mean(rows, axis=-1, keepdims=True)
    spread = jnp.mean(centre * centre, axis=-1, keepdims=True)
    scale = lax.rsqrt(spread + 1e-06)
    return centre * scale, scale


def normalise_back(unit, scale, upstream):
    inner = jnp.mean(upstream * unit, axis=-1, keepdims=True)
    return scale * (upstream - jnp.mean(upstream, axis=-1, keepdims=True) - unit * inner)


def rank_row(index):
    lane = lax.broadcasted_iota(jnp.int32, (1, LANES), 1) // RANK
    return (lane == index).astype(F32)


def zero_tail(rows, n_tok):
    total = rows.shape[0]
    cut = n_tok // 16 * 16
    if n_tok == total:
        return rows
    row = lax.broadcasted_iota(jnp.int32, (total - cut, rows.shape[1]), 0) + cut
    tail = jnp.where(row < n_tok, rows[cut:].astype(F32), 0.0).astype(rows.dtype)
    return jnp.concatenate([rows[:cut], tail], axis=0)


def mask_tail(scores, n_tok):
    total = scores.shape[0]
    cut = n_tok // 16 * 16
    if n_tok == total:
        return scores
    row = lax.broadcasted_iota(jnp.int32, (total - cut, scores.shape[1]), 0) + cut
    tail = jnp.where(row < n_tok, scores[cut:], NEG)
    return jnp.concatenate([scores[:cut], tail], axis=0)


def pad_rows(scratch, ref):
    n_img, n_tok, width = ref.shape
    total = scratch.shape[0] // n_img
    cut = n_tok // 8 * 8
    for slot in range(n_img):
        base = slot * total
        scratch[base + cut : base + total, :] = jnp.zeros((total - cut, width), F32)
        scratch[base : base + n_tok, :] = ref[slot].astype(F32)
    return scratch[...]


def select_rows(rows, index_ref, first, n_img):
    total = rows.shape[0] // n_img
    return jnp.concatenate(
        [
            (rows[i * total : (i + 1) * total] * rank_row(index_ref[first + i])).astype(BF16)
            for i in range(n_img)
        ],
        axis=0,
    )


def flat(ref):
    return ref[...].reshape(ref.shape[0] * ref.shape[1], ref.shape[2])


def assemble(place_ref, chunks, layout, wall):
    pieces, entries = layout
    part = wall.shape[1] // pieces
    for chunk, (replica, neighbour, start) in zip(chunks, entries):
        column = pl.multiple_of(((place_ref[0] % pieces) ^ replica) * part, LANES)
        if neighbour is None:
            wall[:, pl.ds(column, part)] = chunk[:, start : start + part]
            continue
        strips = STRIPS
        rows = chunk.shape[0] // strips
        for strip in range(strips):
            row = pl.multiple_of((2 * strip + (place_ref[1] ^ neighbour)) * rows, 16)
            wall[pl.ds(row, rows), pl.ds(column, part)] = chunk[
                strip * rows : (strip + 1) * rows, start : start + part
            ]


def norm_kernel(image_ref, _, out_ref, pad_ref):
    unit, _ = normalise(pad_rows(pad_ref, image_ref))
    out_ref[...] = unit.astype(BF16).reshape(out_ref.shape)


def group_columns(pack, qkv_ref, group):
    width = qkv_ref.shape[1] // 3
    for piece in range(3):
        start = piece * width + group * GROUP
        pack[:, piece * GROUP : (piece + 1) * GROUP] = qkv_ref[:, start : start + GROUP]


def own_part(place_ref, pack, pieces):
    part = pack.shape[1] // pieces
    return pack[:, pl.ds(pl.multiple_of(place_ref[0] % pieces * part, LANES), part)]


def pack_kernel(
    place_ref, qkv_ref, a_ref, b_ref, ao_ref, ra_ref, bo_ref, wr_ref, out_ref, pack0, pack1
):
    copies, rows, _ = out_ref.shape
    width = qkv_ref.shape[1] // 3
    group_columns(pack0, qkv_ref, 0)
    for piece in range(3):
        column = width + (1 + piece) * LANES
        pack0[:, column : column + LANES] = b_ref[piece * rows : (piece + 1) * rows, :]
    pack0[:, width : width + LANES] = a_ref[...]
    pack0[:, width + 4 * LANES : width + 5 * LANES] = ao_ref[...]
    pack0[:, width + 5 * LANES : width + 6 * LANES] = ra_ref[...]
    group_columns(pack1, qkv_ref, 1)
    pack1[:, width : width + LANES] = bo_ref[...]
    n_exp = wr_ref.shape[0]
    route = jnp.concatenate([wr_ref[...].astype(F32), jnp.zeros((LANES - n_exp, rows), F32)], axis=0)
    pack1[:, width + LANES :] = route.T.astype(BF16)
    mine = jnp.concatenate([own_part(place_ref, pack0, 4), own_part(place_ref, pack1, 4)], axis=1)
    for copy in range(copies):
        out_ref[copy] = mine


def later_pack_kernel(place_ref, qkv_ref, wo_ref, rb_ref, out_ref, pack2, pack3):
    shards, rows, _ = out_ref.shape
    width = wo_ref.shape[1]
    group_columns(pack2, qkv_ref, 2)
    pack3[:, :width] = wo_ref[...]
    n_loc = rb_ref.shape[0]
    second = jnp.concatenate([rb_ref[...].astype(F32), jnp.zeros((rows - n_loc, LANES), F32)], axis=0)
    pack3[:, width : width + LANES] = second.astype(BF16)
    pack3[:, width + LANES :] = jnp.zeros((rows, LANES), BF16)
    mine = jnp.concatenate([own_part(place_ref, pack2, 2), own_part(place_ref, pack3, 4)], axis=1)
    for shard in range(shards):
        out_ref[shard] = mine


def head_mask(value):
    lane = lax.broadcasted_iota(jnp.int32, (1, LANES), 1)
    low = jnp.where(lane < HEAD_DIM, value, 0.0).astype(BF16)
    high = jnp.where(lane < HEAD_DIM, 0.0, value).astype(BF16)
    return low, high


def each_head(columns, value):
    head = lax.broadcasted_iota(jnp.int32, (1, GROUP), 1) // HEAD_DIM
    return jnp.concatenate(
        [
            columns * jnp.where(head == number, value, 0.0).astype(BF16)
            for number in range(GROUP // HEAD_DIM)
        ],
        axis=0,
    )


def merge_pair(low, high):
    lane = lax.broadcasted_iota(jnp.int32, (1, LANES), 1)
    return jnp.where(lane < HEAD_DIM, low, high)


def attention_forward(qkv, n_tok, prob_ref, slot):
    total = qkv.shape[0]
    every = dot(each_head(qkv[:, GROUP : 2 * GROUP], 0.125), qkv[:, :GROUP], NT)
    outs = []
    for head in range(GROUP // HEAD_DIM):
        scores = mask_tail(every[head * total : (head + 1) * total], n_tok)
        powers = jnp.exp(scores - jnp.max(scores, axis=0, keepdims=True))
        probs = (powers * (1.0 / jnp.sum(powers, axis=0, keepdims=True))).astype(BF16)
        prob_ref[slot, head] = probs
        column = 2 * GROUP + head // 2 * LANES
        outs.append(dot(probs, qkv[:, column : column + LANES], TN))
    pairs = [merge_pair(outs[head], outs[head + 1]) for head in range(0, len(outs), 2)]
    return zero_tail(jnp.concatenate(pairs, axis=1).astype(BF16), n_tok)


def first_attention_kernel(
    n_tok, shards, layout, place_ref, index_ref, h1_ref, *rest,
):
    chunks, rest = rest[: len(layout[1])], rest[len(layout[1]) :]
    qkv_ref, att_ref, prob_ref, uq_ref, a_ref, bt_ref, ao_ref, ra_ref, wall = rest
    step = pl.program_id(0)
    n_img, total, width = h1_ref.shape

    @pl.when(step == 0)
    def _():
        assemble(place_ref, chunks, layout, wall)
        a_ref[...] = wall[:, width : width + LANES]
        ao_ref[...] = wall[:, width + 4 * LANES : width + 5 * LANES]
        ra_ref[...] = wall[:, width + 5 * LANES : width + 6 * LANES]
        rows = width // shards
        for shard in range(shards):
            for part in range(3):
                bt_ref[(shard * 3 + part) * rows : (shard * 3 + part + 1) * rows, :] = wall[
                    shard * rows : (shard + 1) * rows,
                    width + (1 + part) * LANES : width + (2 + part) * LANES,
                ]

    h1 = flat(h1_ref)
    both = dot(h1, wall[:, : 3 * GROUP + LANES])
    low = both[:, 3 * GROUP :].astype(BF16).astype(F32)
    uq = select_rows(low, index_ref, step * n_img, n_img)
    uq_ref[...] = uq.reshape(uq_ref.shape)
    attend_group(0, n_tok, both[:, : 3 * GROUP], uq, bt_ref, qkv_ref, att_ref, prob_ref)


def group_rows(group, width, bt_ref):
    return jnp.concatenate(
        [bt_ref[part * width + group * GROUP : part * width + (group + 1) * GROUP, :] for part in range(3)],
        axis=0,
    )


def attend_group(group, n_tok, base, uq, bt_ref, qkv_ref, att_ref, prob_ref):
    n_img, total, _ = att_ref.shape
    second = group_rows(group, bt_ref.shape[0] // 3, bt_ref)
    qkv = (base + dot(uq, second, NT)).astype(BF16)
    qkv_ref[...] = qkv.reshape(qkv_ref.shape)
    for slot in range(n_img):
        att_ref[slot] = attention_forward(
            qkv[slot * total : (slot + 1) * total], n_tok, prob_ref, slot
        )


def next_attention_kernel(
    n_tok, group, extra, layout, place_ref, h1_ref, uq_ref, bt_ref, *rest
):
    chunks, rest = rest[: len(layout[1])], rest[len(layout[1]) :]
    qkv_ref, att_ref, prob_ref = rest[:3]
    wall = rest[-1]

    @pl.when(pl.program_id(0) == 0)
    def _():
        assemble(place_ref, chunks, layout, wall)
        for position in range(extra):
            column = 3 * GROUP + position * LANES
            rest[3 + position][...] = wall[:, column : column + LANES]

    attend_group(
        group, n_tok, dot(flat(h1_ref), wall[:, : 3 * GROUP]), flat(uq_ref), bt_ref, qkv_ref, att_ref, prob_ref,
    )


def route_kernel(
    n_exp, shards, layout, place_ref, index_ref, count_ref, image_ref, cot_ref, att0, att1, att2,
    ao_ref, bo_ref, ra_ref, wr_ref, *rest,
):
    chunks, rest = rest[: len(layout[1])], rest[len(layout[1]) :]
    x2_ref, uo_ref, ur_ref, disp_ref, comb_ref, sg_ref, wrt_ref, rb_ref, *rest = rest
    wall, rb_f, pair_ref, pad_a, pad_b, sent_ref = rest
    every = sg_ref.shape[2]
    n_img, n_tok, width = image_ref.shape
    first = pl.program_id(0) * n_img
    total = x2_ref.shape[1]

    @pl.when(first == 0)
    def _():
        assemble(place_ref, chunks, layout, wall)
        wrt_ref[...] = wr_ref[...].astype(F32).T[:n_exp].astype(BF16)
        n_loc, rows = n_exp // shards, width // shards
        for shard in range(shards):
            rb_f[shard * n_loc : (shard + 1) * n_loc, :] = wall[
                shard * rows : shard * rows + 8, width : width + LANES
            ].astype(F32)[:n_loc]
        rb_ref[...] = rb_f[...].astype(BF16)
        wall[:, width : width + LANES] = ao_ref[...]
        pair_ref[:, :LANES] = ra_ref[...]
        pair_ref[:, LANES:] = wr_ref[...]

    att = jnp.concatenate([flat(att0), flat(att1), flat(att2)], axis=1)
    both = dot(att, wall[:, : width + LANES])
    uo = select_rows(both[:, width:].astype(BF16).astype(F32), index_ref, first, n_img)
    uo_ref[...] = uo.reshape(uo_ref.shape)
    x2 = pad_rows(pad_a, image_ref) + both[:, :width] + dot(uo, bo_ref[...], NT)
    x2_ref[...] = x2.reshape(x2_ref.shape)
    h2 = normalise(x2)[0].astype(BF16)
    both = dot(h2, pair_ref[...])
    ur = select_rows(both[:, :LANES].astype(BF16).astype(F32), index_ref, first, n_img)
    base = both[:, LANES:]
    ur_ref[...] = ur.reshape(ur_ref.shape)
    cot = pad_rows(pad_b, cot_ref)
    for slot in range(n_img):
        rows = slice(slot * total, (slot + 1) * total)
        living = (first + slot < count_ref[0]).astype(F32)
        logits = base[rows].T[:n_exp] + dot(rb_ref[...], ur[rows], NT)
        alive = lax.broadcasted_iota(jnp.int32, logits.shape, 1) < n_tok
        over_tokens = jnp.where(alive, logits, NEG)
        powers = jnp.exp(over_tokens - jnp.max(over_tokens, axis=1, keepdims=True))
        disp = powers / jnp.sum(powers, axis=1, keepdims=True)
        powers = jnp.exp(logits - jnp.max(logits, axis=0, keepdims=True))
        comb = jnp.where(alive, powers / jnp.sum(powers, axis=0, keepdims=True), 0.0)
        disp_ref[slot] = disp
        comb_ref[slot] = comb
        upstream = (cot[rows] * living).astype(BF16)
        sent = jnp.concatenate(
            [
                dot(disp.astype(BF16), h2[rows]),
                dot(comb.astype(BF16), upstream),
                jnp.broadcast_to(rank_row(index_ref[first + slot]), (n_exp, LANES)),
            ],
            axis=1,
        )
        for block in range(sent.shape[1] // LANES):
            start = block * n_exp * every + first + slot
            sent_ref[pl.ds(start, n_exp, stride=every), :] = sent[:, block * LANES : (block + 1) * LANES]

    @pl.when(pl.program_id(0) == pl.num_programs(0) - 1)
    def _():
        for block in range(sg_ref.shape[3] // LANES):
            span = slice(block * LANES, (block + 1) * LANES)
            piece = sent_ref[block * n_exp * every : (block + 1) * n_exp * every, :]
            sg_ref[:, :, :, span] = piece.reshape(sg_ref.shape[:3] + (LANES,)).astype(BF16)


def gelu_both(pre):
    square = pre * pre
    half = jnp.tanh(GELU_C * pre * (1.0 + GELU_A * square))
    both = 0.5 * (1.0 + half)
    slope = both + 0.5 * pre * (1.0 - half * half) * (GELU_C * (1.0 + 3.0 * GELU_A * square))
    return pre * both, slope


def expert_tile(slots, gy, u1, gu2, wu_ref, wd_ref, ub_ref, da_ref):
    pre = dot(slots, wu_ref[0]) + dot(u1, ub_ref[0])
    ghid = (dot(wd_ref[0], gy, NT) + dot(da_ref[0], gu2, NT)).T
    hidden, slope = gelu_both(pre)
    return hidden.astype(BF16), (slope * ghid).astype(BF16)


def gather_rows(part_refs, out_ref):
    rows = part_refs[0].shape[0] * part_refs[0].shape[2]
    for number, part_ref in enumerate(part_refs):
        part = part_ref[:, 0].astype(F32).reshape(rows, part_ref.shape[3])
        out_ref[number * rows : (number + 1) * rows, :] = part.astype(BF16)


def expert_kernel(
    wu_ref, wd_ref, ua_ref, ub_ref, da_ref, db_ref, part_ref, out_ref, hidden_ref, gpre_ref, low_ref,
    sg_ref, u1_ref, gu2_ref, acc_y, acc_s, acc_u2, acc_gu1,
):
    step = pl.program_id(1)
    width = wu_ref.shape[1]

    @pl.when(step == 0)
    def _():
        gather_rows((part_ref,), sg_ref)
        selector = sg_ref[:, 2 * width :].astype(F32)
        u1_ref[...] = (
            dot(sg_ref[:, :width], ua_ref[0]).astype(BF16).astype(F32) * selector
        ).astype(BF16)
        gu2_ref[...] = (dot(sg_ref[:, width : 2 * width], db_ref[0], NT) * selector).astype(BF16)
        acc_y[...] = jnp.zeros_like(acc_y)
        acc_s[...] = jnp.zeros_like(acc_s)
        acc_u2[...] = jnp.zeros_like(acc_u2)
        acc_gu1[...] = jnp.zeros_like(acc_gu1)

    hidden, gpre = expert_tile(
        sg_ref[:, :width], sg_ref[:, width : 2 * width], u1_ref[...], gu2_ref[...],
        wu_ref, wd_ref, ub_ref, da_ref,
    )
    hidden_ref[0] = hidden
    gpre_ref[0] = gpre
    acc_y[...] += dot(hidden, wd_ref[0])
    acc_u2[...] += dot(hidden, da_ref[0])
    acc_s[...] += dot(wu_ref[0], gpre, NT)
    acc_gu1[...] += dot(ub_ref[0], gpre, NT)

    @pl.when(step == pl.num_programs(1) - 1)
    def _():
        selector = sg_ref[:, 2 * width :].astype(F32)
        u2 = (acc_u2[...].astype(BF16).astype(F32) * selector).astype(BF16)
        gu1 = (acc_gu1[...].T * selector).astype(BF16)
        shards, _, n_img, _ = out_ref.shape
        result = acc_y[...] + dot(u2, db_ref[0])
        out_ref[:, 0, :, :width] = result.reshape(shards, n_img, width).astype(BF16)
        result = acc_s[...].T + dot(gu1, ua_ref[0], NT)
        out_ref[:, 0, :, width:] = result.reshape(shards, n_img, width).astype(BF16)
        for place, low in enumerate((u1_ref[...], u2, gu1, gu2_ref[...])):
            low_ref[0, :, place * LANES : (place + 1) * LANES] = low


def expert_grad_kernel(copies, *refs):
    refs = list(refs)
    part_refs, hidden_refs, gpre_refs, low_refs = (
        [refs.pop(0) for _ in range(copies)] for _ in range(4)
    )
    gua_ref, gub_ref, gda_ref, gdb_ref, sg_ref, low_t, rows_ref = refs
    rows = hidden_refs[0].shape[1]
    width = gua_ref.shape[1]

    @pl.when(pl.program_id(1) == 0)
    def _():
        gather_rows(part_refs, sg_ref)
        low = jnp.concatenate([ref[0] for ref in low_refs], axis=0)
        low_t[...] = low.astype(F32).T.astype(BF16)
        u2_t, gu1_t = low_t[LANES : 2 * LANES, :], low_t[2 * LANES : 3 * LANES, :]
        gdb_ref[0] = dot(u2_t, sg_ref[:, width : 2 * width])
        gua_ref[0] = dot(gu1_t, sg_ref[:, :width]).T

    for number in range(copies):
        rows_ref[number * rows : (number + 1) * rows, :] = gpre_refs[number][0]
    gub_ref[0] = dot(low_t[:LANES, :], rows_ref[...])
    for number in range(copies):
        rows_ref[number * rows : (number + 1) * rows, :] = hidden_refs[number][0]
    gda_ref[0] = dot(low_t[3 * LANES :, :], rows_ref[...]).T


def turn_kernel(layouts, place_ref, ao_ref, bo_ref, ra_ref, *refs):
    refs = list(refs)
    chunks = [[refs.pop(0) for _ in layout[1]] for layout in layouts]
    qkv_ref, out_ref, first_ref, route_ref = refs[:4]
    walls = refs[4:]
    for chunk, layout, wall in zip(chunks, layouts, walls):
        assemble(place_ref, chunk, layout, wall)
    width = walls[0].shape[0]
    for group, wall in enumerate(walls[:-1]):
        qkv_ref[group * 3 * GROUP : (group + 1) * 3 * GROUP, :] = wall[:, : 3 * GROUP].T
    qkv_ref[3 * width :, :] = walls[0][:, 3 * GROUP : 3 * GROUP + LANES].T
    out_ref[:, :width] = walls[-1][:, :width].T
    out_ref[:, width:] = bo_ref[...]
    first_ref[...] = ao_ref[...].T
    route_ref[...] = ra_ref[...].T


def route_back_kernel(
    n_exp, index_ref, count_ref, cot_ref, x2_ref, uo_ref, ur_ref, disp_ref, comb_ref,
    att0, att1, att2, ret_ref, wrt_ref, rb_ref, out_ref, first_ref, route_ref,
    block_ref, gx2_ref, gatt_ref, pack_ref, pad_b, back_ref, acc_oa, acc_ob, acc_ra, acc_rb,
):
    n_img, n_tok, width = cot_ref.shape
    first = pl.program_id(0) * n_img
    total = x2_ref.shape[1]

    every = ret_ref.shape[2]

    @pl.when(first == 0)
    def _():
        for block in range(2 * width // LANES):
            piece = ret_ref[:, :, :, block * LANES : (block + 1) * LANES].astype(F32)
            back_ref[block * n_exp * every : (block + 1) * n_exp * every, :] = piece.reshape(
                n_exp * every, LANES
            )
        acc_oa[...] = jnp.zeros_like(acc_oa)
        acc_ob[...] = jnp.zeros_like(acc_ob)
        acc_ra[...] = jnp.zeros_like(acc_ra)
        acc_rb[...] = jnp.zeros_like(acc_rb)

    cot = pad_rows(pad_b, cot_ref)
    x2 = flat(x2_ref)
    unit, scale = normalise(x2)
    h2 = unit.astype(BF16)
    pairs, belows, upstreams = [], [], []
    for slot in range(n_img):
        rows = slice(slot * total, (slot + 1) * total)
        living = (first + slot < count_ref[0]).astype(F32)
        upstream = cot[rows] * living
        upstreams.append(upstream)
        disp, comb = disp_ref[slot], comb_ref[slot]
        blocks = [
            back_ref[pl.ds(block * n_exp * every + first + slot, n_exp, stride=every), :]
            for block in range(2 * width // LANES)
        ]
        back = jnp.concatenate(blocks, axis=1).astype(BF16)
        yexp, gslot = back[:, :width], back[:, width:]
        gcomb = dot(yexp, upstream.astype(BF16), NT)
        gdisp = dot(gslot, h2[rows], NT)
        glog = (
            disp * (gdisp - jnp.sum(gdisp * disp, axis=1, keepdims=True))
            + comb * (gcomb - jnp.sum(gcomb * comb, axis=0, keepdims=True))
        )
        acc_rb[...] += dot(glog.astype(BF16), ur_ref[slot])
        three = jnp.concatenate([disp, glog, comb], axis=0).T.astype(BF16)
        mixed = dot(three[:, 2 * n_exp :], yexp)
        block_ref[slot] = (living * (x2[rows] + mixed)).astype(BF16)[:n_tok]
        pairs.append(three[:, : 2 * n_exp])
        belows.append(jnp.concatenate([route_ref[...], gslot, wrt_ref[...]], axis=0))
    glog_rows = jnp.concatenate([pair[:, n_exp:] for pair in pairs], axis=0)
    gur = select_rows(dot(glog_rows, rb_ref[...]), index_ref, first, n_img)
    acc_ra[...] += dot(gur, h2, TN)
    gh2 = jnp.concatenate(
        [
            dot(jnp.concatenate([gur[i * total : (i + 1) * total], pairs[i]], axis=1), belows[i])
            for i in range(n_img)
        ],
        axis=0,
    )
    gx2 = jnp.concatenate(upstreams, axis=0) + normalise_back(unit, scale, gh2)
    gbr = gx2.astype(BF16)
    gx2_ref[...] = gbr.reshape(gx2_ref.shape)
    acc_ob[...] += dot(flat(uo_ref), gbr, TN)
    both = dot(gbr, out_ref[...])
    guo = select_rows(both[:, width:], index_ref, first, n_img)
    att = jnp.concatenate([flat(att0), flat(att1), flat(att2)], axis=1)
    acc_oa[...] += dot(guo, att, TN)
    gatt = (both[:, :width] + dot(guo, first_ref[...])).astype(BF16)
    gatt_ref[...] = gatt.reshape(gatt_ref.shape)

    @pl.when(pl.program_id(0) == pl.num_programs(0) - 1)
    def _():
        shards = pack_ref.shape[0]
        rows = width // shards
        n_loc = n_exp // shards
        for position, acc in enumerate((acc_oa, acc_ob, acc_ra)):
            summed = acc[...].T.astype(BF16)
            for shard in range(shards):
                pack_ref[shard, position * rows : (position + 1) * rows, :] = summed[
                    shard * rows : (shard + 1) * rows
                ]
        tail = pack_ref.shape[1] - 3 * rows
        for shard in range(shards):
            last = jnp.concatenate(
                [acc_rb[shard * n_loc : (shard + 1) * n_loc, :], jnp.zeros((tail - n_loc, LANES), F32)],
                axis=0,
            )
            pack_ref[shard, 3 * rows :, :] = last.astype(BF16)


def attention_backward(qkv, gatt, prob_ref, slot):
    keep = head_mask(1.0)
    key_t = qkv[:, GROUP : 2 * GROUP].T
    total = qkv.shape[0]
    gq_parts, gk_parts, gv_parts = [], [], []
    for pair in range(GROUP // LANES):
        span = slice(pair * LANES, (pair + 1) * LANES)
        q_pair, ga_pair = qkv[:, span], gatt[:, span]
        v_pair = qkv[:, 2 * GROUP + pair * LANES : 2 * GROUP + (pair + 1) * LANES]
        lows = [prob_ref[slot, 2 * pair], prob_ref[slot, 2 * pair + 1]]
        gv = dot(jnp.concatenate(lows, axis=0), ga_pair)
        gprobs = dot(jnp.concatenate([v_pair * keep[0], v_pair * keep[1]], axis=0), ga_pair, NT)
        gscores = []
        for side in range(2):
            probs = lows[side].astype(F32)
            gprob = gprobs[side * total : (side + 1) * total]
            inner = jnp.sum(gprob * probs, axis=0, keepdims=True)
            gscores.append((probs * (gprob - inner)).astype(BF16))
            head = 2 * pair + side
            gq_parts.append(
                (dot(key_t[head * HEAD_DIM : (head + 1) * HEAD_DIM], gscores[side]) * 0.125).astype(BF16)
            )
        gk = dot(jnp.concatenate(gscores, axis=0), q_pair)
        gk_parts.append((merge_pair(gk[:total], gk[total:]) * 0.125).astype(BF16))
        gv_parts.append(merge_pair(gv[:total], gv[total:]).astype(BF16))
    gq = jnp.concatenate(gq_parts, axis=0).T
    return jnp.concatenate([gq] + gk_parts + gv_parts, axis=1)


def attention_back_kernel(groups, place_ref, index_ref, *refs):
    refs = list(refs)
    qkv_refs = [refs.pop(0) for _ in range(groups)]
    prob_refs = [refs.pop(0) for _ in range(groups)]
    gatt_ref, uq_ref, h1_ref, bt_ref, others_ref = refs[:5]
    refs = refs[5:]
    gqkv_refs = [refs.pop(0) for _ in range(groups)]
    guq_ref, keep_ref, give_ref, pack_ref, acc_b, acc_a = refs
    step = pl.program_id(0)
    n_img, total, width = h1_ref.shape

    @pl.when(step == 0)
    def _():
        acc_b[...] = jnp.zeros_like(acc_b)
        acc_a[...] = jnp.zeros_like(acc_a)

    uq_t = flat(uq_ref).T
    guq = None
    for group in range(groups):
        parts = []
        for i in range(n_img):
            part = attention_backward(
                qkv_refs[group][i], gatt_ref[i, :, group * GROUP : (group + 1) * GROUP],
                prob_refs[group], i,
            )
            gqkv_refs[group][i] = part
            parts.append(part)
        gqkv = jnp.concatenate(parts, axis=0)
        acc_b[:, group * 3 * GROUP : (group + 1) * 3 * GROUP] += dot(uq_t, gqkv)
        part = dot(gqkv, group_rows(group, width, bt_ref))
        guq = part if guq is None else guq + part
    guq = select_rows(guq, index_ref, step * n_img, n_img)
    acc_a[...] += dot(guq, flat(h1_ref), TN)
    guq_ref[...] = guq.reshape(guq_ref.shape)

    @pl.when(step == pl.num_programs(0) - 1)
    def _():
        shards = pack_ref.shape[0]
        rows = width // shards
        pack_ref[:, 4 * rows :, :] = others_ref[...]
        own = acc_a[...].T.astype(BF16)
        for shard in range(shards):
            pack_ref[shard, 3 * rows : 4 * rows, :] = own[shard * rows : (shard + 1) * rows]
        for group in range(groups):
            summed = acc_b[:, group * 3 * GROUP : (group + 1) * 3 * GROUP].T.astype(BF16)
            for part in range(3):
                start = part * width + group * GROUP
                place = start
                while place < start + GROUP:
                    shard, offset = divmod(place, 3 * rows)
                    length = min(start + GROUP - place, 3 * rows - offset)
                    take = part * GROUP + place - start
                    pack_ref[shard, offset : offset + length, :] = summed[take : take + length]
                    place += length
        half = keep_ref.shape[1]
        side = place_ref[2] % 2
        keep_ref[...] = pack_ref[:, pl.ds(pl.multiple_of(side * half, 16), half), :]
        give_ref[...] = pack_ref[:, pl.ds(pl.multiple_of((1 - side) * half, 16), half), :]


def input_grad_kernel(image_ref, gx2_ref, guq_ref, turned_ref, *refs):
    *gqkv, out_ref, pad_a = refs
    n_img, n_tok, width = image_ref.shape
    step = pl.program_id(0)
    parts = width // LANES
    every = out_ref.shape[0] // (n_tok * parts)
    total = gx2_ref.shape[1]
    gh1 = dot(jnp.concatenate([flat(ref) for ref in gqkv] + [flat(guq_ref)], axis=1), turned_ref[...])
    unit, scale = normalise(pad_rows(pad_a, image_ref))
    result = flat(gx2_ref).astype(F32) + normalise_back(unit, scale, gh1)
    for slot in range(n_img):
        for part in range(parts):
            out_ref[pl.ds(part * every + step * n_img + slot, n_tok, stride=parts * every), :] = result[
                slot * total : slot * total + n_tok, part * LANES : (part + 1) * LANES
            ]


ANY = pl.BlockSpec(memory_space=pl.ANY)


def whole(shape):
    return pl.BlockSpec(shape, lambda *_: (0,) * len(shape))


def once(shape):
    return pl.BlockSpec(shape, lambda *_: (0,) * len(shape), pipeline_mode=pl.Buffered(1))


def per_image(*shape, images=1):
    return pl.BlockSpec((images,) + shape, lambda i, *_: (i,) + (0,) * len(shape))


def several(images, limit):
    return max(n for n in range(1, limit + 1) if images % n == 0)


def call(kernel, scalars, grid, inputs, outputs, scratch, flops, exps=0, aliases=None):
    arrays = [array for array, _ in inputs]
    shapes = [jax.ShapeDtypeStruct(shape, dtype) for shape, dtype, _ in outputs]
    moved = sum(array.size * array.dtype.itemsize for array in arrays) + sum(
        shape.size * shape.dtype.itemsize for shape in shapes
    )
    return pl.pallas_call(
        kernel,
        out_shape=shapes,
        grid_spec=pltpu.PrefetchScalarGridSpec(
            num_scalar_prefetch=len(scalars),
            grid=grid,
            in_specs=[spec for _, spec in inputs],
            out_specs=[spec for _, _, spec in outputs],
            scratch_shapes=scratch,
        ),
        input_output_aliases=aliases or {},
        compiler_params=params(*(("arbitrary",) * len(grid))),
        cost_estimate=cost(flops, moved, exps),
    )(*scalars, *arrays)


def norm_call(images, cotangent, total):
    n_img, n_tok, width = images.shape
    each = several(n_img, 4)
    return call(
        norm_kernel, (), (n_img // each,),
        [(images, per_image(n_tok, width, images=each)), (cotangent, ANY)],
        [((n_img, total, width), BF16, per_image(total, width, images=each))],
        [pltpu.VMEM((each * total, width), F32)],
        8 * images.size,
    )[0]


def pack_call(place, weights, copies):
    rows, columns = weights[0].shape
    width = columns // 3
    wide = [width + 6 * LANES, width + 2 * LANES]
    out = (copies, rows, sum(wide) // 4)
    return call(
        pack_kernel, (place,), (1,), [(weight, whole(weight.shape)) for weight in weights],
        [(out, BF16, whole(out))], [pltpu.VMEM((rows, each), BF16) for each in wide], rows * columns,
    )[0]


def later_pack_call(place, weights, shards):
    rows, width = weights[1].shape
    out = (shards, rows, width // 2 + (width + 2 * LANES) // 4)
    return call(
        later_pack_kernel, (place,), (1,), [(weight, whole(weight.shape)) for weight in weights],
        [(out, BF16, whole(out))],
        [pltpu.VMEM((rows, each), BF16) for each in (width, width + 2 * LANES)], rows * width,
    )[0]


def attention_flops(n_img, total, width, parts):
    return n_img * total * (2 * width * 3 * GROUP + parts * 8 * total * HEAD_DIM)


def attention_outputs(n_img, total, each):
    return [
        ((n_img, total, 3 * GROUP), BF16, per_image(total, 3 * GROUP, images=each)),
        ((n_img, total, GROUP), BF16, per_image(total, GROUP, images=each)),
        (
            (n_img, GROUP // HEAD_DIM, total, total), BF16,
            per_image(GROUP // HEAD_DIM, total, total, images=each),
        ),
    ]


def first_attention_call(place, index, h1, pack, n_tok, shards):
    n_img, total, width = h1.shape
    chunks, layout, columns = pack
    each = several(n_img, IMAGES_FORWARD)
    return call(
        functools.partial(first_attention_kernel, n_tok, shards, layout), (place, index), (n_img // each,),
        [(h1, per_image(total, width, images=each))] + [(chunk, once(chunk.shape)) for chunk in chunks],
        attention_outputs(n_img, total, each)
        + [
            ((n_img, total, LANES), BF16, per_image(total, LANES, images=each)),
            ((width, LANES), BF16, whole((width, LANES))),
            ((3 * width, LANES), BF16, whole((3 * width, LANES))),
            ((width, LANES), BF16, whole((width, LANES))),
            ((width, LANES), BF16, whole((width, LANES))),
        ],
        [pltpu.VMEM((width, columns), BF16)],
        attention_flops(n_img, total, width, 2), n_img * total * total * 4,
    )


def next_attention_call(place, h1, uq, bt, pack, n_tok, group, extra):
    n_img, total, width = h1.shape
    chunks, layout, columns = pack
    each = several(n_img, IMAGES_FORWARD)
    return call(
        functools.partial(next_attention_kernel, n_tok, group, extra, layout), (place,), (n_img // each,),
        [
            (h1, per_image(total, width, images=each)),
            (uq, per_image(total, LANES, images=each)),
            (bt, whole(bt.shape)),
        ]
        + [(chunk, once(chunk.shape)) for chunk in chunks],
        attention_outputs(n_img, total, each)
        + [((width, LANES), BF16, whole((width, LANES)))] * extra,
        [pltpu.VMEM((width, columns), BF16)],
        attention_flops(n_img, total, width, 2), n_img * total * total * 4,
    )


def route_call(place, index, count, images, cotangent, atts, banks, pack, n_exp, total, shards):
    n_img, n_tok, width = images.shape
    chunks, layout, columns = pack
    each = several(n_img, IMAGES_ROUTE)
    here = functools.partial(per_image, images=each)
    sent = (shards, n_exp // shards, n_img, 2 * width + LANES)
    return call(
        functools.partial(route_kernel, n_exp, shards, layout), (place, index, count), (n_img // each,),
        [(images, here(n_tok, width)), (cotangent, here(n_tok, width))]
        + [(att, here(total, GROUP)) for att in atts]
        + [(bank, whole(bank.shape)) for bank in banks]
        + [(chunk, once(chunk.shape)) for chunk in chunks],
        [
            ((n_img, total, width), F32, here(total, width)),
            ((n_img, total, LANES), BF16, here(total, LANES)),
            ((n_img, total, LANES), BF16, here(total, LANES)),
            ((n_img, n_exp, total), F32, here(n_exp, total)),
            ((n_img, n_exp, total), F32, here(n_exp, total)),
            (sent, BF16, whole(sent)),
            ((n_exp, width), BF16, whole((n_exp, width))),
            ((n_exp, LANES), BF16, whole((n_exp, LANES))),
        ],
        [
            pltpu.VMEM((width, columns), BF16),
            pltpu.VMEM((n_exp, LANES), F32),
            pltpu.VMEM((width, 2 * LANES), BF16),
            pltpu.VMEM((each * total, width), F32),
            pltpu.VMEM((each * total, width), F32),
            pltpu.VMEM(((2 * width // LANES + 1) * n_exp * n_img, LANES), F32),
        ],
        n_img * total * 2 * width * (width + 3 * LANES), n_img * total * 2 * n_exp,
    )


def hidden_tile(hidden, limit):
    tile = hidden
    while tile > limit:
        tile //= 2
    return tile


def expert_specs(width, tile, first=0):
    return (
        pl.BlockSpec((1, width, tile), lambda e, f: (e + first, 0, f)),
        pl.BlockSpec((1, tile, width), lambda e, f: (e + first, f, 0)),
        pl.BlockSpec((1, width, LANES), lambda e, f: (e + first, 0, 0)),
        pl.BlockSpec((1, LANES, tile), lambda e, f: (e + first, 0, f)),
        pl.BlockSpec((1, tile, LANES), lambda e, f: (e + first, f, 0)),
        pl.BlockSpec((1, LANES, width), lambda e, f: (e + first, 0, 0)),
    )


def expert_rows(shape, first=0):
    shards, _, n_img, columns = shape
    return pl.BlockSpec((shards, 1, n_img, columns), lambda e, f: (0, e + first, 0, 0))


def expert_call(landed, weights):
    shards, n_loc, n_img, columns = landed.shape
    rows = shards * n_img
    width, hidden = weights[0].shape[1:]
    tile = hidden_tile(hidden, 1536)
    out = (shards, n_loc, n_img, 2 * width)
    tiled = pl.BlockSpec((1, rows, tile), lambda e, f: (e, 0, f))
    return call(
        expert_kernel, (), (n_loc, hidden // tile),
        list(zip(weights, expert_specs(width, tile))) + [(landed, expert_rows(landed.shape))],
        [
            (out, BF16, expert_rows(out)),
            ((n_loc, rows, hidden), BF16, tiled),
            ((n_loc, rows, hidden), BF16, tiled),
            (
                (n_loc, rows, 4 * LANES), BF16,
                pl.BlockSpec((1, rows, 4 * LANES), lambda e, f: (e, 0, 0)),
            ),
        ],
        [
            pltpu.VMEM((rows, columns), BF16),
            pltpu.VMEM((rows, LANES), BF16),
            pltpu.VMEM((rows, LANES), BF16),
            pltpu.VMEM((rows, width), F32),
            pltpu.VMEM((width, rows), F32),
            pltpu.VMEM((rows, LANES), F32),
            pltpu.VMEM((LANES, rows), F32),
        ],
        n_loc * rows * 8 * width * hidden, n_loc * rows * hidden,
    )


def expert_grad_call(every, width):
    parts, hiddens, gpres, lows = zip(*every)
    shards, n_loc, n_img, columns = parts[0].shape
    rows, hidden = hiddens[0].shape[1:]
    total = rows * len(every)
    tile = hidden_tile(hidden, 1536 if total <= 512 else 384)
    tiled = pl.BlockSpec((1, rows, tile), lambda e, f: (e, 0, f))
    low = pl.BlockSpec((1, rows, 4 * LANES), lambda e, f: (e, 0, 0))
    return call(
        functools.partial(expert_grad_kernel, len(every)), (), (n_loc, hidden // tile),
        [(part, expert_rows(part.shape)) for part in parts]
        + [(array, tiled) for array in hiddens + gpres]
        + [(array, low) for array in lows],
        [
            ((n_loc, width, LANES), F32, pl.BlockSpec((1, width, LANES), lambda e, f: (e, 0, 0))),
            ((n_loc, LANES, hidden), F32, pl.BlockSpec((1, LANES, tile), lambda e, f: (e, 0, f))),
            ((n_loc, hidden, LANES), F32, pl.BlockSpec((1, tile, LANES), lambda e, f: (e, f, 0))),
            ((n_loc, LANES, width), F32, pl.BlockSpec((1, LANES, width), lambda e, f: (e, 0, 0))),
        ],
        [
            pltpu.VMEM((total, columns), BF16),
            pltpu.VMEM((4 * LANES, total), BF16),
            pltpu.VMEM((total, tile), BF16),
        ],
        4 * n_loc * total * LANES * hidden,
    )


def route_back_call(
    index, count, cotangent, x2, uo, ur, disp, comb, atts, ret, banks, shards, replicas
):
    n_img, n_tok, width = cotangent.shape
    total, n_exp = x2.shape[1], disp.shape[1]
    rows = width // shards
    unit = 16 * replicas
    pack_rows = -(-(7 * rows + n_exp // shards) // unit) * unit - 4 * rows
    each = several(n_img, IMAGES_ROUTE)
    here = functools.partial(per_image, images=each)
    return call(
        functools.partial(route_back_kernel, n_exp), (index, count), (n_img // each,),
        [
            (cotangent, here(n_tok, width)),
            (x2, here(total, width)),
            (uo, here(total, LANES)),
            (ur, here(total, LANES)),
            (disp, here(n_exp, total)),
            (comb, here(n_exp, total)),
        ]
        + [(att, here(total, GROUP)) for att in atts]
        + [(ret, once(ret.shape))]
        + [(bank, once(bank.shape)) for bank in banks],
        [
            ((n_img, n_tok, width), BF16, here(n_tok, width)),
            ((n_img, total, width), BF16, here(total, width)),
            ((n_img, total, width), BF16, here(total, width)),
            ((shards, pack_rows, LANES), BF16, whole((shards, pack_rows, LANES))),
        ],
        [
            pltpu.VMEM((each * total, width), F32),
            pltpu.VMEM((2 * width // LANES * n_exp * n_img, LANES), F32),
            pltpu.VMEM((LANES, width), F32),
            pltpu.VMEM((LANES, width), F32),
            pltpu.VMEM((LANES, width), F32),
            pltpu.VMEM((n_exp, LANES), F32),
        ],
        n_img * total * 2 * width * (width + 6 * LANES),
    )


def attention_back_call(place, index, qkvs, probs, gatt, uq, h1, bt, others):
    n_img, total, width = h1.shape
    groups = len(qkvs)
    shards = others.shape[0]
    each = several(n_img, IMAGES_BACK)
    here = functools.partial(per_image, images=each)
    pack = (shards, 4 * width // shards + others.shape[1], LANES)
    half = (shards, pack[1] // 2, LANES)
    return call(
        functools.partial(attention_back_kernel, groups), (place, index), (n_img // each,),
        [(qkv, here(total, 3 * GROUP)) for qkv in qkvs]
        + [(prob, here(GROUP // HEAD_DIM, total, total)) for prob in probs]
        + [
            (gatt, here(total, width)),
            (uq, here(total, LANES)),
            (h1, here(total, width)),
            (bt, whole(bt.shape)),
            (others, whole(others.shape)),
        ],
        [((n_img, total, 3 * GROUP), BF16, here(total, 3 * GROUP))] * groups
        + [((n_img, total, LANES), BF16, here(total, LANES))]
        + [(half, BF16, whole(half))] * 2,
        [
            pltpu.VMEM(pack, BF16),
            pltpu.VMEM((LANES, 3 * width), F32),
            pltpu.VMEM((LANES, width), F32),
        ],
        groups * attention_flops(n_img, total, LANES, 5), groups * n_img * total * total * 4,
    )


def input_grad_call(images, gx2, guq, gqkvs, turned):
    n_img, n_tok, width = images.shape
    total = gx2.shape[1]
    each = several(n_img, IMAGES_LAST)
    here = functools.partial(per_image, images=each)
    out = call(
        input_grad_kernel, (), (n_img // each,),
        [
            (images, here(n_tok, width)),
            (gx2, here(total, width)),
            (guq, here(total, LANES)),
            (turned, once(turned.shape)),
        ]
        + [(gqkv, here(total, 3 * GROUP)) for gqkv in gqkvs],
        [((images.size // LANES, LANES), F32, whole((images.size // LANES, LANES)))],
        [pltpu.VMEM((each * total, width), F32)],
        n_img * total * 2 * width * (3 * width + LANES),
    )[0]
    out = out.reshape(n_tok, width // LANES, n_img, LANES).transpose(2, 0, 1, 3)
    return out.reshape(n_img, n_tok, width)


def turn_call(place, banks, packs):
    width = banks[0].shape[0]
    shapes = [(3 * width + LANES, width), (width, width + LANES), (LANES, width), (LANES, width)]
    return call(
        functools.partial(turn_kernel, tuple(pack[1] for pack in packs)), (place,), (1,),
        [(bank, once(bank.shape)) for bank in banks]
        + [(chunk, once(chunk.shape)) for pack in packs for chunk in pack[0]],
        [(shape, BF16, once(shape)) for shape in shapes],
        [pltpu.VMEM((width, pack[2]), BF16) for pack in packs],
        8 * width * width,
    )


def swap(array, axis, size, bit):
    return lax.ppermute(array, axis, [(i, i ^ bit) for i in range(size)])


def tie(*arrays):
    return lax.optimization_barrier(arrays)


def over_shard(spread, lines=None):
    own = lax.all_to_all(
        spread, "shard", split_axis=0, concat_axis=0, tiled=True, axis_index_groups=lines
    )
    return own.reshape(-1, spread.shape[2])


def reduce_pack(keep, give, replicas, beside_first, beside_swap, beside_spread):
    where = lax.axis_index("replica")
    bits = []
    bit = 1
    first_work = swap_work = ()
    while bit < replicas:
        got = swap(give, "replica", replicas, bit)
        if bit == 1:
            got, *first_work = tie(got, *beside_first())
        if 2 * bit == replicas:
            got, *swap_work = tie(got, *beside_swap())
        pack = (keep.astype(F32) + got.astype(F32)).astype(BF16)
        bits.append(bit)
        bit *= 2
        if bit < replicas:
            half = pack.shape[1] // 2
            side = (where // bit) % 2
            keep = lax.dynamic_slice_in_dim(pack, side * half, half, axis=1)
            give = lax.dynamic_slice_in_dim(pack, (1 - side) * half, half, axis=1)
    landed = lax.all_to_all(pack, "shard", split_axis=0, concat_axis=0, tiled=True)
    landed, *spread_work = tie(landed, *beside_spread(*first_work))
    total = jnp.sum(landed.astype(F32), axis=0).astype(BF16)
    for bit in reversed(bits):
        got = swap(total, "replica", replicas, bit)
        side = (where // bit) % 2
        total = jnp.where(
            side == 0,
            jnp.concatenate([total, got], axis=0),
            jnp.concatenate([got, total], axis=0),
        )
    return total, first_work, swap_work, spread_work


def per_device(
    replicas,
    shards,
    images,
    image_adapter_index,
    device_image_count,
    cotangent,
    query_key_value_weight,
    frozen_output_weight,
    frozen_dispatch_weight,
    query_key_value_first,
    query_key_value_second,
    output_adapter_first,
    output_adapter_second,
    dispatch_adapter_first,
    dispatch_adapter_second,
    frozen_up_weight,
    frozen_down_weight,
    up_adapter_first,
    up_adapter_second,
    down_adapter_first,
    down_adapter_second,
):
    n_img, n_tok, width = images.shape
    total = -(-n_tok // 16) * 16
    rows = width // shards
    n_loc = frozen_up_weight.shape[0]
    n_exp = n_loc * shards
    groups = width // GROUP
    quarter = lax.axis_index("replica") % 4
    place = jnp.stack(
        [quarter, lax.axis_index("shard") % 2, lax.axis_index("replica")]
    ).astype(jnp.int32)
    by_axis = shards == 2 * STRIPS and replicas == 4

    spread01 = pack_call(
        place,
        (
            query_key_value_weight, query_key_value_first, query_key_value_second.T,
            output_adapter_first, dispatch_adapter_first, output_adapter_second.T,
            frozen_dispatch_weight.T,
        ),
        STRIPS if by_axis else shards,
    )
    spread23 = later_pack_call(
        place, (query_key_value_weight, frozen_output_weight, dispatch_adapter_second.T), shards
    )
    near = functools.partial(swap, axis="replica", size=replicas, bit=1)
    far = functools.partial(swap, axis="replica", size=replicas, bit=2)
    beside = functools.partial(swap, axis="shard", size=shards, bit=1)
    cut = (width + 6 * LANES) // 4

    h1 = norm_call(images, cotangent, total)
    if by_axis:
        lines = [[2 * strip + side for strip in range(STRIPS)] for side in range(2)]
        own01, spread23, h1 = tie(over_shard(spread01, lines), spread23, h1)
        own0, own1 = own01[:, :cut], own01[:, cut:]
        beside0, far0, own1 = tie(beside(own0), far(own0), own1)
        corner0, beside1, far1 = beside(far0), beside(own1), far(own1)
        corner0, far1, spread23 = tie(corner0, far1, spread23)
        held0 = [(own0, 0, 0), (beside0, 0, 1), (far0, 2, 0), (corner0, 2, 1)]
        held1 = [(own1, 0, 0), (beside1, 0, 1), (far1, 2, 0), (beside(far1), 2, 1)]
    else:
        own01, spread23, h1 = tie(over_shard(spread01), spread23, h1)
        own0, own1 = own01[:, :cut], own01[:, cut:]
        held0 = [(own0, 0, None), (far(own0), 2, None)]
        held1 = [(own1, 0, None), (far(own1), 2, None)]
    own23 = over_shard(spread23)

    def four_pieces(held, columns):
        layout = [(replica, side, 0) for _, replica, side in held]
        layout += [(replica ^ 1, side, 0) for _, replica, side in held]
        chunks = [chunk for chunk, _, _ in held] + [near(chunk) for chunk, _, _ in held]
        return tuple(chunks), (4, tuple(layout)), columns

    pack0 = four_pieces(held0, width + 6 * LANES)
    qkv0, att0, prob0, uq, bank_a, bank_bt, bank_ao, bank_ra = first_attention_call(
        place, image_adapter_index, h1, pack0, n_tok, shards
    )
    beside1, last1, uq, own23 = tie(held1[1][0], held1[-1][0], uq, own23)
    held1[1] = (beside1,) + held1[1][1:]
    held1[-1] = (last1,) + held1[-1][1:]
    pack1 = four_pieces(held1, width + 2 * LANES)
    own2, own3 = own23[:, : width // 2], own23[:, width // 2 :]
    far3 = far(own3)
    qkv1, att1, prob1, bank_bo, bank_wr = next_attention_call(
        place, h1, uq, bank_bt, pack1, n_tok, 1, 2
    )
    att1, uq, own2, own3, far3 = tie(att1, uq, own2, own3, far3)
    pack2 = ((own2, near(own2)), (2, ((0, None, 0), (1, None, 0))), width)
    qkv2, att2, prob2 = next_attention_call(place, h1, uq, bank_bt, pack2, n_tok, 2, 0)
    pack3 = four_pieces([(own3, 0, None), (far3, 2, None)], width + 2 * LANES)
    packs = (pack0, pack1, pack2, pack3)
    atts = (att0, att1, att2)
    x2, uo, ur, disp, comb, sg, bank_wrt, bank_rb = route_call(
        place, image_adapter_index, device_image_count, images, cotangent, atts,
        (bank_ao, bank_bo, bank_ra, bank_wr), packs[3], n_exp, total, shards,
    )

    landed = lax.all_to_all(sg, "shard", split_axis=0, concat_axis=0, tiled=True)
    landed, *turned = tie(landed, *turn_call(place, (bank_ao, bank_bo, bank_ra), packs))
    turned_qkv, turned_out, turned_first, turned_route = turned
    weights = (
        frozen_up_weight, frozen_down_weight, up_adapter_first, up_adapter_second,
        down_adapter_first, down_adapter_second,
    )
    far_landed = [swap(landed, "replica", replicas, bit) for bit in range(2, replicas, 2)]
    ret, *kept = expert_call(landed, weights)
    ret, *far_landed = tie(ret, *far_landed)
    back = lax.all_to_all(ret, "shard", split_axis=0, concat_axis=0, tiled=True)
    every = [(landed, *kept)]
    for number, bit in enumerate(range(2, replicas, 2)):
        far_kept = [swap(array, "replica", replicas, bit) for array in kept]
        every.append((far_landed[number], *far_kept))

    block_out, gx2, gatt, out_pack = route_back_call(
        image_adapter_index, device_image_count, cotangent, x2, uo, ur, disp, comb, atts, back,
        (bank_wrt, bank_rb, turned_out, turned_first, turned_route), shards, replicas,
    )
    gatt, *lows = tie(gatt, *[row[3] for row in every])
    held = [array for row, low in zip(every, lows) for array in (*row[:3], low)]
    *gqkvs, guq, keep, give = attention_back_call(
        place, image_adapter_index, (qkv0, qkv1, qkv2), (prob0, prob1, prob2), gatt, uq, h1, bank_bt, out_pack
    )

    def expert_grads(block, *arrays):
        arrays = list(arrays) + [swap(array, "replica", replicas, 1) for array in arrays]
        rows_of = [tuple(arrays[place : place + 4]) for place in range(0, len(arrays), 4)]
        return expert_grad_call(rows_of, width)

    summed, (block_out, *_), (input_grad,), grads = reduce_pack(
        keep, give, replicas,
        lambda: (block_out.transpose(1, 0, 2), *held),
        lambda: (input_grad_call(images, gx2, guq, gqkvs, turned_qkv),),
        expert_grads,
    )
    block_out = block_out.transpose(1, 0, 2)
    summed = summed.astype(F32)
    return (
        block_out,
        input_grad,
        summed[3 * rows : 4 * rows],
        summed[: 3 * rows].T,
        summed[4 * rows : 5 * rows],
        summed[5 * rows : 6 * rows].T,
        summed[6 * rows : 7 * rows],
        summed[7 * rows : 7 * rows + n_loc].T,
        *grads,
    )


def solution(mesh):
    images = P(("replica", "shard"), None, None)
    each = P(("replica", "shard"))
    by_row, by_column, by_expert = P("shard", None), P(None, "shard"), P("shard", None, None)
    in_specs = (
        (images, each, each, images)
        + (by_row, by_row, by_row)
        + (by_row, by_column) * 3
        + (by_expert,) * 6
    )
    out_specs = (images, images) + (by_row, by_column) * 3 + (by_expert,) * 4
    return jax.shard_map(
        functools.partial(per_device, mesh.shape["replica"], mesh.shape["shard"]),
        mesh=mesh,
        in_specs=in_specs,
        out_specs=out_specs,
        check_vma=False,
    )
```

```python
import functools

import jax
import jax.numpy as jnp
from jax import lax
from jax.experimental import pallas as pl
from jax.experimental.pallas import tpu as pltpu
from jax.sharding import PartitionSpec as P

HEADS = 12
RANK = 16
LANES = 128
HEAD_DIM = 64
GROUP = 256
F32 = jnp.float32
BF16 = jnp.bfloat16
NN = (((1,), (0,)), ((), ()))
NT = (((1,), (1,)), ((), ()))
TN = (((0,), (0,)), ((), ()))
NEG = -1e30
VMEM_LIMIT = 56 * 1024 * 1024
GELU_C = 0.7978845608028654
GELU_A = 0.044715
IMAGES_FORWARD = 2
IMAGES_BACK = 2
IMAGES_ROUTE = 2
IMAGES_LAST = 2
STRIPS = 4


def dot(left, right, dims=NN):
    return lax.dot_general(left, right, dims, preferred_element_type=F32)


def params(*axes):
    return pltpu.CompilerParams(
        dimension_semantics=axes or None, vmem_limit_bytes=VMEM_LIMIT
    )


def cost(flops, moved, exps=0):
    return pl.CostEstimate(flops=int(flops), bytes_accessed=int(moved), transcendentals=int(exps))


def normalise(rows):
    centre = rows - jnp.mean(rows, axis=-1, keepdims=True)
    spread = jnp.mean(centre * centre, axis=-1, keepdims=True)
    scale = lax.rsqrt(spread + 1e-06)
    return centre * scale, scale


def normalise_back(unit, scale, upstream):
    inner = jnp.mean(upstream * unit, axis=-1, keepdims=True)
    return scale * (upstream - jnp.mean(upstream, axis=-1, keepdims=True) - unit * inner)


def rank_row(index):
    lane = lax.broadcasted_iota(jnp.int32, (1, LANES), 1) // RANK
    return (lane == index).astype(F32)


def zero_tail(rows, n_tok):
    total = rows.shape[0]
    cut = n_tok // 16 * 16
    if n_tok == total:
        return rows
    row = lax.broadcasted_iota(jnp.int32, (total - cut, rows.shape[1]), 0) + cut
    tail = jnp.where(row < n_tok, rows[cut:].astype(F32), 0.0).astype(rows.dtype)
    return jnp.concatenate([rows[:cut], tail], axis=0)


def mask_tail(scores, n_tok):
    total = scores.shape[0]
    cut = n_tok // 16 * 16
    if n_tok == total:
        return scores
    row = lax.broadcasted_iota(jnp.int32, (total - cut, scores.shape[1]), 0) + cut
    tail = jnp.where(row < n_tok, scores[cut:], NEG)
    return jnp.concatenate([scores[:cut], tail], axis=0)


def pad_rows(scratch, ref):
    n_img, n_tok, width = ref.shape
    total = scratch.shape[0] // n_img
    cut = n_tok // 8 * 8
    for slot in range(n_img):
        base = slot * total
        scratch[base + cut : base + total, :] = jnp.zeros((total - cut, width), F32)
        scratch[base : base + n_tok, :] = ref[slot].astype(F32)
    return scratch[...]


def select_rows(rows, index_ref, first, n_img):
    total = rows.shape[0] // n_img
    return jnp.concatenate(
        [
            (rows[i * total : (i + 1) * total] * rank_row(index_ref[first + i])).astype(BF16)
            for i in range(n_img)
        ],
        axis=0,
    )


def flat(ref):
    return ref[...].reshape(ref.shape[0] * ref.shape[1], ref.shape[2])


def assemble(place_ref, chunks, layout, wall):
    pieces, entries = layout
    part = wall.shape[1] // pieces
    for chunk, (replica, neighbour, start) in zip(chunks, entries):
        column = pl.multiple_of(((place_ref[0] % pieces) ^ replica) * part, LANES)
        if neighbour is None:
            wall[:, pl.ds(column, part)] = chunk[:, start : start + part]
            continue
        strips = STRIPS
        rows = chunk.shape[0] // strips
        for strip in range(strips):
            row = pl.multiple_of((2 * strip + (place_ref[1] ^ neighbour)) * rows, 16)
            wall[pl.ds(row, rows), pl.ds(column, part)] = chunk[
                strip * rows : (strip + 1) * rows, start : start + part
            ]


def norm_kernel(image_ref, _, out_ref, pad_ref):
    unit, _ = normalise(pad_rows(pad_ref, image_ref))
    out_ref[...] = unit.astype(BF16).reshape(out_ref.shape)


def group_columns(pack, qkv_ref, group):
    width = qkv_ref.shape[1] // 3
    for piece in range(3):
        start = piece * width + group * GROUP
        pack[:, piece * GROUP : (piece + 1) * GROUP] = qkv_ref[:, start : start + GROUP]


def own_part(place_ref, pack, pieces):
    part = pack.shape[1] // pieces
    return pack[:, pl.ds(pl.multiple_of(place_ref[0] % pieces * part, LANES), part)]


def pack_kernel(
    place_ref, qkv_ref, a_ref, b_ref, ao_ref, ra_ref, bo_ref, wr_ref, out_ref, pack0, pack1
):
    copies, rows, _ = out_ref.shape
    width = qkv_ref.shape[1] // 3
    group_columns(pack0, qkv_ref, 0)
    for piece in range(3):
        column = width + (1 + piece) * LANES
        pack0[:, column : column + LANES] = b_ref[piece * rows : (piece + 1) * rows, :]
    pack0[:, width : width + LANES] = a_ref[...]
    pack0[:, width + 4 * LANES : width + 5 * LANES] = ao_ref[...]
    pack0[:, width + 5 * LANES : width + 6 * LANES] = ra_ref[...]
    group_columns(pack1, qkv_ref, 1)
    pack1[:, width : width + LANES] = bo_ref[...]
    n_exp = wr_ref.shape[0]
    route = jnp.concatenate([wr_ref[...].astype(F32), jnp.zeros((LANES - n_exp, rows), F32)], axis=0)
    pack1[:, width + LANES :] = route.T.astype(BF16)
    mine = jnp.concatenate([own_part(place_ref, pack0, 4), own_part(place_ref, pack1, 4)], axis=1)
    for copy in range(copies):
        out_ref[copy] = mine


def later_pack_kernel(place_ref, qkv_ref, wo_ref, rb_ref, out_ref, pack2, pack3):
    shards, rows, _ = out_ref.shape
    width = wo_ref.shape[1]
    group_columns(pack2, qkv_ref, 2)
    pack3[:, :width] = wo_ref[...]
    n_loc = rb_ref.shape[0]
    second = jnp.concatenate([rb_ref[...].astype(F32), jnp.zeros((rows - n_loc, LANES), F32)], axis=0)
    pack3[:, width : width + LANES] = second.astype(BF16)
    pack3[:, width + LANES :] = jnp.zeros((rows, LANES), BF16)
    mine = jnp.concatenate([own_part(place_ref, pack2, 2), own_part(place_ref, pack3, 4)], axis=1)
    for shard in range(shards):
        out_ref[shard] = mine


def each_head(columns, value):
    head = lax.broadcasted_iota(jnp.int32, (1, GROUP), 1) // HEAD_DIM
    return jnp.concatenate(
        [
            columns * jnp.where(head == number, value, 0.0).astype(BF16)
            for number in range(GROUP // HEAD_DIM)
        ],
        axis=0,
    )


def merge_pair(low, high):
    lane = lax.broadcasted_iota(jnp.int32, (1, LANES), 1)
    return jnp.where(lane < HEAD_DIM, low, high)


def attention_forward(qkv, n_tok, prob_ref, slot):
    total = qkv.shape[0]
    every = dot(each_head(qkv[:, GROUP : 2 * GROUP], 0.125), qkv[:, :GROUP], NT)
    outs = []
    for head in range(GROUP // HEAD_DIM):
        scores = mask_tail(every[head * total : (head + 1) * total], n_tok)
        powers = jnp.exp(scores - jnp.max(scores, axis=0, keepdims=True))
        probs = (powers * (1.0 / jnp.sum(powers, axis=0, keepdims=True))).astype(BF16)
        prob_ref[slot, head] = probs
        column = 2 * GROUP + head // 2 * LANES
        outs.append(dot(probs, qkv[:, column : column + LANES], TN))
    pairs = [merge_pair(outs[head], outs[head + 1]) for head in range(0, len(outs), 2)]
    return zero_tail(jnp.concatenate(pairs, axis=1).astype(BF16), n_tok)


def first_attention_kernel(
    n_tok, shards, layout, place_ref, index_ref, h1_ref, *rest,
):
    chunks, rest = rest[: len(layout[1])], rest[len(layout[1]) :]
    qkv_ref, att_ref, prob_ref, uq_ref, a_ref, bt_ref, ao_ref, ra_ref, wall = rest
    step = pl.program_id(0)
    n_img, total, width = h1_ref.shape

    @pl.when(step == 0)
    def _():
        assemble(place_ref, chunks, layout, wall)
        a_ref[...] = wall[:, width : width + LANES]
        ao_ref[...] = wall[:, width + 4 * LANES : width + 5 * LANES]
        ra_ref[...] = wall[:, width + 5 * LANES : width + 6 * LANES]
        rows = width // shards
        for shard in range(shards):
            for part in range(3):
                bt_ref[(shard * 3 + part) * rows : (shard * 3 + part + 1) * rows, :] = wall[
                    shard * rows : (shard + 1) * rows,
                    width + (1 + part) * LANES : width + (2 + part) * LANES,
                ]

    h1 = flat(h1_ref)
    both = dot(h1, wall[:, : 3 * GROUP + LANES])
    low = both[:, 3 * GROUP :].astype(BF16).astype(F32)
    uq = select_rows(low, index_ref, step * n_img, n_img)
    uq_ref[...] = uq.reshape(uq_ref.shape)
    attend_group(0, n_tok, both[:, : 3 * GROUP], uq, bt_ref, qkv_ref, att_ref, prob_ref)


def group_rows(group, width, bt_ref):
    return jnp.concatenate(
        [bt_ref[part * width + group * GROUP : part * width + (group + 1) * GROUP, :] for part in range(3)],
        axis=0,
    )


def attend_group(group, n_tok, base, uq, bt_ref, qkv_ref, att_ref, prob_ref):
    n_img, total, _ = att_ref.shape
    second = group_rows(group, bt_ref.shape[0] // 3, bt_ref)
    qkv = (base + dot(uq, second, NT)).astype(BF16)
    qkv_ref[...] = qkv.reshape(qkv_ref.shape)
    for slot in range(n_img):
        att_ref[slot] = attention_forward(
            qkv[slot * total : (slot + 1) * total], n_tok, prob_ref, slot
        )


def next_attention_kernel(
    n_tok, group, extra, layout, place_ref, h1_ref, uq_ref, bt_ref, *rest
):
    chunks, rest = rest[: len(layout[1])], rest[len(layout[1]) :]
    qkv_ref, att_ref, prob_ref = rest[:3]
    wall = rest[-1]

    @pl.when(pl.program_id(0) == 0)
    def _():
        assemble(place_ref, chunks, layout, wall)
        for position in range(extra):
            column = 3 * GROUP + position * LANES
            rest[3 + position][...] = wall[:, column : column + LANES]

    attend_group(
        group, n_tok, dot(flat(h1_ref), wall[:, : 3 * GROUP]), flat(uq_ref), bt_ref, qkv_ref, att_ref, prob_ref,
    )


def route_kernel(
    n_exp, shards, layout, place_ref, index_ref, count_ref, image_ref, cot_ref, att0, att1, att2,
    ao_ref, bo_ref, ra_ref, wr_ref, *rest,
):
    chunks, rest = rest[: len(layout[1])], rest[len(layout[1]) :]
    x2_ref, uo_ref, ur_ref, disp_ref, comb_ref, sg_ref, wrt_ref, rb_ref, *rest = rest
    wall, rb_f, pair_ref, pad_a, pad_b, sent_ref = rest
    every = sg_ref.shape[2]
    n_img, n_tok, width = image_ref.shape
    first = pl.program_id(0) * n_img
    total = x2_ref.shape[1]

    @pl.when(first == 0)
    def _():
        assemble(place_ref, chunks, layout, wall)
        wrt_ref[...] = wr_ref[...].astype(F32).T[:n_exp].astype(BF16)
        n_loc, rows = n_exp // shards, width // shards
        for shard in range(shards):
            rb_f[shard * n_loc : (shard + 1) * n_loc, :] = wall[
                shard * rows : shard * rows + 8, width : width + LANES
            ].astype(F32)[:n_loc]
        rb_ref[...] = rb_f[...].astype(BF16)
        wall[:, width : width + LANES] = ao_ref[...]
        pair_ref[:, :LANES] = ra_ref[...]
        pair_ref[:, LANES:] = wr_ref[...]

    att = jnp.concatenate([flat(att0), flat(att1), flat(att2)], axis=1)
    both = dot(att, wall[:, : width + LANES])
    uo = select_rows(both[:, width:].astype(BF16).astype(F32), index_ref, first, n_img)
    uo_ref[...] = uo.reshape(uo_ref.shape)
    x2 = pad_rows(pad_a, image_ref) + both[:, :width] + dot(uo, bo_ref[...], NT)
    x2_ref[...] = x2.reshape(x2_ref.shape)
    h2 = normalise(x2)[0].astype(BF16)
    both = dot(h2, pair_ref[...])
    ur = select_rows(both[:, :LANES].astype(BF16).astype(F32), index_ref, first, n_img)
    base = both[:, LANES:]
    ur_ref[...] = ur.reshape(ur_ref.shape)
    cot = pad_rows(pad_b, cot_ref)
    firsts = []
    for slot in range(n_img):
        rows = slice(slot * total, (slot + 1) * total)
        living = (first + slot < count_ref[0]).astype(F32)
        logits = base[rows].T[:n_exp] + dot(rb_ref[...], ur[rows], NT)
        alive = lax.broadcasted_iota(jnp.int32, logits.shape, 1) < n_tok
        over_tokens = jnp.where(alive, logits, NEG)
        powers = jnp.exp(over_tokens - jnp.max(over_tokens, axis=1, keepdims=True))
        disp = powers / jnp.sum(powers, axis=1, keepdims=True)
        powers = jnp.exp(logits - jnp.max(logits, axis=0, keepdims=True))
        comb = jnp.where(alive, powers / jnp.sum(powers, axis=0, keepdims=True), 0.0)
        disp_ref[slot] = disp
        comb_ref[slot] = comb
        upstream = (cot[rows] * living).astype(BF16)
        firsts.append((rows, disp, comb, upstream))
    for slot, (rows, disp, comb, upstream) in enumerate(firsts):
        sent = jnp.concatenate(
            [
                dot(disp.astype(BF16), h2[rows]),
                dot(comb.astype(BF16), upstream),
                jnp.broadcast_to(rank_row(index_ref[first + slot]), (n_exp, LANES)),
            ],
            axis=1,
        )
        for block in range(sent.shape[1] // LANES):
            start = block * n_exp * every + first + slot
            sent_ref[pl.ds(start, n_exp, stride=every), :] = sent[:, block * LANES : (block + 1) * LANES]

    @pl.when(pl.program_id(0) == pl.num_programs(0) - 1)
    def _():
        for block in range(sg_ref.shape[3] // LANES):
            span = slice(block * LANES, (block + 1) * LANES)
            piece = sent_ref[block * n_exp * every : (block + 1) * n_exp * every, :]
            sg_ref[:, :, :, span] = piece.reshape(sg_ref.shape[:3] + (LANES,)).astype(BF16)


def gelu_both(pre):
    square = pre * pre
    half = jnp.tanh(GELU_C * pre * (1.0 + GELU_A * square))
    both = 0.5 * (1.0 + half)
    slope = both + 0.5 * pre * (1.0 - half * half) * (GELU_C * (1.0 + 3.0 * GELU_A * square))
    return pre * both, slope


def expert_tile(slots, gy, u1, gu2, wu_ref, wd_ref, ub_ref, da_ref):
    pre = dot(slots, wu_ref[0]) + dot(u1, ub_ref[0])
    ghid = (dot(wd_ref[0], gy, NT) + dot(da_ref[0], gu2, NT)).T
    hidden, slope = gelu_both(pre)
    return hidden.astype(BF16), (slope * ghid).astype(BF16)


def gather_rows(part_refs, out_ref):
    rows = part_refs[0].shape[0] * part_refs[0].shape[2]
    for number, part_ref in enumerate(part_refs):
        part = part_ref[:, 0].astype(F32).reshape(rows, part_ref.shape[3])
        out_ref[number * rows : (number + 1) * rows, :] = part.astype(BF16)


def expert_kernel(
    wu_ref, wd_ref, ua_ref, ub_ref, da_ref, db_ref, part_ref, out_ref, hidden_ref, gpre_ref, low_ref,
    sg_ref, u1_ref, gu2_ref, acc_y, acc_s, acc_u2, acc_gu1,
):
    step = pl.program_id(1)
    width = wu_ref.shape[1]

    @pl.when(step == 0)
    def _():
        gather_rows((part_ref,), sg_ref)
        selector = sg_ref[:, 2 * width :].astype(F32)
        u1_ref[...] = (
            dot(sg_ref[:, :width], ua_ref[0]).astype(BF16).astype(F32) * selector
        ).astype(BF16)
        gu2_ref[...] = (dot(sg_ref[:, width : 2 * width], db_ref[0], NT) * selector).astype(BF16)
        acc_y[...] = jnp.zeros_like(acc_y)
        acc_s[...] = jnp.zeros_like(acc_s)
        acc_u2[...] = jnp.zeros_like(acc_u2)
        acc_gu1[...] = jnp.zeros_like(acc_gu1)

    hidden, gpre = expert_tile(
        sg_ref[:, :width], sg_ref[:, width : 2 * width], u1_ref[...], gu2_ref[...],
        wu_ref, wd_ref, ub_ref, da_ref,
    )
    hidden_ref[0] = hidden
    gpre_ref[0] = gpre
    acc_y[...] += dot(hidden, wd_ref[0])
    acc_u2[...] += dot(hidden, da_ref[0])
    acc_s[...] += dot(wu_ref[0], gpre, NT)
    acc_gu1[...] += dot(ub_ref[0], gpre, NT)

    @pl.when(step == pl.num_programs(1) - 1)
    def _():
        selector = sg_ref[:, 2 * width :].astype(F32)
        u2 = (acc_u2[...].astype(BF16).astype(F32) * selector).astype(BF16)
        gu1 = (acc_gu1[...].T * selector).astype(BF16)
        shards, _, n_img, _ = out_ref.shape
        result = acc_y[...] + dot(u2, db_ref[0])
        out_ref[:, 0, :, :width] = result.reshape(shards, n_img, width).astype(BF16)
        result = acc_s[...].T + dot(gu1, ua_ref[0], NT)
        out_ref[:, 0, :, width:] = result.reshape(shards, n_img, width).astype(BF16)
        for place, low in enumerate((u1_ref[...], u2, gu1, gu2_ref[...])):
            low_ref[0, :, place * LANES : (place + 1) * LANES] = low


def expert_grad_kernel(copies, *refs):
    refs = list(refs)
    part_refs, hidden_refs, gpre_refs, low_refs = (
        [refs.pop(0) for _ in range(copies)] for _ in range(4)
    )
    gua_ref, gub_ref, gda_ref, gdb_ref, sg_ref, low_t, rows_ref = refs
    rows = hidden_refs[0].shape[1]
    width = gua_ref.shape[1]

    @pl.when(pl.program_id(1) == 0)
    def _():
        gather_rows(part_refs, sg_ref)
        low = jnp.concatenate([ref[0] for ref in low_refs], axis=0)
        low_t[...] = low.astype(F32).T.astype(BF16)
        u2_t, gu1_t = low_t[LANES : 2 * LANES, :], low_t[2 * LANES : 3 * LANES, :]
        gdb_ref[0] = dot(u2_t, sg_ref[:, width : 2 * width])
        gua_ref[0] = dot(gu1_t, sg_ref[:, :width]).T

    for number in range(copies):
        rows_ref[number * rows : (number + 1) * rows, :] = gpre_refs[number][0]
    gub_ref[0] = dot(low_t[:LANES, :], rows_ref[...])
    for number in range(copies):
        rows_ref[number * rows : (number + 1) * rows, :] = hidden_refs[number][0]
    gda_ref[0] = dot(low_t[3 * LANES :, :], rows_ref[...]).T


def turn_kernel(layouts, place_ref, ao_ref, bo_ref, ra_ref, *refs):
    refs = list(refs)
    chunks = [[refs.pop(0) for _ in layout[1]] for layout in layouts]
    qkv_ref, out_ref, first_ref, route_ref = refs[:4]
    walls = refs[4:]
    for chunk, layout, wall in zip(chunks, layouts, walls):
        assemble(place_ref, chunk, layout, wall)
    width = walls[0].shape[0]
    for group, wall in enumerate(walls[:-1]):
        qkv_ref[group * 3 * GROUP : (group + 1) * 3 * GROUP, :] = wall[:, : 3 * GROUP].T
    qkv_ref[3 * width :, :] = walls[0][:, 3 * GROUP : 3 * GROUP + LANES].T
    out_ref[:, :width] = walls[-1][:, :width].T
    out_ref[:, width:] = bo_ref[...]
    first_ref[...] = ao_ref[...].T
    route_ref[...] = ra_ref[...].T


def route_back_kernel(
    n_exp, index_ref, count_ref, cot_ref, x2_ref, uo_ref, ur_ref, disp_ref, comb_ref,
    att0, att1, att2, ret_ref, wrt_ref, rb_ref, out_ref, first_ref, route_ref,
    block_ref, gx2_ref, gatt_ref, pack_ref, pad_b, back_ref, acc_oa, acc_ob, acc_ra, acc_rb,
):
    n_img, n_tok, width = cot_ref.shape
    first = pl.program_id(0) * n_img
    total = x2_ref.shape[1]

    every = ret_ref.shape[2]

    @pl.when(first == 0)
    def _():
        for block in range(2 * width // LANES):
            piece = ret_ref[:, :, :, block * LANES : (block + 1) * LANES].astype(F32)
            back_ref[block * n_exp * every : (block + 1) * n_exp * every, :] = piece.reshape(
                n_exp * every, LANES
            )
        acc_oa[...] = jnp.zeros_like(acc_oa)
        acc_ob[...] = jnp.zeros_like(acc_ob)
        acc_ra[...] = jnp.zeros_like(acc_ra)
        acc_rb[...] = jnp.zeros_like(acc_rb)

    cot = pad_rows(pad_b, cot_ref)
    x2 = flat(x2_ref)
    unit, scale = normalise(x2)
    h2 = unit.astype(BF16)
    pairs, belows, upstreams, mixes, firsts = [], [], [], [], []
    for slot in range(n_img):
        rows = slice(slot * total, (slot + 1) * total)
        living = (first + slot < count_ref[0]).astype(F32)
        upstream = cot[rows] * living
        upstreams.append(upstream)
        disp, comb = disp_ref[slot], comb_ref[slot]
        blocks = [
            back_ref[pl.ds(block * n_exp * every + first + slot, n_exp, stride=every), :]
            for block in range(2 * width // LANES)
        ]
        back = jnp.concatenate(blocks, axis=1).astype(BF16)
        yexp, gslot = back[:, :width], back[:, width:]
        gcomb = dot(yexp, upstream.astype(BF16), NT)
        gdisp = dot(gslot, h2[rows], NT)
        firsts.append((rows, living, disp, comb, yexp, gslot, gcomb, gdisp))
    for slot, (rows, living, disp, comb, yexp, gslot, gcomb, gdisp) in enumerate(firsts):
        glog = (
            disp * (gdisp - jnp.sum(gdisp * disp, axis=1, keepdims=True))
            + comb * (gcomb - jnp.sum(gcomb * comb, axis=0, keepdims=True))
        )
        acc_rb[...] += dot(glog.astype(BF16), ur_ref[slot])
        three = jnp.concatenate([disp, glog, comb], axis=0).T.astype(BF16)
        mixes.append((living, three[:, 2 * n_exp :], yexp, rows))
        pairs.append(three[:, : 2 * n_exp])
        belows.append(jnp.concatenate([route_ref[...], gslot, wrt_ref[...]], axis=0))
    glog_rows = jnp.concatenate([pair[:, n_exp:] for pair in pairs], axis=0)
    gur = select_rows(dot(glog_rows, rb_ref[...]), index_ref, first, n_img)
    gh2 = jnp.concatenate(
        [
            dot(jnp.concatenate([gur[i * total : (i + 1) * total], pairs[i]], axis=1), belows[i])
            for i in range(n_img)
        ],
        axis=0,
    )
    gx2 = jnp.concatenate(upstreams, axis=0) + normalise_back(unit, scale, gh2)
    gbr = gx2.astype(BF16)
    gx2_ref[...] = gbr.reshape(gx2_ref.shape)
    both = dot(gbr, out_ref[...])
    guo = select_rows(both[:, width:], index_ref, first, n_img)
    att = jnp.concatenate([flat(att0), flat(att1), flat(att2)], axis=1)
    gatt = (both[:, :width] + dot(guo, first_ref[...])).astype(BF16)
    gatt_ref[...] = gatt.reshape(gatt_ref.shape)
    acc_ra[...] += dot(gur, h2, TN)
    acc_ob[...] += dot(flat(uo_ref), gbr, TN)
    acc_oa[...] += dot(guo, att, TN)
    for slot, (living, left, yexp, rows) in enumerate(mixes):
        block_ref[slot] = (living * (x2[rows] + dot(left, yexp))).astype(BF16)[:n_tok]

    @pl.when(pl.program_id(0) == pl.num_programs(0) - 1)
    def _():
        shards = pack_ref.shape[0]
        rows = width // shards
        n_loc = n_exp // shards
        for position, acc in enumerate((acc_oa, acc_ob, acc_ra)):
            summed = acc[...].T.astype(BF16)
            for shard in range(shards):
                pack_ref[shard, position * rows : (position + 1) * rows, :] = summed[
                    shard * rows : (shard + 1) * rows
                ]
        tail = pack_ref.shape[1] - 3 * rows
        for shard in range(shards):
            last = jnp.concatenate(
                [acc_rb[shard * n_loc : (shard + 1) * n_loc, :], jnp.zeros((tail - n_loc, LANES), F32)],
                axis=0,
            )
            pack_ref[shard, 3 * rows :, :] = last.astype(BF16)


def attention_backward(qkv, gatt, prob_ref, slot):
    total = qkv.shape[0]
    heads = GROUP // HEAD_DIM
    every = dot(each_head(qkv[:, 2 * GROUP :], 1.0), gatt, NT)
    gscores = []
    for head in range(heads):
        probs = prob_ref[slot, head].astype(F32)
        gprobs = every[head * total : (head + 1) * total]
        inner = jnp.sum(gprobs * probs, axis=0, keepdims=True)
        gscores.append((probs * (gprobs - inner)).astype(BF16))

    def products(lefts, right):
        outs = []
        for pair in range(heads // 2):
            both = dot(
                jnp.concatenate(lefts[2 * pair : 2 * pair + 2], axis=0),
                right[:, pair * LANES : (pair + 1) * LANES],
            )
            outs.append(merge_pair(both[:total], both[total:]))
        return outs

    gv = [part.astype(BF16) for part in products([prob_ref[slot, head] for head in range(heads)], gatt)]
    gk = [(part * 0.125).astype(BF16) for part in products(gscores, qkv[:, :GROUP])]
    key_t = qkv[:, GROUP : 2 * GROUP].T
    gq = [
        (dot(key_t[head * HEAD_DIM : (head + 1) * HEAD_DIM], gscores[head]) * 0.125).astype(BF16)
        for head in range(heads)
    ]
    return jnp.concatenate([jnp.concatenate(gq, axis=0).T] + gk + gv, axis=1)


def attention_back_kernel(groups, place_ref, index_ref, *refs):
    refs = list(refs)
    qkv_refs = [refs.pop(0) for _ in range(groups)]
    prob_refs = [refs.pop(0) for _ in range(groups)]
    gatt_ref, uq_ref, h1_ref, bt_ref, others_ref = refs[:5]
    refs = refs[5:]
    gqkv_refs = [refs.pop(0) for _ in range(groups)]
    guq_ref, keep_ref, give_ref, pack_ref, acc_b, acc_a = refs
    step = pl.program_id(0)
    n_img, total, width = h1_ref.shape

    @pl.when(step == 0)
    def _():
        acc_b[...] = jnp.zeros_like(acc_b)
        acc_a[...] = jnp.zeros_like(acc_a)

    uq_t = flat(uq_ref).T
    guq = None
    for group in range(groups):
        parts = []
        for i in range(n_img):
            part = attention_backward(
                qkv_refs[group][i], gatt_ref[i, :, group * GROUP : (group + 1) * GROUP],
                prob_refs[group], i,
            )
            gqkv_refs[group][i] = part
            parts.append(part)
        gqkv = jnp.concatenate(parts, axis=0)
        acc_b[:, group * 3 * GROUP : (group + 1) * 3 * GROUP] += dot(uq_t, gqkv)
        part = dot(gqkv, group_rows(group, width, bt_ref))
        guq = part if guq is None else guq + part
    guq = select_rows(guq, index_ref, step * n_img, n_img)
    acc_a[...] += dot(guq, flat(h1_ref), TN)
    guq_ref[...] = guq.reshape(guq_ref.shape)

    @pl.when(step == pl.num_programs(0) - 1)
    def _():
        shards = pack_ref.shape[0]
        rows = width // shards
        pack_ref[:, 4 * rows :, :] = others_ref[...]
        own = acc_a[...].T.astype(BF16)
        for shard in range(shards):
            pack_ref[shard, 3 * rows : 4 * rows, :] = own[shard * rows : (shard + 1) * rows]
        for group in range(groups):
            summed = acc_b[:, group * 3 * GROUP : (group + 1) * 3 * GROUP].T.astype(BF16)
            for part in range(3):
                start = part * width + group * GROUP
                place = start
                while place < start + GROUP:
                    shard, offset = divmod(place, 3 * rows)
                    length = min(start + GROUP - place, 3 * rows - offset)
                    take = part * GROUP + place - start
                    pack_ref[shard, offset : offset + length, :] = summed[take : take + length]
                    place += length
        half = keep_ref.shape[1]
        side = place_ref[2] % 2
        keep_ref[...] = pack_ref[:, pl.ds(pl.multiple_of(side * half, 16), half), :]
        give_ref[...] = pack_ref[:, pl.ds(pl.multiple_of((1 - side) * half, 16), half), :]


def input_grad_kernel(image_ref, gx2_ref, guq_ref, turned_ref, *refs):
    *gqkv, out_ref, pad_a = refs
    n_img, n_tok, width = image_ref.shape
    step = pl.program_id(0)
    parts = width // LANES
    every = out_ref.shape[0] // (n_tok * parts)
    total = gx2_ref.shape[1]
    gh1 = dot(jnp.concatenate([flat(ref) for ref in gqkv] + [flat(guq_ref)], axis=1), turned_ref[...])
    unit, scale = normalise(pad_rows(pad_a, image_ref))
    result = flat(gx2_ref).astype(F32) + normalise_back(unit, scale, gh1)
    for slot in range(n_img):
        for part in range(parts):
            out_ref[pl.ds(part * every + step * n_img + slot, n_tok, stride=parts * every), :] = result[
                slot * total : slot * total + n_tok, part * LANES : (part + 1) * LANES
            ]


ANY = pl.BlockSpec(memory_space=pl.ANY)


def whole(shape):
    return pl.BlockSpec(shape, lambda *_: (0,) * len(shape))


def once(shape):
    return pl.BlockSpec(shape, lambda *_: (0,) * len(shape), pipeline_mode=pl.Buffered(1))


def per_image(*shape, images=1):
    return pl.BlockSpec((images,) + shape, lambda i, *_: (i,) + (0,) * len(shape))


def several(images, limit):
    return max(n for n in range(1, limit + 1) if images % n == 0)


def call(kernel, scalars, grid, inputs, outputs, scratch, flops, exps=0, aliases=None):
    arrays = [array for array, _ in inputs]
    shapes = [jax.ShapeDtypeStruct(shape, dtype) for shape, dtype, _ in outputs]
    moved = sum(array.size * array.dtype.itemsize for array in arrays) + sum(
        shape.size * shape.dtype.itemsize for shape in shapes
    )
    return pl.pallas_call(
        kernel,
        out_shape=shapes,
        grid_spec=pltpu.PrefetchScalarGridSpec(
            num_scalar_prefetch=len(scalars),
            grid=grid,
            in_specs=[spec for _, spec in inputs],
            out_specs=[spec for _, _, spec in outputs],
            scratch_shapes=scratch,
        ),
        input_output_aliases=aliases or {},
        compiler_params=params(*(("arbitrary",) * len(grid))),
        cost_estimate=cost(flops, moved, exps),
    )(*scalars, *arrays)


def norm_call(images, cotangent, total):
    n_img, n_tok, width = images.shape
    each = several(n_img, 4)
    return call(
        norm_kernel, (), (n_img // each,),
        [(images, per_image(n_tok, width, images=each)), (cotangent, ANY)],
        [((n_img, total, width), BF16, per_image(total, width, images=each))],
        [pltpu.VMEM((each * total, width), F32)],
        8 * images.size,
    )[0]


def pack_call(place, weights, copies):
    rows, columns = weights[0].shape
    width = columns // 3
    wide = [width + 6 * LANES, width + 2 * LANES]
    out = (copies, rows, sum(wide) // 4)
    return call(
        pack_kernel, (place,), (1,), [(weight, whole(weight.shape)) for weight in weights],
        [(out, BF16, whole(out))], [pltpu.VMEM((rows, each), BF16) for each in wide], rows * columns,
    )[0]


def later_pack_call(place, weights, shards):
    rows, width = weights[1].shape
    out = (shards, rows, width // 2 + (width + 2 * LANES) // 4)
    return call(
        later_pack_kernel, (place,), (1,), [(weight, whole(weight.shape)) for weight in weights],
        [(out, BF16, whole(out))],
        [pltpu.VMEM((rows, each), BF16) for each in (width, width + 2 * LANES)], rows * width,
    )[0]


def attention_flops(n_img, total, width, parts):
    return n_img * total * (2 * width * 3 * GROUP + parts * 8 * total * HEAD_DIM)


def attention_outputs(n_img, total, each):
    return [
        ((n_img, total, 3 * GROUP), BF16, per_image(total, 3 * GROUP, images=each)),
        ((n_img, total, GROUP), BF16, per_image(total, GROUP, images=each)),
        (
            (n_img, GROUP // HEAD_DIM, total, total), BF16,
            per_image(GROUP // HEAD_DIM, total, total, images=each),
        ),
    ]


def first_attention_call(place, index, h1, pack, n_tok, shards):
    n_img, total, width = h1.shape
    chunks, layout, columns = pack
    each = several(n_img, IMAGES_FORWARD)
    return call(
        functools.partial(first_attention_kernel, n_tok, shards, layout), (place, index), (n_img // each,),
        [(h1, per_image(total, width, images=each))] + [(chunk, once(chunk.shape)) for chunk in chunks],
        attention_outputs(n_img, total, each)
        + [
            ((n_img, total, LANES), BF16, per_image(total, LANES, images=each)),
            ((width, LANES), BF16, whole((width, LANES))),
            ((3 * width, LANES), BF16, whole((3 * width, LANES))),
            ((width, LANES), BF16, whole((width, LANES))),
            ((width, LANES), BF16, whole((width, LANES))),
        ],
        [pltpu.VMEM((width, columns), BF16)],
        attention_flops(n_img, total, width, 2), n_img * total * total * 4,
    )


def next_attention_call(place, h1, uq, bt, pack, n_tok, group, extra):
    n_img, total, width = h1.shape
    chunks, layout, columns = pack
    each = several(n_img, IMAGES_FORWARD)
    return call(
        functools.partial(next_attention_kernel, n_tok, group, extra, layout), (place,), (n_img // each,),
        [
            (h1, per_image(total, width, images=each)),
            (uq, per_image(total, LANES, images=each)),
            (bt, whole(bt.shape)),
        ]
        + [(chunk, once(chunk.shape)) for chunk in chunks],
        attention_outputs(n_img, total, each)
        + [((width, LANES), BF16, whole((width, LANES)))] * extra,
        [pltpu.VMEM((width, columns), BF16)],
        attention_flops(n_img, total, width, 2), n_img * total * total * 4,
    )


def route_call(place, index, count, images, cotangent, atts, banks, pack, n_exp, total, shards):
    n_img, n_tok, width = images.shape
    chunks, layout, columns = pack
    each = several(n_img, IMAGES_ROUTE)
    here = functools.partial(per_image, images=each)
    sent = (shards, n_exp // shards, n_img, 2 * width + LANES)
    return call(
        functools.partial(route_kernel, n_exp, shards, layout), (place, index, count), (n_img // each,),
        [(images, here(n_tok, width)), (cotangent, here(n_tok, width))]
        + [(att, here(total, GROUP)) for att in atts]
        + [(bank, whole(bank.shape)) for bank in banks]
        + [(chunk, once(chunk.shape)) for chunk in chunks],
        [
            ((n_img, total, width), F32, here(total, width)),
            ((n_img, total, LANES), BF16, here(total, LANES)),
            ((n_img, total, LANES), BF16, here(total, LANES)),
            ((n_img, n_exp, total), F32, here(n_exp, total)),
            ((n_img, n_exp, total), F32, here(n_exp, total)),
            (sent, BF16, whole(sent)),
            ((n_exp, width), BF16, whole((n_exp, width))),
            ((n_exp, LANES), BF16, whole((n_exp, LANES))),
        ],
        [
            pltpu.VMEM((width, columns), BF16),
            pltpu.VMEM((n_exp, LANES), F32),
            pltpu.VMEM((width, 2 * LANES), BF16),
            pltpu.VMEM((each * total, width), F32),
            pltpu.VMEM((each * total, width), F32),
            pltpu.VMEM(((2 * width // LANES + 1) * n_exp * n_img, LANES), F32),
        ],
        n_img * total * 2 * width * (width + 3 * LANES), n_img * total * 2 * n_exp,
    )


def hidden_tile(hidden, limit):
    tile = hidden
    while tile > limit:
        tile //= 2
    return tile


def expert_specs(width, tile, first=0):
    return (
        pl.BlockSpec((1, width, tile), lambda e, f: (e + first, 0, f)),
        pl.BlockSpec((1, tile, width), lambda e, f: (e + first, f, 0)),
        pl.BlockSpec((1, width, LANES), lambda e, f: (e + first, 0, 0)),
        pl.BlockSpec((1, LANES, tile), lambda e, f: (e + first, 0, f)),
        pl.BlockSpec((1, tile, LANES), lambda e, f: (e + first, f, 0)),
        pl.BlockSpec((1, LANES, width), lambda e, f: (e + first, 0, 0)),
    )


def expert_rows(shape, first=0):
    shards, _, n_img, columns = shape
    return pl.BlockSpec((shards, 1, n_img, columns), lambda e, f: (0, e + first, 0, 0))


def expert_call(landed, weights):
    shards, n_loc, n_img, columns = landed.shape
    rows = shards * n_img
    width, hidden = weights[0].shape[1:]
    tile = hidden_tile(hidden, 1536)
    out = (shards, n_loc, n_img, 2 * width)
    tiled = pl.BlockSpec((1, rows, tile), lambda e, f: (e, 0, f))
    return call(
        expert_kernel, (), (n_loc, hidden // tile),
        list(zip(weights, expert_specs(width, tile))) + [(landed, expert_rows(landed.shape))],
        [
            (out, BF16, expert_rows(out)),
            ((n_loc, rows, hidden), BF16, tiled),
            ((n_loc, rows, hidden), BF16, tiled),
            (
                (n_loc, rows, 4 * LANES), BF16,
                pl.BlockSpec((1, rows, 4 * LANES), lambda e, f: (e, 0, 0)),
            ),
        ],
        [
            pltpu.VMEM((rows, columns), BF16),
            pltpu.VMEM((rows, LANES), BF16),
            pltpu.VMEM((rows, LANES), BF16),
            pltpu.VMEM((rows, width), F32),
            pltpu.VMEM((width, rows), F32),
            pltpu.VMEM((rows, LANES), F32),
            pltpu.VMEM((LANES, rows), F32),
        ],
        n_loc * rows * 8 * width * hidden, n_loc * rows * hidden,
    )


def expert_grad_call(every, width):
    parts, hiddens, gpres, lows = zip(*every)
    shards, n_loc, n_img, columns = parts[0].shape
    rows, hidden = hiddens[0].shape[1:]
    total = rows * len(every)
    tile = hidden_tile(hidden, 1536 if total <= 512 else 384)
    tiled = pl.BlockSpec((1, rows, tile), lambda e, f: (e, 0, f))
    low = pl.BlockSpec((1, rows, 4 * LANES), lambda e, f: (e, 0, 0))
    return call(
        functools.partial(expert_grad_kernel, len(every)), (), (n_loc, hidden // tile),
        [(part, expert_rows(part.shape)) for part in parts]
        + [(array, tiled) for array in hiddens + gpres]
        + [(array, low) for array in lows],
        [
            ((n_loc, width, LANES), F32, pl.BlockSpec((1, width, LANES), lambda e, f: (e, 0, 0))),
            ((n_loc, LANES, hidden), F32, pl.BlockSpec((1, LANES, tile), lambda e, f: (e, 0, f))),
            ((n_loc, hidden, LANES), F32, pl.BlockSpec((1, tile, LANES), lambda e, f: (e, f, 0))),
            ((n_loc, LANES, width), F32, pl.BlockSpec((1, LANES, width), lambda e, f: (e, 0, 0))),
        ],
        [
            pltpu.VMEM((total, columns), BF16),
            pltpu.VMEM((4 * LANES, total), BF16),
            pltpu.VMEM((total, tile), BF16),
        ],
        4 * n_loc * total * LANES * hidden,
    )


def route_back_call(
    index, count, cotangent, x2, uo, ur, disp, comb, atts, ret, banks, shards, replicas
):
    n_img, n_tok, width = cotangent.shape
    total, n_exp = x2.shape[1], disp.shape[1]
    rows = width // shards
    unit = 16 * replicas
    pack_rows = -(-(7 * rows + n_exp // shards) // unit) * unit - 4 * rows
    each = several(n_img, IMAGES_ROUTE)
    here = functools.partial(per_image, images=each)
    return call(
        functools.partial(route_back_kernel, n_exp), (index, count), (n_img // each,),
        [
            (cotangent, here(n_tok, width)),
            (x2, here(total, width)),
            (uo, here(total, LANES)),
            (ur, here(total, LANES)),
            (disp, here(n_exp, total)),
            (comb, here(n_exp, total)),
        ]
        + [(att, here(total, GROUP)) for att in atts]
        + [(ret, once(ret.shape))]
        + [(bank, once(bank.shape)) for bank in banks],
        [
            ((n_img, n_tok, width), BF16, here(n_tok, width)),
            ((n_img, total, width), BF16, here(total, width)),
            ((n_img, total, width), BF16, here(total, width)),
            ((shards, pack_rows, LANES), BF16, whole((shards, pack_rows, LANES))),
        ],
        [
            pltpu.VMEM((each * total, width), F32),
            pltpu.VMEM((2 * width // LANES * n_exp * n_img, LANES), F32),
            pltpu.VMEM((LANES, width), F32),
            pltpu.VMEM((LANES, width), F32),
            pltpu.VMEM((LANES, width), F32),
            pltpu.VMEM((n_exp, LANES), F32),
        ],
        n_img * total * 2 * width * (width + 6 * LANES),
    )


def attention_back_call(place, index, qkvs, probs, gatt, uq, h1, bt, others):
    n_img, total, width = h1.shape
    groups = len(qkvs)
    shards = others.shape[0]
    each = several(n_img, IMAGES_BACK)
    here = functools.partial(per_image, images=each)
    pack = (shards, 4 * width // shards + others.shape[1], LANES)
    half = (shards, pack[1] // 2, LANES)
    return call(
        functools.partial(attention_back_kernel, groups), (place, index), (n_img // each,),
        [(qkv, here(total, 3 * GROUP)) for qkv in qkvs]
        + [(prob, here(GROUP // HEAD_DIM, total, total)) for prob in probs]
        + [
            (gatt, here(total, width)),
            (uq, here(total, LANES)),
            (h1, here(total, width)),
            (bt, whole(bt.shape)),
            (others, whole(others.shape)),
        ],
        [((n_img, total, 3 * GROUP), BF16, here(total, 3 * GROUP))] * groups
        + [((n_img, total, LANES), BF16, here(total, LANES))]
        + [(half, BF16, whole(half))] * 2,
        [
            pltpu.VMEM(pack, BF16),
            pltpu.VMEM((LANES, 3 * width), F32),
            pltpu.VMEM((LANES, width), F32),
        ],
        groups * attention_flops(n_img, total, LANES, 5), groups * n_img * total * total * 4,
    )


def input_grad_call(images, gx2, guq, gqkvs, turned):
    n_img, n_tok, width = images.shape
    total = gx2.shape[1]
    each = several(n_img, IMAGES_LAST)
    here = functools.partial(per_image, images=each)
    out = call(
        input_grad_kernel, (), (n_img // each,),
        [
            (images, here(n_tok, width)),
            (gx2, here(total, width)),
            (guq, here(total, LANES)),
            (turned, once(turned.shape)),
        ]
        + [(gqkv, here(total, 3 * GROUP)) for gqkv in gqkvs],
        [((images.size // LANES, LANES), F32, whole((images.size // LANES, LANES)))],
        [pltpu.VMEM((each * total, width), F32)],
        n_img * total * 2 * width * (3 * width + LANES),
    )[0]
    out = out.reshape(n_tok, width // LANES, n_img, LANES).transpose(2, 0, 1, 3)
    return out.reshape(n_img, n_tok, width)


def turn_call(place, banks, packs):
    width = banks[0].shape[0]
    shapes = [(3 * width + LANES, width), (width, width + LANES), (LANES, width), (LANES, width)]
    return call(
        functools.partial(turn_kernel, tuple(pack[1] for pack in packs)), (place,), (1,),
        [(bank, once(bank.shape)) for bank in banks]
        + [(chunk, once(chunk.shape)) for pack in packs for chunk in pack[0]],
        [(shape, BF16, once(shape)) for shape in shapes],
        [pltpu.VMEM((width, pack[2]), BF16) for pack in packs],
        8 * width * width,
    )


def swap(array, axis, size, bit):
    return lax.ppermute(array, axis, [(i, i ^ bit) for i in range(size)])


def tie(*arrays):
    return lax.optimization_barrier(arrays)


def over_shard(spread, lines=None):
    own = lax.all_to_all(
        spread, "shard", split_axis=0, concat_axis=0, tiled=True, axis_index_groups=lines
    )
    return own.reshape(-1, spread.shape[2])


def reduce_pack(keep, give, replicas, beside_first, beside_swap, beside_spread):
    where = lax.axis_index("replica")
    bits = []
    bit = 1
    first_work = swap_work = ()
    while bit < replicas:
        got = swap(give, "replica", replicas, bit)
        if bit == 1:
            got, *first_work = tie(got, *beside_first())
        if 2 * bit == replicas:
            got, *swap_work = tie(got, *beside_swap())
        pack = (keep.astype(F32) + got.astype(F32)).astype(BF16)
        bits.append(bit)
        bit *= 2
        if bit < replicas:
            half = pack.shape[1] // 2
            side = (where // bit) % 2
            keep = lax.dynamic_slice_in_dim(pack, side * half, half, axis=1)
            give = lax.dynamic_slice_in_dim(pack, (1 - side) * half, half, axis=1)
    landed = lax.all_to_all(pack, "shard", split_axis=0, concat_axis=0, tiled=True)
    landed, *spread_work = tie(landed, *beside_spread(*first_work))
    total = jnp.sum(landed.astype(F32), axis=0).astype(BF16)
    for bit in reversed(bits):
        got = swap(total, "replica", replicas, bit)
        side = (where // bit) % 2
        total = jnp.where(
            side == 0,
            jnp.concatenate([total, got], axis=0),
            jnp.concatenate([got, total], axis=0),
        )
    return total, first_work, swap_work, spread_work


def per_device(
    replicas,
    shards,
    images,
    image_adapter_index,
    device_image_count,
    cotangent,
    query_key_value_weight,
    frozen_output_weight,
    frozen_dispatch_weight,
    query_key_value_first,
    query_key_value_second,
    output_adapter_first,
    output_adapter_second,
    dispatch_adapter_first,
    dispatch_adapter_second,
    frozen_up_weight,
    frozen_down_weight,
    up_adapter_first,
    up_adapter_second,
    down_adapter_first,
    down_adapter_second,
):
    n_img, n_tok, width = images.shape
    total = -(-n_tok // 16) * 16
    rows = width // shards
    n_loc = frozen_up_weight.shape[0]
    n_exp = n_loc * shards
    groups = width // GROUP
    quarter = lax.axis_index("replica") % 4
    place = jnp.stack(
        [quarter, lax.axis_index("shard") % 2, lax.axis_index("replica")]
    ).astype(jnp.int32)
    by_axis = shards == 2 * STRIPS and replicas == 4

    spread01 = pack_call(
        place,
        (
            query_key_value_weight, query_key_value_first, query_key_value_second.T,
            output_adapter_first, dispatch_adapter_first, output_adapter_second.T,
            frozen_dispatch_weight.T,
        ),
        STRIPS if by_axis else shards,
    )
    spread23 = later_pack_call(
        place, (query_key_value_weight, frozen_output_weight, dispatch_adapter_second.T), shards
    )
    near = functools.partial(swap, axis="replica", size=replicas, bit=1)
    far = functools.partial(swap, axis="replica", size=replicas, bit=2)
    beside = functools.partial(swap, axis="shard", size=shards, bit=1)
    cut = (width + 6 * LANES) // 4

    h1 = norm_call(images, cotangent, total)
    if by_axis:
        lines = [[2 * strip + side for strip in range(STRIPS)] for side in range(2)]
        own01, spread23, h1 = tie(over_shard(spread01, lines), spread23, h1)
        own0, own1 = own01[:, :cut], own01[:, cut:]
        beside0, far0, own1 = tie(beside(own0), far(own0), own1)
        corner0, beside1, far1 = beside(far0), beside(own1), far(own1)
        corner0, far1, spread23 = tie(corner0, far1, spread23)
        held0 = [(own0, 0, 0), (beside0, 0, 1), (far0, 2, 0), (corner0, 2, 1)]
        held1 = [(own1, 0, 0), (beside1, 0, 1), (far1, 2, 0), (beside(far1), 2, 1)]
    else:
        own01, spread23, h1 = tie(over_shard(spread01), spread23, h1)
        own0, own1 = own01[:, :cut], own01[:, cut:]
        held0 = [(own0, 0, None), (far(own0), 2, None)]
        held1 = [(own1, 0, None), (far(own1), 2, None)]
    own23 = over_shard(spread23)

    def four_pieces(held, columns):
        layout = [(replica, side, 0) for _, replica, side in held]
        layout += [(replica ^ 1, side, 0) for _, replica, side in held]
        chunks = [chunk for chunk, _, _ in held] + [near(chunk) for chunk, _, _ in held]
        return tuple(chunks), (4, tuple(layout)), columns

    pack0 = four_pieces(held0, width + 6 * LANES)
    qkv0, att0, prob0, uq, bank_a, bank_bt, bank_ao, bank_ra = first_attention_call(
        place, image_adapter_index, h1, pack0, n_tok, shards
    )
    beside1, last1, uq, own23 = tie(held1[1][0], held1[-1][0], uq, own23)
    held1[1] = (beside1,) + held1[1][1:]
    held1[-1] = (last1,) + held1[-1][1:]
    pack1 = four_pieces(held1, width + 2 * LANES)
    own2, own3 = own23[:, : width // 2], own23[:, width // 2 :]
    far3 = far(own3)
    qkv1, att1, prob1, bank_bo, bank_wr = next_attention_call(
        place, h1, uq, bank_bt, pack1, n_tok, 1, 2
    )
    att1, uq, own2, own3, far3 = tie(att1, uq, own2, own3, far3)
    pack2 = ((own2, near(own2)), (2, ((0, None, 0), (1, None, 0))), width)
    qkv2, att2, prob2 = next_attention_call(place, h1, uq, bank_bt, pack2, n_tok, 2, 0)
    pack3 = four_pieces([(own3, 0, None), (far3, 2, None)], width + 2 * LANES)
    packs = (pack0, pack1, pack2, pack3)
    atts = (att0, att1, att2)
    x2, uo, ur, disp, comb, sg, bank_wrt, bank_rb = route_call(
        place, image_adapter_index, device_image_count, images, cotangent, atts,
        (bank_ao, bank_bo, bank_ra, bank_wr), packs[3], n_exp, total, shards,
    )

    landed = lax.all_to_all(sg, "shard", split_axis=0, concat_axis=0, tiled=True)
    landed, *turned = tie(landed, *turn_call(place, (bank_ao, bank_bo, bank_ra), packs))
    turned_qkv, turned_out, turned_first, turned_route = turned
    weights = (
        frozen_up_weight, frozen_down_weight, up_adapter_first, up_adapter_second,
        down_adapter_first, down_adapter_second,
    )
    far_landed = [swap(landed, "replica", replicas, bit) for bit in range(2, replicas, 2)]
    ret, *kept = expert_call(landed, weights)
    ret, *far_landed = tie(ret, *far_landed)
    back = lax.all_to_all(ret, "shard", split_axis=0, concat_axis=0, tiled=True)
    every = [(landed, *kept)]
    for number, bit in enumerate(range(2, replicas, 2)):
        far_kept = [swap(array, "replica", replicas, bit) for array in kept]
        every.append((far_landed[number], *far_kept))

    block_out, gx2, gatt, out_pack = route_back_call(
        image_adapter_index, device_image_count, cotangent, x2, uo, ur, disp, comb, atts, back,
        (bank_wrt, bank_rb, turned_out, turned_first, turned_route), shards, replicas,
    )
    gatt, *lows = tie(gatt, *[row[3] for row in every])
    held = [array for row, low in zip(every, lows) for array in (*row[:3], low)]
    *gqkvs, guq, keep, give = attention_back_call(
        place, image_adapter_index, (qkv0, qkv1, qkv2), (prob0, prob1, prob2), gatt, uq, h1, bank_bt, out_pack
    )

    def expert_grads(block, *arrays):
        arrays = list(arrays) + [swap(array, "replica", replicas, 1) for array in arrays]
        rows_of = [tuple(arrays[place : place + 4]) for place in range(0, len(arrays), 4)]
        return expert_grad_call(rows_of, width)

    summed, (block_out, *_), (input_grad,), grads = reduce_pack(
        keep, give, replicas,
        lambda: (block_out.transpose(1, 0, 2), *held),
        lambda: (input_grad_call(images, gx2, guq, gqkvs, turned_qkv),),
        expert_grads,
    )
    block_out = block_out.transpose(1, 0, 2)
    summed = summed.astype(F32)
    return (
        block_out,
        input_grad,
        summed[3 * rows : 4 * rows],
        summed[: 3 * rows].T,
        summed[4 * rows : 5 * rows],
        summed[5 * rows : 6 * rows].T,
        summed[6 * rows : 7 * rows],
        summed[7 * rows : 7 * rows + n_loc].T,
        *grads,
    )


def solution(mesh):
    images = P(("replica", "shard"), None, None)
    each = P(("replica", "shard"))
    by_row, by_column, by_expert = P("shard", None), P(None, "shard"), P("shard", None, None)
    in_specs = (
        (images, each, each, images)
        + (by_row, by_row, by_row)
        + (by_row, by_column) * 3
        + (by_expert,) * 6
    )
    out_specs = (images, images) + (by_row, by_column) * 3 + (by_expert,) * 4
    return jax.shard_map(
        functools.partial(per_device, mesh.shape["replica"], mesh.shape["shard"]),
        mesh=mesh,
        in_specs=in_specs,
        out_specs=out_specs,
        check_vma=False,
    )
```

```python
import functools

import jax
import jax.numpy as jnp
from jax import lax
from jax.experimental import pallas as pl
from jax.experimental.pallas import tpu as pltpu
from jax.sharding import PartitionSpec as P

HEADS = 12
RANK = 16
LANES = 128
HEAD_DIM = 64
GROUP = 256
F32 = jnp.float32
BF16 = jnp.bfloat16
NN = (((1,), (0,)), ((), ()))
NT = (((1,), (1,)), ((), ()))
TN = (((0,), (0,)), ((), ()))
NEG = -1e30
VMEM_LIMIT = 56 * 1024 * 1024
GELU_C = 0.7978845608028654
GELU_A = 0.044715
IMAGES_FORWARD = 2
IMAGES_BACK = 2
IMAGES_ROUTE = 2
IMAGES_LAST = 2
STRIPS = 4


def dot(left, right, dims=NN):
    return lax.dot_general(left, right, dims, preferred_element_type=F32)


def params(*axes):
    return pltpu.CompilerParams(
        dimension_semantics=axes or None, vmem_limit_bytes=VMEM_LIMIT
    )


def cost(flops, moved, exps=0):
    return pl.CostEstimate(flops=int(flops), bytes_accessed=int(moved), transcendentals=int(exps))


def normalise(rows):
    centre = rows - jnp.mean(rows, axis=-1, keepdims=True)
    spread = jnp.mean(centre * centre, axis=-1, keepdims=True)
    scale = lax.rsqrt(spread + 1e-06)
    return centre * scale, scale


def normalise_back(unit, scale, upstream):
    inner = jnp.mean(upstream * unit, axis=-1, keepdims=True)
    return scale * (upstream - jnp.mean(upstream, axis=-1, keepdims=True) - unit * inner)


def rank_row(index):
    lane = lax.broadcasted_iota(jnp.int32, (1, LANES), 1) // RANK
    return (lane == index).astype(F32)


def zero_tail(rows, n_tok):
    total = rows.shape[0]
    cut = n_tok // 16 * 16
    if n_tok == total:
        return rows
    row = lax.broadcasted_iota(jnp.int32, (total - cut, rows.shape[1]), 0) + cut
    tail = jnp.where(row < n_tok, rows[cut:].astype(F32), 0.0).astype(rows.dtype)
    return jnp.concatenate([rows[:cut], tail], axis=0)


def mask_tail(scores, n_tok):
    total = scores.shape[0]
    cut = n_tok // 16 * 16
    if n_tok == total:
        return scores
    row = lax.broadcasted_iota(jnp.int32, (total - cut, scores.shape[1]), 0) + cut
    tail = jnp.where(row < n_tok, scores[cut:], NEG)
    return jnp.concatenate([scores[:cut], tail], axis=0)


def pad_rows(scratch, ref):
    n_img, n_tok, width = ref.shape
    total = scratch.shape[0] // n_img
    cut = n_tok // 8 * 8
    for slot in range(n_img):
        base = slot * total
        scratch[base + cut : base + total, :] = jnp.zeros((total - cut, width), F32)
        scratch[base : base + n_tok, :] = ref[slot].astype(F32)
    return scratch[...]


def select_rows(rows, index_ref, first, n_img):
    total = rows.shape[0] // n_img
    return jnp.concatenate(
        [
            (rows[i * total : (i + 1) * total] * rank_row(index_ref[first + i])).astype(BF16)
            for i in range(n_img)
        ],
        axis=0,
    )


def flat(ref):
    return ref[...].reshape(ref.shape[0] * ref.shape[1], ref.shape[2])


def assemble(place_ref, chunks, layout, wall):
    pieces, entries = layout
    part = wall.shape[1] // pieces
    for chunk, (replica, neighbour, start) in zip(chunks, entries):
        column = pl.multiple_of(((place_ref[0] % pieces) ^ replica) * part, LANES)
        if neighbour is None:
            wall[:, pl.ds(column, part)] = chunk[:, start : start + part]
            continue
        strips = STRIPS
        rows = chunk.shape[0] // strips
        for strip in range(strips):
            row = pl.multiple_of((2 * strip + (place_ref[1] ^ neighbour)) * rows, 16)
            wall[pl.ds(row, rows), pl.ds(column, part)] = chunk[
                strip * rows : (strip + 1) * rows, start : start + part
            ]


def norm_kernel(image_ref, _, out_ref, pad_ref):
    unit, _ = normalise(pad_rows(pad_ref, image_ref))
    out_ref[...] = unit.astype(BF16).reshape(out_ref.shape)


def group_columns(pack, qkv_ref, group):
    width = qkv_ref.shape[1] // 3
    for piece in range(3):
        start = piece * width + group * GROUP
        pack[:, piece * GROUP : (piece + 1) * GROUP] = qkv_ref[:, start : start + GROUP]


def own_part(place_ref, pack, pieces):
    part = pack.shape[1] // pieces
    return pack[:, pl.ds(pl.multiple_of(place_ref[0] % pieces * part, LANES), part)]


def pack_kernel(
    place_ref, qkv_ref, a_ref, b_ref, ao_ref, ra_ref, bo_ref, wr_ref, out_ref, pack0, pack1
):
    copies, rows, _ = out_ref.shape
    width = qkv_ref.shape[1] // 3
    group_columns(pack0, qkv_ref, 0)
    for piece in range(3):
        column = width + (1 + piece) * LANES
        pack0[:, column : column + LANES] = b_ref[piece * rows : (piece + 1) * rows, :]
    pack0[:, width : width + LANES] = a_ref[...]
    pack0[:, width + 4 * LANES : width + 5 * LANES] = ao_ref[...]
    pack0[:, width + 5 * LANES : width + 6 * LANES] = ra_ref[...]
    group_columns(pack1, qkv_ref, 1)
    pack1[:, width : width + LANES] = bo_ref[...]
    n_exp = wr_ref.shape[0]
    route = jnp.concatenate([wr_ref[...].astype(F32), jnp.zeros((LANES - n_exp, rows), F32)], axis=0)
    pack1[:, width + LANES :] = route.T.astype(BF16)
    mine = jnp.concatenate([own_part(place_ref, pack0, 4), own_part(place_ref, pack1, 4)], axis=1)
    for copy in range(copies):
        out_ref[copy] = mine


def later_pack_kernel(place_ref, qkv_ref, wo_ref, rb_ref, out_ref, pack2, pack3):
    shards, rows, _ = out_ref.shape
    width = wo_ref.shape[1]
    group_columns(pack2, qkv_ref, 2)
    pack3[:, :width] = wo_ref[...]
    n_loc = rb_ref.shape[0]
    second = jnp.concatenate([rb_ref[...].astype(F32), jnp.zeros((rows - n_loc, LANES), F32)], axis=0)
    pack3[:, width : width + LANES] = second.astype(BF16)
    pack3[:, width + LANES :] = jnp.zeros((rows, LANES), BF16)
    mine = jnp.concatenate([own_part(place_ref, pack2, 2), own_part(place_ref, pack3, 4)], axis=1)
    for shard in range(shards):
        out_ref[shard] = mine


def each_head(columns, value):
    head = lax.broadcasted_iota(jnp.int32, (1, GROUP), 1) // HEAD_DIM
    return jnp.concatenate(
        [
            columns * jnp.where(head == number, value, 0.0).astype(BF16)
            for number in range(GROUP // HEAD_DIM)
        ],
        axis=0,
    )


def merge_pair(low, high):
    lane = lax.broadcasted_iota(jnp.int32, (1, LANES), 1)
    return jnp.where(lane < HEAD_DIM, low, high)


def attention_forward(qkv, n_tok, prob_ref, slot):
    total = qkv.shape[0]
    every = dot(each_head(qkv[:, GROUP : 2 * GROUP], 0.125), qkv[:, :GROUP], NT)
    outs = []
    for head in range(GROUP // HEAD_DIM):
        scores = mask_tail(every[head * total : (head + 1) * total], n_tok)
        powers = jnp.exp(scores - jnp.max(scores, axis=0, keepdims=True))
        probs = (powers * (1.0 / jnp.sum(powers, axis=0, keepdims=True))).astype(BF16)
        prob_ref[slot, head] = probs
        column = 2 * GROUP + head // 2 * LANES
        outs.append(dot(probs, qkv[:, column : column + LANES], TN))
    pairs = [merge_pair(outs[head], outs[head + 1]) for head in range(0, len(outs), 2)]
    return zero_tail(jnp.concatenate(pairs, axis=1).astype(BF16), n_tok)


def first_attention_kernel(
    n_tok, shards, layout, place_ref, index_ref, h1_ref, *rest,
):
    chunks, rest = rest[: len(layout[1])], rest[len(layout[1]) :]
    qkv_ref, att_ref, prob_ref, uq_ref, a_ref, bt_ref, ao_ref, ra_ref, wall = rest
    step = pl.program_id(0)
    n_img, total, width = h1_ref.shape

    @pl.when(step == 0)
    def _():
        assemble(place_ref, chunks, layout, wall)
        a_ref[...] = wall[:, width : width + LANES]
        ao_ref[...] = wall[:, width + 4 * LANES : width + 5 * LANES]
        ra_ref[...] = wall[:, width + 5 * LANES : width + 6 * LANES]
        rows = width // shards
        for shard in range(shards):
            for part in range(3):
                bt_ref[(shard * 3 + part) * rows : (shard * 3 + part + 1) * rows, :] = wall[
                    shard * rows : (shard + 1) * rows,
                    width + (1 + part) * LANES : width + (2 + part) * LANES,
                ]

    h1 = flat(h1_ref)
    both = dot(h1, wall[:, : 3 * GROUP + LANES])
    low = both[:, 3 * GROUP :].astype(BF16).astype(F32)
    uq = select_rows(low, index_ref, step * n_img, n_img)
    uq_ref[...] = uq.reshape(uq_ref.shape)
    attend_group(0, n_tok, both[:, : 3 * GROUP], uq, bt_ref, qkv_ref, att_ref, prob_ref)


def group_rows(group, width, bt_ref):
    return jnp.concatenate(
        [bt_ref[part * width + group * GROUP : part * width + (group + 1) * GROUP, :] for part in range(3)],
        axis=0,
    )


def attend_group(group, n_tok, base, uq, bt_ref, qkv_ref, att_ref, prob_ref):
    n_img, total, _ = att_ref.shape
    second = group_rows(group, bt_ref.shape[0] // 3, bt_ref)
    qkv = (base + dot(uq, second, NT)).astype(BF16)
    qkv_ref[...] = qkv.reshape(qkv_ref.shape)
    for slot in range(n_img):
        att_ref[slot] = attention_forward(
            qkv[slot * total : (slot + 1) * total], n_tok, prob_ref, slot
        )


def next_attention_kernel(
    n_tok, group, extra, layout, place_ref, h1_ref, uq_ref, bt_ref, *rest
):
    chunks, rest = rest[: len(layout[1])], rest[len(layout[1]) :]
    qkv_ref, att_ref, prob_ref = rest[:3]
    wall = rest[-1]

    @pl.when(pl.program_id(0) == 0)
    def _():
        assemble(place_ref, chunks, layout, wall)
        for position in range(extra):
            column = 3 * GROUP + position * LANES
            rest[3 + position][...] = wall[:, column : column + LANES]

    attend_group(
        group, n_tok, dot(flat(h1_ref), wall[:, : 3 * GROUP]), flat(uq_ref), bt_ref, qkv_ref, att_ref, prob_ref,
    )


def route_kernel(
    n_exp, shards, layout, place_ref, index_ref, count_ref, image_ref, cot_ref, att0, att1, att2,
    ao_ref, bo_ref, ra_ref, wr_ref, *rest,
):
    chunks, rest = rest[: len(layout[1])], rest[len(layout[1]) :]
    x2_ref, uo_ref, ur_ref, disp_ref, comb_ref, sg_ref, wrt_ref, rb_ref, *rest = rest
    wall, rb_f, pair_ref, pad_a, pad_b, sent_ref = rest
    every = sg_ref.shape[2]
    n_img, n_tok, width = image_ref.shape
    first = pl.program_id(0) * n_img
    total = x2_ref.shape[1]

    @pl.when(first == 0)
    def _():
        assemble(place_ref, chunks, layout, wall)
        wrt_ref[...] = wr_ref[...].astype(F32).T[:n_exp].astype(BF16)
        n_loc, rows = n_exp // shards, width // shards
        for shard in range(shards):
            rb_f[shard * n_loc : (shard + 1) * n_loc, :] = wall[
                shard * rows : shard * rows + 8, width : width + LANES
            ].astype(F32)[:n_loc]
        rb_ref[...] = rb_f[...].astype(BF16)
        wall[:, width : width + LANES] = ao_ref[...]
        pair_ref[:, :LANES] = ra_ref[...]
        pair_ref[:, LANES:] = wr_ref[...]

    att = jnp.concatenate([flat(att0), flat(att1), flat(att2)], axis=1)
    both = dot(att, wall[:, : width + LANES])
    uo = select_rows(both[:, width:].astype(BF16).astype(F32), index_ref, first, n_img)
    uo_ref[...] = uo.reshape(uo_ref.shape)
    x2 = pad_rows(pad_a, image_ref) + both[:, :width] + dot(uo, bo_ref[...], NT)
    x2_ref[...] = x2.reshape(x2_ref.shape)
    h2 = normalise(x2)[0].astype(BF16)
    both = dot(h2, pair_ref[...])
    ur = select_rows(both[:, :LANES].astype(BF16).astype(F32), index_ref, first, n_img)
    base = both[:, LANES:]
    ur_ref[...] = ur.reshape(ur_ref.shape)
    cot = pad_rows(pad_b, cot_ref)
    firsts = []
    for slot in range(n_img):
        rows = slice(slot * total, (slot + 1) * total)
        living = (first + slot < count_ref[0]).astype(F32)
        logits = base[rows].T[:n_exp] + dot(rb_ref[...], ur[rows], NT)
        alive = lax.broadcasted_iota(jnp.int32, logits.shape, 1) < n_tok
        over_tokens = jnp.where(alive, logits, NEG)
        powers = jnp.exp(over_tokens - jnp.max(over_tokens, axis=1, keepdims=True))
        disp = powers / jnp.sum(powers, axis=1, keepdims=True)
        powers = jnp.exp(logits - jnp.max(logits, axis=0, keepdims=True))
        comb = jnp.where(alive, powers / jnp.sum(powers, axis=0, keepdims=True), 0.0)
        disp_ref[slot] = disp
        comb_ref[slot] = comb
        upstream = (cot[rows] * living).astype(BF16)
        firsts.append((rows, disp, comb, upstream))
    for slot, (rows, disp, comb, upstream) in enumerate(firsts):
        sent = jnp.concatenate(
            [
                dot(disp.astype(BF16), h2[rows]),
                dot(comb.astype(BF16), upstream),
                jnp.broadcast_to(rank_row(index_ref[first + slot]), (n_exp, LANES)),
            ],
            axis=1,
        )
        for block in range(sent.shape[1] // LANES):
            start = block * n_exp * every + first + slot
            sent_ref[pl.ds(start, n_exp, stride=every), :] = sent[:, block * LANES : (block + 1) * LANES]

    @pl.when(pl.program_id(0) == pl.num_programs(0) - 1)
    def _():
        for block in range(sg_ref.shape[3] // LANES):
            span = slice(block * LANES, (block + 1) * LANES)
            piece = sent_ref[block * n_exp * every : (block + 1) * n_exp * every, :]
            sg_ref[:, :, :, span] = piece.reshape(sg_ref.shape[:3] + (LANES,)).astype(BF16)


def gelu_both(pre):
    square = pre * pre
    half = jnp.tanh(GELU_C * pre * (1.0 + GELU_A * square))
    both = 0.5 * (1.0 + half)
    slope = both + 0.5 * pre * (1.0 - half * half) * (GELU_C * (1.0 + 3.0 * GELU_A * square))
    return pre * both, slope


def expert_tile(slots, gy, u1, gu2, wu_ref, wd_ref, ub_ref, da_ref):
    ghid = (dot(wd_ref[0], gy, NT) + dot(da_ref[0], gu2, NT)).T
    pre = dot(slots, wu_ref[0]) + dot(u1, ub_ref[0])
    hidden, slope = gelu_both(pre)
    return hidden.astype(BF16), (slope * ghid).astype(BF16)


def gather_rows(part_refs, out_ref):
    rows = part_refs[0].shape[0] * part_refs[0].shape[2]
    for number, part_ref in enumerate(part_refs):
        part = part_ref[:, 0].astype(F32).reshape(rows, part_ref.shape[3])
        out_ref[number * rows : (number + 1) * rows, :] = part.astype(BF16)


def expert_kernel(
    wu_ref, wd_ref, ua_ref, ub_ref, da_ref, db_ref, part_ref, out_ref, hidden_ref, gpre_ref, low_ref,
    sg_ref, u1_ref, gu2_ref, acc_y, acc_s, acc_u2, acc_gu1,
):
    step = pl.program_id(1)
    width = wu_ref.shape[1]

    @pl.when(step == 0)
    def _():
        gather_rows((part_ref,), sg_ref)
        selector = sg_ref[:, 2 * width :].astype(F32)
        u1_ref[...] = (
            dot(sg_ref[:, :width], ua_ref[0]).astype(BF16).astype(F32) * selector
        ).astype(BF16)
        gu2_ref[...] = (dot(sg_ref[:, width : 2 * width], db_ref[0], NT) * selector).astype(BF16)
        acc_y[...] = jnp.zeros_like(acc_y)
        acc_s[...] = jnp.zeros_like(acc_s)
        acc_u2[...] = jnp.zeros_like(acc_u2)
        acc_gu1[...] = jnp.zeros_like(acc_gu1)

    hidden, gpre = expert_tile(
        sg_ref[:, :width], sg_ref[:, width : 2 * width], u1_ref[...], gu2_ref[...],
        wu_ref, wd_ref, ub_ref, da_ref,
    )
    hidden_ref[0] = hidden
    gpre_ref[0] = gpre
    acc_y[...] += dot(hidden, wd_ref[0])
    acc_u2[...] += dot(hidden, da_ref[0])
    acc_s[...] += dot(wu_ref[0], gpre, NT)
    acc_gu1[...] += dot(ub_ref[0], gpre, NT)

    @pl.when(step == pl.num_programs(1) - 1)
    def _():
        selector = sg_ref[:, 2 * width :].astype(F32)
        u2 = (acc_u2[...].astype(BF16).astype(F32) * selector).astype(BF16)
        gu1 = (acc_gu1[...].T * selector).astype(BF16)
        shards, _, n_img, _ = out_ref.shape
        result = acc_y[...] + dot(u2, db_ref[0])
        out_ref[:, 0, :, :width] = result.reshape(shards, n_img, width).astype(BF16)
        result = acc_s[...].T + dot(gu1, ua_ref[0], NT)
        out_ref[:, 0, :, width:] = result.reshape(shards, n_img, width).astype(BF16)
        for place, low in enumerate((u1_ref[...], u2, gu1, gu2_ref[...])):
            low_ref[0, :, place * LANES : (place + 1) * LANES] = low


def expert_grad_kernel(copies, *refs):
    refs = list(refs)
    part_refs, hidden_refs, gpre_refs, low_refs = (
        [refs.pop(0) for _ in range(copies)] for _ in range(4)
    )
    gua_ref, gub_ref, gda_ref, gdb_ref, sg_ref, low_t, rows_ref = refs
    rows = hidden_refs[0].shape[1]
    width = gua_ref.shape[1]

    @pl.when(pl.program_id(1) == 0)
    def _():
        gather_rows(part_refs, sg_ref)
        low = jnp.concatenate([ref[0] for ref in low_refs], axis=0)
        low_t[...] = low.astype(F32).T.astype(BF16)
        u2_t, gu1_t = low_t[LANES : 2 * LANES, :], low_t[2 * LANES : 3 * LANES, :]
        gdb_ref[0] = dot(u2_t, sg_ref[:, width : 2 * width])
        gua_ref[0] = dot(gu1_t, sg_ref[:, :width]).T

    for number in range(copies):
        rows_ref[number * rows : (number + 1) * rows, :] = gpre_refs[number][0]
    gub_ref[0] = dot(low_t[:LANES, :], rows_ref[...])
    for number in range(copies):
        rows_ref[number * rows : (number + 1) * rows, :] = hidden_refs[number][0]
    gda_ref[0] = dot(low_t[3 * LANES :, :], rows_ref[...]).T


def turn_kernel(layouts, place_ref, ao_ref, bo_ref, ra_ref, *refs):
    refs = list(refs)
    chunks = [[refs.pop(0) for _ in layout[1]] for layout in layouts]
    qkv_ref, out_ref, first_ref, route_ref = refs[:4]
    walls = refs[4:]
    for chunk, layout, wall in zip(chunks, layouts, walls):
        assemble(place_ref, chunk, layout, wall)
    width = walls[0].shape[0]
    for group, wall in enumerate(walls[:-1]):
        qkv_ref[group * 3 * GROUP : (group + 1) * 3 * GROUP, :] = wall[:, : 3 * GROUP].T
    qkv_ref[3 * width :, :] = walls[0][:, 3 * GROUP : 3 * GROUP + LANES].T
    out_ref[:, :width] = walls[-1][:, :width].T
    out_ref[:, width:] = bo_ref[...]
    first_ref[...] = ao_ref[...].T
    route_ref[...] = ra_ref[...].T


def route_back_kernel(
    n_exp, index_ref, count_ref, cot_ref, x2_ref, uo_ref, ur_ref, disp_ref, comb_ref,
    att0, att1, att2, ret_ref, wrt_ref, rb_ref, out_ref, first_ref, route_ref,
    block_ref, gx2_ref, gatt_ref, pack_ref, pad_b, back_ref, acc_oa, acc_ob, acc_ra, acc_rb,
):
    n_img, n_tok, width = cot_ref.shape
    first = pl.program_id(0) * n_img
    total = x2_ref.shape[1]

    every = ret_ref.shape[2]

    @pl.when(first == 0)
    def _():
        for block in range(2 * width // LANES):
            piece = ret_ref[:, :, :, block * LANES : (block + 1) * LANES].astype(F32)
            back_ref[block * n_exp * every : (block + 1) * n_exp * every, :] = piece.reshape(
                n_exp * every, LANES
            )
        acc_oa[...] = jnp.zeros_like(acc_oa)
        acc_ob[...] = jnp.zeros_like(acc_ob)
        acc_ra[...] = jnp.zeros_like(acc_ra)
        acc_rb[...] = jnp.zeros_like(acc_rb)

    cot = pad_rows(pad_b, cot_ref)
    x2 = flat(x2_ref)
    unit, scale = normalise(x2)
    h2 = unit.astype(BF16)
    pairs, belows, upstreams, mixes, firsts = [], [], [], [], []
    for slot in range(n_img):
        rows = slice(slot * total, (slot + 1) * total)
        living = (first + slot < count_ref[0]).astype(F32)
        upstream = cot[rows] * living
        upstreams.append(upstream)
        disp, comb = disp_ref[slot], comb_ref[slot]
        blocks = [
            back_ref[pl.ds(block * n_exp * every + first + slot, n_exp, stride=every), :]
            for block in range(2 * width // LANES)
        ]
        back = jnp.concatenate(blocks, axis=1).astype(BF16)
        yexp, gslot = back[:, :width], back[:, width:]
        gcomb = dot(yexp, upstream.astype(BF16), NT)
        gdisp = dot(gslot, h2[rows], NT)
        firsts.append((rows, living, disp, comb, yexp, gslot, gcomb, gdisp))
    for slot, (rows, living, disp, comb, yexp, gslot, gcomb, gdisp) in enumerate(firsts):
        glog = (
            disp * (gdisp - jnp.sum(gdisp * disp, axis=1, keepdims=True))
            + comb * (gcomb - jnp.sum(gcomb * comb, axis=0, keepdims=True))
        )
        acc_rb[...] += dot(glog.astype(BF16), ur_ref[slot])
        three = jnp.concatenate([disp, glog, comb], axis=0).T.astype(BF16)
        mixes.append((living, three[:, 2 * n_exp :], yexp, rows))
        pairs.append(three[:, : 2 * n_exp])
        belows.append(jnp.concatenate([route_ref[...], gslot, wrt_ref[...]], axis=0))
    glog_rows = jnp.concatenate([pair[:, n_exp:] for pair in pairs], axis=0)
    gur = select_rows(dot(glog_rows, rb_ref[...]), index_ref, first, n_img)
    gh2 = jnp.concatenate(
        [
            dot(jnp.concatenate([gur[i * total : (i + 1) * total], pairs[i]], axis=1), belows[i])
            for i in range(n_img)
        ],
        axis=0,
    )
    gx2 = jnp.concatenate(upstreams, axis=0) + normalise_back(unit, scale, gh2)
    gbr = gx2.astype(BF16)
    gx2_ref[...] = gbr.reshape(gx2_ref.shape)
    both = dot(gbr, out_ref[...])
    guo = select_rows(both[:, width:], index_ref, first, n_img)
    att = jnp.concatenate([flat(att0), flat(att1), flat(att2)], axis=1)
    gatt = (both[:, :width] + dot(guo, first_ref[...])).astype(BF16)
    gatt_ref[...] = gatt.reshape(gatt_ref.shape)
    acc_ra[...] += dot(gur, h2, TN)
    acc_ob[...] += dot(flat(uo_ref), gbr, TN)
    acc_oa[...] += dot(guo, att, TN)
    for slot, (living, left, yexp, rows) in enumerate(mixes):
        block_ref[slot] = (living * (x2[rows] + dot(left, yexp))).astype(BF16)[:n_tok]

    @pl.when(pl.program_id(0) == pl.num_programs(0) - 1)
    def _():
        shards = pack_ref.shape[0]
        rows = width // shards
        n_loc = n_exp // shards
        for position, acc in enumerate((acc_oa, acc_ob, acc_ra)):
            summed = acc[...].T.astype(BF16)
            for shard in range(shards):
                pack_ref[shard, position * rows : (position + 1) * rows, :] = summed[
                    shard * rows : (shard + 1) * rows
                ]
        tail = pack_ref.shape[1] - 3 * rows
        for shard in range(shards):
            last = jnp.concatenate(
                [acc_rb[shard * n_loc : (shard + 1) * n_loc, :], jnp.zeros((tail - n_loc, LANES), F32)],
                axis=0,
            )
            pack_ref[shard, 3 * rows :, :] = last.astype(BF16)


def attention_backward(qkv, gatt, prob_ref, slot):
    total = qkv.shape[0]
    heads = GROUP // HEAD_DIM
    every = dot(each_head(qkv[:, 2 * GROUP :], 1.0), gatt, NT)
    gscores = []
    for head in range(heads):
        probs = prob_ref[slot, head].astype(F32)
        gprobs = every[head * total : (head + 1) * total]
        inner = jnp.sum(gprobs * probs, axis=0, keepdims=True)
        gscores.append((probs * (gprobs - inner)).astype(BF16))

    def products(lefts, right):
        outs = []
        for pair in range(heads // 2):
            both = dot(
                jnp.concatenate(lefts[2 * pair : 2 * pair + 2], axis=0),
                right[:, pair * LANES : (pair + 1) * LANES],
            )
            outs.append(merge_pair(both[:total], both[total:]))
        return outs

    gv = [part.astype(BF16) for part in products([prob_ref[slot, head] for head in range(heads)], gatt)]
    gk = [(part * 0.125).astype(BF16) for part in products(gscores, qkv[:, :GROUP])]
    key_t = qkv[:, GROUP : 2 * GROUP].T
    gq = [
        (dot(key_t[head * HEAD_DIM : (head + 1) * HEAD_DIM], gscores[head]) * 0.125).astype(BF16)
        for head in range(heads)
    ]
    return jnp.concatenate([jnp.concatenate(gq, axis=0).T] + gk + gv, axis=1)


def attention_back_kernel(groups, place_ref, index_ref, *refs):
    refs = list(refs)
    qkv_refs = [refs.pop(0) for _ in range(groups)]
    prob_refs = [refs.pop(0) for _ in range(groups)]
    gatt_ref, uq_ref, h1_ref, bt_ref, others_ref = refs[:5]
    refs = refs[5:]
    gqkv_refs = [refs.pop(0) for _ in range(groups)]
    guq_ref, keep_ref, give_ref, pack_ref, acc_b, acc_a = refs
    step = pl.program_id(0)
    n_img, total, width = h1_ref.shape

    @pl.when(step == 0)
    def _():
        acc_b[...] = jnp.zeros_like(acc_b)
        acc_a[...] = jnp.zeros_like(acc_a)

    uq_t = flat(uq_ref).T
    guq = None
    gqkvs = []
    for group in range(groups):
        parts = []
        for i in range(n_img):
            part = attention_backward(
                qkv_refs[group][i], gatt_ref[i, :, group * GROUP : (group + 1) * GROUP],
                prob_refs[group], i,
            )
            gqkv_refs[group][i] = part
            parts.append(part)
        gqkv = jnp.concatenate(parts, axis=0)
        part = dot(gqkv, group_rows(group, width, bt_ref))
        guq = part if guq is None else guq + part
        gqkvs.append(gqkv)
    for group, gqkv in enumerate(gqkvs):
        acc_b[:, group * 3 * GROUP : (group + 1) * 3 * GROUP] += dot(uq_t, gqkv)
    guq = select_rows(guq, index_ref, step * n_img, n_img)
    acc_a[...] += dot(guq, flat(h1_ref), TN)
    guq_ref[...] = guq.reshape(guq_ref.shape)

    @pl.when(step == pl.num_programs(0) - 1)
    def _():
        shards = pack_ref.shape[0]
        rows = width // shards
        pack_ref[:, 4 * rows :, :] = others_ref[...]
        own = acc_a[...].T.astype(BF16)
        for shard in range(shards):
            pack_ref[shard, 3 * rows : 4 * rows, :] = own[shard * rows : (shard + 1) * rows]
        for group in range(groups):
            summed = acc_b[:, group * 3 * GROUP : (group + 1) * 3 * GROUP].T.astype(BF16)
            for part in range(3):
                start = part * width + group * GROUP
                place = start
                while place < start + GROUP:
                    shard, offset = divmod(place, 3 * rows)
                    length = min(start + GROUP - place, 3 * rows - offset)
                    take = part * GROUP + place - start
                    pack_ref[shard, offset : offset + length, :] = summed[take : take + length]
                    place += length
        half = keep_ref.shape[1]
        side = place_ref[2] % 2
        keep_ref[...] = pack_ref[:, pl.ds(pl.multiple_of(side * half, 16), half), :]
        give_ref[...] = pack_ref[:, pl.ds(pl.multiple_of((1 - side) * half, 16), half), :]


def input_grad_kernel(image_ref, gx2_ref, guq_ref, turned_ref, *refs):
    *gqkv, out_ref, pad_a = refs
    n_img, n_tok, width = image_ref.shape
    step = pl.program_id(0)
    parts = width // LANES
    every = out_ref.shape[0] // (n_tok * parts)
    total = gx2_ref.shape[1]
    gh1 = dot(jnp.concatenate([flat(ref) for ref in gqkv] + [flat(guq_ref)], axis=1), turned_ref[...])
    unit, scale = normalise(pad_rows(pad_a, image_ref))
    result = flat(gx2_ref).astype(F32) + normalise_back(unit, scale, gh1)
    for slot in range(n_img):
        for part in range(parts):
            out_ref[pl.ds(part * every + step * n_img + slot, n_tok, stride=parts * every), :] = result[
                slot * total : slot * total + n_tok, part * LANES : (part + 1) * LANES
            ]


ANY = pl.BlockSpec(memory_space=pl.ANY)


def whole(shape):
    return pl.BlockSpec(shape, lambda *_: (0,) * len(shape))


def once(shape):
    return pl.BlockSpec(shape, lambda *_: (0,) * len(shape), pipeline_mode=pl.Buffered(1))


def per_image(*shape, images=1):
    return pl.BlockSpec((images,) + shape, lambda i, *_: (i,) + (0,) * len(shape))


def several(images, limit):
    return max(n for n in range(1, limit + 1) if images % n == 0)


def call(kernel, scalars, grid, inputs, outputs, scratch, flops, exps=0, aliases=None):
    arrays = [array for array, _ in inputs]
    shapes = [jax.ShapeDtypeStruct(shape, dtype) for shape, dtype, _ in outputs]
    moved = sum(array.size * array.dtype.itemsize for array in arrays) + sum(
        shape.size * shape.dtype.itemsize for shape in shapes
    )
    return pl.pallas_call(
        kernel,
        out_shape=shapes,
        grid_spec=pltpu.PrefetchScalarGridSpec(
            num_scalar_prefetch=len(scalars),
            grid=grid,
            in_specs=[spec for _, spec in inputs],
            out_specs=[spec for _, _, spec in outputs],
            scratch_shapes=scratch,
        ),
        input_output_aliases=aliases or {},
        compiler_params=params(*(("arbitrary",) * len(grid))),
        cost_estimate=cost(flops, moved, exps),
    )(*scalars, *arrays)


def norm_call(images, cotangent, total):
    n_img, n_tok, width = images.shape
    each = several(n_img, 4)
    return call(
        norm_kernel, (), (n_img // each,),
        [(images, per_image(n_tok, width, images=each)), (cotangent, ANY)],
        [((n_img, total, width), BF16, per_image(total, width, images=each))],
        [pltpu.VMEM((each * total, width), F32)],
        8 * images.size,
    )[0]


def pack_call(place, weights, copies):
    rows, columns = weights[0].shape
    width = columns // 3
    wide = [width + 6 * LANES, width + 2 * LANES]
    out = (copies, rows, sum(wide) // 4)
    return call(
        pack_kernel, (place,), (1,), [(weight, whole(weight.shape)) for weight in weights],
        [(out, BF16, whole(out))], [pltpu.VMEM((rows, each), BF16) for each in wide], rows * columns,
    )[0]


def later_pack_call(place, weights, shards):
    rows, width = weights[1].shape
    out = (shards, rows, width // 2 + (width + 2 * LANES) // 4)
    return call(
        later_pack_kernel, (place,), (1,), [(weight, whole(weight.shape)) for weight in weights],
        [(out, BF16, whole(out))],
        [pltpu.VMEM((rows, each), BF16) for each in (width, width + 2 * LANES)], rows * width,
    )[0]


def attention_flops(n_img, total, width, parts):
    return n_img * total * (2 * width * 3 * GROUP + parts * 8 * total * HEAD_DIM)


def attention_outputs(n_img, total, each):
    return [
        ((n_img, total, 3 * GROUP), BF16, per_image(total, 3 * GROUP, images=each)),
        ((n_img, total, GROUP), BF16, per_image(total, GROUP, images=each)),
        (
            (n_img, GROUP // HEAD_DIM, total, total), BF16,
            per_image(GROUP // HEAD_DIM, total, total, images=each),
        ),
    ]


def first_attention_call(place, index, h1, pack, n_tok, shards):
    n_img, total, width = h1.shape
    chunks, layout, columns = pack
    each = several(n_img, IMAGES_FORWARD)
    return call(
        functools.partial(first_attention_kernel, n_tok, shards, layout), (place, index), (n_img // each,),
        [(h1, per_image(total, width, images=each))] + [(chunk, once(chunk.shape)) for chunk in chunks],
        attention_outputs(n_img, total, each)
        + [
            ((n_img, total, LANES), BF16, per_image(total, LANES, images=each)),
            ((width, LANES), BF16, whole((width, LANES))),
            ((3 * width, LANES), BF16, whole((3 * width, LANES))),
            ((width, LANES), BF16, whole((width, LANES))),
            ((width, LANES), BF16, whole((width, LANES))),
        ],
        [pltpu.VMEM((width, columns), BF16)],
        attention_flops(n_img, total, width, 2), n_img * total * total * 4,
    )


def next_attention_call(place, h1, uq, bt, pack, n_tok, group, extra):
    n_img, total, width = h1.shape
    chunks, layout, columns = pack
    each = several(n_img, IMAGES_FORWARD)
    return call(
        functools.partial(next_attention_kernel, n_tok, group, extra, layout), (place,), (n_img // each,),
        [
            (h1, per_image(total, width, images=each)),
            (uq, per_image(total, LANES, images=each)),
            (bt, whole(bt.shape)),
        ]
        + [(chunk, once(chunk.shape)) for chunk in chunks],
        attention_outputs(n_img, total, each)
        + [((width, LANES), BF16, whole((width, LANES)))] * extra,
        [pltpu.VMEM((width, columns), BF16)],
        attention_flops(n_img, total, width, 2), n_img * total * total * 4,
    )


def route_call(place, index, count, images, cotangent, atts, banks, pack, n_exp, total, shards):
    n_img, n_tok, width = images.shape
    chunks, layout, columns = pack
    each = several(n_img, IMAGES_ROUTE)
    here = functools.partial(per_image, images=each)
    sent = (shards, n_exp // shards, n_img, 2 * width + LANES)
    return call(
        functools.partial(route_kernel, n_exp, shards, layout), (place, index, count), (n_img // each,),
        [(images, here(n_tok, width)), (cotangent, here(n_tok, width))]
        + [(att, here(total, GROUP)) for att in atts]
        + [(bank, whole(bank.shape)) for bank in banks]
        + [(chunk, once(chunk.shape)) for chunk in chunks],
        [
            ((n_img, total, width), F32, here(total, width)),
            ((n_img, total, LANES), BF16, here(total, LANES)),
            ((n_img, total, LANES), BF16, here(total, LANES)),
            ((n_img, n_exp, total), F32, here(n_exp, total)),
            ((n_img, n_exp, total), F32, here(n_exp, total)),
            (sent, BF16, whole(sent)),
            ((n_exp, width), BF16, whole((n_exp, width))),
            ((n_exp, LANES), BF16, whole((n_exp, LANES))),
        ],
        [
            pltpu.VMEM((width, columns), BF16),
            pltpu.VMEM((n_exp, LANES), F32),
            pltpu.VMEM((width, 2 * LANES), BF16),
            pltpu.VMEM((each * total, width), F32),
            pltpu.VMEM((each * total, width), F32),
            pltpu.VMEM(((2 * width // LANES + 1) * n_exp * n_img, LANES), F32),
        ],
        n_img * total * 2 * width * (width + 3 * LANES), n_img * total * 2 * n_exp,
    )


def hidden_tile(hidden, limit):
    tile = hidden
    while tile > limit:
        tile //= 2
    return tile


def expert_specs(width, tile, first=0):
    return (
        pl.BlockSpec((1, width, tile), lambda e, f: (e + first, 0, f)),
        pl.BlockSpec((1, tile, width), lambda e, f: (e + first, f, 0)),
        pl.BlockSpec((1, width, LANES), lambda e, f: (e + first, 0, 0)),
        pl.BlockSpec((1, LANES, tile), lambda e, f: (e + first, 0, f)),
        pl.BlockSpec((1, tile, LANES), lambda e, f: (e + first, f, 0)),
        pl.BlockSpec((1, LANES, width), lambda e, f: (e + first, 0, 0)),
    )


def expert_rows(shape, first=0):
    shards, _, n_img, columns = shape
    return pl.BlockSpec((shards, 1, n_img, columns), lambda e, f: (0, e + first, 0, 0))


def expert_call(landed, weights):
    shards, n_loc, n_img, columns = landed.shape
    rows = shards * n_img
    width, hidden = weights[0].shape[1:]
    tile = hidden_tile(hidden, 1536)
    out = (shards, n_loc, n_img, 2 * width)
    tiled = pl.BlockSpec((1, rows, tile), lambda e, f: (e, 0, f))
    return call(
        expert_kernel, (), (n_loc, hidden // tile),
        list(zip(weights, expert_specs(width, tile))) + [(landed, expert_rows(landed.shape))],
        [
            (out, BF16, expert_rows(out)),
            ((n_loc, rows, hidden), BF16, tiled),
            ((n_loc, rows, hidden), BF16, tiled),
            (
                (n_loc, rows, 4 * LANES), BF16,
                pl.BlockSpec((1, rows, 4 * LANES), lambda e, f: (e, 0, 0)),
            ),
        ],
        [
            pltpu.VMEM((rows, columns), BF16),
            pltpu.VMEM((rows, LANES), BF16),
            pltpu.VMEM((rows, LANES), BF16),
            pltpu.VMEM((rows, width), F32),
            pltpu.VMEM((width, rows), F32),
            pltpu.VMEM((rows, LANES), F32),
            pltpu.VMEM((LANES, rows), F32),
        ],
        n_loc * rows * 8 * width * hidden, n_loc * rows * hidden,
    )


def expert_grad_call(every, width):
    parts, hiddens, gpres, lows = zip(*every)
    shards, n_loc, n_img, columns = parts[0].shape
    rows, hidden = hiddens[0].shape[1:]
    total = rows * len(every)
    tile = hidden_tile(hidden, 1536 if total <= 512 else 384)
    tiled = pl.BlockSpec((1, rows, tile), lambda e, f: (e, 0, f))
    low = pl.BlockSpec((1, rows, 4 * LANES), lambda e, f: (e, 0, 0))
    return call(
        functools.partial(expert_grad_kernel, len(every)), (), (n_loc, hidden // tile),
        [(part, expert_rows(part.shape)) for part in parts]
        + [(array, tiled) for array in hiddens + gpres]
        + [(array, low) for array in lows],
        [
            ((n_loc, width, LANES), F32, pl.BlockSpec((1, width, LANES), lambda e, f: (e, 0, 0))),
            ((n_loc, LANES, hidden), F32, pl.BlockSpec((1, LANES, tile), lambda e, f: (e, 0, f))),
            ((n_loc, hidden, LANES), F32, pl.BlockSpec((1, tile, LANES), lambda e, f: (e, f, 0))),
            ((n_loc, LANES, width), F32, pl.BlockSpec((1, LANES, width), lambda e, f: (e, 0, 0))),
        ],
        [
            pltpu.VMEM((total, columns), BF16),
            pltpu.VMEM((4 * LANES, total), BF16),
            pltpu.VMEM((total, tile), BF16),
        ],
        4 * n_loc * total * LANES * hidden,
    )


def route_back_call(
    index, count, cotangent, x2, uo, ur, disp, comb, atts, ret, banks, shards, replicas
):
    n_img, n_tok, width = cotangent.shape
    total, n_exp = x2.shape[1], disp.shape[1]
    rows = width // shards
    unit = 16 * replicas
    pack_rows = -(-(7 * rows + n_exp // shards) // unit) * unit - 4 * rows
    each = several(n_img, IMAGES_ROUTE)
    here = functools.partial(per_image, images=each)
    return call(
        functools.partial(route_back_kernel, n_exp), (index, count), (n_img // each,),
        [
            (cotangent, here(n_tok, width)),
            (x2, here(total, width)),
            (uo, here(total, LANES)),
            (ur, here(total, LANES)),
            (disp, here(n_exp, total)),
            (comb, here(n_exp, total)),
        ]
        + [(att, here(total, GROUP)) for att in atts]
        + [(ret, once(ret.shape))]
        + [(bank, once(bank.shape)) for bank in banks],
        [
            ((n_img, n_tok, width), BF16, here(n_tok, width)),
            ((n_img, total, width), BF16, here(total, width)),
            ((n_img, total, width), BF16, here(total, width)),
            ((shards, pack_rows, LANES), BF16, whole((shards, pack_rows, LANES))),
        ],
        [
            pltpu.VMEM((each * total, width), F32),
            pltpu.VMEM((2 * width // LANES * n_exp * n_img, LANES), F32),
            pltpu.VMEM((LANES, width), F32),
            pltpu.VMEM((LANES, width), F32),
            pltpu.VMEM((LANES, width), F32),
            pltpu.VMEM((n_exp, LANES), F32),
        ],
        n_img * total * 2 * width * (width + 6 * LANES),
    )


def attention_back_call(place, index, qkvs, probs, gatt, uq, h1, bt, others):
    n_img, total, width = h1.shape
    groups = len(qkvs)
    shards = others.shape[0]
    each = several(n_img, IMAGES_BACK)
    here = functools.partial(per_image, images=each)
    pack = (shards, 4 * width // shards + others.shape[1], LANES)
    half = (shards, pack[1] // 2, LANES)
    return call(
        functools.partial(attention_back_kernel, groups), (place, index), (n_img // each,),
        [(qkv, here(total, 3 * GROUP)) for qkv in qkvs]
        + [(prob, here(GROUP // HEAD_DIM, total, total)) for prob in probs]
        + [
            (gatt, here(total, width)),
            (uq, here(total, LANES)),
            (h1, here(total, width)),
            (bt, whole(bt.shape)),
            (others, whole(others.shape)),
        ],
        [((n_img, total, 3 * GROUP), BF16, here(total, 3 * GROUP))] * groups
        + [((n_img, total, LANES), BF16, here(total, LANES))]
        + [(half, BF16, whole(half))] * 2,
        [
            pltpu.VMEM(pack, BF16),
            pltpu.VMEM((LANES, 3 * width), F32),
            pltpu.VMEM((LANES, width), F32),
        ],
        groups * attention_flops(n_img, total, LANES, 5), groups * n_img * total * total * 4,
    )


def input_grad_call(images, gx2, guq, gqkvs, turned):
    n_img, n_tok, width = images.shape
    total = gx2.shape[1]
    each = several(n_img, IMAGES_LAST)
    here = functools.partial(per_image, images=each)
    out = call(
        input_grad_kernel, (), (n_img // each,),
        [
            (images, here(n_tok, width)),
            (gx2, here(total, width)),
            (guq, here(total, LANES)),
            (turned, once(turned.shape)),
        ]
        + [(gqkv, here(total, 3 * GROUP)) for gqkv in gqkvs],
        [((images.size // LANES, LANES), F32, whole((images.size // LANES, LANES)))],
        [pltpu.VMEM((each * total, width), F32)],
        n_img * total * 2 * width * (3 * width + LANES),
    )[0]
    out = out.reshape(n_tok, width // LANES, n_img, LANES).transpose(2, 0, 1, 3)
    return out.reshape(n_img, n_tok, width)


def turn_call(place, banks, packs):
    width = banks[0].shape[0]
    shapes = [(3 * width + LANES, width), (width, width + LANES), (LANES, width), (LANES, width)]
    return call(
        functools.partial(turn_kernel, tuple(pack[1] for pack in packs)), (place,), (1,),
        [(bank, once(bank.shape)) for bank in banks]
        + [(chunk, once(chunk.shape)) for pack in packs for chunk in pack[0]],
        [(shape, BF16, once(shape)) for shape in shapes],
        [pltpu.VMEM((width, pack[2]), BF16) for pack in packs],
        8 * width * width,
    )


def swap(array, axis, size, bit):
    return lax.ppermute(array, axis, [(i, i ^ bit) for i in range(size)])


def tie(*arrays):
    return lax.optimization_barrier(arrays)


def over_shard(spread, lines=None):
    own = lax.all_to_all(
        spread, "shard", split_axis=0, concat_axis=0, tiled=True, axis_index_groups=lines
    )
    return own.reshape(-1, spread.shape[2])


def reduce_pack(keep, give, replicas, beside_first, beside_swap, beside_spread):
    where = lax.axis_index("replica")
    bits = []
    bit = 1
    first_work = swap_work = ()
    while bit < replicas:
        got = swap(give, "replica", replicas, bit)
        if bit == 1:
            got, *first_work = tie(got, *beside_first())
        if 2 * bit == replicas:
            got, *swap_work = tie(got, *beside_swap())
        pack = (keep.astype(F32) + got.astype(F32)).astype(BF16)
        bits.append(bit)
        bit *= 2
        if bit < replicas:
            half = pack.shape[1] // 2
            side = (where // bit) % 2
            keep = lax.dynamic_slice_in_dim(pack, side * half, half, axis=1)
            give = lax.dynamic_slice_in_dim(pack, (1 - side) * half, half, axis=1)
    landed = lax.all_to_all(pack, "shard", split_axis=0, concat_axis=0, tiled=True)
    landed, *spread_work = tie(landed, *beside_spread(*first_work))
    total = jnp.sum(landed.astype(F32), axis=0).astype(BF16)
    for bit in reversed(bits):
        got = swap(total, "replica", replicas, bit)
        side = (where // bit) % 2
        total = jnp.where(
            side == 0,
            jnp.concatenate([total, got], axis=0),
            jnp.concatenate([got, total], axis=0),
        )
    return total, first_work, swap_work, spread_work


def per_device(
    replicas,
    shards,
    images,
    image_adapter_index,
    device_image_count,
    cotangent,
    query_key_value_weight,
    frozen_output_weight,
    frozen_dispatch_weight,
    query_key_value_first,
    query_key_value_second,
    output_adapter_first,
    output_adapter_second,
    dispatch_adapter_first,
    dispatch_adapter_second,
    frozen_up_weight,
    frozen_down_weight,
    up_adapter_first,
    up_adapter_second,
    down_adapter_first,
    down_adapter_second,
):
    n_img, n_tok, width = images.shape
    total = -(-n_tok // 16) * 16
    rows = width // shards
    n_loc = frozen_up_weight.shape[0]
    n_exp = n_loc * shards
    groups = width // GROUP
    quarter = lax.axis_index("replica") % 4
    place = jnp.stack(
        [quarter, lax.axis_index("shard") % 2, lax.axis_index("replica")]
    ).astype(jnp.int32)
    by_axis = shards == 2 * STRIPS and replicas == 4

    spread01 = pack_call(
        place,
        (
            query_key_value_weight, query_key_value_first, query_key_value_second.T,
            output_adapter_first, dispatch_adapter_first, output_adapter_second.T,
            frozen_dispatch_weight.T,
        ),
        STRIPS if by_axis else shards,
    )
    spread23 = later_pack_call(
        place, (query_key_value_weight, frozen_output_weight, dispatch_adapter_second.T), shards
    )
    near = functools.partial(swap, axis="replica", size=replicas, bit=1)
    far = functools.partial(swap, axis="replica", size=replicas, bit=2)
    beside = functools.partial(swap, axis="shard", size=shards, bit=1)
    cut = (width + 6 * LANES) // 4

    h1 = norm_call(images, cotangent, total)
    if by_axis:
        lines = [[2 * strip + side for strip in range(STRIPS)] for side in range(2)]
        own01, spread23, h1 = tie(over_shard(spread01, lines), spread23, h1)
        own0, own1 = own01[:, :cut], own01[:, cut:]
        beside0, far0, own1 = tie(beside(own0), far(own0), own1)
        corner0, beside1, far1 = beside(far0), beside(own1), far(own1)
        corner0, far1, spread23 = tie(corner0, far1, spread23)
        held0 = [(own0, 0, 0), (beside0, 0, 1), (far0, 2, 0), (corner0, 2, 1)]
        held1 = [(own1, 0, 0), (beside1, 0, 1), (far1, 2, 0), (beside(far1), 2, 1)]
    else:
        own01, spread23, h1 = tie(over_shard(spread01), spread23, h1)
        own0, own1 = own01[:, :cut], own01[:, cut:]
        held0 = [(own0, 0, None), (far(own0), 2, None)]
        held1 = [(own1, 0, None), (far(own1), 2, None)]
    own23 = over_shard(spread23)

    def four_pieces(held, columns):
        layout = [(replica, side, 0) for _, replica, side in held]
        layout += [(replica ^ 1, side, 0) for _, replica, side in held]
        chunks = [chunk for chunk, _, _ in held] + [near(chunk) for chunk, _, _ in held]
        return tuple(chunks), (4, tuple(layout)), columns

    pack0 = four_pieces(held0, width + 6 * LANES)
    qkv0, att0, prob0, uq, bank_a, bank_bt, bank_ao, bank_ra = first_attention_call(
        place, image_adapter_index, h1, pack0, n_tok, shards
    )
    beside1, last1, uq, own23 = tie(held1[1][0], held1[-1][0], uq, own23)
    held1[1] = (beside1,) + held1[1][1:]
    held1[-1] = (last1,) + held1[-1][1:]
    pack1 = four_pieces(held1, width + 2 * LANES)
    own2, own3 = own23[:, : width // 2], own23[:, width // 2 :]
    far3 = far(own3)
    qkv1, att1, prob1, bank_bo, bank_wr = next_attention_call(
        place, h1, uq, bank_bt, pack1, n_tok, 1, 2
    )
    att1, uq, own2, own3, far3 = tie(att1, uq, own2, own3, far3)
    pack2 = ((own2, near(own2)), (2, ((0, None, 0), (1, None, 0))), width)
    qkv2, att2, prob2 = next_attention_call(place, h1, uq, bank_bt, pack2, n_tok, 2, 0)
    pack3 = four_pieces([(own3, 0, None), (far3, 2, None)], width + 2 * LANES)
    packs = (pack0, pack1, pack2, pack3)
    atts = (att0, att1, att2)
    x2, uo, ur, disp, comb, sg, bank_wrt, bank_rb = route_call(
        place, image_adapter_index, device_image_count, images, cotangent, atts,
        (bank_ao, bank_bo, bank_ra, bank_wr), packs[3], n_exp, total, shards,
    )

    landed = lax.all_to_all(sg, "shard", split_axis=0, concat_axis=0, tiled=True)
    landed, *turned = tie(landed, *turn_call(place, (bank_ao, bank_bo, bank_ra), packs))
    turned_qkv, turned_out, turned_first, turned_route = turned
    weights = (
        frozen_up_weight, frozen_down_weight, up_adapter_first, up_adapter_second,
        down_adapter_first, down_adapter_second,
    )
    far_landed = [swap(landed, "replica", replicas, bit) for bit in range(2, replicas, 2)]
    ret, *kept = expert_call(landed, weights)
    ret, *far_landed = tie(ret, *far_landed)
    back = lax.all_to_all(ret, "shard", split_axis=0, concat_axis=0, tiled=True)
    every = [(landed, *kept)]
    for number, bit in enumerate(range(2, replicas, 2)):
        far_kept = [swap(array, "replica", replicas, bit) for array in kept]
        every.append((far_landed[number], *far_kept))

    block_out, gx2, gatt, out_pack = route_back_call(
        image_adapter_index, device_image_count, cotangent, x2, uo, ur, disp, comb, atts, back,
        (bank_wrt, bank_rb, turned_out, turned_first, turned_route), shards, replicas,
    )
    gatt, *lows = tie(gatt, *[row[3] for row in every])
    held = [array for row, low in zip(every, lows) for array in (*row[:3], low)]
    *gqkvs, guq, keep, give = attention_back_call(
        place, image_adapter_index, (qkv0, qkv1, qkv2), (prob0, prob1, prob2), gatt, uq, h1, bank_bt, out_pack
    )

    def expert_grads(block, *arrays):
        arrays = list(arrays) + [swap(array, "replica", replicas, 1) for array in arrays]
        rows_of = [tuple(arrays[place : place + 4]) for place in range(0, len(arrays), 4)]
        return expert_grad_call(rows_of, width)

    summed, (block_out, *_), (input_grad,), grads = reduce_pack(
        keep, give, replicas,
        lambda: (block_out.transpose(1, 0, 2), *held),
        lambda: (input_grad_call(images, gx2, guq, gqkvs, turned_qkv),),
        expert_grads,
    )
    block_out = block_out.transpose(1, 0, 2)
    summed = summed.astype(F32)
    return (
        block_out,
        input_grad,
        summed[3 * rows : 4 * rows],
        summed[: 3 * rows].T,
        summed[4 * rows : 5 * rows],
        summed[5 * rows : 6 * rows].T,
        summed[6 * rows : 7 * rows],
        summed[7 * rows : 7 * rows + n_loc].T,
        *grads,
    )


def solution(mesh):
    images = P(("replica", "shard"), None, None)
    each = P(("replica", "shard"))
    by_row, by_column, by_expert = P("shard", None), P(None, "shard"), P("shard", None, None)
    in_specs = (
        (images, each, each, images)
        + (by_row, by_row, by_row)
        + (by_row, by_column) * 3
        + (by_expert,) * 6
    )
    out_specs = (images, images) + (by_row, by_column) * 3 + (by_expert,) * 4
    return jax.shard_map(
        functools.partial(per_device, mesh.shape["replica"], mesh.shape["shard"]),
        mesh=mesh,
        in_specs=in_specs,
        out_specs=out_specs,
        check_vma=False,
    )
```

```python
import functools

import jax
import jax.numpy as jnp
from jax import lax
from jax.experimental import pallas as pl
from jax.experimental.pallas import tpu as pltpu
from jax.sharding import PartitionSpec as P

HEADS = 12
RANK = 16
LANES = 128
HEAD_DIM = 64
GROUP = 256
F32 = jnp.float32
BF16 = jnp.bfloat16
NN = (((1,), (0,)), ((), ()))
NT = (((1,), (1,)), ((), ()))
TN = (((0,), (0,)), ((), ()))
NEG = -1e30
VMEM_LIMIT = 56 * 1024 * 1024
GELU_C = 0.7978845608028654
GELU_A = 0.044715
IMAGES_FORWARD = 2
IMAGES_BACK = 2
IMAGES_ROUTE = 2
IMAGES_LAST = 2
STRIPS = 4


def dot(left, right, dims=NN):
    return lax.dot_general(left, right, dims, preferred_element_type=F32)


def params(*axes):
    return pltpu.CompilerParams(
        dimension_semantics=axes or None, vmem_limit_bytes=VMEM_LIMIT
    )


def cost(flops, moved, exps=0):
    return pl.CostEstimate(flops=int(flops), bytes_accessed=int(moved), transcendentals=int(exps))


def normalise(rows):
    centre = rows - jnp.mean(rows, axis=-1, keepdims=True)
    spread = jnp.mean(centre * centre, axis=-1, keepdims=True)
    scale = lax.rsqrt(spread + 1e-06)
    return centre * scale, scale


def normalise_back(unit, scale, upstream):
    inner = jnp.mean(upstream * unit, axis=-1, keepdims=True)
    return scale * (upstream - jnp.mean(upstream, axis=-1, keepdims=True) - unit * inner)


def rank_row(index):
    lane = lax.broadcasted_iota(jnp.int32, (1, LANES), 1) // RANK
    return (lane == index).astype(F32)


def zero_tail(rows, n_tok):
    total = rows.shape[0]
    cut = n_tok // 16 * 16
    if n_tok == total:
        return rows
    row = lax.broadcasted_iota(jnp.int32, (total - cut, rows.shape[1]), 0) + cut
    tail = jnp.where(row < n_tok, rows[cut:].astype(F32), 0.0).astype(rows.dtype)
    return jnp.concatenate([rows[:cut], tail], axis=0)


def mask_tail(scores, n_tok):
    total = scores.shape[0]
    cut = n_tok // 16 * 16
    if n_tok == total:
        return scores
    row = lax.broadcasted_iota(jnp.int32, (total - cut, scores.shape[1]), 0) + cut
    tail = jnp.where(row < n_tok, scores[cut:], NEG)
    return jnp.concatenate([scores[:cut], tail], axis=0)


def pad_rows(scratch, ref):
    n_img, n_tok, width = ref.shape
    total = scratch.shape[0] // n_img
    cut = n_tok // 8 * 8
    for slot in range(n_img):
        base = slot * total
        scratch[base + cut : base + total, :] = jnp.zeros((total - cut, width), F32)
        scratch[base : base + n_tok, :] = ref[slot].astype(F32)
    return scratch[...]


def select_rows(rows, index_ref, first, n_img):
    total = rows.shape[0] // n_img
    return jnp.concatenate(
        [
            (rows[i * total : (i + 1) * total] * rank_row(index_ref[first + i])).astype(BF16)
            for i in range(n_img)
        ],
        axis=0,
    )


def flat(ref):
    return ref[...].reshape(ref.shape[0] * ref.shape[1], ref.shape[2])


def assemble(place_ref, chunks, layout, wall):
    pieces, entries = layout
    part = wall.shape[1] // pieces
    for chunk, (replica, neighbour, start) in zip(chunks, entries):
        column = pl.multiple_of(((place_ref[0] % pieces) ^ replica) * part, LANES)
        if neighbour is None:
            wall[:, pl.ds(column, part)] = chunk[:, start : start + part]
            continue
        strips = STRIPS
        rows = chunk.shape[0] // strips
        for strip in range(strips):
            row = pl.multiple_of((2 * strip + (place_ref[1] ^ neighbour)) * rows, 16)
            wall[pl.ds(row, rows), pl.ds(column, part)] = chunk[
                strip * rows : (strip + 1) * rows, start : start + part
            ]


def norm_kernel(image_ref, _, out_ref, pad_ref):
    unit, _ = normalise(pad_rows(pad_ref, image_ref))
    out_ref[...] = unit.astype(BF16).reshape(out_ref.shape)


def group_columns(pack, qkv_ref, group):
    width = qkv_ref.shape[1] // 3
    for piece in range(3):
        start = piece * width + group * GROUP
        pack[:, piece * GROUP : (piece + 1) * GROUP] = qkv_ref[:, start : start + GROUP]


def own_part(place_ref, pack, pieces):
    part = pack.shape[1] // pieces
    return pack[:, pl.ds(pl.multiple_of(place_ref[0] % pieces * part, LANES), part)]


def pack_kernel(
    place_ref, qkv_ref, a_ref, b_ref, ao_ref, ra_ref, bo_ref, wr_ref, out_ref, pack0, pack1
):
    copies, rows, _ = out_ref.shape
    width = qkv_ref.shape[1] // 3
    group_columns(pack0, qkv_ref, 0)
    for piece in range(3):
        column = width + (1 + piece) * LANES
        pack0[:, column : column + LANES] = b_ref[piece * rows : (piece + 1) * rows, :]
    pack0[:, width : width + LANES] = a_ref[...]
    pack0[:, width + 4 * LANES : width + 5 * LANES] = ao_ref[...]
    pack0[:, width + 5 * LANES : width + 6 * LANES] = ra_ref[...]
    group_columns(pack1, qkv_ref, 1)
    pack1[:, width : width + LANES] = bo_ref[...]
    n_exp = wr_ref.shape[0]
    route = jnp.concatenate([wr_ref[...].astype(F32), jnp.zeros((LANES - n_exp, rows), F32)], axis=0)
    pack1[:, width + LANES :] = route.T.astype(BF16)
    mine = jnp.concatenate([own_part(place_ref, pack0, 4), own_part(place_ref, pack1, 4)], axis=1)
    for copy in range(copies):
        out_ref[copy] = mine


def later_pack_kernel(place_ref, qkv_ref, wo_ref, rb_ref, out_ref, pack2, pack3):
    shards, rows, _ = out_ref.shape
    width = wo_ref.shape[1]
    group_columns(pack2, qkv_ref, 2)
    pack3[:, :width] = wo_ref[...]
    n_loc = rb_ref.shape[0]
    second = jnp.concatenate([rb_ref[...].astype(F32), jnp.zeros((rows - n_loc, LANES), F32)], axis=0)
    pack3[:, width : width + LANES] = second.astype(BF16)
    pack3[:, width + LANES :] = jnp.zeros((rows, LANES), BF16)
    mine = jnp.concatenate([own_part(place_ref, pack2, 2), own_part(place_ref, pack3, 4)], axis=1)
    for shard in range(shards):
        out_ref[shard] = mine


def each_head(columns, value):
    head = lax.broadcasted_iota(jnp.int32, (1, GROUP), 1) // HEAD_DIM
    return jnp.concatenate(
        [
            columns * jnp.where(head == number, value, 0.0).astype(BF16)
            for number in range(GROUP // HEAD_DIM)
        ],
        axis=0,
    )


def merge_pair(low, high):
    lane = lax.broadcasted_iota(jnp.int32, (1, LANES), 1)
    return jnp.where(lane < HEAD_DIM, low, high)


def attention_forward(qkv, n_tok, prob_ref, slot):
    total = qkv.shape[0]
    every = dot(each_head(qkv[:, GROUP : 2 * GROUP], 0.125), qkv[:, :GROUP], NT)
    outs = []
    for head in range(GROUP // HEAD_DIM):
        scores = mask_tail(every[head * total : (head + 1) * total], n_tok)
        powers = jnp.exp(scores - jnp.max(scores, axis=0, keepdims=True))
        probs = (powers * (1.0 / jnp.sum(powers, axis=0, keepdims=True))).astype(BF16)
        prob_ref[slot, head] = probs
        column = 2 * GROUP + head // 2 * LANES
        outs.append(dot(probs, qkv[:, column : column + LANES], TN))
    pairs = [merge_pair(outs[head], outs[head + 1]) for head in range(0, len(outs), 2)]
    return zero_tail(jnp.concatenate(pairs, axis=1).astype(BF16), n_tok)


def first_attention_kernel(
    n_tok, shards, layout, place_ref, index_ref, h1_ref, *rest,
):
    chunks, rest = rest[: len(layout[1])], rest[len(layout[1]) :]
    qkv_ref, att_ref, prob_ref, uq_ref, a_ref, bt_ref, ao_ref, ra_ref, wall = rest
    step = pl.program_id(0)
    n_img, total, width = h1_ref.shape

    @pl.when(step == 0)
    def _():
        assemble(place_ref, chunks, layout, wall)
        a_ref[...] = wall[:, width : width + LANES]
        ao_ref[...] = wall[:, width + 4 * LANES : width + 5 * LANES]
        ra_ref[...] = wall[:, width + 5 * LANES : width + 6 * LANES]
        rows = width // shards
        for shard in range(shards):
            for part in range(3):
                bt_ref[(shard * 3 + part) * rows : (shard * 3 + part + 1) * rows, :] = wall[
                    shard * rows : (shard + 1) * rows,
                    width + (1 + part) * LANES : width + (2 + part) * LANES,
                ]

    h1 = flat(h1_ref)
    both = dot(h1, wall[:, : 3 * GROUP + LANES])
    low = both[:, 3 * GROUP :].astype(BF16).astype(F32)
    uq = select_rows(low, index_ref, step * n_img, n_img)
    uq_ref[...] = uq.reshape(uq_ref.shape)
    attend_group(0, n_tok, both[:, : 3 * GROUP], uq, bt_ref, qkv_ref, att_ref, prob_ref)


def group_rows(group, width, bt_ref):
    return jnp.concatenate(
        [bt_ref[part * width + group * GROUP : part * width + (group + 1) * GROUP, :] for part in range(3)],
        axis=0,
    )


def attend_group(group, n_tok, base, uq, bt_ref, qkv_ref, att_ref, prob_ref):
    n_img, total, _ = att_ref.shape
    second = group_rows(group, bt_ref.shape[0] // 3, bt_ref)
    qkv = (base + dot(uq, second, NT)).astype(BF16)
    qkv_ref[...] = qkv.reshape(qkv_ref.shape)
    for slot in range(n_img):
        att_ref[slot] = attention_forward(
            qkv[slot * total : (slot + 1) * total], n_tok, prob_ref, slot
        )


def next_attention_kernel(
    n_tok, group, extra, layout, place_ref, h1_ref, uq_ref, bt_ref, *rest
):
    chunks, rest = rest[: len(layout[1])], rest[len(layout[1]) :]
    qkv_ref, att_ref, prob_ref = rest[:3]
    wall = rest[-1]

    @pl.when(pl.program_id(0) == 0)
    def _():
        assemble(place_ref, chunks, layout, wall)
        for position in range(extra):
            column = 3 * GROUP + position * LANES
            rest[3 + position][...] = wall[:, column : column + LANES]

    attend_group(
        group, n_tok, dot(flat(h1_ref), wall[:, : 3 * GROUP]), flat(uq_ref), bt_ref, qkv_ref, att_ref, prob_ref,
    )


def route_kernel(
    n_exp, shards, layout, place_ref, index_ref, count_ref, image_ref, cot_ref, att0, att1, att2,
    ao_ref, bo_ref, ra_ref, wr_ref, *rest,
):
    chunks, rest = rest[: len(layout[1])], rest[len(layout[1]) :]
    x2_ref, uo_ref, ur_ref, disp_ref, comb_ref, sg_ref, wrt_ref, rb_ref, *rest = rest
    wall, rb_f, pair_ref, pad_a, pad_b, sent_ref = rest
    every = sg_ref.shape[2]
    n_img, n_tok, width = image_ref.shape
    first = pl.program_id(0) * n_img
    total = x2_ref.shape[1]

    @pl.when(first == 0)
    def _():
        assemble(place_ref, chunks, layout, wall)
        wrt_ref[...] = wr_ref[...].astype(F32).T[:n_exp].astype(BF16)
        n_loc, rows = n_exp // shards, width // shards
        for shard in range(shards):
            rb_f[shard * n_loc : (shard + 1) * n_loc, :] = wall[
                shard * rows : shard * rows + 8, width : width + LANES
            ].astype(F32)[:n_loc]
        rb_ref[...] = rb_f[...].astype(BF16)
        wall[:, width : width + LANES] = ao_ref[...]
        pair_ref[:, :LANES] = ra_ref[...]
        pair_ref[:, LANES:] = wr_ref[...]

    att = jnp.concatenate([flat(att0), flat(att1), flat(att2)], axis=1)
    both = dot(att, wall[:, : width + LANES])
    uo = select_rows(both[:, width:].astype(BF16).astype(F32), index_ref, first, n_img)
    uo_ref[...] = uo.reshape(uo_ref.shape)
    x2 = pad_rows(pad_a, image_ref) + both[:, :width] + dot(uo, bo_ref[...], NT)
    x2_ref[...] = x2.reshape(x2_ref.shape)
    h2 = normalise(x2)[0].astype(BF16)
    both = dot(h2, pair_ref[...])
    ur = select_rows(both[:, :LANES].astype(BF16).astype(F32), index_ref, first, n_img)
    base = both[:, LANES:]
    ur_ref[...] = ur.reshape(ur_ref.shape)
    cot = pad_rows(pad_b, cot_ref)
    firsts = []
    for slot in range(n_img):
        rows = slice(slot * total, (slot + 1) * total)
        living = (first + slot < count_ref[0]).astype(F32)
        logits = base[rows].T[:n_exp] + dot(rb_ref[...], ur[rows], NT)
        alive = lax.broadcasted_iota(jnp.int32, logits.shape, 1) < n_tok
        over_tokens = jnp.where(alive, logits, NEG)
        powers = jnp.exp(over_tokens - jnp.max(over_tokens, axis=1, keepdims=True))
        disp = powers / jnp.sum(powers, axis=1, keepdims=True)
        powers = jnp.exp(logits - jnp.max(logits, axis=0, keepdims=True))
        comb = jnp.where(alive, powers / jnp.sum(powers, axis=0, keepdims=True), 0.0)
        disp_ref[slot] = disp
        comb_ref[slot] = comb
        upstream = (cot[rows] * living).astype(BF16)
        firsts.append((rows, disp, comb, upstream))
    for slot, (rows, disp, comb, upstream) in enumerate(firsts):
        sent = jnp.concatenate(
            [
                dot(disp.astype(BF16), h2[rows]),
                dot(comb.astype(BF16), upstream),
                jnp.broadcast_to(rank_row(index_ref[first + slot]), (n_exp, LANES)),
            ],
            axis=1,
        )
        for block in range(sent.shape[1] // LANES):
            start = block * n_exp * every + first + slot
            sent_ref[pl.ds(start, n_exp, stride=every), :] = sent[:, block * LANES : (block + 1) * LANES]

    @pl.when(pl.program_id(0) == pl.num_programs(0) - 1)
    def _():
        for block in range(sg_ref.shape[3] // LANES):
            span = slice(block * LANES, (block + 1) * LANES)
            piece = sent_ref[block * n_exp * every : (block + 1) * n_exp * every, :]
            sg_ref[:, :, :, span] = piece.reshape(sg_ref.shape[:3] + (LANES,)).astype(BF16)


def gelu_both(pre):
    square = pre * pre
    half = jnp.tanh(GELU_C * pre * (1.0 + GELU_A * square))
    both = 0.5 * (1.0 + half)
    slope = both + 0.5 * pre * (1.0 - half * half) * (GELU_C * (1.0 + 3.0 * GELU_A * square))
    return pre * both, slope


def expert_tile(slots, gy, u1, gu2, wu_ref, wd_ref, ub_ref, da_ref):
    ghid = (dot(wd_ref[0], gy, NT) + dot(da_ref[0], gu2, NT)).T
    pre = dot(slots, wu_ref[0]) + dot(u1, ub_ref[0])
    hidden, slope = gelu_both(pre)
    return hidden.astype(BF16), (slope * ghid).astype(BF16)


def gather_rows(part_refs, out_ref):
    rows = part_refs[0].shape[0] * part_refs[0].shape[2]
    for number, part_ref in enumerate(part_refs):
        part = part_ref[:, 0].astype(F32).reshape(rows, part_ref.shape[3])
        out_ref[number * rows : (number + 1) * rows, :] = part.astype(BF16)


def expert_kernel(
    wu_ref, wd_ref, ua_ref, ub_ref, da_ref, db_ref, part_ref, out_ref, hidden_ref, gpre_ref, low_ref,
    sg_ref, u1_ref, gu2_ref, acc_y, acc_s, acc_u2, acc_gu1,
):
    step = pl.program_id(1)
    width = wu_ref.shape[1]

    @pl.when(step == 0)
    def _():
        gather_rows((part_ref,), sg_ref)
        selector = sg_ref[:, 2 * width :].astype(F32)
        u1_ref[...] = (
            dot(sg_ref[:, :width], ua_ref[0]).astype(BF16).astype(F32) * selector
        ).astype(BF16)
        gu2_ref[...] = (dot(sg_ref[:, width : 2 * width], db_ref[0], NT) * selector).astype(BF16)
        acc_y[...] = jnp.zeros_like(acc_y)
        acc_s[...] = jnp.zeros_like(acc_s)
        acc_u2[...] = jnp.zeros_like(acc_u2)
        acc_gu1[...] = jnp.zeros_like(acc_gu1)

    hidden, gpre = expert_tile(
        sg_ref[:, :width], sg_ref[:, width : 2 * width], u1_ref[...], gu2_ref[...],
        wu_ref, wd_ref, ub_ref, da_ref,
    )
    hidden_ref[0] = hidden
    gpre_ref[0] = gpre
    acc_y[...] += dot(hidden, wd_ref[0])
    acc_u2[...] += dot(hidden, da_ref[0])
    acc_s[...] += dot(wu_ref[0], gpre, NT)
    acc_gu1[...] += dot(ub_ref[0], gpre, NT)

    @pl.when(step == pl.num_programs(1) - 1)
    def _():
        selector = sg_ref[:, 2 * width :].astype(F32)
        u2 = (acc_u2[...].astype(BF16).astype(F32) * selector).astype(BF16)
        gu1 = (acc_gu1[...].T * selector).astype(BF16)
        shards, _, n_img, _ = out_ref.shape
        result = acc_y[...] + dot(u2, db_ref[0])
        out_ref[:, 0, :, :width] = result.reshape(shards, n_img, width).astype(BF16)
        result = acc_s[...].T + dot(gu1, ua_ref[0], NT)
        out_ref[:, 0, :, width:] = result.reshape(shards, n_img, width).astype(BF16)
        for place, low in enumerate((u1_ref[...], u2, gu1, gu2_ref[...])):
            low_ref[0, :, place * LANES : (place + 1) * LANES] = low


def expert_grad_kernel(copies, *refs):
    refs = list(refs)
    part_refs, hidden_refs, gpre_refs, low_refs = (
        [refs.pop(0) for _ in range(copies)] for _ in range(4)
    )
    gua_ref, gub_ref, gda_ref, gdb_ref, sg_ref, low_t, rows_ref = refs
    rows = hidden_refs[0].shape[1]
    width = gua_ref.shape[1]

    @pl.when(pl.program_id(1) == 0)
    def _():
        gather_rows(part_refs, sg_ref)
        low = jnp.concatenate([ref[0] for ref in low_refs], axis=0)
        low_t[...] = low.astype(F32).T.astype(BF16)
        u2_t, gu1_t = low_t[LANES : 2 * LANES, :], low_t[2 * LANES : 3 * LANES, :]
        gdb_ref[0] = dot(u2_t, sg_ref[:, width : 2 * width])
        gua_ref[0] = dot(gu1_t, sg_ref[:, :width]).T

    for number in range(copies):
        rows_ref[number * rows : (number + 1) * rows, :] = gpre_refs[number][0]
    gub_ref[0] = dot(low_t[:LANES, :], rows_ref[...])
    for number in range(copies):
        rows_ref[number * rows : (number + 1) * rows, :] = hidden_refs[number][0]
    gda_ref[0] = dot(low_t[3 * LANES :, :], rows_ref[...]).T


def turn_kernel(layouts, place_ref, ao_ref, bo_ref, ra_ref, *refs):
    refs = list(refs)
    chunks = [[refs.pop(0) for _ in layout[1]] for layout in layouts]
    qkv_ref, out_ref, first_ref, route_ref = refs[:4]
    walls = refs[4:]
    for chunk, layout, wall in zip(chunks, layouts, walls):
        assemble(place_ref, chunk, layout, wall)
    width = walls[0].shape[0]
    for group, wall in enumerate(walls[:-1]):
        qkv_ref[group * 3 * GROUP : (group + 1) * 3 * GROUP, :] = wall[:, : 3 * GROUP].T
    qkv_ref[3 * width :, :] = walls[0][:, 3 * GROUP : 3 * GROUP + LANES].T
    out_ref[:, :width] = walls[-1][:, :width].T
    out_ref[:, width:] = bo_ref[...]
    first_ref[...] = ao_ref[...].T
    route_ref[...] = ra_ref[...].T


def route_back_kernel(
    n_exp, index_ref, count_ref, cot_ref, x2_ref, uo_ref, ur_ref, disp_ref, comb_ref,
    att0, att1, att2, ret_ref, wrt_ref, rb_ref, out_ref, first_ref, route_ref,
    block_ref, gx2_ref, gatt_ref, pack_ref, pad_b, back_ref, acc_oa, acc_ob, acc_ra, acc_rb,
):
    n_img, n_tok, width = cot_ref.shape
    first = pl.program_id(0) * n_img
    total = x2_ref.shape[1]

    every = ret_ref.shape[2]

    @pl.when(first == 0)
    def _():
        for block in range(2 * width // LANES):
            piece = ret_ref[:, :, :, block * LANES : (block + 1) * LANES].astype(F32)
            back_ref[block * n_exp * every : (block + 1) * n_exp * every, :] = piece.reshape(
                n_exp * every, LANES
            )
        acc_oa[...] = jnp.zeros_like(acc_oa)
        acc_ob[...] = jnp.zeros_like(acc_ob)
        acc_ra[...] = jnp.zeros_like(acc_ra)
        acc_rb[...] = jnp.zeros_like(acc_rb)

    cot = pad_rows(pad_b, cot_ref)
    x2 = flat(x2_ref)
    unit, scale = normalise(x2)
    h2 = unit.astype(BF16)
    pairs, belows, upstreams, mixes, firsts = [], [], [], [], []
    for slot in range(n_img):
        rows = slice(slot * total, (slot + 1) * total)
        living = (first + slot < count_ref[0]).astype(F32)
        upstream = cot[rows] * living
        upstreams.append(upstream)
        disp, comb = disp_ref[slot], comb_ref[slot]
        blocks = [
            back_ref[pl.ds(block * n_exp * every + first + slot, n_exp, stride=every), :]
            for block in range(2 * width // LANES)
        ]
        back = jnp.concatenate(blocks, axis=1).astype(BF16)
        yexp, gslot = back[:, :width], back[:, width:]
        gcomb = dot(yexp, upstream.astype(BF16), NT)
        gdisp = dot(gslot, h2[rows], NT)
        firsts.append((rows, living, disp, comb, yexp, gslot, gcomb, gdisp))
    for slot, (rows, living, disp, comb, yexp, gslot, gcomb, gdisp) in enumerate(firsts):
        glog = (
            disp * (gdisp - jnp.sum(gdisp * disp, axis=1, keepdims=True))
            + comb * (gcomb - jnp.sum(gcomb * comb, axis=0, keepdims=True))
        )
        acc_rb[...] += dot(glog.astype(BF16), ur_ref[slot])
        three = jnp.concatenate([disp, glog, comb], axis=0).T.astype(BF16)
        mixes.append((living, three[:, 2 * n_exp :], yexp, rows))
        pairs.append(three[:, : 2 * n_exp])
        belows.append(jnp.concatenate([route_ref[...], gslot, wrt_ref[...]], axis=0))
    glog_rows = jnp.concatenate([pair[:, n_exp:] for pair in pairs], axis=0)
    gur = select_rows(dot(glog_rows, rb_ref[...]), index_ref, first, n_img)
    gh2 = jnp.concatenate(
        [
            dot(jnp.concatenate([gur[i * total : (i + 1) * total], pairs[i]], axis=1), belows[i])
            for i in range(n_img)
        ],
        axis=0,
    )
    gx2 = jnp.concatenate(upstreams, axis=0) + normalise_back(unit, scale, gh2)
    gbr = gx2.astype(BF16)
    gx2_ref[...] = gbr.reshape(gx2_ref.shape)
    both = dot(gbr, out_ref[...])
    guo = select_rows(both[:, width:], index_ref, first, n_img)
    att = jnp.concatenate([flat(att0), flat(att1), flat(att2)], axis=1)
    gatt = (both[:, :width] + dot(guo, first_ref[...])).astype(BF16)
    gatt_ref[...] = gatt.reshape(gatt_ref.shape)
    acc_ra[...] += dot(gur, h2, TN)
    acc_ob[...] += dot(flat(uo_ref), gbr, TN)
    acc_oa[...] += dot(guo, att, TN)
    for slot, (living, left, yexp, rows) in enumerate(mixes):
        block_ref[slot] = (living * (x2[rows] + dot(left, yexp))).astype(BF16)[:n_tok]

    @pl.when(pl.program_id(0) == pl.num_programs(0) - 1)
    def _():
        shards = pack_ref.shape[0]
        rows = width // shards
        n_loc = n_exp // shards
        for position, acc in enumerate((acc_oa, acc_ob, acc_ra)):
            summed = acc[...].T.astype(BF16)
            for shard in range(shards):
                pack_ref[shard, position * rows : (position + 1) * rows, :] = summed[
                    shard * rows : (shard + 1) * rows
                ]
        tail = pack_ref.shape[1] - 3 * rows
        for shard in range(shards):
            last = jnp.concatenate(
                [acc_rb[shard * n_loc : (shard + 1) * n_loc, :], jnp.zeros((tail - n_loc, LANES), F32)],
                axis=0,
            )
            pack_ref[shard, 3 * rows :, :] = last.astype(BF16)


def attention_backward(qkv, gatt, prob_ref, slot):
    total = qkv.shape[0]
    heads = GROUP // HEAD_DIM
    every = dot(each_head(qkv[:, 2 * GROUP :], 1.0), gatt, NT)
    gscores = []
    for head in range(heads):
        probs = prob_ref[slot, head].astype(F32)
        gprobs = every[head * total : (head + 1) * total]
        inner = jnp.sum(gprobs * probs, axis=0, keepdims=True)
        gscores.append((probs * (gprobs - inner)).astype(BF16))

    def products(lefts, right):
        outs = []
        for pair in range(heads // 2):
            both = dot(
                jnp.concatenate(lefts[2 * pair : 2 * pair + 2], axis=0),
                right[:, pair * LANES : (pair + 1) * LANES],
            )
            outs.append(merge_pair(both[:total], both[total:]))
        return outs

    gv = [part.astype(BF16) for part in products([prob_ref[slot, head] for head in range(heads)], gatt)]
    gk = [(part * 0.125).astype(BF16) for part in products(gscores, qkv[:, :GROUP])]
    key_t = qkv[:, GROUP : 2 * GROUP].T
    gq = [
        (dot(key_t[head * HEAD_DIM : (head + 1) * HEAD_DIM], gscores[head]) * 0.125).astype(BF16)
        for head in range(heads)
    ]
    return jnp.concatenate([jnp.concatenate(gq, axis=0).T] + gk + gv, axis=1)


def attention_back_kernel(groups, place_ref, index_ref, *refs):
    refs = list(refs)
    qkv_refs = [refs.pop(0) for _ in range(groups)]
    prob_refs = [refs.pop(0) for _ in range(groups)]
    gatt_ref, uq_ref, h1_ref, bt_ref, others_ref = refs[:5]
    refs = refs[5:]
    gqkv_refs = [refs.pop(0) for _ in range(groups)]
    guq_ref, keep_ref, give_ref, pack_ref, acc_b, acc_a = refs
    step = pl.program_id(0)
    n_img, total, width = h1_ref.shape

    @pl.when(step == 0)
    def _():
        acc_b[...] = jnp.zeros_like(acc_b)
        acc_a[...] = jnp.zeros_like(acc_a)

    uq_t = flat(uq_ref).T
    guq = None
    gqkvs = []
    for group in range(groups):
        parts = []
        for i in range(n_img):
            part = attention_backward(
                qkv_refs[group][i], gatt_ref[i, :, group * GROUP : (group + 1) * GROUP],
                prob_refs[group], i,
            )
            gqkv_refs[group][i] = part
            parts.append(part)
        gqkv = jnp.concatenate(parts, axis=0)
        part = dot(gqkv, group_rows(group, width, bt_ref))
        guq = part if guq is None else guq + part
        gqkvs.append(gqkv)
    for group, gqkv in enumerate(gqkvs):
        acc_b[:, group * 3 * GROUP : (group + 1) * 3 * GROUP] += dot(uq_t, gqkv)
    guq = select_rows(guq, index_ref, step * n_img, n_img)
    acc_a[...] += dot(guq, flat(h1_ref), TN)
    guq_ref[...] = guq.reshape(guq_ref.shape)

    @pl.when(step == pl.num_programs(0) - 1)
    def _():
        shards = pack_ref.shape[0]
        rows = width // shards
        pack_ref[:, 4 * rows :, :] = others_ref[...]
        own = acc_a[...].T.astype(BF16)
        for shard in range(shards):
            pack_ref[shard, 3 * rows : 4 * rows, :] = own[shard * rows : (shard + 1) * rows]
        for group in range(groups):
            summed = acc_b[:, group * 3 * GROUP : (group + 1) * 3 * GROUP].T.astype(BF16)
            for part in range(3):
                start = part * width + group * GROUP
                place = start
                while place < start + GROUP:
                    shard, offset = divmod(place, 3 * rows)
                    length = min(start + GROUP - place, 3 * rows - offset)
                    take = part * GROUP + place - start
                    pack_ref[shard, offset : offset + length, :] = summed[take : take + length]
                    place += length
        half = keep_ref.shape[1]
        side = place_ref[2] % 2
        keep_ref[...] = pack_ref[:, pl.ds(pl.multiple_of(side * half, 16), half), :]
        give_ref[...] = pack_ref[:, pl.ds(pl.multiple_of((1 - side) * half, 16), half), :]


def input_grad_kernel(image_ref, gx2_ref, guq_ref, turned_ref, *refs):
    *gqkv, out_ref, pad_a = refs
    n_img, n_tok, width = image_ref.shape
    step = pl.program_id(0)
    parts = width // LANES
    every = out_ref.shape[0] // (n_tok * parts)
    total = gx2_ref.shape[1]
    gh1 = dot(jnp.concatenate([flat(ref) for ref in gqkv] + [flat(guq_ref)], axis=1), turned_ref[...])
    unit, scale = normalise(pad_rows(pad_a, image_ref))
    result = flat(gx2_ref).astype(F32) + normalise_back(unit, scale, gh1)
    for slot in range(n_img):
        image = step * n_img + slot
        cut = n_tok // 8 * 8
        row = lax.broadcasted_iota(jnp.int32, (every, LANES), 0)
        for part in range(parts):
            columns = result[slot * total : slot * total + n_tok, part * LANES : (part + 1) * LANES]
            out_ref[pl.ds(part * every + image, cut, stride=parts * every), :] = columns[:cut]
            for token in range(cut, n_tok):
                start = (token * parts + part) * every
                kept = out_ref[start : start + every, :]
                out_ref[start : start + every, :] = jnp.where(
                    row == image, columns[token : token + 1], kept
                )


ANY = pl.BlockSpec(memory_space=pl.ANY)


def whole(shape):
    return pl.BlockSpec(shape, lambda *_: (0,) * len(shape))


def once(shape):
    return pl.BlockSpec(shape, lambda *_: (0,) * len(shape), pipeline_mode=pl.Buffered(1))


def per_image(*shape, images=1):
    return pl.BlockSpec((images,) + shape, lambda i, *_: (i,) + (0,) * len(shape))


def several(images, limit):
    return max(n for n in range(1, limit + 1) if images % n == 0)


def call(kernel, scalars, grid, inputs, outputs, scratch, flops, exps=0, aliases=None):
    arrays = [array for array, _ in inputs]
    shapes = [jax.ShapeDtypeStruct(shape, dtype) for shape, dtype, _ in outputs]
    moved = sum(array.size * array.dtype.itemsize for array in arrays) + sum(
        shape.size * shape.dtype.itemsize for shape in shapes
    )
    return pl.pallas_call(
        kernel,
        out_shape=shapes,
        grid_spec=pltpu.PrefetchScalarGridSpec(
            num_scalar_prefetch=len(scalars),
            grid=grid,
            in_specs=[spec for _, spec in inputs],
            out_specs=[spec for _, _, spec in outputs],
            scratch_shapes=scratch,
        ),
        input_output_aliases=aliases or {},
        compiler_params=params(*(("arbitrary",) * len(grid))),
        cost_estimate=cost(flops, moved, exps),
    )(*scalars, *arrays)


def norm_call(images, cotangent, total):
    n_img, n_tok, width = images.shape
    each = several(n_img, 4)
    return call(
        norm_kernel, (), (n_img // each,),
        [(images, per_image(n_tok, width, images=each)), (cotangent, ANY)],
        [((n_img, total, width), BF16, per_image(total, width, images=each))],
        [pltpu.VMEM((each * total, width), F32)],
        8 * images.size,
    )[0]


def pack_call(place, weights, copies):
    rows, columns = weights[0].shape
    width = columns // 3
    wide = [width + 6 * LANES, width + 2 * LANES]
    out = (copies, rows, sum(wide) // 4)
    return call(
        pack_kernel, (place,), (1,), [(weight, whole(weight.shape)) for weight in weights],
        [(out, BF16, whole(out))], [pltpu.VMEM((rows, each), BF16) for each in wide], rows * columns,
    )[0]


def later_pack_call(place, weights, shards):
    rows, width = weights[1].shape
    out = (shards, rows, width // 2 + (width + 2 * LANES) // 4)
    return call(
        later_pack_kernel, (place,), (1,), [(weight, whole(weight.shape)) for weight in weights],
        [(out, BF16, whole(out))],
        [pltpu.VMEM((rows, each), BF16) for each in (width, width + 2 * LANES)], rows * width,
    )[0]


def attention_flops(n_img, total, width, parts):
    return n_img * total * (2 * width * 3 * GROUP + parts * 8 * total * HEAD_DIM)


def attention_outputs(n_img, total, each):
    return [
        ((n_img, total, 3 * GROUP), BF16, per_image(total, 3 * GROUP, images=each)),
        ((n_img, total, GROUP), BF16, per_image(total, GROUP, images=each)),
        (
            (n_img, GROUP // HEAD_DIM, total, total), BF16,
            per_image(GROUP // HEAD_DIM, total, total, images=each),
        ),
    ]


def first_attention_call(place, index, h1, pack, n_tok, shards):
    n_img, total, width = h1.shape
    chunks, layout, columns = pack
    each = several(n_img, IMAGES_FORWARD)
    return call(
        functools.partial(first_attention_kernel, n_tok, shards, layout), (place, index), (n_img // each,),
        [(h1, per_image(total, width, images=each))] + [(chunk, once(chunk.shape)) for chunk in chunks],
        attention_outputs(n_img, total, each)
        + [
            ((n_img, total, LANES), BF16, per_image(total, LANES, images=each)),
            ((width, LANES), BF16, whole((width, LANES))),
            ((3 * width, LANES), BF16, whole((3 * width, LANES))),
            ((width, LANES), BF16, whole((width, LANES))),
            ((width, LANES), BF16, whole((width, LANES))),
        ],
        [pltpu.VMEM((width, columns), BF16)],
        attention_flops(n_img, total, width, 2), n_img * total * total * 4,
    )


def next_attention_call(place, h1, uq, bt, pack, n_tok, group, extra):
    n_img, total, width = h1.shape
    chunks, layout, columns = pack
    each = several(n_img, IMAGES_FORWARD)
    return call(
        functools.partial(next_attention_kernel, n_tok, group, extra, layout), (place,), (n_img // each,),
        [
            (h1, per_image(total, width, images=each)),
            (uq, per_image(total, LANES, images=each)),
            (bt, whole(bt.shape)),
        ]
        + [(chunk, once(chunk.shape)) for chunk in chunks],
        attention_outputs(n_img, total, each)
        + [((width, LANES), BF16, whole((width, LANES)))] * extra,
        [pltpu.VMEM((width, columns), BF16)],
        attention_flops(n_img, total, width, 2), n_img * total * total * 4,
    )


def route_call(place, index, count, images, cotangent, atts, banks, pack, n_exp, total, shards):
    n_img, n_tok, width = images.shape
    chunks, layout, columns = pack
    each = several(n_img, IMAGES_ROUTE)
    here = functools.partial(per_image, images=each)
    sent = (shards, n_exp // shards, n_img, 2 * width + LANES)
    return call(
        functools.partial(route_kernel, n_exp, shards, layout), (place, index, count), (n_img // each,),
        [(images, here(n_tok, width)), (cotangent, here(n_tok, width))]
        + [(att, here(total, GROUP)) for att in atts]
        + [(bank, whole(bank.shape)) for bank in banks]
        + [(chunk, once(chunk.shape)) for chunk in chunks],
        [
            ((n_img, total, width), F32, here(total, width)),
            ((n_img, total, LANES), BF16, here(total, LANES)),
            ((n_img, total, LANES), BF16, here(total, LANES)),
            ((n_img, n_exp, total), F32, here(n_exp, total)),
            ((n_img, n_exp, total), F32, here(n_exp, total)),
            (sent, BF16, whole(sent)),
            ((n_exp, width), BF16, whole((n_exp, width))),
            ((n_exp, LANES), BF16, whole((n_exp, LANES))),
        ],
        [
            pltpu.VMEM((width, columns), BF16),
            pltpu.VMEM((n_exp, LANES), F32),
            pltpu.VMEM((width, 2 * LANES), BF16),
            pltpu.VMEM((each * total, width), F32),
            pltpu.VMEM((each * total, width), F32),
            pltpu.VMEM(((2 * width // LANES + 1) * n_exp * n_img + n_img, LANES), F32),
        ],
        n_img * total * 2 * width * (width + 3 * LANES), n_img * total * 2 * n_exp,
    )


def hidden_tile(hidden, limit):
    tile = hidden
    while tile > limit:
        tile //= 2
    return tile


def expert_specs(width, tile, first=0):
    return (
        pl.BlockSpec((1, width, tile), lambda e, f: (e + first, 0, f)),
        pl.BlockSpec((1, tile, width), lambda e, f: (e + first, f, 0)),
        pl.BlockSpec((1, width, LANES), lambda e, f: (e + first, 0, 0)),
        pl.BlockSpec((1, LANES, tile), lambda e, f: (e + first, 0, f)),
        pl.BlockSpec((1, tile, LANES), lambda e, f: (e + first, f, 0)),
        pl.BlockSpec((1, LANES, width), lambda e, f: (e + first, 0, 0)),
    )


def expert_rows(shape, first=0):
    shards, _, n_img, columns = shape
    return pl.BlockSpec((shards, 1, n_img, columns), lambda e, f: (0, e + first, 0, 0))


def expert_call(landed, weights):
    shards, n_loc, n_img, columns = landed.shape
    rows = shards * n_img
    width, hidden = weights[0].shape[1:]
    tile = hidden_tile(hidden, 1536)
    out = (shards, n_loc, n_img, 2 * width)
    tiled = pl.BlockSpec((1, rows, tile), lambda e, f: (e, 0, f))
    return call(
        expert_kernel, (), (n_loc, hidden // tile),
        list(zip(weights, expert_specs(width, tile))) + [(landed, expert_rows(landed.shape))],
        [
            (out, BF16, expert_rows(out)),
            ((n_loc, rows, hidden), BF16, tiled),
            ((n_loc, rows, hidden), BF16, tiled),
            (
                (n_loc, rows, 4 * LANES), BF16,
                pl.BlockSpec((1, rows, 4 * LANES), lambda e, f: (e, 0, 0)),
            ),
        ],
        [
            pltpu.VMEM((rows, columns), BF16),
            pltpu.VMEM((rows, LANES), BF16),
            pltpu.VMEM((rows, LANES), BF16),
            pltpu.VMEM((rows, width), F32),
            pltpu.VMEM((width, rows), F32),
            pltpu.VMEM((rows, LANES), F32),
            pltpu.VMEM((LANES, rows), F32),
        ],
        n_loc * rows * 8 * width * hidden, n_loc * rows * hidden,
    )


def expert_grad_call(every, width):
    parts, hiddens, gpres, lows = zip(*every)
    shards, n_loc, n_img, columns = parts[0].shape
    rows, hidden = hiddens[0].shape[1:]
    total = rows * len(every)
    tile = hidden_tile(hidden, 1536 if total <= 512 else 384)
    tiled = pl.BlockSpec((1, rows, tile), lambda e, f: (e, 0, f))
    low = pl.BlockSpec((1, rows, 4 * LANES), lambda e, f: (e, 0, 0))
    return call(
        functools.partial(expert_grad_kernel, len(every)), (), (n_loc, hidden // tile),
        [(part, expert_rows(part.shape)) for part in parts]
        + [(array, tiled) for array in hiddens + gpres]
        + [(array, low) for array in lows],
        [
            ((n_loc, width, LANES), F32, pl.BlockSpec((1, width, LANES), lambda e, f: (e, 0, 0))),
            ((n_loc, LANES, hidden), F32, pl.BlockSpec((1, LANES, tile), lambda e, f: (e, 0, f))),
            ((n_loc, hidden, LANES), F32, pl.BlockSpec((1, tile, LANES), lambda e, f: (e, f, 0))),
            ((n_loc, LANES, width), F32, pl.BlockSpec((1, LANES, width), lambda e, f: (e, 0, 0))),
        ],
        [
            pltpu.VMEM((total, columns), BF16),
            pltpu.VMEM((4 * LANES, total), BF16),
            pltpu.VMEM((total, tile), BF16),
        ],
        4 * n_loc * total * LANES * hidden,
    )


def route_back_call(
    index, count, cotangent, x2, uo, ur, disp, comb, atts, ret, banks, shards, replicas
):
    n_img, n_tok, width = cotangent.shape
    total, n_exp = x2.shape[1], disp.shape[1]
    rows = width // shards
    unit = 16 * replicas
    pack_rows = -(-(7 * rows + n_exp // shards) // unit) * unit - 4 * rows
    each = several(n_img, IMAGES_ROUTE)
    here = functools.partial(per_image, images=each)
    return call(
        functools.partial(route_back_kernel, n_exp), (index, count), (n_img // each,),
        [
            (cotangent, here(n_tok, width)),
            (x2, here(total, width)),
            (uo, here(total, LANES)),
            (ur, here(total, LANES)),
            (disp, here(n_exp, total)),
            (comb, here(n_exp, total)),
        ]
        + [(att, here(total, GROUP)) for att in atts]
        + [(ret, once(ret.shape))]
        + [(bank, once(bank.shape)) for bank in banks],
        [
            ((n_img, n_tok, width), BF16, here(n_tok, width)),
            ((n_img, total, width), BF16, here(total, width)),
            ((n_img, total, width), BF16, here(total, width)),
            ((shards, pack_rows, LANES), BF16, whole((shards, pack_rows, LANES))),
        ],
        [
            pltpu.VMEM((each * total, width), F32),
            pltpu.VMEM((2 * width // LANES * n_exp * n_img + n_img, LANES), F32),
            pltpu.VMEM((LANES, width), F32),
            pltpu.VMEM((LANES, width), F32),
            pltpu.VMEM((LANES, width), F32),
            pltpu.VMEM((n_exp, LANES), F32),
        ],
        n_img * total * 2 * width * (width + 6 * LANES),
    )


def attention_back_call(place, index, qkvs, probs, gatt, uq, h1, bt, others):
    n_img, total, width = h1.shape
    groups = len(qkvs)
    shards = others.shape[0]
    each = several(n_img, IMAGES_BACK)
    here = functools.partial(per_image, images=each)
    pack = (shards, 4 * width // shards + others.shape[1], LANES)
    half = (shards, pack[1] // 2, LANES)
    return call(
        functools.partial(attention_back_kernel, groups), (place, index), (n_img // each,),
        [(qkv, here(total, 3 * GROUP)) for qkv in qkvs]
        + [(prob, here(GROUP // HEAD_DIM, total, total)) for prob in probs]
        + [
            (gatt, here(total, width)),
            (uq, here(total, LANES)),
            (h1, here(total, width)),
            (bt, whole(bt.shape)),
            (others, whole(others.shape)),
        ],
        [((n_img, total, 3 * GROUP), BF16, here(total, 3 * GROUP))] * groups
        + [((n_img, total, LANES), BF16, here(total, LANES))]
        + [(half, BF16, whole(half))] * 2,
        [
            pltpu.VMEM(pack, BF16),
            pltpu.VMEM((LANES, 3 * width), F32),
            pltpu.VMEM((LANES, width), F32),
        ],
        groups * attention_flops(n_img, total, LANES, 5), groups * n_img * total * total * 4,
    )


def input_grad_call(images, gx2, guq, gqkvs, turned):
    n_img, n_tok, width = images.shape
    total = gx2.shape[1]
    each = several(n_img, IMAGES_LAST)
    here = functools.partial(per_image, images=each)
    out = call(
        input_grad_kernel, (), (n_img // each,),
        [
            (images, here(n_tok, width)),
            (gx2, here(total, width)),
            (guq, here(total, LANES)),
            (turned, once(turned.shape)),
        ]
        + [(gqkv, here(total, 3 * GROUP)) for gqkv in gqkvs],
        [((images.size // LANES, LANES), F32, whole((images.size // LANES, LANES)))],
        [pltpu.VMEM((each * total, width), F32)],
        n_img * total * 2 * width * (3 * width + LANES),
    )[0]
    out = out.reshape(n_tok, width // LANES, n_img, LANES).transpose(2, 0, 1, 3)
    return out.reshape(n_img, n_tok, width)


def turn_call(place, banks, packs):
    width = banks[0].shape[0]
    shapes = [(3 * width + LANES, width), (width, width + LANES), (LANES, width), (LANES, width)]
    return call(
        functools.partial(turn_kernel, tuple(pack[1] for pack in packs)), (place,), (1,),
        [(bank, once(bank.shape)) for bank in banks]
        + [(chunk, once(chunk.shape)) for pack in packs for chunk in pack[0]],
        [(shape, BF16, once(shape)) for shape in shapes],
        [pltpu.VMEM((width, pack[2]), BF16) for pack in packs],
        8 * width * width,
    )


def swap(array, axis, size, bit):
    return lax.ppermute(array, axis, [(i, i ^ bit) for i in range(size)])


def tie(*arrays):
    return lax.optimization_barrier(arrays)


def over_shard(spread, lines=None):
    own = lax.all_to_all(
        spread, "shard", split_axis=0, concat_axis=0, tiled=True, axis_index_groups=lines
    )
    return own.reshape(-1, spread.shape[2])


def reduce_pack(keep, give, replicas, beside_first, beside_swap, beside_spread):
    where = lax.axis_index("replica")
    bits = []
    bit = 1
    first_work = swap_work = ()
    while bit < replicas:
        got = swap(give, "replica", replicas, bit)
        if bit == 1:
            got, *first_work = tie(got, *beside_first())
        if 2 * bit == replicas:
            got, *swap_work = tie(got, *beside_swap())
        pack = (keep.astype(F32) + got.astype(F32)).astype(BF16)
        bits.append(bit)
        bit *= 2
        if bit < replicas:
            half = pack.shape[1] // 2
            side = (where // bit) % 2
            keep = lax.dynamic_slice_in_dim(pack, side * half, half, axis=1)
            give = lax.dynamic_slice_in_dim(pack, (1 - side) * half, half, axis=1)
    landed = lax.all_to_all(pack, "shard", split_axis=0, concat_axis=0, tiled=True)
    landed, *spread_work = tie(landed, *beside_spread(*first_work))
    total = jnp.sum(landed.astype(F32), axis=0).astype(BF16)
    for bit in reversed(bits):
        got = swap(total, "replica", replicas, bit)
        side = (where // bit) % 2
        total = jnp.where(
            side == 0,
            jnp.concatenate([total, got], axis=0),
            jnp.concatenate([got, total], axis=0),
        )
    return total, first_work, swap_work, spread_work


def per_device(
    replicas,
    shards,
    images,
    image_adapter_index,
    device_image_count,
    cotangent,
    query_key_value_weight,
    frozen_output_weight,
    frozen_dispatch_weight,
    query_key_value_first,
    query_key_value_second,
    output_adapter_first,
    output_adapter_second,
    dispatch_adapter_first,
    dispatch_adapter_second,
    frozen_up_weight,
    frozen_down_weight,
    up_adapter_first,
    up_adapter_second,
    down_adapter_first,
    down_adapter_second,
):
    n_img, n_tok, width = images.shape
    total = -(-n_tok // 16) * 16
    rows = width // shards
    n_loc = frozen_up_weight.shape[0]
    n_exp = n_loc * shards
    groups = width // GROUP
    quarter = lax.axis_index("replica") % 4
    place = jnp.stack(
        [quarter, lax.axis_index("shard") % 2, lax.axis_index("replica")]
    ).astype(jnp.int32)
    by_axis = shards == 2 * STRIPS and replicas == 4

    spread01 = pack_call(
        place,
        (
            query_key_value_weight, query_key_value_first, query_key_value_second.T,
            output_adapter_first, dispatch_adapter_first, output_adapter_second.T,
            frozen_dispatch_weight.T,
        ),
        STRIPS if by_axis else shards,
    )
    spread23 = later_pack_call(
        place, (query_key_value_weight, frozen_output_weight, dispatch_adapter_second.T), shards
    )
    near = functools.partial(swap, axis="replica", size=replicas, bit=1)
    far = functools.partial(swap, axis="replica", size=replicas, bit=2)
    beside = functools.partial(swap, axis="shard", size=shards, bit=1)
    cut = (width + 6 * LANES) // 4

    h1 = norm_call(images, cotangent, total)
    if by_axis:
        lines = [[2 * strip + side for strip in range(STRIPS)] for side in range(2)]
        own01, spread23, h1 = tie(over_shard(spread01, lines), spread23, h1)
        own0, own1 = own01[:, :cut], own01[:, cut:]
        beside0, far0, own1 = tie(beside(own0), far(own0), own1)
        corner0, beside1, far1 = beside(far0), beside(own1), far(own1)
        corner0, far1, spread23 = tie(corner0, far1, spread23)
        held0 = [(own0, 0, 0), (beside0, 0, 1), (far0, 2, 0), (corner0, 2, 1)]
        held1 = [(own1, 0, 0), (beside1, 0, 1), (far1, 2, 0), (beside(far1), 2, 1)]
    else:
        own01, spread23, h1 = tie(over_shard(spread01), spread23, h1)
        own0, own1 = own01[:, :cut], own01[:, cut:]
        held0 = [(own0, 0, None), (far(own0), 2, None)]
        held1 = [(own1, 0, None), (far(own1), 2, None)]
    own23 = over_shard(spread23)

    def four_pieces(held, columns):
        layout = [(replica, side, 0) for _, replica, side in held]
        layout += [(replica ^ 1, side, 0) for _, replica, side in held]
        chunks = [chunk for chunk, _, _ in held] + [near(chunk) for chunk, _, _ in held]
        return tuple(chunks), (4, tuple(layout)), columns

    pack0 = four_pieces(held0, width + 6 * LANES)
    qkv0, att0, prob0, uq, bank_a, bank_bt, bank_ao, bank_ra = first_attention_call(
        place, image_adapter_index, h1, pack0, n_tok, shards
    )
    beside1, last1, uq, own23 = tie(held1[1][0], held1[-1][0], uq, own23)
    held1[1] = (beside1,) + held1[1][1:]
    held1[-1] = (last1,) + held1[-1][1:]
    pack1 = four_pieces(held1, width + 2 * LANES)
    own2, own3 = own23[:, : width // 2], own23[:, width // 2 :]
    far3 = far(own3)
    qkv1, att1, prob1, bank_bo, bank_wr = next_attention_call(
        place, h1, uq, bank_bt, pack1, n_tok, 1, 2
    )
    att1, uq, own2, own3, far3 = tie(att1, uq, own2, own3, far3)
    pack2 = ((own2, near(own2)), (2, ((0, None, 0), (1, None, 0))), width)
    qkv2, att2, prob2 = next_attention_call(place, h1, uq, bank_bt, pack2, n_tok, 2, 0)
    pack3 = four_pieces([(own3, 0, None), (far3, 2, None)], width + 2 * LANES)
    packs = (pack0, pack1, pack2, pack3)
    atts = (att0, att1, att2)
    x2, uo, ur, disp, comb, sg, bank_wrt, bank_rb = route_call(
        place, image_adapter_index, device_image_count, images, cotangent, atts,
        (bank_ao, bank_bo, bank_ra, bank_wr), packs[3], n_exp, total, shards,
    )

    landed = lax.all_to_all(sg, "shard", split_axis=0, concat_axis=0, tiled=True)
    landed, *turned = tie(landed, *turn_call(place, (bank_ao, bank_bo, bank_ra), packs))
    turned_qkv, turned_out, turned_first, turned_route = turned
    weights = (
        frozen_up_weight, frozen_down_weight, up_adapter_first, up_adapter_second,
        down_adapter_first, down_adapter_second,
    )
    far_landed = [swap(landed, "replica", replicas, bit) for bit in range(2, replicas, 2)]
    ret, *kept = expert_call(landed, weights)
    ret, *far_landed = tie(ret, *far_landed)
    back = lax.all_to_all(ret, "shard", split_axis=0, concat_axis=0, tiled=True)
    every = [(landed, *kept)]
    for number, bit in enumerate(range(2, replicas, 2)):
        far_kept = [swap(array, "replica", replicas, bit) for array in kept]
        every.append((far_landed[number], *far_kept))

    block_out, gx2, gatt, out_pack = route_back_call(
        image_adapter_index, device_image_count, cotangent, x2, uo, ur, disp, comb, atts, back,
        (bank_wrt, bank_rb, turned_out, turned_first, turned_route), shards, replicas,
    )
    gatt, *lows = tie(gatt, *[row[3] for row in every])
    held = [array for row, low in zip(every, lows) for array in (*row[:3], low)]
    *gqkvs, guq, keep, give = attention_back_call(
        place, image_adapter_index, (qkv0, qkv1, qkv2), (prob0, prob1, prob2), gatt, uq, h1, bank_bt, out_pack
    )

    def expert_grads(block, *arrays):
        arrays = list(arrays) + [swap(array, "replica", replicas, 1) for array in arrays]
        rows_of = [tuple(arrays[place : place + 4]) for place in range(0, len(arrays), 4)]
        return expert_grad_call(rows_of, width)

    summed, (block_out, *_), (input_grad,), grads = reduce_pack(
        keep, give, replicas,
        lambda: (block_out.transpose(1, 0, 2), *held),
        lambda: (input_grad_call(images, gx2, guq, gqkvs, turned_qkv),),
        expert_grads,
    )
    block_out = block_out.transpose(1, 0, 2)
    summed = summed.astype(F32)
    return (
        block_out,
        input_grad,
        summed[3 * rows : 4 * rows],
        summed[: 3 * rows].T,
        summed[4 * rows : 5 * rows],
        summed[5 * rows : 6 * rows].T,
        summed[6 * rows : 7 * rows],
        summed[7 * rows : 7 * rows + n_loc].T,
        *grads,
    )


def solution(mesh):
    images = P(("replica", "shard"), None, None)
    each = P(("replica", "shard"))
    by_row, by_column, by_expert = P("shard", None), P(None, "shard"), P("shard", None, None)
    in_specs = (
        (images, each, each, images)
        + (by_row, by_row, by_row)
        + (by_row, by_column) * 3
        + (by_expert,) * 6
    )
    out_specs = (images, images) + (by_row, by_column) * 3 + (by_expert,) * 4
    return jax.shard_map(
        functools.partial(per_device, mesh.shape["replica"], mesh.shape["shard"]),
        mesh=mesh,
        in_specs=in_specs,
        out_specs=out_specs,
        check_vma=False,
    )
```
